32 devices in a mesh: groups: 2 (over x), mem: 16 (over z, y, core).
Axes of the slice: x: 2, y: 2, z: 4, core: 2. Of those that a mesh axis runs over, the one named last changes fastest.
Arguments:
- tokens: bfloat16 [8192, 2048], P(('groups', 'mem')), parts along dimension 0, may hold values from -6 to 6
- cotangent: bfloat16 [8192, 2048], P(('groups', 'mem')), parts along dimension 0, may hold values from -6 to 6
- w_query: bfloat16 [2048, 1024], P(None, 'mem'), may hold values from -0.125 to 0.125
- key_row: bfloat16 [1024, 256], P('mem'), may hold values from -0.375 to 0.375
- key_col: bfloat16 [1024, 256], P('mem'), may hold values from -0.375 to 0.375
- tucker_core: float32 [2, 2], replicated, may hold values from -3 to 3
- table: bfloat16 [1048576, 512], P('mem'), may hold values from -6 to 6
- w_proj: bfloat16 [4, 512, 2048], P(None, None, 'mem'), may hold values from -0.125 to 0.125
- send_ids: int32 [32, 16, 32], P(('groups', 'mem')), parts along dimension 0, may hold values from -1 to 65535, as said below
- pick_slot: int32 [8192, 32], P(('groups', 'mem')), parts along dimension 0, may hold values from 0 to 511, as said below
Outputs:
- memory_out: bfloat16 [8192, 2048], P(('groups', 'mem')), parts along dimension 0
- token_grad: bfloat16 [8192, 2048], P(('groups', 'mem')), parts along dimension 0
The draws below stay inside these ranges and needn't reach their ends.
There are 2 independent parts, one for each index of `groups`. The reference program is written for one: setup_inputs(seed, part) draws one part's arguments, and reference() takes and returns one part's arrays. A program takes and returns all parts, laid end to end along the dimension named above; an argument that names none is the same for every part. Nothing has to cross between parts.
Inputs may be any that keep to these rules, and one draw needn't show every extreme that they name: send_ids[s, d, j] is -1 or an owner-local row; in each (s, d) the first 1 to 32 entries are distinct rows and the rest are -1; in every draw one owner receives 32 rows from every device, and the last device requests 32 rows from the last owner. pick_slot[t, k] = d * 32 + j names an entry send_ids[s, d, j] that is not -1, where s = t // 256.
All inputs are finite; a program needn't handle non-finite values.
Results may differ from the reference program's by a relative error of at most 0.012.
The reference program's roundings to bfloat16 on the way (of `queries`, `mix_weights`, `mixed_values`, `value_grad`, `row_grad` and `query_grad`) count: a program that leaves them out, or rounds other values in their place, can miss the bound.
Values may be sent and summed in bfloat16 or wider, within the bound.
No kernel may reach another device: no remote copies, remote signals or barrier semaphores. Data moves between devices by JAX's collectives and lax.ppermute only.
A program may use at most 192 MiB of HBM per device.

```python
import jax
import jax.numpy as jnp
from jax import lax

D = 2048
KW = 256
NKEY = 1024
V = 512
RANK = 2
PROJ = 4
KTOP = 32
TOK_DEV = 256
CAP = 32
TOKENS = 4096
TABLE = 1048576
ROWS_DEV = 65536
N_MEM = 16


def shared_counts(key):
    hottest = jax.random.randint(jax.random.fold_in(key, 5), (), 0, N_MEM)
    first = jax.random.randint(jax.random.fold_in(key, 6), (N_MEM, N_MEM), 0, CAP)
    second = jax.random.randint(jax.random.fold_in(key, 7), (N_MEM, N_MEM), 0, CAP)
    counts = CAP // 2 + first * second // (2 * CAP)
    columns = jnp.arange(N_MEM)[None, :]
    rows = jnp.arange(N_MEM)[:, None]
    filled = (columns == hottest) | (rows == N_MEM - 1) & (columns == N_MEM - 1)
    return (jnp.where(filled, CAP, counts).astype(jnp.int32), hottest)


def draw_send_ids(key, part):
    counts, hottest = shared_counts(key)
    key = jax.random.fold_in(key, 11)
    stride = max(1, ROWS_DEV // CAP)
    starting = jax.random.randint(jax.random.fold_in(key, 1), (N_MEM, N_MEM, 1), 0, ROWS_DEV)
    starting = starting.at[0, hottest, 0].set(ROWS_DEV - 1)
    jitter = jax.random.randint(jax.random.fold_in(key, 2), (N_MEM, N_MEM, CAP), 0, stride)
    jitter = jitter.at[0, hottest, 0].set(0)
    positions = jnp.arange(CAP)[None, None, :]
    chosen = (starting + positions * stride + jitter) % ROWS_DEV
    return jnp.where(positions < counts[:, :, None], chosen, -1).astype(jnp.int32)


def draw_pick_slot(key, part):
    counts, hottest = shared_counts(key)
    key = jax.random.fold_in(key, 12)
    owners = jax.random.randint(jax.random.fold_in(key, 1), (TOKENS, KTOP), 0, N_MEM)
    source = (jnp.arange(TOKENS) // TOK_DEV)[:, None]
    raw_draw = jax.random.randint(jax.random.fold_in(key, 2), (TOKENS, KTOP), 0, CAP * 1024)
    live = counts[source, owners]
    slots = (owners * CAP + raw_draw % live).astype(jnp.int32)
    slots = slots.at[0, 0].set(0)
    slots = slots.at[TOKENS - 1, KTOP - 1].set(N_MEM * CAP - 1)
    return slots.astype(jnp.int32)


def steps_of(rng, dims, pieces, low, top_value):
    loudness = 1.0
    for axis_at, shards_of in pieces:
        heights = jax.random.uniform(jax.random.fold_in(jax.random.fold_in(rng, 6), axis_at), (shards_of,), jnp.float32, low / len(pieces), top_value / len(pieces))
        loudness = loudness * jnp.repeat(jnp.exp(heights), dims[axis_at] // shards_of).reshape((-1,) + (1,) * (len(dims) - 1 - axis_at))
    return loudness


def bell_draw(rng, extent, scale, limit, split=(), held_as=jnp.bfloat16):
    values = jax.random.normal(rng, extent, jnp.float32) * scale
    if len(split) > 0:
        values = steps_of(rng, extent, split, -0.22, 0.18) * values
    return jnp.clip(values, min=-limit, max=limit).astype(held_as)


def setup_inputs(seed: int = 0, part: int = 0) -> dict:
    splits = jax.random.split(jax.random.key(seed), 11)
    part_splits = jax.random.split(jax.random.fold_in(splits[10], part), 11)
    tokens = bell_draw(part_splits[0], (TOKENS, D), 1.0, 6.0, ((0, 16),))
    cotangent = bell_draw(part_splits[1], (TOKENS, D), 1.0, 6.0, ((0, 16),))
    w_query = bell_draw(splits[2], (D, 2 * RANK * KW), D ** -0.5, 0.125, ((1, 16),))
    key_row = bell_draw(splits[3], (NKEY, KW), KW ** -0.5, 0.375, ((0, 16),))
    key_col = bell_draw(splits[4], (NKEY, KW), KW ** -0.5, 0.375, ((0, 16),))
    tucker_core = bell_draw(splits[5], (RANK, RANK), 1.0, 3.0, (), jnp.float32)
    table = bell_draw(splits[6], (TABLE, V), 1.0, 6.0, ((0, 16),))
    w_proj = bell_draw(splits[7], (PROJ, V, D), (PROJ * V) ** -0.5, 0.125, ((2, 16),))
    send_ids = draw_send_ids(jax.random.fold_in(jax.random.fold_in(splits[10], part), 71), part)
    pick_slot = draw_pick_slot(jax.random.fold_in(jax.random.fold_in(splits[10], part), 71), part)
    return {"tokens": tokens, "cotangent": cotangent, "w_query": w_query, "key_row": key_row, "key_col": key_col, "tucker_core": tucker_core, "table": table, "w_proj": w_proj, "send_ids": send_ids, "pick_slot": pick_slot}


def block_pass(parts, w_query, key_row, key_col, tucker_core, table, w_proj):
    tokens_b, cot_b, slot_b, wanted_b = parts
    owner_index = (slot_b // CAP).astype(jnp.int32)
    local_row = jnp.take(wanted_b.reshape(-1), slot_b.astype(jnp.int32), axis=0).astype(jnp.int32)
    global_row = (owner_index * ROWS_DEV + local_row).astype(jnp.int32)
    row_pick = (global_row // NKEY).astype(jnp.int32)
    col_pick = (global_row % NKEY).astype(jnp.int32)
    proj_pick = (col_pick % PROJ).astype(jnp.int32)
    gathered = jnp.take(table, global_row, axis=0).astype(jnp.float32)
    key_rows = jnp.take(key_row, row_pick, axis=0).astype(jnp.float32)
    key_cols = jnp.take(key_col, col_pick, axis=0).astype(jnp.float32)
    queries = jnp.dot(tokens_b, w_query, preferred_element_type=jnp.float32).astype(jnp.bfloat16)
    queries = queries.reshape(TOK_DEV, 2 * RANK, KW).astype(jnp.float32)
    row_scores = jnp.einsum('trc,tkc->trk', queries[:, :RANK], key_rows)
    col_scores = jnp.einsum('trc,tkc->trk', queries[:, RANK:], key_cols)
    col_mixed = jnp.einsum('rs,tsk->trk', tucker_core, col_scores, precision=lax.Precision.HIGHEST)
    row_mixed = jnp.einsum('trk,rs->tsk', row_scores, tucker_core, precision=lax.Precision.HIGHEST)
    score = jnp.sum(row_scores * col_mixed, axis=1)
    gate_value = jax.nn.sigmoid(score)
    one_hot = (proj_pick[:, :, None] == jnp.arange(PROJ, dtype=jnp.int32)[None, None, :]).astype(jnp.float32)
    mix_weights = (gate_value[:, :, None] * one_hot).astype(jnp.bfloat16).astype(jnp.float32)
    mixed_values = jnp.einsum('tke,tkv->tev', mix_weights, gathered).astype(jnp.bfloat16)
    memory_out = jnp.einsum('tev,evd->td', mixed_values.astype(jnp.float32), w_proj.astype(jnp.float32)).astype(jnp.bfloat16)
    value_grad = jnp.einsum('td,evd->tev', cot_b.astype(jnp.float32), w_proj.astype(jnp.float32)).astype(jnp.bfloat16)
    per_proj = jnp.einsum('tkv,tev->tke', gathered, value_grad.astype(jnp.float32))
    pick_grad = jnp.sum(per_proj * one_hot, axis=2)
    score_grad = pick_grad * gate_value * (1.0 - gate_value)
    row_grad = (score_grad[:, None, :] * col_mixed).astype(jnp.bfloat16).astype(jnp.float32)
    col_grad = (score_grad[:, None, :] * row_mixed).astype(jnp.bfloat16).astype(jnp.float32)
    grad_rows = jnp.einsum('trk,tkc->trc', row_grad, key_rows)
    grad_cols = jnp.einsum('trk,tkc->trc', col_grad, key_cols)
    query_grad = jnp.concatenate([grad_rows, grad_cols], axis=1).reshape(TOK_DEV, 2 * RANK * KW).astype(jnp.bfloat16)
    token_grad = lax.dot_general(query_grad, w_query, (((1,), (1,)), ((), ())), preferred_element_type=jnp.float32).astype(jnp.bfloat16)
    return memory_out, token_grad


def reference(tokens, cotangent, w_query, key_row, key_col, tucker_core, table, w_proj, send_ids, pick_slot):
    def one_device(parts):
        return block_pass(parts, w_query, key_row, key_col, tucker_core, table, w_proj)

    stacked = (tokens.reshape(N_MEM, TOK_DEV, D), cotangent.reshape(N_MEM, TOK_DEV, D),
               pick_slot.reshape(N_MEM, TOK_DEV, KTOP), send_ids)
    memory_out, token_grad = lax.map(one_device, stacked)
    return memory_out.reshape(TOKENS, D), token_grad.reshape(TOKENS, D)
```

```python
import jax
import jax.numpy as jnp
from jax import lax
from jax.sharding import PartitionSpec as P

F32 = jnp.float32
BF16 = jnp.bfloat16


def dot(a, b, dims):
    return lax.dot_general(a, b, (dims, ((), ())), preferred_element_type=F32)


def two_terms(x):
    high = x.astype(BF16)
    return high, (x - high.astype(F32)).astype(BF16)


def counted_dot(x, b, dims):
    high, low = two_terms(x)
    return dot(high, b, dims) + dot(low, b, dims)


def fetch_rows(requests, table):
    wanted = lax.all_to_all(requests, "mem", split_axis=0, concat_axis=0, tiled=True)
    found = jnp.take(table, jnp.maximum(wanted, 0).reshape(-1), axis=0, mode="clip")
    found = found.reshape(wanted.shape + (table.shape[1],))
    return lax.all_to_all(found, "mem", split_axis=0, concat_axis=0, tiled=True)


def shards(
    tokens, cotangent, w_query, key_row, key_col, tucker_core, table, w_proj, send_ids, pick_slot
):
    rank = tucker_core.shape[0]
    width = key_row.shape[1]
    proj_count, value_width, _ = w_proj.shape
    requests = send_ids[0]
    owners, capacity = requests.shape
    slots = owners * capacity
    query_full = lax.all_gather(w_query.T, "mem", axis=0, tiled=True)
    keys = lax.all_gather(jnp.concatenate([key_row, key_col], axis=1), "mem", axis=0, tiled=True)
    proj_full = lax.all_gather(w_proj, "mem", axis=2, tiled=True)
    nkey = keys.shape[0]

    fetched = fetch_rows(requests, table).reshape(slots, value_width)

    row_id = jnp.maximum(requests, 0) + jnp.arange(owners, dtype=jnp.int32)[:, None] * table.shape[0]
    row_id = row_id.reshape(slots, 1)
    key_at = jnp.arange(nkey, dtype=jnp.int32)[None, :]
    row_hot = (row_id // nkey == key_at).astype(BF16)
    col_hot = (row_id % nkey == key_at).astype(BF16)
    slot_row = dot(row_hot, keys[:, :width], ((1,), (0,))).astype(BF16)
    slot_col = dot(col_hot, keys[:, width:], ((1,), (0,))).astype(BF16)
    slot_proj = (row_id % nkey) % proj_count
    spread = jnp.where(
        slot_proj[:, :, None] == jnp.arange(proj_count, dtype=jnp.int32)[None, :, None],
        fetched[:, None, :], jnp.zeros((), BF16)
    ).reshape(slots, proj_count * value_width)
    counts = jnp.sum(
        (pick_slot[:, :, None] == jnp.arange(slots, dtype=jnp.int32)[None, None, :]).astype(F32), axis=1
    )

    queries = dot(tokens, query_full, ((1,), (1,))).astype(BF16)
    last = ((1,), (1,))
    row_scores = [dot(queries[:, r * width:(r + 1) * width], slot_row, last) for r in range(rank)]
    col_scores = [
        dot(queries[:, (rank + r) * width:(rank + r + 1) * width], slot_col, last) for r in range(rank)
    ]
    col_mixed = [sum(tucker_core[r, s] * col_scores[s] for s in range(rank)) for r in range(rank)]
    row_mixed = [sum(row_scores[r] * tucker_core[r, s] for r in range(rank)) for s in range(rank)]
    score = sum(row_scores[r] * col_mixed[r] for r in range(rank))
    gate = jax.nn.sigmoid(score)
    weights = counts * gate.astype(BF16).astype(F32)
    mixed = counted_dot(weights, spread, ((1,), (0,))).astype(BF16)
    memory_out = dot(mixed, proj_full.reshape(proj_count * value_width, -1), ((1,), (0,)))
    value_grad = dot(cotangent, proj_full.reshape(proj_count * value_width, -1), last).astype(BF16)
    pick_grad = dot(value_grad, spread, last)
    score_grad = pick_grad * gate * (1.0 - gate)
    blocks = []
    for mixed_scores, slot_key in ((col_mixed, slot_row), (row_mixed, slot_col)):
        for r in range(rank):
            grad = (score_grad * mixed_scores[r]).astype(BF16).astype(F32) * counts
            blocks.append(counted_dot(grad, slot_key, ((1,), (0,))).astype(BF16))
    query_grad = jnp.concatenate(blocks, axis=1)
    token_grad = dot(query_grad, query_full, ((1,), (0,)))
    return memory_out.astype(BF16), token_grad.astype(BF16)


def solution(mesh):
    in_specs = (
        P(("groups", "mem"), None),
        P(("groups", "mem"), None),
        P(None, "mem"),
        P("mem", None),
        P("mem", None),
        P(),
        P("mem", None),
        P(None, None, "mem"),
        P(("groups", "mem"), None, None),
        P(("groups", "mem"), None),
    )
    out_specs = (P(("groups", "mem"), None), P(("groups", "mem"), None))
    return jax.shard_map(shards, mesh=mesh, in_specs=in_specs, out_specs=out_specs, check_vma=False)
```

```python
import functools

import jax
import jax.numpy as jnp
from jax import lax
from jax.experimental import pallas as pl
from jax.experimental.pallas import tpu as pltpu
from jax.sharding import PartitionSpec as P

F32 = jnp.float32
BF16 = jnp.bfloat16
RING = (0, 2, 3, 1)
LAST = ((1,), (1,))
PLAIN = ((1,), (0,))
VMEM_LIMIT = 56 * 1024 * 1024


def dot(a, b, dims):
    return lax.dot_general(a, b, (dims, ((), ())), preferred_element_type=F32)


def two_terms(x):
    high = x.astype(BF16)
    return high, (x - high.astype(F32)).astype(BF16)


def counted_dot(x, b, dims):
    high, low = two_terms(x)
    return dot(high, b, dims) + dot(low, b, dims)


def fetch_rows(requests, table):
    wanted = lax.all_to_all(requests, "mem", split_axis=0, concat_axis=0, tiled=True)
    found = jnp.take(table, jnp.maximum(wanted, 0).reshape(-1), axis=0, mode="clip")
    found = found.reshape(wanted.shape + (table.shape[1],))
    return lax.all_to_all(found, "mem", split_axis=0, concat_axis=0, tiled=True)


def place(z, y, core):
    return (z * 2 + y) * 2 + core


def everywhere(move):
    pairs = []
    for z in range(4):
        for y in range(2):
            for core in range(2):
                pairs.append((place(z, y, core), place(*move(z, y, core))))
    return pairs


def next_z(x):
    step = {RING[i]: RING[(i + 1) % 4] for i in range(4)}
    return lax.ppermute(x, "mem", everywhere(lambda z, y, c: (step[z], y, c)))


def other_y(x):
    return lax.ppermute(x, "mem", everywhere(lambda z, y, c: (z, 1 - y, c)))


def other_core(x):
    return lax.ppermute(x, "mem", everywhere(lambda z, y, c: (z, y, 1 - c)))


def other_x(x):
    return lax.ppermute(x, "groups", [(0, 1), (1, 0)])


def ring_source(z, steps):
    order = jnp.array([[RING[(RING.index(a) - s) % 4] for a in range(4)] for s in range(4)], jnp.int32)
    return order[steps, z]


def gather_pieces(query_part, proj_part):
    me = lax.axis_index("mem")
    z, y, core = me // 4, (me // 2) % 2, me % 2
    x = lax.axis_index("groups")
    half = proj_part.shape[0] // 2
    proj_half = lax.dynamic_slice_in_dim(proj_part, x * half, half, axis=0)

    proj_rings, query_rings = [proj_half], [query_part]
    for _ in range(3):
        query_rings.append(next_z(query_rings[-1]))
        proj_rings.append(next_z(proj_rings[-1]))
    query_pieces, proj_pieces = [], []
    for step in range(4):
        at = ring_source(z, step)
        query_here = [(query_rings[step], at, y), (other_y(query_rings[step]), at, 1 - y)]
        query_pieces += [(a, place(at, b, core)) for a, at, b in query_here]
        query_pieces += [(other_core(a), place(at, b, 1 - core)) for a, at, b in query_here]
        near, far = proj_rings[step], other_y(proj_rings[step])
        proj_here = [(far, y * 0 + 1 - y, x), (other_x(far), 1 - y, 1 - x)]
        if step == 0:
            proj_here.append((proj_part, y, 0 * x))
        else:
            proj_here += [(near, y, x), (other_x(near), y, 1 - x)]
        proj_pieces += [(a, place(at, b, core), h * half) for a, b, h in proj_here]
        proj_pieces += [(other_core(a), place(at, b, 1 - core), h * half) for a, b, h in proj_here]
    return query_pieces, proj_pieces


def scores_kernel(
    rank, width, nkey, count, at_ref, core_ref, row_id_ref, pick_ref, tokens_ref, *refs
):
    pieces, rest = refs[:count], refs[count:]
    row_ref, col_ref, counts_ref, weights_ref, row_factor_ref, col_factor_ref, held, sems = rest
    copies = []
    for i, piece in enumerate(pieces):
        rows = piece.shape[0]
        start = pl.multiple_of(at_ref[i], rows)
        copies.append(pltpu.make_async_copy(piece, held.at[pl.ds(start, rows)], sems.at[i]))
        copies[-1].start()
    slots = row_id_ref.shape[0]
    token_rows, picks = pick_ref.shape
    lane = lax.broadcasted_iota(jnp.int32, (token_rows, slots), 1)
    pick = pick_ref[...]
    counts = jnp.zeros((token_rows, slots), F32)
    for k in range(picks):
        counts += jnp.where(pick[:, k:k + 1] == lane, 1.0, 0.0)
    counts_ref[...] = counts
    key_at = lax.broadcasted_iota(jnp.int32, (slots, nkey), 1)
    row_id = row_id_ref[...]
    row_hot = jnp.where(row_id // nkey == key_at, 1.0, 0.0).astype(BF16)
    col_hot = jnp.where(row_id % nkey == key_at, 1.0, 0.0).astype(BF16)
    for copy in copies:
        copy.wait()
    features = tokens_ref.shape[1]
    slot_row = dot(row_hot, held[:, features:features + width], PLAIN).astype(BF16)
    slot_col = dot(col_hot, held[:, features + width:features + 2 * width], PLAIN).astype(BF16)
    row_ref[...] = slot_row
    col_ref[...] = slot_col
    queries = dot(tokens_ref[...], held[:, :features], LAST).astype(BF16)
    block = [queries[:, r * width:(r + 1) * width] for r in range(2 * rank)]
    row_scores = [dot(block[r], slot_row, LAST) for r in range(rank)]
    col_scores = [dot(block[rank + r], slot_col, LAST) for r in range(rank)]
    col_mixed = [sum(core_ref[r, s] * col_scores[s] for s in range(rank)) for r in range(rank)]
    row_mixed = [sum(row_scores[r] * core_ref[r, s] for r in range(rank)) for s in range(rank)]
    score = sum(row_scores[r] * col_mixed[r] for r in range(rank))
    gate = 1.0 / (1.0 + jnp.exp(-score))
    weights_ref[...] = counts * gate.astype(BF16).astype(F32)
    slope = gate * (1.0 - gate)
    for r in range(rank):
        row_factor_ref[r] = slope * col_mixed[r]
        col_factor_ref[r] = slope * row_mixed[r]


def outputs_kernel(
    rank, width, proj_count, query_count, proj_count_pieces, query_at, proj_at, proj_row, proj_ref,
    row_ref, col_ref, counts_ref, weights_ref, row_factor_ref, col_factor_ref, fetched_ref, cot_ref, *refs
):
    query_pieces = refs[:query_count]
    proj_pieces = refs[query_count:query_count + proj_count_pieces]
    out_ref, grad_ref, query_held, proj_held, value_grad, query_grad, query_sem, proj_sem = refs[
        query_count + proj_count_pieces:
    ]
    value_width = fetched_ref.shape[1]
    features = cot_ref.shape[1]
    for part in range(proj_count):
        for i, piece in enumerate(proj_pieces):
            parts = piece.shape[0] // value_width
            if part >= parts:
                continue
            wide = piece.shape[1]
            row = pl.multiple_of(proj_row[i] + part * value_width, value_width)
            pltpu.make_async_copy(
                piece.at[pl.ds(part * value_width, value_width)],
                proj_held.at[pl.ds(row, value_width), pl.ds(pl.multiple_of(proj_at[i], wide), wide)],
                proj_sem.at[row // value_width],
            ).start()
    for i, piece in enumerate(query_pieces):
        rows = piece.shape[0]
        start = pl.multiple_of(query_at[i], rows)
        pltpu.make_async_copy(
            piece.at[:, pl.ds(0, features)], query_held.at[pl.ds(start, rows)], query_sem
        ).start()

    proj = proj_ref[...]
    fetched = fetched_ref[...]
    cot = cot_ref[...]
    pick_grad = jnp.zeros(counts_ref.shape, F32)
    for e in range(proj_count):
        block = proj_held.at[pl.ds(e * value_width, value_width)]
        pltpu.make_async_copy(block, block, proj_sem.at[e]).wait()
        grad = dot(cot, block[...], LAST).astype(BF16)
        pick_grad = jnp.where(proj == e, dot(grad, fetched, LAST), pick_grad)
    counts = counts_ref[...]
    for side, (factor, key_ref) in enumerate(((row_factor_ref, row_ref), (col_factor_ref, col_ref))):
        for r in range(rank):
            grad = (pick_grad * factor[r]).astype(BF16).astype(F32) * counts
            at = (side * rank + r) * width
            query_grad[:, at:at + width] = counted_dot(grad, key_ref[...], PLAIN).astype(BF16)
    high, low = two_terms(weights_ref[...])
    zero = jnp.zeros((), BF16)
    for e in range(proj_count):
        mixed = dot(jnp.where(proj == e, high, zero), fetched, PLAIN)
        mixed += dot(jnp.where(proj == e, low, zero), fetched, PLAIN)
        value_grad[:, e * value_width:(e + 1) * value_width] = mixed.astype(BF16)
    pltpu.make_async_copy(query_held, query_held, query_sem).wait()
    step = features // 4
    for c in range(4):
        cols = slice(c * step, (c + 1) * step)
        grad_ref[:, cols] = dot(query_grad[...], query_held[:, cols], PLAIN).astype(BF16)
        out_ref[:, cols] = dot(value_grad[...], proj_held[:, cols], PLAIN).astype(BF16)


def vmem():
    return pl.BlockSpec(memory_space=pltpu.VMEM)


def smem():
    return pl.BlockSpec(memory_space=pltpu.SMEM)


def anywhere():
    return pl.BlockSpec(memory_space=pl.ANY)


def pieces_path(tokens, cotangent, w_query, key_row, key_col, tucker_core, proj_part, fetched, row_id, slot_proj,
                pick_slot, nkey, proj_count):
    rank = tucker_core.shape[0]
    width = key_row.shape[1]
    token_rows, features = tokens.shape
    slots, value_width = fetched.shape
    query_part = jnp.concatenate([w_query.T, key_row, key_col], axis=1)
    query_pieces, proj_pieces = gather_pieces(query_part, proj_part)
    query_at = jnp.stack([at for _, at in query_pieces]) * query_part.shape[0]
    proj_at = jnp.stack([at for _, at, _ in proj_pieces]) * proj_part.shape[1]
    proj_row = jnp.stack([row for _, _, row in proj_pieces])
    query_pieces = [a for a, _ in query_pieces]
    proj_pieces = [a for a, _, _ in proj_pieces]
    params = pltpu.CompilerParams(vmem_limit_bytes=VMEM_LIMIT)
    plane = jax.ShapeDtypeStruct((token_rows, slots), F32)
    planes = jax.ShapeDtypeStruct((rank, token_rows, slots), F32)
    slot_key = jax.ShapeDtypeStruct((slots, width), BF16)
    slot_row, slot_col, counts, weights, row_factor, col_factor = pl.pallas_call(
        functools.partial(scores_kernel, rank, width, nkey, len(query_pieces)),
        out_shape=(slot_key, slot_key, plane, plane, planes, planes),
        in_specs=[smem(), smem(), vmem(), vmem(), vmem()] + [anywhere()] * len(query_pieces),
        out_specs=(vmem(),) * 6,
        scratch_shapes=[
            pltpu.VMEM((nkey, features + 2 * width), BF16),
            pltpu.SemaphoreType.DMA((len(query_pieces),)),
        ],
        compiler_params=params,
        cost_estimate=pl.CostEstimate(flops=2 * 10**9, bytes_accessed=10**7, transcendentals=10**5),
        name="scores",
    )(query_at, tucker_core, row_id[:, None], pick_slot, tokens, *query_pieces)
    return pl.pallas_call(
        functools.partial(
            outputs_kernel, rank, width, proj_count, len(query_pieces), len(proj_pieces)
        ),
        out_shape=(jax.ShapeDtypeStruct((token_rows, features), BF16),) * 2,
        in_specs=[smem()] * 3 + [vmem()] * 9 + [anywhere()] * (len(query_pieces) + len(proj_pieces)),
        out_specs=(vmem(), vmem()),
        scratch_shapes=[
            pltpu.VMEM((nkey, features), BF16),
            pltpu.VMEM((proj_count * value_width, features), BF16),
            pltpu.VMEM((token_rows, proj_count * value_width), BF16),
            pltpu.VMEM((token_rows, 2 * rank * width), BF16),
            pltpu.SemaphoreType.DMA,
            pltpu.SemaphoreType.DMA((proj_count,)),
        ],
        compiler_params=params,
        cost_estimate=pl.CostEstimate(flops=7 * 10**9, bytes_accessed=2 * 10**7, transcendentals=0),
        name="outputs",
    )(
        query_at, proj_at, proj_row, slot_proj[None, :], slot_row, slot_col, counts, weights, row_factor, col_factor,
        fetched, cotangent, *query_pieces, *proj_pieces,
    )


def whole_path(tokens, cotangent, w_query, key_row, key_col, tucker_core, proj_part, fetched, row_id, slot_proj,
               pick_slot, nkey, proj_count):
    rank = tucker_core.shape[0]
    width = key_row.shape[1]
    slots = row_id.shape[0]
    query_full = lax.all_gather(w_query.T, "mem", axis=0, tiled=True)
    keys = lax.all_gather(jnp.concatenate([key_row, key_col], axis=1), "mem", axis=0, tiled=True)
    proj_full = lax.all_gather(proj_part, "mem", axis=1, tiled=True)
    key_at = jnp.arange(nkey, dtype=jnp.int32)[None, :]
    row_hot = ((row_id // nkey)[:, None] == key_at).astype(BF16)
    col_hot = ((row_id % nkey)[:, None] == key_at).astype(BF16)
    slot_row = dot(row_hot, keys[:, :width], PLAIN).astype(BF16)
    slot_col = dot(col_hot, keys[:, width:], PLAIN).astype(BF16)
    spread = jnp.where(
        slot_proj[:, None, None] == jnp.arange(proj_count, dtype=jnp.int32)[None, :, None],
        fetched[:, None, :], jnp.zeros((), BF16)
    ).reshape(slots, -1)
    counts = jnp.sum(
        (pick_slot[:, :, None] == jnp.arange(slots, dtype=jnp.int32)[None, None, :]).astype(F32), axis=1
    )
    queries = dot(tokens, query_full, LAST).astype(BF16)
    row_scores = [dot(queries[:, r * width:(r + 1) * width], slot_row, LAST) for r in range(rank)]
    col_scores = [
        dot(queries[:, (rank + r) * width:(rank + r + 1) * width], slot_col, LAST) for r in range(rank)
    ]
    col_mixed = [sum(tucker_core[r, s] * col_scores[s] for s in range(rank)) for r in range(rank)]
    row_mixed = [sum(row_scores[r] * tucker_core[r, s] for r in range(rank)) for s in range(rank)]
    score = sum(row_scores[r] * col_mixed[r] for r in range(rank))
    gate = jax.nn.sigmoid(score)
    weights = counts * gate.astype(BF16).astype(F32)
    mixed = counted_dot(weights, spread, PLAIN).astype(BF16)
    memory_out = dot(mixed, proj_full, PLAIN)
    value_grad = dot(cotangent, proj_full, LAST).astype(BF16)
    pick_grad = dot(value_grad, spread, LAST)
    score_grad = pick_grad * gate * (1.0 - gate)
    blocks = []
    for mixed_scores, slot_key in ((col_mixed, slot_row), (row_mixed, slot_col)):
        for r in range(rank):
            grad = (score_grad * mixed_scores[r]).astype(BF16).astype(F32) * counts
            blocks.append(counted_dot(grad, slot_key, PLAIN).astype(BF16))
    query_grad = jnp.concatenate(blocks, axis=1)
    token_grad = dot(query_grad, query_full, PLAIN)
    return memory_out.astype(BF16), token_grad.astype(BF16)


def shards(
    mem, tokens, cotangent, w_query, key_row, key_col, tucker_core, table, w_proj, send_ids, pick_slot
):
    proj_count, value_width, _ = w_proj.shape
    requests = send_ids[0]
    owners, capacity = requests.shape
    slots = owners * capacity
    nkey = key_row.shape[0] * mem
    fetched = fetch_rows(requests, table).reshape(slots, value_width)
    row_id = jnp.maximum(requests, 0) + jnp.arange(owners, dtype=jnp.int32)[:, None] * table.shape[0]
    row_id = row_id.reshape(slots)
    slot_proj = (row_id % nkey) % proj_count
    proj_part = w_proj.reshape(proj_count * value_width, -1)
    path = pieces_path if mem == 16 else whole_path
    return path(tokens, cotangent, w_query, key_row, key_col, tucker_core, proj_part, fetched, row_id, slot_proj,
                pick_slot, nkey, proj_count)


def solution(mesh):
    in_specs = (
        P(("groups", "mem"), None),
        P(("groups", "mem"), None),
        P(None, "mem"),
        P("mem", None),
        P("mem", None),
        P(),
        P("mem", None),
        P(None, None, "mem"),
        P(("groups", "mem"), None, None),
        P(("groups", "mem"), None),
    )
    out_specs = (P(("groups", "mem"), None), P(("groups", "mem"), None))
    body = functools.partial(shards, mesh.shape["mem"])
    return jax.shard_map(body, mesh=mesh, in_specs=in_specs, out_specs=out_specs, check_vma=False)
```

```python
import functools

import jax
import jax.numpy as jnp
from jax import lax
from jax.experimental import pallas as pl
from jax.experimental.pallas import tpu as pltpu
from jax.sharding import PartitionSpec as P

F32 = jnp.float32
BF16 = jnp.bfloat16
LANES = 128
LAST = ((1,), (1,))
PLAIN = ((1,), (0,))
VMEM_LIMIT = 56 * 1024 * 1024


def dot(a, b, dims):
    return lax.dot_general(a, b, (dims, ((), ())), preferred_element_type=F32)


def two_terms(x):
    high = x.astype(BF16)
    return high, (x - high.astype(F32)).astype(BF16)


def counted_dot(x, b, dims):
    high, low = two_terms(x)
    return dot(high, b, dims) + dot(low, b, dims)


def fetch_rows(requests, table):
    wanted = lax.all_to_all(requests, "mem", split_axis=0, concat_axis=0, tiled=True)
    found = jnp.take(table, jnp.maximum(wanted, 0).reshape(-1), axis=0, mode="clip")
    found = found.reshape(wanted.shape + (table.shape[1],))
    return lax.all_to_all(found, "mem", split_axis=0, concat_axis=0, tiled=True)


def own_half(w_query, key_row, key_col, proj_part):
    x = lax.axis_index("groups")
    columns = w_query.shape[1]
    proj = proj_part.reshape(-1, columns, LANES)
    query = jnp.concatenate([w_query.T, key_row, key_col], axis=1)
    query = query.reshape(columns, -1, LANES).transpose(1, 0, 2)
    halves = [lax.dynamic_slice_in_dim(a, x * (a.shape[0] // 2), a.shape[0] // 2, axis=0) for a in (proj, query)]
    return jnp.concatenate(halves, axis=0)


def copy_query(gathered, held, sem, blocks):
    half = held.shape[0] // 2
    total = gathered.shape[1]
    count = gathered.shape[0] // 2
    columns = gathered.shape[2]
    for x in range(2):
        taken = max(0, min(half, blocks - x * half))
        for m in range(count):
            pltpu.make_async_copy(
                gathered.at[x * count + m, pl.ds(total - half, taken)],
                held.at[pl.ds(x * half, taken), pl.ds(m * columns, columns)],
                sem,
            ).start()


def wait_all(held, sem):
    pltpu.make_async_copy(held, held, sem).wait()


def wide(held, first, last):
    return jnp.concatenate([held[j] for j in range(first, last)], axis=1)


def scores_kernel(
    rank, width, nkey, core_ref, row_id_ref, pick_ref, tokens_ref, gathered_ref,
    row_ref, col_ref, counts_ref, weights_ref, row_factor_ref, col_factor_ref, held, sem
):
    copy_query(gathered_ref, held, sem, held.shape[0])
    slots = row_id_ref.shape[0]
    token_rows, picks = pick_ref.shape
    lane = lax.broadcasted_iota(jnp.int32, (token_rows, slots), 1)
    pick = pick_ref[...]
    counts = jnp.zeros((token_rows, slots), F32)
    for k in range(picks):
        counts += jnp.where(pick[:, k:k + 1] == lane, 1.0, 0.0)
    counts_ref[...] = counts
    key_at = lax.broadcasted_iota(jnp.int32, (slots, nkey), 1)
    row_id = row_id_ref[...]
    row_hot = jnp.where(row_id // nkey == key_at, 1.0, 0.0).astype(BF16)
    col_hot = jnp.where(row_id % nkey == key_at, 1.0, 0.0).astype(BF16)
    wait_all(held, sem)
    key = tokens_ref.shape[1] // LANES
    step = width // LANES
    slot_row = dot(row_hot, wide(held, key, key + step), PLAIN).astype(BF16)
    slot_col = dot(col_hot, wide(held, key + step, key + 2 * step), PLAIN).astype(BF16)
    row_ref[...] = slot_row
    col_ref[...] = slot_col
    queries = dot(tokens_ref[...], wide(held, 0, key), LAST).astype(BF16)
    block = [queries[:, r * width:(r + 1) * width] for r in range(2 * rank)]
    row_scores = [dot(block[r], slot_row, LAST) for r in range(rank)]
    col_scores = [dot(block[rank + r], slot_col, LAST) for r in range(rank)]
    col_mixed = [sum(core_ref[r, s] * col_scores[s] for s in range(rank)) for r in range(rank)]
    row_mixed = [sum(row_scores[r] * core_ref[r, s] for r in range(rank)) for s in range(rank)]
    score = sum(row_scores[r] * col_mixed[r] for r in range(rank))
    gate = 1.0 / (1.0 + jnp.exp(-score))
    weights_ref[...] = counts * gate.astype(BF16).astype(F32)
    slope = gate * (1.0 - gate)
    for r in range(rank):
        row_factor_ref[r] = slope * col_mixed[r]
        col_factor_ref[r] = slope * row_mixed[r]


def outputs_kernel(
    rank, width, proj_count, proj_ref, row_ref, col_ref, counts_ref, weights_ref, row_factor_ref, col_factor_ref,
    fetched_ref, cot_ref, gathered_ref, out_ref, grad_ref, query_held, proj_held, mixed_values, query_grad,
    query_sem, proj_sem
):
    value_width = fetched_ref.shape[1]
    features = cot_ref.shape[1]
    columns = proj_held.shape[1]
    parts = value_width // columns
    count = gathered_ref.shape[0] // 2
    for e in range(proj_count):
        x, inner = divmod(e, proj_count // 2)
        for m in range(count):
            pltpu.make_async_copy(
                gathered_ref.at[x * count + m, pl.ds(inner * parts, parts)],
                proj_held.at[pl.ds(e * parts, parts), :, pl.ds(m * LANES, LANES)],
                proj_sem.at[e],
            ).start()
    copy_query(gathered_ref, query_held, query_sem, features // LANES)

    proj = proj_ref[...]
    fetched = fetched_ref[...]
    cot = cot_ref[...]
    pick_grad = jnp.zeros(counts_ref.shape, F32)
    for e in range(proj_count):
        block = proj_held.at[pl.ds(e * parts, parts)]
        wait_all(block, proj_sem.at[e])
        grad = dot(cot, block[...].reshape(value_width, features), LAST).astype(BF16)
        pick_grad = jnp.where(proj == e, dot(grad, fetched, LAST), pick_grad)
    counts = counts_ref[...]
    for side, (factor, key_ref) in enumerate(((row_factor_ref, row_ref), (col_factor_ref, col_ref))):
        for r in range(rank):
            grad = (pick_grad * factor[r]).astype(BF16).astype(F32) * counts
            at = (side * rank + r) * width
            query_grad[:, at:at + width] = counted_dot(grad, key_ref[...], PLAIN).astype(BF16)
    high, low = two_terms(weights_ref[...])
    zero = jnp.zeros((), BF16)
    for e in range(proj_count):
        mixed = dot(jnp.where(proj == e, high, zero), fetched, PLAIN)
        mixed += dot(jnp.where(proj == e, low, zero), fetched, PLAIN)
        mixed_values[:, e * value_width:(e + 1) * value_width] = mixed.astype(BF16)
    queried = query_held.at[pl.ds(0, features // LANES)]
    wait_all(queried, query_sem)
    blocks = features // LANES // 4
    for c in range(4):
        cols = slice(c * blocks * LANES, (c + 1) * blocks * LANES)
        grad_ref[:, cols] = dot(query_grad[...], wide(query_held, c * blocks, (c + 1) * blocks), PLAIN).astype(BF16)
        held = proj_held[:, :, cols].reshape(proj_count * value_width, blocks * LANES)
        out_ref[:, cols] = dot(mixed_values[...], held, PLAIN).astype(BF16)


def vmem():
    return pl.BlockSpec(memory_space=pltpu.VMEM)


def smem():
    return pl.BlockSpec(memory_space=pltpu.SMEM)


def anywhere():
    return pl.BlockSpec(memory_space=pl.ANY)


def halves_path(tokens, cotangent, w_query, key_row, key_col, tucker_core, proj_part, fetched, row_id, slot_proj,
                pick_slot, nkey, proj_count):
    rank = tucker_core.shape[0]
    width = key_row.shape[1]
    token_rows, features = tokens.shape
    slots, value_width = fetched.shape
    columns = w_query.shape[1]
    query_blocks = (features + 2 * width) // LANES
    own = own_half(w_query, key_row, key_col, proj_part)
    gathered = lax.all_gather(own, ("groups", "mem"), axis=0, tiled=False)
    params = pltpu.CompilerParams(vmem_limit_bytes=VMEM_LIMIT)
    plane = jax.ShapeDtypeStruct((token_rows, slots), F32)
    planes = jax.ShapeDtypeStruct((rank, token_rows, slots), F32)
    slot_key = jax.ShapeDtypeStruct((slots, width), BF16)
    slot_row, slot_col, counts, weights, row_factor, col_factor = pl.pallas_call(
        functools.partial(scores_kernel, rank, width, nkey),
        out_shape=(slot_key, slot_key, plane, plane, planes, planes),
        in_specs=[smem(), vmem(), vmem(), vmem(), anywhere()],
        out_specs=(vmem(),) * 6,
        scratch_shapes=[pltpu.VMEM((query_blocks, nkey, LANES), BF16), pltpu.SemaphoreType.DMA],
        compiler_params=params,
        cost_estimate=pl.CostEstimate(flops=2 * 10**9, bytes_accessed=10**7, transcendentals=10**5),
        name="scores",
    )(tucker_core, row_id[:, None], pick_slot, tokens, gathered)
    return pl.pallas_call(
        functools.partial(outputs_kernel, rank, width, proj_count),
        out_shape=(jax.ShapeDtypeStruct((token_rows, features), BF16),) * 2,
        in_specs=[vmem()] * 9 + [anywhere()],
        out_specs=(vmem(), vmem()),
        scratch_shapes=[
            pltpu.VMEM((query_blocks, nkey, LANES), BF16),
            pltpu.VMEM((proj_count * value_width // columns, columns, features), BF16),
            pltpu.VMEM((token_rows, proj_count * value_width), BF16),
            pltpu.VMEM((token_rows, 2 * rank * width), BF16),
            pltpu.SemaphoreType.DMA,
            pltpu.SemaphoreType.DMA((proj_count,)),
        ],
        compiler_params=params,
        cost_estimate=pl.CostEstimate(flops=7 * 10**9, bytes_accessed=2 * 10**7, transcendentals=0),
        name="outputs",
    )(
        slot_proj[None, :], slot_row, slot_col, counts, weights, row_factor, col_factor, fetched, cotangent, gathered
    )


def whole_path(tokens, cotangent, w_query, key_row, key_col, tucker_core, proj_part, fetched, row_id, slot_proj,
               pick_slot, nkey, proj_count):
    rank = tucker_core.shape[0]
    width = key_row.shape[1]
    slots = row_id.shape[0]
    query_full = lax.all_gather(w_query.T, "mem", axis=0, tiled=True)
    keys = lax.all_gather(jnp.concatenate([key_row, key_col], axis=1), "mem", axis=0, tiled=True)
    proj_full = lax.all_gather(proj_part, "mem", axis=1, tiled=True)
    key_at = jnp.arange(nkey, dtype=jnp.int32)[None, :]
    row_hot = ((row_id // nkey)[:, None] == key_at).astype(BF16)
    col_hot = ((row_id % nkey)[:, None] == key_at).astype(BF16)
    slot_row = dot(row_hot, keys[:, :width], PLAIN).astype(BF16)
    slot_col = dot(col_hot, keys[:, width:], PLAIN).astype(BF16)
    spread = jnp.where(
        slot_proj[:, None, None] == jnp.arange(proj_count, dtype=jnp.int32)[None, :, None],
        fetched[:, None, :], jnp.zeros((), BF16)
    ).reshape(slots, -1)
    counts = jnp.sum(
        (pick_slot[:, :, None] == jnp.arange(slots, dtype=jnp.int32)[None, None, :]).astype(F32), axis=1
    )
    queries = dot(tokens, query_full, LAST).astype(BF16)
    row_scores = [dot(queries[:, r * width:(r + 1) * width], slot_row, LAST) for r in range(rank)]
    col_scores = [
        dot(queries[:, (rank + r) * width:(rank + r + 1) * width], slot_col, LAST) for r in range(rank)
    ]
    col_mixed = [sum(tucker_core[r, s] * col_scores[s] for s in range(rank)) for r in range(rank)]
    row_mixed = [sum(row_scores[r] * tucker_core[r, s] for r in range(rank)) for s in range(rank)]
    score = sum(row_scores[r] * col_mixed[r] for r in range(rank))
    gate = jax.nn.sigmoid(score)
    weights = counts * gate.astype(BF16).astype(F32)
    mixed = counted_dot(weights, spread, PLAIN).astype(BF16)
    memory_out = dot(mixed, proj_full, PLAIN)
    value_grad = dot(cotangent, proj_full, LAST).astype(BF16)
    pick_grad = dot(value_grad, spread, LAST)
    score_grad = pick_grad * gate * (1.0 - gate)
    blocks = []
    for mixed_scores, slot_key in ((col_mixed, slot_row), (row_mixed, slot_col)):
        for r in range(rank):
            grad = (score_grad * mixed_scores[r]).astype(BF16).astype(F32) * counts
            blocks.append(counted_dot(grad, slot_key, PLAIN).astype(BF16))
    query_grad = jnp.concatenate(blocks, axis=1)
    token_grad = dot(query_grad, query_full, PLAIN)
    return memory_out.astype(BF16), token_grad.astype(BF16)


def shards(
    mem, tokens, cotangent, w_query, key_row, key_col, tucker_core, table, w_proj, send_ids, pick_slot
):
    proj_count, value_width, _ = w_proj.shape
    requests = send_ids[0]
    owners, capacity = requests.shape
    slots = owners * capacity
    nkey = key_row.shape[0] * mem
    fetched = fetch_rows(requests, table).reshape(slots, value_width)
    row_id = jnp.maximum(requests, 0) + jnp.arange(owners, dtype=jnp.int32)[:, None] * table.shape[0]
    row_id = row_id.reshape(slots)
    slot_proj = (row_id % nkey) % proj_count
    proj_part = w_proj.reshape(proj_count * value_width, -1)
    path = halves_path if w_proj.shape[2] == LANES else whole_path
    return path(tokens, cotangent, w_query, key_row, key_col, tucker_core, proj_part, fetched, row_id, slot_proj,
                pick_slot, nkey, proj_count)


def solution(mesh):
    in_specs = (
        P(("groups", "mem"), None),
        P(("groups", "mem"), None),
        P(None, "mem"),
        P("mem", None),
        P("mem", None),
        P(),
        P("mem", None),
        P(None, None, "mem"),
        P(("groups", "mem"), None, None),
        P(("groups", "mem"), None),
    )
    out_specs = (P(("groups", "mem"), None), P(("groups", "mem"), None))
    body = functools.partial(shards, mesh.shape["mem"])
    return jax.shard_map(body, mesh=mesh, in_specs=in_specs, out_specs=out_specs, check_vma=False)
```

```python
import functools

import jax
import jax.numpy as jnp
from jax import lax
from jax.experimental import pallas as pl
from jax.experimental.pallas import tpu as pltpu
from jax.sharding import PartitionSpec as P

F32 = jnp.float32
BF16 = jnp.bfloat16
RING = (0, 2, 3, 1)
LAST = ((1,), (1,))
PLAIN = ((1,), (0,))
VMEM_LIMIT = 56 * 1024 * 1024


def dot(a, b, dims):
    return lax.dot_general(a, b, (dims, ((), ())), preferred_element_type=F32)


def two_terms(x):
    high = x.astype(BF16)
    return high, (x - high.astype(F32)).astype(BF16)


def counted_dot(x, b, dims):
    high, low = two_terms(x)
    return dot(high, b, dims) + dot(low, b, dims)


def wanted_rows(requests):
    return lax.all_to_all(requests, "mem", split_axis=0, concat_axis=0, tiled=True)


def found_rows(wanted, table):
    found = jnp.take(table, jnp.maximum(wanted, 0).reshape(-1), axis=0, mode="clip")
    return found.reshape(wanted.shape + (table.shape[1],))


def returned_rows(found):
    return lax.all_to_all(found, "mem", split_axis=0, concat_axis=0, tiled=True)


def place(z, y, core):
    return (z * 2 + y) * 2 + core


def everywhere(move):
    pairs = []
    for z in range(4):
        for y in range(2):
            for core in range(2):
                pairs.append((place(z, y, core), place(*move(z, y, core))))
    return pairs


def next_z(x):
    step = {RING[i]: RING[(i + 1) % 4] for i in range(4)}
    return lax.ppermute(x, "mem", everywhere(lambda z, y, c: (step[z], y, c)))


def other_y(x):
    return lax.ppermute(x, "mem", everywhere(lambda z, y, c: (z, 1 - y, c)))


def other_core(x):
    return lax.ppermute(x, "mem", everywhere(lambda z, y, c: (z, y, 1 - c)))


def other_x(x):
    return lax.ppermute(x, "groups", [(0, 1), (1, 0)])


def ring_source(z, steps):
    order = jnp.array([[RING[(RING.index(a) - s) % 4] for a in range(4)] for s in range(4)], jnp.int32)
    return order[steps, z]


def after(value, *earlier):
    return lax.optimization_barrier((value,) + earlier)[0]


def gather_pieces(query_part, proj_part, wanted, found):
    me = lax.axis_index("mem")
    z, y, core = me // 4, (me // 2) % 2, me % 2
    x = lax.axis_index("groups")
    half = proj_part.shape[0] // 2

    query_rings = [query_part, next_z(query_part)]
    proj_other = other_y(proj_part)
    query_rings.append(next_z(after(query_rings[-1], wanted)))
    query_rings.append(next_z(query_rings[-1]))
    pair = jnp.stack([lax.dynamic_slice_in_dim(a, x * half, half, axis=0) for a in (proj_part, proj_other)])
    pairs = [pair, next_z(pair)]
    pairs.append(next_z(pairs[-1]))
    pairs.append(next_z(after(pairs[-1], found)))

    query_pieces, proj_pieces = [], []
    for step in range(4):
        at = ring_source(z, step)
        here = [(query_rings[step], y), (other_y(query_rings[step]), 1 - y)]
        query_pieces += [(a, place(at, b, core)) for a, b in here]
        query_pieces += [(other_core(a), place(at, b, 1 - core)) for a, b in here]
        if step == 0:
            here = [(proj_part, [(y, 0)]), (proj_other, [(1 - y, 0)])]
        else:
            here = [(pairs[step], [(y, x * half), (1 - y, x * half)])]
            here += [(other_x(pairs[step]), [(y, (1 - x) * half), (1 - y, (1 - x) * half)])]
        for a, spots in here:
            proj_pieces.append((a, [(place(at, b, core), row) for b, row in spots]))
            proj_pieces.append((other_core(a), [(place(at, b, 1 - core), row) for b, row in spots]))
    return query_pieces, proj_pieces


def counts_kernel(pick_ref, counts_ref):
    token_rows, slots = counts_ref.shape
    lane = lax.broadcasted_iota(jnp.int32, (token_rows, slots), 1)
    pick = pick_ref[...]
    counts = jnp.zeros((token_rows, slots), F32)
    for k in range(pick.shape[1]):
        counts += jnp.where(pick[:, k:k + 1] == lane, 1.0, 0.0)
    counts_ref[...] = counts


def scores_kernel(
    rank, width, nkey, count, at_ref, core_ref, row_id_ref, counts_ref, tokens_ref, *refs
):
    pieces, rest = refs[:count], refs[count:]
    row_ref, col_ref, weights_ref, row_factor_ref, col_factor_ref, held, sems = rest
    copies = []
    for i, piece in enumerate(pieces):
        rows = piece.shape[0]
        start = pl.multiple_of(at_ref[i], rows)
        copies.append(pltpu.make_async_copy(piece, held.at[pl.ds(start, rows)], sems.at[i]))
        copies[-1].start()
    slots = row_id_ref.shape[0]
    key_at = lax.broadcasted_iota(jnp.int32, (slots, nkey), 1)
    row_id = row_id_ref[...]
    row_hot = jnp.where(row_id // nkey == key_at, 1.0, 0.0).astype(BF16)
    col_hot = jnp.where(row_id % nkey == key_at, 1.0, 0.0).astype(BF16)
    for copy in copies:
        copy.wait()
    features = tokens_ref.shape[1]
    slot_row = dot(row_hot, held[:, features:features + width], PLAIN).astype(BF16)
    slot_col = dot(col_hot, held[:, features + width:features + 2 * width], PLAIN).astype(BF16)
    row_ref[...] = slot_row
    col_ref[...] = slot_col
    queries = dot(tokens_ref[...], held[:, :features], LAST).astype(BF16)
    block = [queries[:, r * width:(r + 1) * width] for r in range(2 * rank)]
    row_scores = [dot(block[r], slot_row, LAST) for r in range(rank)]
    col_scores = [dot(block[rank + r], slot_col, LAST) for r in range(rank)]
    col_mixed = [sum(core_ref[r, s] * col_scores[s] for s in range(rank)) for r in range(rank)]
    row_mixed = [sum(row_scores[r] * core_ref[r, s] for r in range(rank)) for s in range(rank)]
    score = sum(row_scores[r] * col_mixed[r] for r in range(rank))
    gate = 1.0 / (1.0 + jnp.exp(-score))
    weights_ref[...] = (counts_ref[...] * gate.astype(BF16).astype(F32)).astype(BF16)
    slope = gate * (1.0 - gate)
    for r in range(rank):
        row_factor_ref[r] = slope * col_mixed[r]
        col_factor_ref[r] = slope * row_mixed[r]


def outputs_kernel(
    rank, width, proj_count, query_count, proj_count_pieces, query_at, proj_at, proj_row, proj_ref,
    row_ref, col_ref, counts_ref, weights_ref, row_factor_ref, col_factor_ref, fetched_ref, cot_ref, *refs
):
    query_pieces = refs[:query_count]
    proj_pieces = refs[query_count:query_count + proj_count_pieces]
    out_ref, grad_ref, query_held, proj_held, mixed_values, query_grad, query_sem, proj_sem = refs[
        query_count + proj_count_pieces:
    ]
    value_width = fetched_ref.shape[1]
    features = cot_ref.shape[1]
    for part in range(proj_count):
        for i, piece in enumerate(proj_pieces):
            spots = [piece] if len(piece.shape) == 2 else [piece.at[s] for s in range(piece.shape[0])]
            for s, spot in enumerate(spots):
                rows, wide = spot.shape
                if part * value_width >= rows:
                    continue
                row = pl.multiple_of(proj_row[i, s] + part * value_width, value_width)
                pltpu.make_async_copy(
                    spot.at[pl.ds(part * value_width, value_width)],
                    proj_held.at[pl.ds(row, value_width), pl.ds(pl.multiple_of(proj_at[i, s], wide), wide)],
                    proj_sem.at[row // value_width],
                ).start()
    for i, piece in enumerate(query_pieces):
        rows = piece.shape[0]
        start = pl.multiple_of(query_at[i], rows)
        pltpu.make_async_copy(
            piece.at[:, pl.ds(0, features)], query_held.at[pl.ds(start, rows)], query_sem
        ).start()

    proj = proj_ref[...]
    fetched = fetched_ref[...]
    weights = weights_ref[...]
    for e in range(proj_count):
        mixed = dot(jnp.where(proj == e, weights, jnp.zeros((), BF16)), fetched, PLAIN)
        mixed_values[:, e * value_width:(e + 1) * value_width] = mixed.astype(BF16)
    cot = cot_ref[...]
    pick_grad = jnp.zeros(counts_ref.shape, F32)
    for e in range(proj_count):
        block = proj_held.at[pl.ds(e * value_width, value_width)]
        pltpu.make_async_copy(block, block, proj_sem.at[e]).wait()
        grad = dot(cot, block[...], LAST).astype(BF16)
        pick_grad = jnp.where(proj == e, dot(grad, fetched, LAST), pick_grad)
    counts = counts_ref[...]
    for side, (factor, key_ref) in enumerate(((row_factor_ref, row_ref), (col_factor_ref, col_ref))):
        for r in range(rank):
            grad = ((pick_grad * factor[r]).astype(BF16).astype(F32) * counts).astype(BF16)
            at = (side * rank + r) * width
            query_grad[:, at:at + width] = dot(grad, key_ref[...], PLAIN).astype(BF16)
    pltpu.make_async_copy(query_held, query_held, query_sem).wait()
    step = features // 4
    for c in range(4):
        cols = slice(c * step, (c + 1) * step)
        grad_ref[:, cols] = dot(query_grad[...], query_held[:, cols], PLAIN).astype(BF16)
        out_ref[:, cols] = dot(mixed_values[...], proj_held[:, cols], PLAIN).astype(BF16)


def vmem():
    return pl.BlockSpec(memory_space=pltpu.VMEM)


def smem():
    return pl.BlockSpec(memory_space=pltpu.SMEM)


def anywhere():
    return pl.BlockSpec(memory_space=pl.ANY)


def pieces_path(tokens, cotangent, w_query, key_row, key_col, tucker_core, proj_part, requests, table, row_id,
                slot_proj, pick_slot, nkey, proj_count):
    rank = tucker_core.shape[0]
    width = key_row.shape[1]
    token_rows, features = tokens.shape
    slots = row_id.shape[0]
    value_width = table.shape[1]
    wanted = wanted_rows(requests)
    found = found_rows(wanted, table)
    fetched = returned_rows(found).reshape(slots, value_width)
    query_part = jnp.concatenate([w_query.T, key_row, key_col], axis=1)
    query_pieces, proj_pieces = gather_pieces(query_part, proj_part, wanted, found)
    query_at = jnp.stack([at for _, at in query_pieces]) * query_part.shape[0]
    proj_at = jnp.stack([jnp.stack([s[0][0], s[-1][0]]) for _, s in proj_pieces]) * proj_part.shape[1]
    proj_row = jnp.stack([jnp.stack([s[0][1], s[-1][1]]) for _, s in proj_pieces])
    query_pieces = [a for a, _ in query_pieces]
    proj_pieces = [a for a, _ in proj_pieces]
    params = pltpu.CompilerParams(vmem_limit_bytes=VMEM_LIMIT)
    plane = jax.ShapeDtypeStruct((token_rows, slots), F32)
    planes = jax.ShapeDtypeStruct((rank, token_rows, slots), F32)
    slot_key = jax.ShapeDtypeStruct((slots, width), BF16)
    counts = pl.pallas_call(
        counts_kernel,
        out_shape=plane,
        in_specs=[vmem()],
        out_specs=vmem(),
        compiler_params=params,
        cost_estimate=pl.CostEstimate(flops=2 * 10**9, bytes_accessed=10**6, transcendentals=0),
        name="counts",
    )(pick_slot)
    slot_row, slot_col, weights, row_factor, col_factor = pl.pallas_call(
        functools.partial(scores_kernel, rank, width, nkey, len(query_pieces)),
        out_shape=(slot_key, slot_key, jax.ShapeDtypeStruct((token_rows, slots), BF16), planes, planes),
        in_specs=[smem(), smem(), vmem(), vmem(), vmem()] + [anywhere()] * len(query_pieces),
        out_specs=(vmem(),) * 5,
        scratch_shapes=[
            pltpu.VMEM((nkey, features + 2 * width), BF16),
            pltpu.SemaphoreType.DMA((len(query_pieces),)),
        ],
        compiler_params=params,
        cost_estimate=pl.CostEstimate(flops=5 * 10**9, bytes_accessed=10**7, transcendentals=10**5),
        name="scores",
    )(query_at, tucker_core, row_id[:, None], counts, tokens, *query_pieces)
    return pl.pallas_call(
        functools.partial(
            outputs_kernel, rank, width, proj_count, len(query_pieces), len(proj_pieces)
        ),
        out_shape=(jax.ShapeDtypeStruct((token_rows, features), BF16),) * 2,
        in_specs=[smem()] * 3 + [vmem()] * 9 + [anywhere()] * (len(query_pieces) + len(proj_pieces)),
        out_specs=(vmem(), vmem()),
        scratch_shapes=[
            pltpu.VMEM((nkey, features), BF16),
            pltpu.VMEM((proj_count * value_width, features), BF16),
            pltpu.VMEM((token_rows, proj_count * value_width), BF16),
            pltpu.VMEM((token_rows, 2 * rank * width), BF16),
            pltpu.SemaphoreType.DMA,
            pltpu.SemaphoreType.DMA((proj_count,)),
        ],
        compiler_params=params,
        cost_estimate=pl.CostEstimate(flops=7 * 10**9, bytes_accessed=2 * 10**7, transcendentals=0),
        name="outputs",
    )(
        query_at, proj_at, proj_row, slot_proj[None, :], slot_row, slot_col, counts, weights, row_factor, col_factor,
        fetched, cotangent, *query_pieces, *proj_pieces,
    )


def whole_path(tokens, cotangent, w_query, key_row, key_col, tucker_core, proj_part, requests, table, row_id,
               slot_proj, pick_slot, nkey, proj_count):
    rank = tucker_core.shape[0]
    width = key_row.shape[1]
    slots = row_id.shape[0]
    fetched = returned_rows(found_rows(wanted_rows(requests), table)).reshape(slots, -1)
    query_full = lax.all_gather(w_query.T, "mem", axis=0, tiled=True)
    keys = lax.all_gather(jnp.concatenate([key_row, key_col], axis=1), "mem", axis=0, tiled=True)
    proj_full = lax.all_gather(proj_part, "mem", axis=1, tiled=True)
    key_at = jnp.arange(nkey, dtype=jnp.int32)[None, :]
    row_hot = ((row_id // nkey)[:, None] == key_at).astype(BF16)
    col_hot = ((row_id % nkey)[:, None] == key_at).astype(BF16)
    slot_row = dot(row_hot, keys[:, :width], PLAIN).astype(BF16)
    slot_col = dot(col_hot, keys[:, width:], PLAIN).astype(BF16)
    spread = jnp.where(
        slot_proj[:, None, None] == jnp.arange(proj_count, dtype=jnp.int32)[None, :, None],
        fetched[:, None, :], jnp.zeros((), BF16)
    ).reshape(slots, -1)
    counts = jnp.sum(
        (pick_slot[:, :, None] == jnp.arange(slots, dtype=jnp.int32)[None, None, :]).astype(F32), axis=1
    )
    queries = dot(tokens, query_full, LAST).astype(BF16)
    row_scores = [dot(queries[:, r * width:(r + 1) * width], slot_row, LAST) for r in range(rank)]
    col_scores = [
        dot(queries[:, (rank + r) * width:(rank + r + 1) * width], slot_col, LAST) for r in range(rank)
    ]
    col_mixed = [sum(tucker_core[r, s] * col_scores[s] for s in range(rank)) for r in range(rank)]
    row_mixed = [sum(row_scores[r] * tucker_core[r, s] for r in range(rank)) for s in range(rank)]
    score = sum(row_scores[r] * col_mixed[r] for r in range(rank))
    gate = jax.nn.sigmoid(score)
    weights = counts * gate.astype(BF16).astype(F32)
    mixed = counted_dot(weights, spread, PLAIN).astype(BF16)
    memory_out = dot(mixed, proj_full, PLAIN)
    value_grad = dot(cotangent, proj_full, LAST).astype(BF16)
    pick_grad = dot(value_grad, spread, LAST)
    score_grad = pick_grad * gate * (1.0 - gate)
    blocks = []
    for mixed_scores, slot_key in ((col_mixed, slot_row), (row_mixed, slot_col)):
        for r in range(rank):
            grad = (score_grad * mixed_scores[r]).astype(BF16).astype(F32) * counts
            blocks.append(counted_dot(grad, slot_key, PLAIN).astype(BF16))
    query_grad = jnp.concatenate(blocks, axis=1)
    token_grad = dot(query_grad, query_full, PLAIN)
    return memory_out.astype(BF16), token_grad.astype(BF16)


def shards(
    mem, tokens, cotangent, w_query, key_row, key_col, tucker_core, table, w_proj, send_ids, pick_slot
):
    proj_count, value_width, _ = w_proj.shape
    requests = send_ids[0]
    owners, capacity = requests.shape
    slots = owners * capacity
    nkey = key_row.shape[0] * mem
    row_id = jnp.maximum(requests, 0) + jnp.arange(owners, dtype=jnp.int32)[:, None] * table.shape[0]
    row_id = row_id.reshape(slots)
    slot_proj = (row_id % nkey) % proj_count
    proj_part = w_proj.reshape(proj_count * value_width, -1)
    path = pieces_path if mem == 16 and w_proj.shape[2] % 128 == 0 else whole_path
    return path(tokens, cotangent, w_query, key_row, key_col, tucker_core, proj_part, requests, table, row_id,
                slot_proj, pick_slot, nkey, proj_count)


def solution(mesh):
    in_specs = (
        P(("groups", "mem"), None),
        P(("groups", "mem"), None),
        P(None, "mem"),
        P("mem", None),
        P("mem", None),
        P(),
        P("mem", None),
        P(None, None, "mem"),
        P(("groups", "mem"), None, None),
        P(("groups", "mem"), None),
    )
    out_specs = (P(("groups", "mem"), None), P(("groups", "mem"), None))
    body = functools.partial(shards, mesh.shape["mem"])
    return jax.shard_map(body, mesh=mesh, in_specs=in_specs, out_specs=out_specs, check_vma=False)
```

```python
import functools

import jax
import jax.numpy as jnp
from jax import lax
from jax.experimental import pallas as pl
from jax.experimental.pallas import tpu as pltpu
from jax.sharding import PartitionSpec as P

F32 = jnp.float32
BF16 = jnp.bfloat16
RING = (0, 2, 3, 1)
LANES = 128
LAST = ((1,), (1,))
PLAIN = ((1,), (0,))
VMEM_LIMIT = 56 * 1024 * 1024


def dot(a, b, dims):
    return lax.dot_general(a, b, (dims, ((), ())), preferred_element_type=F32)


def two_terms(x):
    high = x.astype(BF16)
    return high, (x - high.astype(F32)).astype(BF16)


def counted_dot(x, b, dims):
    high, low = two_terms(x)
    return dot(high, b, dims) + dot(low, b, dims)


def wanted_rows(requests):
    return lax.all_to_all(requests, "mem", split_axis=0, concat_axis=0, tiled=True)


def found_rows(wanted, table):
    found = jnp.take(table, jnp.maximum(wanted, 0).reshape(-1), axis=0, mode="clip")
    return found.reshape(wanted.shape + (table.shape[1],))


def returned_rows(found):
    return lax.all_to_all(found, "mem", split_axis=0, concat_axis=0, tiled=True)


def place(z, y, core):
    return (z * 2 + y) * 2 + core


def everywhere(move):
    pairs = []
    for z in range(4):
        for y in range(2):
            for core in range(2):
                pairs.append((place(z, y, core), place(*move(z, y, core))))
    return pairs


def next_z(x):
    step = {RING[i]: RING[(i + 1) % 4] for i in range(4)}
    return lax.ppermute(x, "mem", everywhere(lambda z, y, c: (step[z], y, c)))


def other_y(x):
    return lax.ppermute(x, "mem", everywhere(lambda z, y, c: (z, 1 - y, c)))


def other_core(x):
    return lax.ppermute(x, "mem", everywhere(lambda z, y, c: (z, y, 1 - c)))


def other_x(x):
    return lax.ppermute(x, "groups", [(0, 1), (1, 0)])


def ring_source(z, steps):
    order = jnp.array([[RING[(RING.index(a) - s) % 4] for a in range(4)] for s in range(4)], jnp.int32)
    return order[steps, z]


def tie(*values):
    return lax.optimization_barrier(values)


def own_halves(w_query, key_row, key_col, proj_part):
    columns = w_query.shape[1]
    proj = proj_part.reshape(2, -1, columns, LANES)
    query = jnp.concatenate([w_query.T, key_row, key_col], axis=1)
    query = query.reshape(columns, 2, -1, LANES).transpose(1, 2, 0, 3)
    return jnp.concatenate([proj, query], axis=1)


def gather_pieces(own, requests, table):
    me = lax.axis_index("mem")
    z, y, core = me // 4, (me // 2) % 2, me % 2
    x = lax.axis_index("groups")
    near = [lax.dynamic_index_in_dim(own, x, axis=0, keepdims=False)]
    near_own_far = lax.dynamic_index_in_dim(own, 1 - x, axis=0, keepdims=False)
    near.append(next_z(near[0]))
    side = [other_y(near[0])]
    near[1], wanted = tie(near[1], wanted_rows(requests))
    near.append(next_z(near[1]))
    side.append(other_y(near[1]))
    side_far = [other_x(side[0])]
    near[2], found = tie(near[2], found_rows(wanted, table))
    fetched = returned_rows(found)
    near.append(next_z(near[2]))
    side.append(other_y(near[2]))
    side_far.append(other_x(side[1]))
    near_own_far, near[3], fetched = tie(near_own_far, near[3], fetched)
    near_far = [None, next_z(near_own_far)]
    side.append(other_y(near[3]))
    near_3_far = other_x(near[3])
    near_far.append(next_z(near_far[1]))
    near_far.append(near_3_far)
    side_far.append(other_x(side[2]))
    side_far.append(other_y(near_far[3]))

    pieces = []
    for step in range(4):
        at = ring_source(z, step)
        here = [(side[step], 1 - y, x), (side_far[step], 1 - y, 1 - x)]
        if step > 0:
            here += [(near[step], y, x), (near_far[step], y, 1 - x)]
        for a, b, half in here:
            pieces.append((a, place(at, b, core), half))
            pieces.append((other_core(a), place(at, b, 1 - core), half))
    return pieces, (own, other_core(own)), (me, place(z, y, 1 - core)), fetched


def counts_kernel(pick_ref, counts_ref):
    token_rows, slots = counts_ref.shape
    lane = lax.broadcasted_iota(jnp.int32, (token_rows, slots), 1)
    pick = pick_ref[...]
    counts = jnp.zeros((token_rows, slots), F32)
    for k in range(pick.shape[1]):
        counts += jnp.where(pick[:, k:k + 1] == lane, 1.0, 0.0)
    counts_ref[...] = counts


def wide(held, first, last):
    return jnp.concatenate([held[j] for j in range(first, last)], axis=1)


def dense_kernel(
    rank, width, proj_count, piece_count, at_ref, half_ref, core_ref, row_id_ref, proj_ref, counts_ref, tokens_ref,
    cot_ref, fetched_ref, *refs
):
    pieces = refs[:piece_count]
    out_ref, grad_ref, query_held, proj_held, mixed_values, query_grad, query_sem, proj_sem = refs[piece_count:]
    features = tokens_ref.shape[1]
    token_rows, slots = counts_ref.shape
    value_width = fetched_ref.shape[1]
    columns = proj_held.shape[1]
    parts = value_width // columns
    spots = []
    for i, piece in enumerate(pieces):
        if len(piece.shape) == 3:
            spots.append((piece, at_ref[i], half_ref[i]))
        else:
            spots += [(piece.at[half], at_ref[i], half) for half in range(2)]
    half_proj = proj_held.shape[0] // 2
    half_query = query_held.shape[0] // 2
    for piece, at, half in spots:
        pltpu.make_async_copy(
            piece.at[pl.ds(half_proj, half_query)],
            query_held.at[pl.ds(half * half_query, half_query), pl.ds(pl.multiple_of(at * columns, columns), columns)],
            query_sem,
        ).start()
    for inner in range(proj_count // 2):
        for piece, at, half in spots:
            e = half * (proj_count // 2) + inner
            pltpu.make_async_copy(
                piece.at[pl.ds(inner * parts, parts)],
                proj_held.at[pl.ds(e * parts, parts), :, pl.ds(pl.multiple_of(at * LANES, LANES), LANES)],
                proj_sem.at[e],
            ).start()

    nkey = query_held.shape[1]
    key_at = lax.broadcasted_iota(jnp.int32, (slots, nkey), 1)
    row_id = row_id_ref[...]
    row_hot = jnp.where(row_id // nkey == key_at, 1.0, 0.0).astype(BF16)
    col_hot = jnp.where(row_id % nkey == key_at, 1.0, 0.0).astype(BF16)
    pltpu.make_async_copy(query_held, query_held, query_sem).wait()
    key = features // LANES
    step = width // LANES
    slot_row = dot(row_hot, wide(query_held, key, key + step), PLAIN).astype(BF16)
    slot_col = dot(col_hot, wide(query_held, key + step, key + 2 * step), PLAIN).astype(BF16)
    queries = dot(tokens_ref[...], wide(query_held, 0, key), LAST).astype(BF16)
    block = [queries[:, r * width:(r + 1) * width] for r in range(2 * rank)]
    row_scores = [dot(block[r], slot_row, LAST) for r in range(rank)]
    col_scores = [dot(block[rank + r], slot_col, LAST) for r in range(rank)]
    col_mixed = [sum(core_ref[r, s] * col_scores[s] for s in range(rank)) for r in range(rank)]
    row_mixed = [sum(row_scores[r] * core_ref[r, s] for r in range(rank)) for s in range(rank)]
    score = sum(row_scores[r] * col_mixed[r] for r in range(rank))
    gate = 1.0 / (1.0 + jnp.exp(-score))
    counts = counts_ref[...]
    weights = (counts * gate.astype(BF16).astype(F32)).astype(BF16)
    slope = gate * (1.0 - gate)
    factors = [slope * m for m in col_mixed] + [slope * m for m in row_mixed]

    proj = proj_ref[...]
    fetched = fetched_ref[...]
    for e in range(proj_count):
        mixed = dot(jnp.where(proj == e, weights, jnp.zeros((), BF16)), fetched, PLAIN)
        mixed_values[:, e * value_width:(e + 1) * value_width] = mixed.astype(BF16)
    cot = cot_ref[...]
    pick_grad = jnp.zeros(counts.shape, F32)
    for inner in range(proj_count // 2):
        for e in (inner, proj_count // 2 + inner):
            held = proj_held.at[pl.ds(e * parts, parts)]
            pltpu.make_async_copy(held, held, proj_sem.at[e]).wait()
            grad = dot(cot, held[...].reshape(value_width, features), LAST).astype(BF16)
            pick_grad = jnp.where(proj == e, dot(grad, fetched, LAST), pick_grad)
    for i, factor in enumerate(factors):
        slot_key = slot_row if i < rank else slot_col
        grad = ((pick_grad * factor).astype(BF16).astype(F32) * counts).astype(BF16)
        query_grad[:, i * width:(i + 1) * width] = dot(grad, slot_key, PLAIN).astype(BF16)
    blocks = features // LANES // 4
    for c in range(4):
        cols = slice(c * blocks * LANES, (c + 1) * blocks * LANES)
        grad_ref[:, cols] = dot(query_grad[...], wide(query_held, c * blocks, (c + 1) * blocks), PLAIN).astype(BF16)
        held = proj_held[:, :, cols].reshape(proj_count * value_width, blocks * LANES)
        out_ref[:, cols] = dot(mixed_values[...], held, PLAIN).astype(BF16)


def vmem():
    return pl.BlockSpec(memory_space=pltpu.VMEM)


def smem():
    return pl.BlockSpec(memory_space=pltpu.SMEM)


def anywhere():
    return pl.BlockSpec(memory_space=pl.ANY)


def pieces_path(tokens, cotangent, w_query, key_row, key_col, tucker_core, proj_part, requests, table, row_id,
                slot_proj, pick_slot, nkey, proj_count):
    rank = tucker_core.shape[0]
    width = key_row.shape[1]
    token_rows, features = tokens.shape
    slots = row_id.shape[0]
    value_width = table.shape[1]
    columns = w_query.shape[1]
    own = own_halves(w_query, key_row, key_col, proj_part)
    pieces, pairs, pair_at, fetched = gather_pieces(own, requests, table)
    fetched = fetched.reshape(slots, value_width)
    at = jnp.stack(list(pair_at) + [p[1] for p in pieces])
    half = jnp.stack([jnp.int32(0)] * 2 + [p[2] for p in pieces])
    pieces = list(pairs) + [p[0] for p in pieces]
    params = pltpu.CompilerParams(vmem_limit_bytes=VMEM_LIMIT)
    counts = pl.pallas_call(
        counts_kernel,
        out_shape=jax.ShapeDtypeStruct((token_rows, slots), F32),
        in_specs=[vmem()],
        out_specs=vmem(),
        compiler_params=params,
        cost_estimate=pl.CostEstimate(flops=3 * 10**9, bytes_accessed=10**6, transcendentals=0),
        name="counts",
    )(pick_slot)
    return pl.pallas_call(
        functools.partial(dense_kernel, rank, width, proj_count, len(pieces)),
        out_shape=(jax.ShapeDtypeStruct((token_rows, features), BF16),) * 2,
        in_specs=[smem()] * 3 + [vmem()] * 6 + [anywhere()] * len(pieces),
        out_specs=(vmem(), vmem()),
        scratch_shapes=[
            pltpu.VMEM(((features + 2 * width) // LANES, nkey, LANES), BF16),
            pltpu.VMEM((proj_count * value_width // columns, columns, features), BF16),
            pltpu.VMEM((token_rows, proj_count * value_width), BF16),
            pltpu.VMEM((token_rows, 2 * rank * width), BF16),
            pltpu.SemaphoreType.DMA,
            pltpu.SemaphoreType.DMA((proj_count,)),
        ],
        compiler_params=params,
        cost_estimate=pl.CostEstimate(flops=10**10, bytes_accessed=2 * 10**7, transcendentals=10**5),
        name="dense",
    )(at, half, tucker_core, row_id[:, None], slot_proj[None, :], counts, tokens, cotangent, fetched, *pieces)


def whole_path(tokens, cotangent, w_query, key_row, key_col, tucker_core, proj_part, requests, table, row_id,
               slot_proj, pick_slot, nkey, proj_count):
    rank = tucker_core.shape[0]
    width = key_row.shape[1]
    slots = row_id.shape[0]
    fetched = returned_rows(found_rows(wanted_rows(requests), table)).reshape(slots, -1)
    query_full = lax.all_gather(w_query.T, "mem", axis=0, tiled=True)
    keys = lax.all_gather(jnp.concatenate([key_row, key_col], axis=1), "mem", axis=0, tiled=True)
    proj_full = lax.all_gather(proj_part, "mem", axis=1, tiled=True)
    key_at = jnp.arange(nkey, dtype=jnp.int32)[None, :]
    row_hot = ((row_id // nkey)[:, None] == key_at).astype(BF16)
    col_hot = ((row_id % nkey)[:, None] == key_at).astype(BF16)
    slot_row = dot(row_hot, keys[:, :width], PLAIN).astype(BF16)
    slot_col = dot(col_hot, keys[:, width:], PLAIN).astype(BF16)
    spread = jnp.where(
        slot_proj[:, None, None] == jnp.arange(proj_count, dtype=jnp.int32)[None, :, None],
        fetched[:, None, :], jnp.zeros((), BF16)
    ).reshape(slots, -1)
    counts = jnp.sum(
        (pick_slot[:, :, None] == jnp.arange(slots, dtype=jnp.int32)[None, None, :]).astype(F32), axis=1
    )
    queries = dot(tokens, query_full, LAST).astype(BF16)
    row_scores = [dot(queries[:, r * width:(r + 1) * width], slot_row, LAST) for r in range(rank)]
    col_scores = [
        dot(queries[:, (rank + r) * width:(rank + r + 1) * width], slot_col, LAST) for r in range(rank)
    ]
    col_mixed = [sum(tucker_core[r, s] * col_scores[s] for s in range(rank)) for r in range(rank)]
    row_mixed = [sum(row_scores[r] * tucker_core[r, s] for r in range(rank)) for s in range(rank)]
    score = sum(row_scores[r] * col_mixed[r] for r in range(rank))
    gate = jax.nn.sigmoid(score)
    weights = counts * gate.astype(BF16).astype(F32)
    mixed = counted_dot(weights, spread, PLAIN).astype(BF16)
    memory_out = dot(mixed, proj_full, PLAIN)
    value_grad = dot(cotangent, proj_full, LAST).astype(BF16)
    pick_grad = dot(value_grad, spread, LAST)
    score_grad = pick_grad * gate * (1.0 - gate)
    blocks = []
    for mixed_scores, slot_key in ((col_mixed, slot_row), (row_mixed, slot_col)):
        for r in range(rank):
            grad = (score_grad * mixed_scores[r]).astype(BF16).astype(F32) * counts
            blocks.append(counted_dot(grad, slot_key, PLAIN).astype(BF16))
    query_grad = jnp.concatenate(blocks, axis=1)
    token_grad = dot(query_grad, query_full, PLAIN)
    return memory_out.astype(BF16), token_grad.astype(BF16)


def shards(
    mem, tokens, cotangent, w_query, key_row, key_col, tucker_core, table, w_proj, send_ids, pick_slot
):
    proj_count, value_width, _ = w_proj.shape
    requests = send_ids[0]
    owners, capacity = requests.shape
    slots = owners * capacity
    nkey = key_row.shape[0] * mem
    row_id = jnp.maximum(requests, 0) + jnp.arange(owners, dtype=jnp.int32)[:, None] * table.shape[0]
    row_id = row_id.reshape(slots)
    slot_proj = (row_id % nkey) % proj_count
    proj_part = w_proj.reshape(proj_count * value_width, -1)
    path = pieces_path if mem == 16 and w_proj.shape[2] == LANES else whole_path
    return path(tokens, cotangent, w_query, key_row, key_col, tucker_core, proj_part, requests, table, row_id,
                slot_proj, pick_slot, nkey, proj_count)


def solution(mesh):
    in_specs = (
        P(("groups", "mem"), None),
        P(("groups", "mem"), None),
        P(None, "mem"),
        P("mem", None),
        P("mem", None),
        P(),
        P("mem", None),
        P(None, None, "mem"),
        P(("groups", "mem"), None, None),
        P(("groups", "mem"), None),
    )
    out_specs = (P(("groups", "mem"), None), P(("groups", "mem"), None))
    body = functools.partial(shards, mesh.shape["mem"])
    return jax.shard_map(body, mesh=mesh, in_specs=in_specs, out_specs=out_specs, check_vma=False)
```

```python
import functools

import jax
import jax.numpy as jnp
from jax import lax
from jax.experimental import pallas as pl
from jax.experimental.pallas import tpu as pltpu
from jax.sharding import PartitionSpec as P

F32 = jnp.float32
BF16 = jnp.bfloat16
RING = (0, 2, 3, 1)
LANES = 128
LAST = ((1,), (1,))
PLAIN = ((1,), (0,))
VMEM_LIMIT = 56 * 1024 * 1024


def dot(a, b, dims):
    return lax.dot_general(a, b, (dims, ((), ())), preferred_element_type=F32)


def two_terms(x):
    high = x.astype(BF16)
    return high, (x - high.astype(F32)).astype(BF16)


def counted_dot(x, b, dims):
    high, low = two_terms(x)
    return dot(high, b, dims) + dot(low, b, dims)


def wanted_rows(requests):
    return lax.all_to_all(requests, "mem", split_axis=0, concat_axis=0, tiled=True)


def found_rows(wanted, table):
    found = jnp.take(table, jnp.maximum(wanted, 0).reshape(-1), axis=0, mode="clip")
    return found.reshape(wanted.shape + (table.shape[1],))


def returned_rows(found):
    return lax.all_to_all(found, "mem", split_axis=0, concat_axis=0, tiled=True)


def place(z, y, core):
    return (z * 2 + y) * 2 + core


def everywhere(move):
    pairs = []
    for z in range(4):
        for y in range(2):
            for core in range(2):
                pairs.append((place(z, y, core), place(*move(z, y, core))))
    return pairs


def next_z(x):
    step = {RING[i]: RING[(i + 1) % 4] for i in range(4)}
    return lax.ppermute(x, "mem", everywhere(lambda z, y, c: (step[z], y, c)))


def other_y(x):
    return lax.ppermute(x, "mem", everywhere(lambda z, y, c: (z, 1 - y, c)))


def other_core(x):
    return lax.ppermute(x, "mem", everywhere(lambda z, y, c: (z, y, 1 - c)))


def other_x(x):
    return lax.ppermute(x, "groups", [(0, 1), (1, 0)])


def ring_source(z, steps):
    index = jnp.where(z == 0, 0, jnp.where(z == 2, 1, jnp.where(z == 3, 2, 3)))
    index = (index + 4 - steps) % 4
    return jnp.where(index == 0, 0, jnp.where(index == 1, 2, jnp.where(index == 2, 3, 1)))


def tie(*values):
    return lax.optimization_barrier(values)


def own_halves(w_query, key_row, key_col, proj_part):
    columns = w_query.shape[1]
    proj = proj_part.reshape(2, -1, columns, LANES)
    query = jnp.concatenate([w_query.T, key_row, key_col], axis=1)
    query = query.reshape(columns, 2, -1, LANES).transpose(1, 2, 0, 3)
    return jnp.concatenate([proj, query], axis=1)


def other_cores(first, second):
    first = other_core(first)
    second, first = tie(second, first)
    return first, other_core(second)


def gather_pieces(own, requests, table, prepared):
    x = lax.axis_index("groups")
    own_near = lax.dynamic_index_in_dim(own, x, axis=0, keepdims=False)
    own_far = lax.dynamic_index_in_dim(own, 1 - x, axis=0, keepdims=False)
    pieces = {}
    z1, y0, wanted, own_other = tie(next_z(own_near), other_y(own_near), wanted_rows(requests), other_core(own))
    pieces[1, 0, 0, 0], pieces[0, 1, 0, 0] = z1, y0
    z2, y1, y0f, found, pieces[1, 0, 1, 0], pieces[0, 1, 1, 0] = tie(
        next_z(z1), other_y(z1), other_x(y0), found_rows(wanted, table), *other_cores(z1, y0)
    )
    pieces[2, 0, 0, 0], pieces[1, 1, 0, 0], pieces[0, 1, 0, 1] = z2, y1, y0f
    z3, y2, y1f, prepared, pieces[2, 0, 1, 0], pieces[1, 1, 1, 0] = tie(
        next_z(z2), other_y(z2), other_x(y1), prepared, *other_cores(z2, y1)
    )
    pieces[3, 0, 0, 0], pieces[2, 1, 0, 0], pieces[1, 1, 0, 1] = z3, y2, y1f
    z1f, y3, z3f, fetched, pieces[3, 0, 1, 0], pieces[0, 1, 1, 1] = tie(
        next_z(own_far), other_y(z3), other_x(z3), returned_rows(found), *other_cores(z3, y0f)
    )
    pieces[1, 0, 0, 1], pieces[3, 1, 0, 0], pieces[3, 0, 0, 1] = z1f, y3, z3f
    z2f, y3f, y2f, pieces[2, 1, 1, 0], pieces[1, 1, 1, 1] = tie(
        next_z(z1f), other_y(z3f), other_x(y2), *other_cores(y2, y1f)
    )
    pieces[2, 0, 0, 1], pieces[3, 1, 0, 1], pieces[2, 1, 0, 1] = z2f, y3f, y2f
    for steps, side, far in ((1, 0, 1), (3, 1, 0), (3, 0, 1), (2, 0, 1), (3, 1, 1), (2, 1, 1)):
        pieces[steps, side, 1, far] = other_core(pieces[steps, side, 0, far])
    return pieces, (own, own_other), fetched, prepared


def prepare_kernel(pick_ref, row_id_ref, counts_ref, wide_id_ref):
    wide_id_ref[...] = jnp.broadcast_to(row_id_ref[...], wide_id_ref.shape)
    token_rows, slots = counts_ref.shape
    lane = lax.broadcasted_iota(jnp.int32, (token_rows, slots), 1)
    pick = pick_ref[...]
    counts = jnp.zeros((token_rows, slots), F32)
    for k in range(pick.shape[1]):
        counts += jnp.where(pick[:, k:k + 1] == lane, 1.0, 0.0)
    counts_ref[...] = counts


def wide(held, first, last):
    return jnp.concatenate([held[j] for j in range(first, last)], axis=1)


def dense_kernel(
    rank, width, proj_count, keys, core_ref, row_id_ref, proj_ref, counts_ref, tokens_ref, cot_ref, fetched_ref, *refs
):
    piece_count = 2 + len(keys)
    pieces = refs[:piece_count]
    out_ref, grad_ref, query_held, proj_held, mixed_values, query_grad, query_sem, proj_sem = refs[piece_count:]
    features = tokens_ref.shape[1]
    token_rows, slots = counts_ref.shape
    value_width = fetched_ref.shape[1]
    columns = proj_held.shape[1]
    parts = value_width // columns
    me, x = lax.axis_index("mem"), lax.axis_index("groups")
    z, y, core = me // 4, (me // 2) % 2, me % 2
    spots = []
    for i, piece in enumerate(pieces):
        if i < 2:
            spots += [(piece.at[half], place(z, y, core if i == 0 else 1 - core), half) for half in range(2)]
        else:
            steps, side, other, far = keys[i - 2]
            at = place(ring_source(z, steps), 1 - y if side else y, 1 - core if other else core)
            spots.append((piece, at, 1 - x if far else x))
    half_proj = proj_held.shape[0] // 2
    half_query = query_held.shape[0] // 2
    for piece, at, half in spots:
        pltpu.make_async_copy(
            piece.at[pl.ds(half_proj, half_query)],
            query_held.at[pl.ds(half * half_query, half_query), pl.ds(pl.multiple_of(at * columns, columns), columns)],
            query_sem,
        ).start()
    for inner in range(proj_count // 2):
        for piece, at, half in spots:
            e = half * (proj_count // 2) + inner
            pltpu.make_async_copy(
                piece.at[pl.ds(inner * parts, parts)],
                proj_held.at[pl.ds(e * parts, parts), :, pl.ds(pl.multiple_of(at * LANES, LANES), LANES)],
                proj_sem.at[e],
            ).start()

    nkey = query_held.shape[1]
    key_at = lax.broadcasted_iota(jnp.int32, (slots, nkey), 1)
    row_id = row_id_ref[:, :1]
    row_hot = jnp.where(row_id // nkey == key_at, 1.0, 0.0).astype(BF16)
    col_hot = jnp.where(row_id % nkey == key_at, 1.0, 0.0).astype(BF16)
    pltpu.make_async_copy(query_held, query_held, query_sem).wait()
    key = features // LANES
    step = width // LANES
    slot_row = dot(row_hot, wide(query_held, key, key + step), PLAIN).astype(BF16)
    slot_col = dot(col_hot, wide(query_held, key + step, key + 2 * step), PLAIN).astype(BF16)
    queries = dot(tokens_ref[...], wide(query_held, 0, key), LAST).astype(BF16)
    block = [queries[:, r * width:(r + 1) * width] for r in range(2 * rank)]
    row_scores = [dot(block[r], slot_row, LAST) for r in range(rank)]
    col_scores = [dot(block[rank + r], slot_col, LAST) for r in range(rank)]
    col_mixed = [sum(core_ref[r, s] * col_scores[s] for s in range(rank)) for r in range(rank)]
    row_mixed = [sum(row_scores[r] * core_ref[r, s] for r in range(rank)) for s in range(rank)]
    score = sum(row_scores[r] * col_mixed[r] for r in range(rank))
    gate = 1.0 / (1.0 + jnp.exp(-score))
    counts = counts_ref[...]
    weights = (counts * gate.astype(BF16).astype(F32)).astype(BF16)
    slope = gate * (1.0 - gate)
    factors = [slope * m for m in col_mixed] + [slope * m for m in row_mixed]

    proj = proj_ref[...]
    fetched = fetched_ref[...]
    for e in range(proj_count):
        mixed = dot(jnp.where(proj == e, weights, jnp.zeros((), BF16)), fetched, PLAIN)
        mixed_values[:, e * value_width:(e + 1) * value_width] = mixed.astype(BF16)
    cot = cot_ref[...]
    pick_grad = jnp.zeros(counts.shape, F32)
    for inner in range(proj_count // 2):
        for e in (inner, proj_count // 2 + inner):
            held = proj_held.at[pl.ds(e * parts, parts)]
            pltpu.make_async_copy(held, held, proj_sem.at[e]).wait()
            grad = dot(cot, held[...].reshape(value_width, features), LAST).astype(BF16)
            pick_grad = jnp.where(proj == e, dot(grad, fetched, LAST), pick_grad)
    for i, factor in enumerate(factors):
        slot_key = slot_row if i < rank else slot_col
        grad = ((pick_grad * factor).astype(BF16).astype(F32) * counts).astype(BF16)
        query_grad[:, i * width:(i + 1) * width] = dot(grad, slot_key, PLAIN).astype(BF16)
    blocks = features // LANES // 4
    for c in range(4):
        cols = slice(c * blocks * LANES, (c + 1) * blocks * LANES)
        grad_ref[:, cols] = dot(query_grad[...], wide(query_held, c * blocks, (c + 1) * blocks), PLAIN).astype(BF16)
        held = proj_held[:, :, cols].reshape(proj_count * value_width, blocks * LANES)
        out_ref[:, cols] = dot(mixed_values[...], held, PLAIN).astype(BF16)


def vmem():
    return pl.BlockSpec(memory_space=pltpu.VMEM)


def smem():
    return pl.BlockSpec(memory_space=pltpu.SMEM)


def anywhere():
    return pl.BlockSpec(memory_space=pl.ANY)


def pieces_path(tokens, cotangent, w_query, key_row, key_col, tucker_core, proj_part, requests, table, row_id,
                slot_proj, pick_slot, nkey, proj_count):
    rank = tucker_core.shape[0]
    width = key_row.shape[1]
    token_rows, features = tokens.shape
    slots = row_id.shape[0]
    value_width = table.shape[1]
    columns = w_query.shape[1]
    own = own_halves(w_query, key_row, key_col, proj_part)
    params = pltpu.CompilerParams(vmem_limit_bytes=VMEM_LIMIT)
    prepared = pl.pallas_call(
        prepare_kernel,
        out_shape=(
            jax.ShapeDtypeStruct((token_rows, slots), F32),
            jax.ShapeDtypeStruct((slots, LANES), jnp.int32),
        ),
        in_specs=[vmem(), vmem()],
        out_specs=(vmem(), vmem()),
        compiler_params=params,
        cost_estimate=pl.CostEstimate(flops=3 * 10**9, bytes_accessed=10**6, transcendentals=0),
        name="prepare",
    )(pick_slot, row_id[:, None])
    pieces, pair, fetched, (counts, wide_id) = gather_pieces(own, requests, table, prepared)
    fetched = fetched.reshape(slots, value_width)
    keys = tuple(pieces)
    return pl.pallas_call(
        functools.partial(dense_kernel, rank, width, proj_count, keys),
        out_shape=(jax.ShapeDtypeStruct((token_rows, features), BF16),) * 2,
        in_specs=[smem()] + [vmem()] * 6 + [anywhere()] * (2 + len(keys)),
        out_specs=(vmem(), vmem()),
        scratch_shapes=[
            pltpu.VMEM(((features + 2 * width) // LANES, nkey, LANES), BF16),
            pltpu.VMEM((proj_count * value_width // columns, columns, features), BF16),
            pltpu.VMEM((token_rows, proj_count * value_width), BF16),
            pltpu.VMEM((token_rows, 2 * rank * width), BF16),
            pltpu.SemaphoreType.DMA,
            pltpu.SemaphoreType.DMA((proj_count,)),
        ],
        compiler_params=params,
        cost_estimate=pl.CostEstimate(flops=10**10, bytes_accessed=2 * 10**7, transcendentals=10**5),
        name="dense",
    )(
        tucker_core, wide_id, slot_proj[None, :], counts, tokens, cotangent, fetched, *pair,
        *[pieces[k] for k in keys],
    )


def whole_path(tokens, cotangent, w_query, key_row, key_col, tucker_core, proj_part, requests, table, row_id,
               slot_proj, pick_slot, nkey, proj_count):
    rank = tucker_core.shape[0]
    width = key_row.shape[1]
    slots = row_id.shape[0]
    fetched = returned_rows(found_rows(wanted_rows(requests), table)).reshape(slots, -1)
    query_full = lax.all_gather(w_query.T, "mem", axis=0, tiled=True)
    keys = lax.all_gather(jnp.concatenate([key_row, key_col], axis=1), "mem", axis=0, tiled=True)
    proj_full = lax.all_gather(proj_part, "mem", axis=1, tiled=True)
    key_at = jnp.arange(nkey, dtype=jnp.int32)[None, :]
    row_hot = ((row_id // nkey)[:, None] == key_at).astype(BF16)
    col_hot = ((row_id % nkey)[:, None] == key_at).astype(BF16)
    slot_row = dot(row_hot, keys[:, :width], PLAIN).astype(BF16)
    slot_col = dot(col_hot, keys[:, width:], PLAIN).astype(BF16)
    spread = jnp.where(
        slot_proj[:, None, None] == jnp.arange(proj_count, dtype=jnp.int32)[None, :, None],
        fetched[:, None, :], jnp.zeros((), BF16)
    ).reshape(slots, -1)
    counts = jnp.sum(
        (pick_slot[:, :, None] == jnp.arange(slots, dtype=jnp.int32)[None, None, :]).astype(F32), axis=1
    )
    queries = dot(tokens, query_full, LAST).astype(BF16)
    row_scores = [dot(queries[:, r * width:(r + 1) * width], slot_row, LAST) for r in range(rank)]
    col_scores = [
        dot(queries[:, (rank + r) * width:(rank + r + 1) * width], slot_col, LAST) for r in range(rank)
    ]
    col_mixed = [sum(tucker_core[r, s] * col_scores[s] for s in range(rank)) for r in range(rank)]
    row_mixed = [sum(row_scores[r] * tucker_core[r, s] for r in range(rank)) for s in range(rank)]
    score = sum(row_scores[r] * col_mixed[r] for r in range(rank))
    gate = jax.nn.sigmoid(score)
    weights = counts * gate.astype(BF16).astype(F32)
    mixed = counted_dot(weights, spread, PLAIN).astype(BF16)
    memory_out = dot(mixed, proj_full, PLAIN)
    value_grad = dot(cotangent, proj_full, LAST).astype(BF16)
    pick_grad = dot(value_grad, spread, LAST)
    score_grad = pick_grad * gate * (1.0 - gate)
    blocks = []
    for mixed_scores, slot_key in ((col_mixed, slot_row), (row_mixed, slot_col)):
        for r in range(rank):
            grad = (score_grad * mixed_scores[r]).astype(BF16).astype(F32) * counts
            blocks.append(counted_dot(grad, slot_key, PLAIN).astype(BF16))
    query_grad = jnp.concatenate(blocks, axis=1)
    token_grad = dot(query_grad, query_full, PLAIN)
    return memory_out.astype(BF16), token_grad.astype(BF16)


def shards(
    mem, tokens, cotangent, w_query, key_row, key_col, tucker_core, table, w_proj, send_ids, pick_slot
):
    proj_count, value_width, _ = w_proj.shape
    requests = send_ids[0]
    owners, capacity = requests.shape
    slots = owners * capacity
    nkey = key_row.shape[0] * mem
    row_id = jnp.maximum(requests, 0) + jnp.arange(owners, dtype=jnp.int32)[:, None] * table.shape[0]
    row_id = row_id.reshape(slots)
    slot_proj = (row_id % nkey) % proj_count
    proj_part = w_proj.reshape(proj_count * value_width, -1)
    path = pieces_path if mem == 16 and w_proj.shape[2] == LANES else whole_path
    return path(tokens, cotangent, w_query, key_row, key_col, tucker_core, proj_part, requests, table, row_id,
                slot_proj, pick_slot, nkey, proj_count)


def solution(mesh):
    in_specs = (
        P(("groups", "mem"), None),
        P(("groups", "mem"), None),
        P(None, "mem"),
        P("mem", None),
        P("mem", None),
        P(),
        P("mem", None),
        P(None, None, "mem"),
        P(("groups", "mem"), None, None),
        P(("groups", "mem"), None),
    )
    out_specs = (P(("groups", "mem"), None), P(("groups", "mem"), None))
    body = functools.partial(shards, mesh.shape["mem"])
    return jax.shard_map(body, mesh=mesh, in_specs=in_specs, out_specs=out_specs, check_vma=False)
```

```python
import functools

import jax
import jax.numpy as jnp
from jax import lax
from jax.experimental import pallas as pl
from jax.experimental.pallas import tpu as pltpu
from jax.sharding import PartitionSpec as P

F32 = jnp.float32
BF16 = jnp.bfloat16
RING = (0, 2, 3, 1)
LANES = 128
LAST = ((1,), (1,))
PLAIN = ((1,), (0,))
VMEM_LIMIT = 56 * 1024 * 1024


def dot(a, b, dims):
    return lax.dot_general(a, b, (dims, ((), ())), preferred_element_type=F32)


def two_terms(x):
    high = x.astype(BF16)
    return high, (x - high.astype(F32)).astype(BF16)


def counted_dot(x, b, dims):
    high, low = two_terms(x)
    return dot(high, b, dims) + dot(low, b, dims)


def wanted_rows(requests):
    return lax.all_to_all(requests, "mem", split_axis=0, concat_axis=0, tiled=True)


def found_rows(wanted, table):
    found = jnp.take(table, jnp.maximum(wanted, 0).reshape(-1), axis=0, mode="clip")
    return found.reshape(wanted.shape + (table.shape[1],))


def returned_rows(found):
    return lax.all_to_all(found, "mem", split_axis=0, concat_axis=0, tiled=True)


def place(z, y, core):
    return (z * 2 + y) * 2 + core


def everywhere(move):
    pairs = []
    for z in range(4):
        for y in range(2):
            for core in range(2):
                pairs.append((place(z, y, core), place(*move(z, y, core))))
    return pairs


def next_z(x):
    step = {RING[i]: RING[(i + 1) % 4] for i in range(4)}
    return lax.ppermute(x, "mem", everywhere(lambda z, y, c: (step[z], y, c)))


def other_y(x):
    return lax.ppermute(x, "mem", everywhere(lambda z, y, c: (z, 1 - y, c)))


def other_core(x):
    return lax.ppermute(x, "mem", everywhere(lambda z, y, c: (z, y, 1 - c)))


def other_x(x):
    return lax.ppermute(x, "groups", [(0, 1), (1, 0)])


def ring_source(z, steps):
    index = jnp.where(z == 0, 0, jnp.where(z == 2, 1, jnp.where(z == 3, 2, 3)))
    index = (index + 4 - steps) % 4
    return jnp.where(index == 0, 0, jnp.where(index == 1, 2, jnp.where(index == 2, 3, 1)))


def tie(*values):
    return lax.optimization_barrier(values)


def own_halves(w_query, key_row, key_col, proj_part):
    columns = w_query.shape[1]
    proj = proj_part.reshape(2, -1, columns, LANES)
    query = jnp.concatenate([w_query.T, key_row, key_col], axis=1)
    query = query.reshape(columns, 2, -1, LANES).transpose(1, 2, 0, 3)
    return proj, query


def other_cores(first, second):
    first = other_core(first)
    second, first = tie(second, first)
    return first, other_core(second)


def gather_pieces(own, requests, table, prepared):
    x = lax.axis_index("groups")
    own_near, own_far = [
        jnp.concatenate([lax.dynamic_index_in_dim(a, half, axis=0, keepdims=False) for a in own], axis=0)
        for half in (x, 1 - x)
    ]
    own_near, *own = tie(own_near, *own)
    own = jnp.concatenate(own, axis=1)
    pieces = {}
    z1, y0, wanted, own_other = tie(next_z(own_near), other_y(own_near), wanted_rows(requests), other_core(own))
    pieces[1, 0, 0, 0], pieces[0, 1, 0, 0] = z1, y0
    z2, y1, y0f, found, pieces[1, 0, 1, 0], pieces[0, 1, 1, 0] = tie(
        next_z(z1), other_y(z1), other_x(y0), found_rows(wanted, table), *other_cores(z1, y0)
    )
    pieces[2, 0, 0, 0], pieces[1, 1, 0, 0], pieces[0, 1, 0, 1] = z2, y1, y0f
    z3, y2, y1f, pieces[2, 0, 1, 0], pieces[1, 1, 1, 0] = tie(
        next_z(z2), other_y(z2), other_x(y1), *other_cores(z2, y1)
    )
    pieces[3, 0, 0, 0], pieces[2, 1, 0, 0], pieces[1, 1, 0, 1] = z3, y2, y1f
    z1f, y3, z3f, fetched, pieces[3, 0, 1, 0], pieces[0, 1, 1, 1] = tie(
        next_z(own_far), other_y(z3), other_x(z3), returned_rows(found), *other_cores(z3, y0f)
    )
    pieces[1, 0, 0, 1], pieces[3, 1, 0, 0], pieces[3, 0, 0, 1] = z1f, y3, z3f
    z2f, y3f, y2f, prepared, pieces[2, 1, 1, 0], pieces[1, 1, 1, 1] = tie(
        next_z(z1f), other_y(z3f), other_x(y2), tuple(prepared), *other_cores(y2, y1f)
    )
    pieces[2, 0, 0, 1], pieces[3, 1, 0, 1], pieces[2, 1, 0, 1] = z2f, y3f, y2f
    for steps, side, far in ((1, 0, 1), (3, 1, 0), (3, 0, 1), (2, 0, 1), (3, 1, 1), (2, 1, 1)):
        pieces[steps, side, 1, far] = other_core(pieces[steps, side, 0, far])
    return pieces, (own, own_other), fetched, prepared


def prepare_kernel(pick_ref, row_id_ref, tokens_ref, cot_ref, counts_ref, wide_id_ref, tokens_out, cot_out):
    wide_id_ref[...] = jnp.broadcast_to(row_id_ref[...], wide_id_ref.shape)
    slots, token_rows = counts_ref.shape
    place_at = lax.broadcasted_iota(jnp.int32, (slots, token_rows), 0)
    counts = jnp.zeros((slots, token_rows), F32)
    for k in range(pick_ref.shape[0]):
        counts += jnp.where(pick_ref[k:k + 1, :] == place_at, 1.0, 0.0)
    counts_ref[...] = counts
    tokens_out[...] = tokens_ref[...].T
    cot_out[...] = cot_ref[...].T


def wide(held, first, last):
    return jnp.concatenate([held[j] for j in range(first, last)], axis=1)


def dense_kernel(
    rank, width, proj_count, keys, core_ref, row_id_ref, proj_ref, counts_ref, tokens_ref, cot_ref, fetched_ref, *refs
):
    piece_count = 2 + len(keys)
    pieces = refs[:piece_count]
    out_ref, grad_ref, query_held, proj_held, mixed_values, query_grad, query_sem, proj_sem = refs[piece_count:]
    features = tokens_ref.shape[0]
    slots, token_rows = counts_ref.shape
    value_width = fetched_ref.shape[1]
    columns = proj_held.shape[1]
    parts = value_width // columns
    me, x = lax.axis_index("mem"), lax.axis_index("groups")
    z, y, core = me // 4, (me // 2) % 2, me % 2
    spots = []
    for i, piece in enumerate(pieces):
        if i < 2:
            spots += [(piece.at[half], place(z, y, core if i == 0 else 1 - core), half) for half in range(2)]
        else:
            steps, side, other, far = keys[i - 2]
            at = place(ring_source(z, steps), 1 - y if side else y, 1 - core if other else core)
            spots.append((piece, at, 1 - x if far else x))
    half_proj = proj_held.shape[0] // 2
    half_query = query_held.shape[0] // 2
    for piece, at, half in spots:
        pltpu.make_async_copy(
            piece.at[pl.ds(half_proj, half_query)],
            query_held.at[pl.ds(half * half_query, half_query), pl.ds(pl.multiple_of(at * columns, columns), columns)],
            query_sem,
        ).start()
    for inner in range(proj_count // 2):
        for piece, at, half in spots:
            e = half * (proj_count // 2) + inner
            pltpu.make_async_copy(
                piece.at[pl.ds(inner * parts, parts)],
                proj_held.at[pl.ds(e * parts, parts), :, pl.ds(pl.multiple_of(at * LANES, LANES), LANES)],
                proj_sem.at[e],
            ).start()

    nkey = query_held.shape[1]
    key_at = lax.broadcasted_iota(jnp.int32, (slots, nkey), 1)
    row_id = row_id_ref[:, :1]
    row_hot = jnp.where(row_id // nkey == key_at, 1.0, 0.0).astype(BF16)
    col_hot = jnp.where(row_id % nkey == key_at, 1.0, 0.0).astype(BF16)
    pltpu.make_async_copy(query_held, query_held, query_sem).wait()
    key = features // LANES
    step = width // LANES
    slot_row = dot(row_hot, wide(query_held, key, key + step), PLAIN).astype(BF16)
    slot_col = dot(col_hot, wide(query_held, key + step, key + 2 * step), PLAIN).astype(BF16)
    queries = dot(wide(query_held, 0, key), tokens_ref[...], PLAIN).astype(BF16)
    block = [queries[r * width:(r + 1) * width] for r in range(2 * rank)]
    row_scores = [dot(slot_row, block[r], PLAIN) for r in range(rank)]
    col_scores = [dot(slot_col, block[rank + r], PLAIN) for r in range(rank)]
    col_mixed = [sum(core_ref[r, s] * col_scores[s] for s in range(rank)) for r in range(rank)]
    row_mixed = [sum(row_scores[r] * core_ref[r, s] for r in range(rank)) for s in range(rank)]
    score = sum(row_scores[r] * col_mixed[r] for r in range(rank))
    gate = 1.0 / (1.0 + jnp.exp(-score))
    counts = counts_ref[...]
    weights = (counts * gate.astype(BF16).astype(F32)).T.astype(BF16)
    slope = gate * (1.0 - gate)
    factors = [slope * m for m in col_mixed] + [slope * m for m in row_mixed]

    proj = proj_ref[...]
    proj_tall = row_id % nkey % proj_count
    fetched = fetched_ref[...]
    for e in range(proj_count):
        mixed = dot(jnp.where(proj == e, weights, jnp.zeros((), BF16)), fetched, PLAIN)
        mixed_values[:, e * value_width:(e + 1) * value_width] = mixed.astype(BF16)
    cot = cot_ref[...]
    pick_grad = jnp.zeros(counts.shape, F32)
    for inner in range(proj_count // 2):
        for e in (inner, proj_count // 2 + inner):
            held = proj_held.at[pl.ds(e * parts, parts)]
            pltpu.make_async_copy(held, held, proj_sem.at[e]).wait()
            grad = dot(held[...].reshape(value_width, features), cot, PLAIN).astype(BF16)
            pick_grad = jnp.where(proj_tall == e, dot(fetched, grad, PLAIN), pick_grad)
    for i, factor in enumerate(factors):
        slot_key = slot_row if i < rank else slot_col
        grad = ((pick_grad * factor).astype(BF16).astype(F32) * counts).T.astype(BF16)
        query_grad[:, i * width:(i + 1) * width] = dot(grad, slot_key, PLAIN).astype(BF16)
    blocks = features // LANES // 4
    for c in range(4):
        cols = slice(c * blocks * LANES, (c + 1) * blocks * LANES)
        grad_ref[:, cols] = dot(query_grad[...], wide(query_held, c * blocks, (c + 1) * blocks), PLAIN).astype(BF16)
        held = proj_held[:, :, cols].reshape(proj_count * value_width, blocks * LANES)
        out_ref[:, cols] = dot(mixed_values[...], held, PLAIN).astype(BF16)


def vmem():
    return pl.BlockSpec(memory_space=pltpu.VMEM)


def smem():
    return pl.BlockSpec(memory_space=pltpu.SMEM)


def anywhere():
    return pl.BlockSpec(memory_space=pl.ANY)


def pieces_path(tokens, cotangent, w_query, key_row, key_col, tucker_core, proj_part, requests, table, row_id,
                slot_proj, pick_slot, nkey, proj_count):
    rank = tucker_core.shape[0]
    width = key_row.shape[1]
    token_rows, features = tokens.shape
    slots = row_id.shape[0]
    value_width = table.shape[1]
    columns = w_query.shape[1]
    own = own_halves(w_query, key_row, key_col, proj_part)
    params = pltpu.CompilerParams(vmem_limit_bytes=VMEM_LIMIT)
    prepared = pl.pallas_call(
        prepare_kernel,
        out_shape=(
            jax.ShapeDtypeStruct((slots, token_rows), F32),
            jax.ShapeDtypeStruct((slots, LANES), jnp.int32),
            jax.ShapeDtypeStruct((features, token_rows), BF16),
            jax.ShapeDtypeStruct((features, token_rows), BF16),
        ),
        in_specs=[vmem()] * 4,
        out_specs=(vmem(),) * 4,
        compiler_params=params,
        cost_estimate=pl.CostEstimate(flops=3 * 10**9, bytes_accessed=4 * 10**6, transcendentals=0),
        name="prepare",
    )(pick_slot.T, row_id[:, None], tokens, cotangent)
    pieces, pair, fetched, (counts, wide_id, tokens_tall, cot_tall) = gather_pieces(own, requests, table, prepared)
    fetched = fetched.reshape(slots, value_width)
    keys = tuple(pieces)
    return pl.pallas_call(
        functools.partial(dense_kernel, rank, width, proj_count, keys),
        out_shape=(jax.ShapeDtypeStruct((token_rows, features), BF16),) * 2,
        in_specs=[smem()] + [vmem()] * 6 + [anywhere()] * (2 + len(keys)),
        out_specs=(vmem(), vmem()),
        scratch_shapes=[
            pltpu.VMEM(((features + 2 * width) // LANES, nkey, LANES), BF16),
            pltpu.VMEM((proj_count * value_width // columns, columns, features), BF16),
            pltpu.VMEM((token_rows, proj_count * value_width), BF16),
            pltpu.VMEM((token_rows, 2 * rank * width), BF16),
            pltpu.SemaphoreType.DMA,
            pltpu.SemaphoreType.DMA((proj_count,)),
        ],
        compiler_params=params,
        cost_estimate=pl.CostEstimate(flops=10**10, bytes_accessed=2 * 10**7, transcendentals=10**5),
        name="dense",
    )(
        tucker_core, wide_id, slot_proj[None, :], counts, tokens_tall, cot_tall, fetched, *pair,
        *[pieces[k] for k in keys],
    )


def whole_path(tokens, cotangent, w_query, key_row, key_col, tucker_core, proj_part, requests, table, row_id,
               slot_proj, pick_slot, nkey, proj_count):
    rank = tucker_core.shape[0]
    width = key_row.shape[1]
    slots = row_id.shape[0]
    fetched = returned_rows(found_rows(wanted_rows(requests), table)).reshape(slots, -1)
    query_full = lax.all_gather(w_query.T, "mem", axis=0, tiled=True)
    keys = lax.all_gather(jnp.concatenate([key_row, key_col], axis=1), "mem", axis=0, tiled=True)
    proj_full = lax.all_gather(proj_part, "mem", axis=1, tiled=True)
    key_at = jnp.arange(nkey, dtype=jnp.int32)[None, :]
    row_hot = ((row_id // nkey)[:, None] == key_at).astype(BF16)
    col_hot = ((row_id % nkey)[:, None] == key_at).astype(BF16)
    slot_row = dot(row_hot, keys[:, :width], PLAIN).astype(BF16)
    slot_col = dot(col_hot, keys[:, width:], PLAIN).astype(BF16)
    spread = jnp.where(
        slot_proj[:, None, None] == jnp.arange(proj_count, dtype=jnp.int32)[None, :, None],
        fetched[:, None, :], jnp.zeros((), BF16)
    ).reshape(slots, -1)
    counts = jnp.sum(
        (pick_slot[:, :, None] == jnp.arange(slots, dtype=jnp.int32)[None, None, :]).astype(F32), axis=1
    )
    queries = dot(tokens, query_full, LAST).astype(BF16)
    row_scores = [dot(queries[:, r * width:(r + 1) * width], slot_row, LAST) for r in range(rank)]
    col_scores = [
        dot(queries[:, (rank + r) * width:(rank + r + 1) * width], slot_col, LAST) for r in range(rank)
    ]
    col_mixed = [sum(tucker_core[r, s] * col_scores[s] for s in range(rank)) for r in range(rank)]
    row_mixed = [sum(row_scores[r] * tucker_core[r, s] for r in range(rank)) for s in range(rank)]
    score = sum(row_scores[r] * col_mixed[r] for r in range(rank))
    gate = jax.nn.sigmoid(score)
    weights = counts * gate.astype(BF16).astype(F32)
    mixed = counted_dot(weights, spread, PLAIN).astype(BF16)
    memory_out = dot(mixed, proj_full, PLAIN)
    value_grad = dot(cotangent, proj_full, LAST).astype(BF16)
    pick_grad = dot(value_grad, spread, LAST)
    score_grad = pick_grad * gate * (1.0 - gate)
    blocks = []
    for mixed_scores, slot_key in ((col_mixed, slot_row), (row_mixed, slot_col)):
        for r in range(rank):
            grad = (score_grad * mixed_scores[r]).astype(BF16).astype(F32) * counts
            blocks.append(counted_dot(grad, slot_key, PLAIN).astype(BF16))
    query_grad = jnp.concatenate(blocks, axis=1)
    token_grad = dot(query_grad, query_full, PLAIN)
    return memory_out.astype(BF16), token_grad.astype(BF16)


def shards(
    mem, tokens, cotangent, w_query, key_row, key_col, tucker_core, table, w_proj, send_ids, pick_slot
):
    proj_count, value_width, _ = w_proj.shape
    requests = send_ids[0]
    owners, capacity = requests.shape
    slots = owners * capacity
    nkey = key_row.shape[0] * mem
    row_id = jnp.maximum(requests, 0) + jnp.arange(owners, dtype=jnp.int32)[:, None] * table.shape[0]
    row_id = row_id.reshape(slots)
    slot_proj = (row_id % nkey) % proj_count
    proj_part = w_proj.reshape(proj_count * value_width, -1)
    path = pieces_path if mem == 16 and w_proj.shape[2] == LANES else whole_path
    return path(tokens, cotangent, w_query, key_row, key_col, tucker_core, proj_part, requests, table, row_id,
                slot_proj, pick_slot, nkey, proj_count)


def solution(mesh):
    in_specs = (
        P(("groups", "mem"), None),
        P(("groups", "mem"), None),
        P(None, "mem"),
        P("mem", None),
        P("mem", None),
        P(),
        P("mem", None),
        P(None, None, "mem"),
        P(("groups", "mem"), None, None),
        P(("groups", "mem"), None),
    )
    out_specs = (P(("groups", "mem"), None), P(("groups", "mem"), None))
    body = functools.partial(shards, mesh.shape["mem"])
    return jax.shard_map(body, mesh=mesh, in_specs=in_specs, out_specs=out_specs, check_vma=False)
```

```python
import functools

import jax
import jax.numpy as jnp
from jax import lax
from jax.experimental import pallas as pl
from jax.experimental.pallas import tpu as pltpu
from jax.sharding import PartitionSpec as P

F32 = jnp.float32
BF16 = jnp.bfloat16
RING = (0, 2, 3, 1)
LANES = 128
LAST = ((1,), (1,))
PLAIN = ((1,), (0,))
VMEM_LIMIT = 56 * 1024 * 1024


def dot(a, b, dims):
    return lax.dot_general(a, b, (dims, ((), ())), preferred_element_type=F32)


def two_terms(x):
    high = x.astype(BF16)
    return high, (x - high.astype(F32)).astype(BF16)


def counted_dot(x, b, dims):
    high, low = two_terms(x)
    return dot(high, b, dims) + dot(low, b, dims)


def wanted_rows(requests):
    return lax.all_to_all(requests, "mem", split_axis=0, concat_axis=0, tiled=True)


def found_rows(wanted, table):
    found = jnp.take(table, jnp.maximum(wanted, 0).reshape(-1), axis=0, mode="clip")
    return found.reshape(wanted.shape + (table.shape[1],))


def returned_rows(found):
    return lax.all_to_all(found, "mem", split_axis=0, concat_axis=0, tiled=True)


def place(z, y, core):
    return (z * 2 + y) * 2 + core


def everywhere(move):
    pairs = []
    for z in range(4):
        for y in range(2):
            for core in range(2):
                pairs.append((place(z, y, core), place(*move(z, y, core))))
    return pairs


def next_z(x):
    step = {RING[i]: RING[(i + 1) % 4] for i in range(4)}
    return lax.ppermute(x, "mem", everywhere(lambda z, y, c: (step[z], y, c)))


def other_y(x):
    return lax.ppermute(x, "mem", everywhere(lambda z, y, c: (z, 1 - y, c)))


def other_core(x):
    return lax.ppermute(x, "mem", everywhere(lambda z, y, c: (z, y, 1 - c)))


def other_x(x):
    return lax.ppermute(x, "groups", [(0, 1), (1, 0)])


def ring_source(z, steps):
    index = jnp.where(z == 0, 0, jnp.where(z == 2, 1, jnp.where(z == 3, 2, 3)))
    index = (index + 4 - steps) % 4
    return jnp.where(index == 0, 0, jnp.where(index == 1, 2, jnp.where(index == 2, 3, 1)))


def tie(*values):
    return lax.optimization_barrier(values)


def own_halves(w_query, key_row, key_col, proj_part):
    columns = w_query.shape[1]
    proj = proj_part.reshape(2, -1, columns, LANES)
    query = jnp.concatenate([w_query.T, key_row, key_col], axis=1)
    query = query.reshape(columns, 2, -1, LANES).transpose(1, 2, 0, 3)
    return proj, query


def other_cores(first, second):
    first = other_core(first)
    second, first = tie(second, first)
    return first, other_core(second)


def gather_pieces(own, requests, table, prepared):
    x = lax.axis_index("groups")
    own_near, own_far = [
        jnp.concatenate([lax.dynamic_index_in_dim(a, half, axis=0, keepdims=False) for a in own], axis=0)
        for half in (x, 1 - x)
    ]
    own_near, *own = tie(own_near, *own)
    own = jnp.concatenate(own, axis=1)
    pieces = {}
    z1, y0, wanted, own_other = tie(next_z(own_near), other_y(own_near), wanted_rows(requests), other_core(own))
    pieces[1, 0, 0, 0], pieces[0, 1, 0, 0] = z1, y0
    z2, y1, y0f, found, pieces[1, 0, 1, 0], pieces[0, 1, 1, 0] = tie(
        next_z(z1), other_y(z1), other_x(y0), found_rows(wanted, table), *other_cores(z1, y0)
    )
    pieces[2, 0, 0, 0], pieces[1, 1, 0, 0], pieces[0, 1, 0, 1] = z2, y1, y0f
    z3, y2, y1f, pieces[2, 0, 1, 0], pieces[1, 1, 1, 0] = tie(
        next_z(z2), other_y(z2), other_x(y1), *other_cores(z2, y1)
    )
    pieces[3, 0, 0, 0], pieces[2, 1, 0, 0], pieces[1, 1, 0, 1] = z3, y2, y1f
    z1f, y3, z3f, pieces[3, 0, 1, 0], pieces[0, 1, 1, 1] = tie(
        next_z(own_far), other_y(z3), other_x(z3), *other_cores(z3, y0f)
    )
    pieces[1, 0, 0, 1], pieces[3, 1, 0, 0], pieces[3, 0, 0, 1] = z1f, y3, z3f
    z2f, y3f, y2f, fetched, prepared, pieces[2, 1, 1, 0], pieces[1, 1, 1, 1] = tie(
        next_z(z1f), other_y(z3f), other_x(y2), returned_rows(found), tuple(prepared), *other_cores(y2, y1f)
    )
    pieces[2, 0, 0, 1], pieces[3, 1, 0, 1], pieces[2, 1, 0, 1] = z2f, y3f, y2f
    for steps, side, far in ((1, 0, 1), (3, 1, 0), (3, 0, 1), (2, 0, 1), (3, 1, 1), (2, 1, 1)):
        pieces[steps, side, 1, far] = other_core(pieces[steps, side, 0, far])
    return pieces, (own, own_other), fetched, prepared


def prepare_kernel(nkey, proj_count, pick_ref, row_id_ref, counts_ref, wide_id_ref, proj_ref):
    wide_id = jnp.broadcast_to(row_id_ref[...], wide_id_ref.shape)
    wide_id_ref[...] = wide_id
    proj_ref[...] = (wide_id % nkey % proj_count).T[:proj_ref.shape[0]]
    token_rows, slots = counts_ref.shape
    lane = lax.broadcasted_iota(jnp.int32, (token_rows, slots), 1)
    pick = pick_ref[...]
    counts = jnp.zeros((token_rows, slots), F32)
    for k in range(pick.shape[1]):
        counts += jnp.where(pick[:, k:k + 1] == lane, 1.0, 0.0)
    counts_ref[...] = counts


def wide(held, first, last):
    return jnp.concatenate([held[j] for j in range(first, last)], axis=1)


def dense_kernel(
    rank, width, proj_count, keys, core_ref, row_id_ref, proj_ref, counts_ref, tokens_ref, cot_ref, fetched_ref, *refs
):
    piece_count = 2 + len(keys)
    pieces = refs[:piece_count]
    out_ref, grad_ref, query_held, proj_held, mixed_values, query_grad, tokens, cot, fetched_held, counts_held = refs[
        piece_count:piece_count + 10
    ]
    out_held, grad_held, query_sem, proj_sem, in_sem, out_sem = refs[piece_count + 10:]
    token_rows, features = tokens.shape
    slots, value_width = fetched_held.shape
    columns = proj_held.shape[1]
    parts = value_width // columns
    me, x = lax.axis_index("mem"), lax.axis_index("groups")
    z, y, core = me // 4, (me // 2) % 2, me % 2
    spots = []
    for i, piece in enumerate(pieces):
        if i < 2:
            spots += [(piece.at[half], place(z, y, core if i == 0 else 1 - core), half) for half in range(2)]
        else:
            steps, side, other, far = keys[i - 2]
            at = place(ring_source(z, steps), 1 - y if side else y, 1 - core if other else core)
            spots.append((piece, at, 1 - x if far else x))
    half_proj = proj_held.shape[0] // 2
    half_query = query_held.shape[0] // 2
    half_count = proj_count // 2

    def start_proj(inner):
        for piece, at, half in spots:
            e = half * half_count + inner
            pltpu.make_async_copy(
                piece.at[pl.ds(inner * parts, parts)],
                proj_held.at[pl.ds(e * parts, parts), :, pl.ds(pl.multiple_of(at * LANES, LANES), LANES)],
                proj_sem.at[e],
            ).start()

    inputs = [
        pltpu.make_async_copy(source, target, in_sem.at[i])
        for i, (source, target) in enumerate(
            ((cot_ref, cot), (tokens_ref, tokens), (counts_ref, counts_held), (fetched_ref, fetched_held))
        )
    ]
    inputs[0].start()
    start_proj(0)
    inputs[1].start()
    for piece, at, half in spots:
        pltpu.make_async_copy(
            piece.at[pl.ds(half_proj, half_query)],
            query_held.at[pl.ds(half * half_query, half_query), pl.ds(pl.multiple_of(at * columns, columns), columns)],
            query_sem,
        ).start()
    inputs[2].start()
    inputs[3].start()
    for inner in range(1, half_count):
        start_proj(inner)

    def value_grad(e):
        return dot(cot[...], proj_held[e * parts:(e + 1) * parts].reshape(value_width, features), LAST).astype(BF16)

    def wait_proj(e):
        held = proj_held.at[pl.ds(e * parts, parts)]
        pltpu.make_async_copy(held, held, proj_sem.at[e]).wait()

    nkey = query_held.shape[1]
    key_at = lax.broadcasted_iota(jnp.int32, (slots, nkey), 1)
    row_id = row_id_ref[:, :1]
    row_hot = jnp.where(row_id // nkey == key_at, 1.0, 0.0).astype(BF16)
    col_hot = jnp.where(row_id % nkey == key_at, 1.0, 0.0).astype(BF16)
    inputs[0].wait()
    value_grads = {}
    for e in (0, half_count):
        wait_proj(e)
        value_grads[e] = value_grad(e)
    inputs[1].wait()
    pltpu.make_async_copy(query_held, query_held, query_sem).wait()
    inputs[2].wait()
    inputs[3].wait()
    for e in range(proj_count):
        if e % half_count:
            wait_proj(e)

    key = features // LANES
    step = width // LANES
    slot_row = dot(row_hot, wide(query_held, key, key + step), PLAIN).astype(BF16)
    slot_col = dot(col_hot, wide(query_held, key + step, key + 2 * step), PLAIN).astype(BF16)
    queries = dot(tokens[...], wide(query_held, 0, key), LAST).astype(BF16)
    proj = proj_ref[:1]
    fetched = fetched_held[...]
    late = [e for e in range(proj_count) if e % half_count]
    rows = token_rows // 4
    weights, factors = [], []
    for c in range(4):
        block = [queries[c * rows:(c + 1) * rows, r * width:(r + 1) * width] for r in range(2 * rank)]
        row_scores = [dot(block[r], slot_row, LAST) for r in range(rank)]
        col_scores = [dot(block[rank + r], slot_col, LAST) for r in range(rank)]
        if c < len(late):
            value_grads[late[c]] = value_grad(late[c])
        col_mixed = [sum(core_ref[r, s] * col_scores[s] for s in range(rank)) for r in range(rank)]
        row_mixed = [sum(row_scores[r] * core_ref[r, s] for r in range(rank)) for s in range(rank)]
        score = sum(row_scores[r] * col_mixed[r] for r in range(rank))
        gate = 1.0 / (1.0 + jnp.exp(-score))
        weights.append((counts_held[c * rows:(c + 1) * rows] * gate.astype(BF16).astype(F32)).astype(BF16))
        slope = gate * (1.0 - gate)
        factors.append([slope * m for m in col_mixed] + [slope * m for m in row_mixed])
    weights = jnp.concatenate(weights, axis=0)
    for e in range(proj_count):
        mixed = dot(jnp.where(proj == e, weights, jnp.zeros((), BF16)), fetched, PLAIN)
        mixed_values[:, e * value_width:(e + 1) * value_width] = mixed.astype(BF16)

    def columns_of(c):
        return slice(c * (features // 4), (c + 1) * (features // 4))

    def send(held, target, c, sem):
        pltpu.make_async_copy(held.at[:, columns_of(c)], target.at[:, columns_of(c)], sem).start()

    for c in range(4):
        part = slice(c * rows, (c + 1) * rows)
        pick_grad = jnp.zeros((rows, slots), F32)
        for e in range(proj_count):
            pick_grad = jnp.where(proj == e, dot(value_grads[e][part], fetched, LAST), pick_grad)
        held = proj_held[:, :, columns_of(c)].reshape(proj_count * value_width, features // 4)
        out_held[:, columns_of(c)] = dot(mixed_values[...], held, PLAIN).astype(BF16)
        send(out_held, out_ref, c, out_sem.at[0])
        for i in range(2 * rank):
            slot_key = slot_row if i < rank else slot_col
            grad = ((pick_grad * factors[c][i]).astype(BF16).astype(F32) * counts_held[part]).astype(BF16)
            query_grad[part, i * width:(i + 1) * width] = dot(grad, slot_key, PLAIN).astype(BF16)
    blocks = features // LANES // 4
    for c in range(4):
        held = wide(query_held, c * blocks, (c + 1) * blocks)
        grad_held[:, columns_of(c)] = dot(query_grad[...], held, PLAIN).astype(BF16)
        send(grad_held, grad_ref, c, out_sem.at[1])
    pltpu.make_async_copy(out_held, out_ref, out_sem.at[0]).wait()
    pltpu.make_async_copy(grad_held, grad_ref, out_sem.at[1]).wait()


def vmem():
    return pl.BlockSpec(memory_space=pltpu.VMEM)


def smem():
    return pl.BlockSpec(memory_space=pltpu.SMEM)


def anywhere():
    return pl.BlockSpec(memory_space=pl.ANY)


def pieces_path(tokens, cotangent, w_query, key_row, key_col, tucker_core, proj_part, requests, table, row_id,
                slot_proj, pick_slot, nkey, proj_count):
    rank = tucker_core.shape[0]
    width = key_row.shape[1]
    token_rows, features = tokens.shape
    slots = row_id.shape[0]
    value_width = table.shape[1]
    columns = w_query.shape[1]
    own = own_halves(w_query, key_row, key_col, proj_part)
    params = pltpu.CompilerParams(vmem_limit_bytes=VMEM_LIMIT)
    prepared = pl.pallas_call(
        functools.partial(prepare_kernel, nkey, proj_count),
        out_shape=(
            jax.ShapeDtypeStruct((token_rows, slots), F32),
            jax.ShapeDtypeStruct((slots, LANES), jnp.int32),
            jax.ShapeDtypeStruct((8, slots), jnp.int32),
        ),
        in_specs=[vmem(), vmem()],
        out_specs=(vmem(),) * 3,
        compiler_params=params,
        cost_estimate=pl.CostEstimate(flops=3 * 10**9, bytes_accessed=10**6, transcendentals=0),
        name="prepare",
    )(pick_slot, row_id[:, None])
    pieces, pair, fetched, (counts, wide_id, slot_proj) = gather_pieces(own, requests, table, prepared)
    fetched = fetched.reshape(slots, value_width)
    keys = tuple(pieces)
    tall = (token_rows, features)
    return pl.pallas_call(
        functools.partial(dense_kernel, rank, width, proj_count, keys),
        out_shape=(jax.ShapeDtypeStruct(tall, BF16),) * 2,
        in_specs=[smem(), vmem(), vmem()] + [anywhere()] * (6 + len(keys)),
        out_specs=(anywhere(), anywhere()),
        scratch_shapes=[
            pltpu.VMEM(((features + 2 * width) // LANES, nkey, LANES), BF16),
            pltpu.VMEM((proj_count * value_width // columns, columns, features), BF16),
            pltpu.VMEM((token_rows, proj_count * value_width), BF16),
            pltpu.VMEM((token_rows, 2 * rank * width), BF16),
            pltpu.VMEM(tall, BF16),
            pltpu.VMEM(tall, BF16),
            pltpu.VMEM((slots, value_width), BF16),
            pltpu.VMEM((token_rows, slots), F32),
            pltpu.VMEM(tall, BF16),
            pltpu.VMEM(tall, BF16),
            pltpu.SemaphoreType.DMA,
            pltpu.SemaphoreType.DMA((proj_count,)),
            pltpu.SemaphoreType.DMA((4,)),
            pltpu.SemaphoreType.DMA((2,)),
        ],
        compiler_params=params,
        cost_estimate=pl.CostEstimate(flops=10**10, bytes_accessed=2 * 10**7, transcendentals=10**5),
        name="dense",
    )(
        tucker_core, wide_id, slot_proj, counts, tokens, cotangent, fetched, *pair, *[pieces[k] for k in keys]
    )


def whole_path(tokens, cotangent, w_query, key_row, key_col, tucker_core, proj_part, requests, table, row_id,
               slot_proj, pick_slot, nkey, proj_count):
    rank = tucker_core.shape[0]
    width = key_row.shape[1]
    slots = row_id.shape[0]
    fetched = returned_rows(found_rows(wanted_rows(requests), table)).reshape(slots, -1)
    query_full = lax.all_gather(w_query.T, "mem", axis=0, tiled=True)
    keys = lax.all_gather(jnp.concatenate([key_row, key_col], axis=1), "mem", axis=0, tiled=True)
    proj_full = lax.all_gather(proj_part, "mem", axis=1, tiled=True)
    key_at = jnp.arange(nkey, dtype=jnp.int32)[None, :]
    row_hot = ((row_id // nkey)[:, None] == key_at).astype(BF16)
    col_hot = ((row_id % nkey)[:, None] == key_at).astype(BF16)
    slot_row = dot(row_hot, keys[:, :width], PLAIN).astype(BF16)
    slot_col = dot(col_hot, keys[:, width:], PLAIN).astype(BF16)
    spread = jnp.where(
        slot_proj[:, None, None] == jnp.arange(proj_count, dtype=jnp.int32)[None, :, None],
        fetched[:, None, :], jnp.zeros((), BF16)
    ).reshape(slots, -1)
    counts = jnp.sum(
        (pick_slot[:, :, None] == jnp.arange(slots, dtype=jnp.int32)[None, None, :]).astype(F32), axis=1
    )
    queries = dot(tokens, query_full, LAST).astype(BF16)
    row_scores = [dot(queries[:, r * width:(r + 1) * width], slot_row, LAST) for r in range(rank)]
    col_scores = [
        dot(queries[:, (rank + r) * width:(rank + r + 1) * width], slot_col, LAST) for r in range(rank)
    ]
    col_mixed = [sum(tucker_core[r, s] * col_scores[s] for s in range(rank)) for r in range(rank)]
    row_mixed = [sum(row_scores[r] * tucker_core[r, s] for r in range(rank)) for s in range(rank)]
    score = sum(row_scores[r] * col_mixed[r] for r in range(rank))
    gate = jax.nn.sigmoid(score)
    weights = counts * gate.astype(BF16).astype(F32)
    mixed = counted_dot(weights, spread, PLAIN).astype(BF16)
    memory_out = dot(mixed, proj_full, PLAIN)
    value_grad = dot(cotangent, proj_full, LAST).astype(BF16)
    pick_grad = dot(value_grad, spread, LAST)
    score_grad = pick_grad * gate * (1.0 - gate)
    blocks = []
    for mixed_scores, slot_key in ((col_mixed, slot_row), (row_mixed, slot_col)):
        for r in range(rank):
            grad = (score_grad * mixed_scores[r]).astype(BF16).astype(F32) * counts
            blocks.append(counted_dot(grad, slot_key, PLAIN).astype(BF16))
    query_grad = jnp.concatenate(blocks, axis=1)
    token_grad = dot(query_grad, query_full, PLAIN)
    return memory_out.astype(BF16), token_grad.astype(BF16)


def shards(
    mem, tokens, cotangent, w_query, key_row, key_col, tucker_core, table, w_proj, send_ids, pick_slot
):
    proj_count, value_width, _ = w_proj.shape
    requests = send_ids[0]
    owners, capacity = requests.shape
    slots = owners * capacity
    nkey = key_row.shape[0] * mem
    row_id = jnp.maximum(requests, 0) + jnp.arange(owners, dtype=jnp.int32)[:, None] * table.shape[0]
    row_id = row_id.reshape(slots)
    slot_proj = (row_id % nkey) % proj_count
    proj_part = w_proj.reshape(proj_count * value_width, -1)
    path = pieces_path if mem == 16 and w_proj.shape[2] == LANES else whole_path
    return path(tokens, cotangent, w_query, key_row, key_col, tucker_core, proj_part, requests, table, row_id,
                slot_proj, pick_slot, nkey, proj_count)


def solution(mesh):
    in_specs = (
        P(("groups", "mem"), None),
        P(("groups", "mem"), None),
        P(None, "mem"),
        P("mem", None),
        P("mem", None),
        P(),
        P("mem", None),
        P(None, None, "mem"),
        P(("groups", "mem"), None, None),
        P(("groups", "mem"), None),
    )
    out_specs = (P(("groups", "mem"), None), P(("groups", "mem"), None))
    body = functools.partial(shards, mesh.shape["mem"])
    return jax.shard_map(body, mesh=mesh, in_specs=in_specs, out_specs=out_specs, check_vma=False)
```

```python
import functools

import jax
import jax.numpy as jnp
from jax import lax
from jax.experimental import pallas as pl
from jax.experimental.pallas import tpu as pltpu
from jax.sharding import PartitionSpec as P

F32 = jnp.float32
BF16 = jnp.bfloat16
RING = (0, 2, 3, 1)
LANES = 128
LAST = ((1,), (1,))
PLAIN = ((1,), (0,))
VMEM_LIMIT = 36 * 1024 * 1024
SMALL_LIMIT = 8 * 1024 * 1024


def dot(a, b, dims):
    return lax.dot_general(a, b, (dims, ((), ())), preferred_element_type=F32)


def two_terms(x):
    high = x.astype(BF16)
    return high, (x - high.astype(F32)).astype(BF16)


def counted_dot(x, b, dims):
    high, low = two_terms(x)
    return dot(high, b, dims) + dot(low, b, dims)


def wanted_rows(requests):
    return lax.all_to_all(requests, "mem", split_axis=0, concat_axis=0, tiled=True)


def found_rows(wanted, table):
    found = jnp.take(table, jnp.maximum(wanted, 0).reshape(-1), axis=0, mode="clip")
    return found.reshape(wanted.shape + (table.shape[1],))


def returned_rows(found):
    return lax.all_to_all(found, "mem", split_axis=0, concat_axis=0, tiled=True)


def place(z, y, core):
    return (z * 2 + y) * 2 + core


def everywhere(move):
    pairs = []
    for z in range(4):
        for y in range(2):
            for core in range(2):
                pairs.append((place(z, y, core), place(*move(z, y, core))))
    return pairs


def next_z(x):
    step = {RING[i]: RING[(i + 1) % 4] for i in range(4)}
    return lax.ppermute(x, "mem", everywhere(lambda z, y, c: (step[z], y, c)))


def other_y(x):
    return lax.ppermute(x, "mem", everywhere(lambda z, y, c: (z, 1 - y, c)))


def other_core(x):
    return lax.ppermute(x, "mem", everywhere(lambda z, y, c: (z, y, 1 - c)))


def other_x(x):
    return lax.ppermute(x, "groups", [(0, 1), (1, 0)])


def ring_source(z, steps):
    index = jnp.where(z == 0, 0, jnp.where(z == 2, 1, jnp.where(z == 3, 2, 3)))
    index = (index + 4 - steps) % 4
    return jnp.where(index == 0, 0, jnp.where(index == 1, 2, jnp.where(index == 2, 3, 1)))


def tie(*values):
    return lax.optimization_barrier(values)


def halves_kernel(query_ref, key_row_ref, key_col_ref, proj_ref, near_ref, far_ref, held, sems):
    x = lax.axis_index("groups")
    half_proj = proj_ref.shape[1]
    half_query = held.shape[0] // 2
    copies = []
    for i, (target, half) in enumerate(((near_ref, x), (far_ref, 1 - x))):
        copies.append(pltpu.make_async_copy(proj_ref.at[half], target.at[pl.ds(0, half_proj)], sems.at[2 * i]))
        copies[-1].start()
    j = 0
    for ref in (query_ref, key_row_ref, key_col_ref):
        for c in range(ref.shape[1] // LANES):
            held[j] = ref[:, c * LANES:(c + 1) * LANES]
            j += 1
    for i, (target, half) in enumerate(((near_ref, x), (far_ref, 1 - x))):
        copies.append(
            pltpu.make_async_copy(
                held.at[pl.ds(half * half_query, half_query)], target.at[pl.ds(half_proj, half_query)],
                sems.at[2 * i + 1],
            )
        )
        copies[-1].start()
    for copy in copies:
        copy.wait()


def own_halves(w_query, key_row, key_col, proj_part):
    features, columns = w_query.shape
    proj = proj_part.reshape(2, -1, columns, LANES)
    query_blocks = (features + key_row.shape[1] + key_col.shape[1]) // LANES
    half = jax.ShapeDtypeStruct((proj.shape[1] + query_blocks // 2, columns, LANES), BF16)
    return pl.pallas_call(
        halves_kernel,
        out_shape=(half, half),
        in_specs=[vmem()] * 3 + [anywhere()],
        out_specs=(anywhere(), anywhere()),
        scratch_shapes=[pltpu.VMEM((query_blocks, columns, LANES), BF16), pltpu.SemaphoreType.DMA((4,))],
        compiler_params=pltpu.CompilerParams(vmem_limit_bytes=SMALL_LIMIT),
        cost_estimate=pl.CostEstimate(flops=0, bytes_accessed=4 * 10**6, transcendentals=0),
        name="halves",
    )(w_query.T, key_row, key_col, proj)


def other_cores(first, second):
    first = other_core(first)
    second, first = tie(second, first)
    return first, other_core(second)


def gather_pieces(own_near, own_far, requests, table, prepared):
    pieces = {(0, 0, 0, 0): own_near, (0, 0, 0, 1): own_far}
    z1, y0, wanted, pieces[0, 0, 1, 0], pieces[0, 0, 1, 1] = tie(
        next_z(own_near), other_y(own_near), wanted_rows(requests), other_core(own_near), other_core(own_far)
    )
    pieces[1, 0, 0, 0], pieces[0, 1, 0, 0] = z1, y0
    z2, y1, y0f, found, pieces[1, 0, 1, 0], pieces[0, 1, 1, 0] = tie(
        next_z(z1), other_y(z1), other_x(y0), found_rows(wanted, table), *other_cores(z1, y0)
    )
    pieces[2, 0, 0, 0], pieces[1, 1, 0, 0], pieces[0, 1, 0, 1] = z2, y1, y0f
    z3, y2, y1f, pieces[2, 0, 1, 0], pieces[1, 1, 1, 0] = tie(
        next_z(z2), other_y(z2), other_x(y1), *other_cores(z2, y1)
    )
    pieces[3, 0, 0, 0], pieces[2, 1, 0, 0], pieces[1, 1, 0, 1] = z3, y2, y1f
    z1f, y3, z3f, fetched, pieces[3, 0, 1, 0], pieces[0, 1, 1, 1] = tie(
        next_z(own_far), other_y(z3), other_x(z3), returned_rows(found), *other_cores(z3, y0f)
    )
    pieces[1, 0, 0, 1], pieces[3, 1, 0, 0], pieces[3, 0, 0, 1] = z1f, y3, z3f
    z2f, y3f, y2f, prepared, pieces[2, 1, 1, 0], pieces[1, 1, 1, 1] = tie(
        next_z(z1f), other_y(z3f), other_x(y2), tuple(prepared), *other_cores(y2, y1f)
    )
    pieces[2, 0, 0, 1], pieces[3, 1, 0, 1], pieces[2, 1, 0, 1] = z2f, y3f, y2f
    for steps, side, far in ((1, 0, 1), (3, 1, 0), (3, 0, 1), (2, 0, 1), (3, 1, 1), (2, 1, 1)):
        pieces[steps, side, 1, far] = other_core(pieces[steps, side, 0, far])
    return pieces, fetched, prepared


def prepare_kernel(nkey, proj_count, pick_ref, row_id_ref, counts_ref, wide_id_ref, proj_ref):
    wide_id = jnp.broadcast_to(row_id_ref[...], wide_id_ref.shape)
    wide_id_ref[...] = wide_id
    proj_ref[...] = (wide_id % nkey % proj_count).T[:proj_ref.shape[0]]
    token_rows, slots = counts_ref.shape
    lane = lax.broadcasted_iota(jnp.int32, (token_rows, slots), 1)
    pick = pick_ref[...]
    counts = jnp.zeros((token_rows, slots), F32)
    for k in range(pick.shape[1]):
        counts += jnp.where(pick[:, k:k + 1] == lane, 1.0, 0.0)
    counts_ref[...] = counts


def dense_kernel(
    rank, width, proj_count, keys, core_ref, row_id_ref, proj_ref, counts_ref, tokens_ref, cot_ref, fetched_ref, *refs
):
    piece_count = len(keys)
    pieces = refs[:piece_count]
    out_ref, grad_ref, query_held, proj_held, mixed_values, query_grad, tokens, cot, fetched_held, counts_held = refs[
        piece_count:piece_count + 10
    ]
    out_held, grad_held, query_sem, proj_sem, in_sem, out_sem = refs[piece_count + 10:]
    token_rows, features = tokens.shape
    slots, value_width = fetched_held.shape
    members, _, columns, _ = proj_held.shape
    parts = value_width // columns
    me, x = lax.axis_index("mem"), lax.axis_index("groups")
    z, y, core = me // 4, (me // 2) % 2, me % 2
    spots = []
    for (steps, side, other, far), piece in zip(keys, pieces):
        at = place(ring_source(z, steps), 1 - y if side else y, 1 - core if other else core)
        spots.append((piece, at, 1 - x if far else x))
    half_proj = proj_held.shape[1] // 2
    half_query = query_held.shape[1] // 2
    half_count = proj_count // 2

    inputs = [
        pltpu.make_async_copy(source, target, in_sem.at[i])
        for i, (source, target) in enumerate(
            ((cot_ref, cot), (tokens_ref, tokens), (counts_ref, counts_held), (fetched_ref, fetched_held))
        )
    ]
    inputs[1].start()
    for piece, at, half in spots:
        pltpu.make_async_copy(
            piece.at[pl.ds(half_proj, half_query)], query_held.at[at, pl.ds(half * half_query, half_query)], query_sem
        ).start()
    inputs[2].start()
    inputs[3].start()
    inputs[0].start()
    for piece, at, half in spots:
        pltpu.make_async_copy(
            piece.at[pl.ds(0, half_proj)], proj_held.at[at, pl.ds(half * half_proj, half_proj)], proj_sem
        ).start()

    def query_lanes(first, last):
        return jnp.concatenate([query_held[:, j].reshape(-1, LANES) for j in range(first, last)], axis=1)

    def proj_lanes(first, last, part, size):
        return jnp.concatenate(
            [proj_held[m, part:part + size].reshape(-1, LANES) for m in range(first, last)], axis=1
        )

    def value_grad(e):
        return dot(cot[...], proj_lanes(0, members, e * parts, parts), LAST).astype(BF16)

    nkey = members * columns
    key_at = lax.broadcasted_iota(jnp.int32, (slots, nkey), 1)
    row_id = row_id_ref[:, :1]
    row_hot = jnp.where(row_id // nkey == key_at, 1.0, 0.0).astype(BF16)
    col_hot = jnp.where(row_id % nkey == key_at, 1.0, 0.0).astype(BF16)
    inputs[1].wait()
    pltpu.make_async_copy(query_held, query_held, query_sem).wait()
    key = features // LANES
    step = width // LANES
    slot_row = dot(row_hot, query_lanes(key, key + step), PLAIN).astype(BF16)
    slot_col = dot(col_hot, query_lanes(key + step, key + 2 * step), PLAIN).astype(BF16)
    queries = dot(tokens[...], query_lanes(0, key), LAST).astype(BF16)
    for copy in (inputs[0], inputs[2], inputs[3]):
        copy.wait()
    pltpu.make_async_copy(proj_held, proj_held, proj_sem).wait()
    proj = proj_ref[:1]
    fetched = fetched_held[...]
    value_grads = []
    rows = token_rows // 4
    weights, factors = [], []
    for c in range(4):
        block = [queries[c * rows:(c + 1) * rows, r * width:(r + 1) * width] for r in range(2 * rank)]
        row_scores = [dot(block[r], slot_row, LAST) for r in range(rank)]
        col_scores = [dot(block[rank + r], slot_col, LAST) for r in range(rank)]
        value_grads += [value_grad(e) for e in range(proj_count) if e % 4 == c]
        col_mixed = [sum(core_ref[r, s] * col_scores[s] for s in range(rank)) for r in range(rank)]
        row_mixed = [sum(row_scores[r] * core_ref[r, s] for r in range(rank)) for s in range(rank)]
        score = sum(row_scores[r] * col_mixed[r] for r in range(rank))
        gate = 1.0 / (1.0 + jnp.exp(-score))
        weights.append((counts_held[c * rows:(c + 1) * rows] * gate.astype(BF16).astype(F32)).astype(BF16))
        slope = gate * (1.0 - gate)
        factors.append([slope * m for m in col_mixed] + [slope * m for m in row_mixed])
    weights = jnp.concatenate(weights, axis=0)
    for e in range(proj_count):
        mixed = dot(jnp.where(proj == e, weights, jnp.zeros((), BF16)), fetched, PLAIN)
        mixed_values[:, e * value_width:(e + 1) * value_width] = mixed.astype(BF16)

    def columns_of(c):
        return slice(c * (features // 4), (c + 1) * (features // 4))

    def send(held, target, c, sem):
        pltpu.make_async_copy(held.at[:, columns_of(c)], target.at[:, columns_of(c)], sem).start()

    for c in range(4):
        part = slice(c * rows, (c + 1) * rows)
        pick_grad = jnp.zeros((rows, slots), F32)
        for e in range(proj_count):
            pick_grad = jnp.where(proj == e, dot(value_grads[e][part], fetched, LAST), pick_grad)
        held = proj_lanes(c * (members // 4), (c + 1) * (members // 4), 0, proj_held.shape[1])
        out_held[:, columns_of(c)] = dot(mixed_values[...], held, PLAIN).astype(BF16)
        send(out_held, out_ref, c, out_sem.at[0])
        for i in range(2 * rank):
            slot_key = slot_row if i < rank else slot_col
            grad = ((pick_grad * factors[c][i]).astype(BF16).astype(F32) * counts_held[part]).astype(BF16)
            query_grad[part, i * width:(i + 1) * width] = dot(grad, slot_key, PLAIN).astype(BF16)
    blocks = features // LANES // 4
    for c in range(4):
        held = query_lanes(c * blocks, (c + 1) * blocks)
        grad_held[:, columns_of(c)] = dot(query_grad[...], held, PLAIN).astype(BF16)
        send(grad_held, grad_ref, c, out_sem.at[1])
    pltpu.make_async_copy(out_held, out_ref, out_sem.at[0]).wait()
    pltpu.make_async_copy(grad_held, grad_ref, out_sem.at[1]).wait()


def vmem():
    return pl.BlockSpec(memory_space=pltpu.VMEM)


def smem():
    return pl.BlockSpec(memory_space=pltpu.SMEM)


def anywhere():
    return pl.BlockSpec(memory_space=pl.ANY)


def pieces_path(tokens, cotangent, w_query, key_row, key_col, tucker_core, proj_part, requests, table, row_id,
                slot_proj, pick_slot, nkey, proj_count):
    rank = tucker_core.shape[0]
    width = key_row.shape[1]
    token_rows, features = tokens.shape
    slots = row_id.shape[0]
    value_width = table.shape[1]
    columns = w_query.shape[1]
    own_near, own_far = own_halves(w_query, key_row, key_col, proj_part)
    prepared = pl.pallas_call(
        functools.partial(prepare_kernel, nkey, proj_count),
        out_shape=(
            jax.ShapeDtypeStruct((token_rows, slots), F32),
            jax.ShapeDtypeStruct((slots, LANES), jnp.int32),
            jax.ShapeDtypeStruct((8, slots), jnp.int32),
        ),
        in_specs=[vmem(), vmem()],
        out_specs=(vmem(),) * 3,
        compiler_params=pltpu.CompilerParams(vmem_limit_bytes=SMALL_LIMIT),
        cost_estimate=pl.CostEstimate(flops=3 * 10**9, bytes_accessed=10**6, transcendentals=0),
        name="prepare",
    )(pick_slot, row_id[:, None])
    pieces, fetched, (counts, wide_id, slot_proj) = gather_pieces(own_near, own_far, requests, table, prepared)
    fetched = fetched.reshape(slots, value_width)
    keys = tuple(pieces)
    tall = (token_rows, features)
    return pl.pallas_call(
        functools.partial(dense_kernel, rank, width, proj_count, keys),
        out_shape=(jax.ShapeDtypeStruct(tall, BF16),) * 2,
        in_specs=[smem(), vmem(), vmem()] + [anywhere()] * (4 + len(keys)),
        out_specs=(anywhere(), anywhere()),
        scratch_shapes=[
            pltpu.VMEM((nkey // columns, (features + 2 * width) // LANES, columns, LANES), BF16),
            pltpu.VMEM((features // LANES, proj_count * value_width // columns, columns, LANES), BF16),
            pltpu.VMEM((token_rows, proj_count * value_width), BF16),
            pltpu.VMEM((token_rows, 2 * rank * width), BF16),
            pltpu.VMEM(tall, BF16),
            pltpu.VMEM(tall, BF16),
            pltpu.VMEM((slots, value_width), BF16),
            pltpu.VMEM((token_rows, slots), F32),
            pltpu.VMEM(tall, BF16),
            pltpu.VMEM(tall, BF16),
            pltpu.SemaphoreType.DMA,
            pltpu.SemaphoreType.DMA,
            pltpu.SemaphoreType.DMA((4,)),
            pltpu.SemaphoreType.DMA((2,)),
        ],
        compiler_params=pltpu.CompilerParams(vmem_limit_bytes=VMEM_LIMIT),
        cost_estimate=pl.CostEstimate(flops=10**10, bytes_accessed=2 * 10**7, transcendentals=10**5),
        name="dense",
    )(
        tucker_core, wide_id, slot_proj, counts, tokens, cotangent, fetched, *[pieces[k] for k in keys]
    )


def whole_path(tokens, cotangent, w_query, key_row, key_col, tucker_core, proj_part, requests, table, row_id,
               slot_proj, pick_slot, nkey, proj_count):
    rank = tucker_core.shape[0]
    width = key_row.shape[1]
    slots = row_id.shape[0]
    fetched = returned_rows(found_rows(wanted_rows(requests), table)).reshape(slots, -1)
    query_full = lax.all_gather(w_query.T, "mem", axis=0, tiled=True)
    keys = lax.all_gather(jnp.concatenate([key_row, key_col], axis=1), "mem", axis=0, tiled=True)
    proj_full = lax.all_gather(proj_part, "mem", axis=1, tiled=True)
    key_at = jnp.arange(nkey, dtype=jnp.int32)[None, :]
    row_hot = ((row_id // nkey)[:, None] == key_at).astype(BF16)
    col_hot = ((row_id % nkey)[:, None] == key_at).astype(BF16)
    slot_row = dot(row_hot, keys[:, :width], PLAIN).astype(BF16)
    slot_col = dot(col_hot, keys[:, width:], PLAIN).astype(BF16)
    spread = jnp.where(
        slot_proj[:, None, None] == jnp.arange(proj_count, dtype=jnp.int32)[None, :, None],
        fetched[:, None, :], jnp.zeros((), BF16)
    ).reshape(slots, -1)
    counts = jnp.sum(
        (pick_slot[:, :, None] == jnp.arange(slots, dtype=jnp.int32)[None, None, :]).astype(F32), axis=1
    )
    queries = dot(tokens, query_full, LAST).astype(BF16)
    row_scores = [dot(queries[:, r * width:(r + 1) * width], slot_row, LAST) for r in range(rank)]
    col_scores = [
        dot(queries[:, (rank + r) * width:(rank + r + 1) * width], slot_col, LAST) for r in range(rank)
    ]
    col_mixed = [sum(tucker_core[r, s] * col_scores[s] for s in range(rank)) for r in range(rank)]
    row_mixed = [sum(row_scores[r] * tucker_core[r, s] for r in range(rank)) for s in range(rank)]
    score = sum(row_scores[r] * col_mixed[r] for r in range(rank))
    gate = jax.nn.sigmoid(score)
    weights = counts * gate.astype(BF16).astype(F32)
    mixed = counted_dot(weights, spread, PLAIN).astype(BF16)
    memory_out = dot(mixed, proj_full, PLAIN)
    value_grad = dot(cotangent, proj_full, LAST).astype(BF16)
    pick_grad = dot(value_grad, spread, LAST)
    score_grad = pick_grad * gate * (1.0 - gate)
    blocks = []
    for mixed_scores, slot_key in ((col_mixed, slot_row), (row_mixed, slot_col)):
        for r in range(rank):
            grad = (score_grad * mixed_scores[r]).astype(BF16).astype(F32) * counts
            blocks.append(counted_dot(grad, slot_key, PLAIN).astype(BF16))
    query_grad = jnp.concatenate(blocks, axis=1)
    token_grad = dot(query_grad, query_full, PLAIN)
    return memory_out.astype(BF16), token_grad.astype(BF16)


def shards(
    mem, tokens, cotangent, w_query, key_row, key_col, tucker_core, table, w_proj, send_ids, pick_slot
):
    proj_count, value_width, _ = w_proj.shape
    requests = send_ids[0]
    owners, capacity = requests.shape
    slots = owners * capacity
    nkey = key_row.shape[0] * mem
    row_id = jnp.maximum(requests, 0) + jnp.arange(owners, dtype=jnp.int32)[:, None] * table.shape[0]
    row_id = row_id.reshape(slots)
    slot_proj = (row_id % nkey) % proj_count
    proj_part = w_proj.reshape(proj_count * value_width, -1)
    path = pieces_path if mem == 16 and w_proj.shape[2] == LANES else whole_path
    return path(tokens, cotangent, w_query, key_row, key_col, tucker_core, proj_part, requests, table, row_id,
                slot_proj, pick_slot, nkey, proj_count)


def solution(mesh):
    in_specs = (
        P(("groups", "mem"), None),
        P(("groups", "mem"), None),
        P(None, "mem"),
        P("mem", None),
        P("mem", None),
        P(),
        P("mem", None),
        P(None, None, "mem"),
        P(("groups", "mem"), None, None),
        P(("groups", "mem"), None),
    )
    out_specs = (P(("groups", "mem"), None), P(("groups", "mem"), None))
    body = functools.partial(shards, mesh.shape["mem"])
    return jax.shard_map(body, mesh=mesh, in_specs=in_specs, out_specs=out_specs, check_vma=False)
```

```python
import functools

import jax
import jax.numpy as jnp
from jax import lax
from jax.experimental import pallas as pl
from jax.experimental.pallas import tpu as pltpu
from jax.sharding import PartitionSpec as P

F32 = jnp.float32
BF16 = jnp.bfloat16
RING = (0, 2, 3, 1)
LANES = 128
LAST = ((1,), (1,))
PLAIN = ((1,), (0,))
VMEM_LIMIT = 56 * 1024 * 1024
SMALL_LIMIT = 8 * 1024 * 1024


def dot(a, b, dims):
    return lax.dot_general(a, b, (dims, ((), ())), preferred_element_type=F32)


def two_terms(x):
    high = x.astype(BF16)
    return high, (x - high.astype(F32)).astype(BF16)


def counted_dot(x, b, dims):
    high, low = two_terms(x)
    return dot(high, b, dims) + dot(low, b, dims)


def wanted_rows(requests):
    return lax.all_to_all(requests, "mem", split_axis=0, concat_axis=0, tiled=True)


def found_rows(wanted, table):
    found = jnp.take(table, jnp.maximum(wanted, 0).reshape(-1), axis=0, mode="clip")
    return found.reshape(wanted.shape + (table.shape[1],))


def returned_rows(found):
    return lax.all_to_all(found, "mem", split_axis=0, concat_axis=0, tiled=True)


def place(z, y, core):
    return (z * 2 + y) * 2 + core


def everywhere(move):
    pairs = []
    for z in range(4):
        for y in range(2):
            for core in range(2):
                pairs.append((place(z, y, core), place(*move(z, y, core))))
    return pairs


def next_z(x):
    step = {RING[i]: RING[(i + 1) % 4] for i in range(4)}
    return lax.ppermute(x, "mem", everywhere(lambda z, y, c: (step[z], y, c)))


def other_y(x):
    return lax.ppermute(x, "mem", everywhere(lambda z, y, c: (z, 1 - y, c)))


def other_core(x):
    return lax.ppermute(x, "mem", everywhere(lambda z, y, c: (z, y, 1 - c)))


def other_x(x):
    return lax.ppermute(x, "groups", [(0, 1), (1, 0)])


def ring_source(z, steps):
    index = jnp.where(z == 0, 0, jnp.where(z == 2, 1, jnp.where(z == 3, 2, 3)))
    index = (index + 4 - steps) % 4
    return jnp.where(index == 0, 0, jnp.where(index == 1, 2, jnp.where(index == 2, 3, 1)))


def tie(*values):
    return lax.optimization_barrier(values)


def other_cores(first, second):
    first = other_core(first)
    second, first = tie(second, first)
    return first, other_core(second)


def gather_pieces(proj_part, requests, table, prepared):
    x = lax.axis_index("groups")
    half = proj_part.shape[0] // 2
    own_near = lax.dynamic_slice_in_dim(proj_part, x * half, half, axis=0)
    pieces = {}
    z1, y0, wanted, own_other = tie(
        next_z(own_near), other_y(own_near), wanted_rows(requests), other_core(proj_part)
    )
    pieces[1, 0, 0, 0], pieces[0, 1, 0, 0] = z1, y0
    z2, y1, y0f, found, pieces[1, 0, 1, 0], pieces[0, 1, 1, 0] = tie(
        next_z(z1), other_y(z1), other_x(y0), found_rows(wanted, table), *other_cores(z1, y0)
    )
    pieces[2, 0, 0, 0], pieces[1, 1, 0, 0], pieces[0, 1, 0, 1] = z2, y1, y0f
    z3, y2, y1f, z1f, pieces[2, 0, 1, 0], pieces[1, 1, 1, 0] = tie(
        next_z(z2), other_y(z2), other_x(y1), other_x(z1), *other_cores(z2, y1)
    )
    pieces[3, 0, 0, 0], pieces[2, 1, 0, 0], pieces[1, 1, 0, 1], pieces[1, 0, 0, 1] = z3, y2, y1f, z1f
    y3, z3f, z2f, fetched, pieces[3, 0, 1, 0], pieces[0, 1, 1, 1] = tie(
        other_y(z3), other_x(z3), other_x(z2), returned_rows(found), *other_cores(z3, y0f)
    )
    pieces[3, 1, 0, 0], pieces[3, 0, 0, 1], pieces[2, 0, 0, 1] = y3, z3f, z2f
    y3f, y2f, prepared, pieces[2, 1, 1, 0], pieces[1, 1, 1, 1] = tie(
        other_y(z3f), other_x(y2), tuple(prepared), *other_cores(y2, y1f)
    )
    pieces[3, 1, 0, 1], pieces[2, 1, 0, 1] = y3f, y2f
    for steps, side, far in ((1, 0, 1), (3, 1, 0), (3, 0, 1), (2, 0, 1), (3, 1, 1), (2, 1, 1)):
        pieces[steps, side, 1, far] = other_core(pieces[steps, side, 0, far])
    return pieces, (proj_part, own_other), fetched, prepared


def prepare_kernel(nkey, proj_count, pick_ref, row_id_ref, counts_ref, wide_id_ref, proj_ref):
    wide_id = jnp.broadcast_to(row_id_ref[...], wide_id_ref.shape)
    wide_id_ref[...] = wide_id
    proj_ref[...] = (wide_id % nkey % proj_count).T[:proj_ref.shape[0]]
    token_rows, slots = counts_ref.shape
    lane = lax.broadcasted_iota(jnp.int32, (token_rows, slots), 1)
    pick = pick_ref[...]
    counts = jnp.zeros((token_rows, slots), F32)
    for k in range(pick.shape[1]):
        counts += jnp.where(pick[:, k:k + 1] == lane, 1.0, 0.0)
    counts_ref[...] = counts


def copy_pieces(keys, pieces, held, sem):
    me, x = lax.axis_index("mem"), lax.axis_index("groups")
    z, y, core = me // 4, (me // 2) % 2, me % 2
    half = held.shape[1] // 2
    for i, piece in enumerate(pieces):
        if i < 2:
            at, target = place(z, y, core if i == 0 else 1 - core), pl.ds(0, 2 * half)
        else:
            steps, side, other, far = keys[i - 2]
            at = place(ring_source(z, steps), 1 - y if side else y, 1 - core if other else core)
            target = pl.ds(pl.multiple_of((1 - x if far else x) * half, half), half)
        pltpu.make_async_copy(piece, held.at[at, target], sem).start()


def wait_for(held, sem):
    pltpu.make_async_copy(held, held, sem).wait()


def lanes(held, first, last, rows):
    return jnp.concatenate([held[m, rows] for m in range(first, last)], axis=1)


def values_kernel(proj_count, keys, proj_ref, cot_ref, fetched_ref, *refs):
    pick_grad_ref, held, sem = refs[-3:]
    copy_pieces(keys, refs[:-3], held, sem)
    value_width = fetched_ref.shape[1]
    proj = proj_ref[:1]
    cot = cot_ref[...]
    fetched = fetched_ref[...]
    pick_grad = jnp.zeros(pick_grad_ref.shape, F32)
    wait_for(held, sem)
    for e in range(proj_count):
        block = lanes(held, 0, held.shape[0], slice(e * value_width, (e + 1) * value_width))
        grad = dot(cot, block, LAST).astype(BF16)
        pick_grad = jnp.where(proj == e, dot(grad, fetched, LAST), pick_grad)
    pick_grad_ref[...] = pick_grad


def dense_kernel(
    rank, width, proj_count, keys, core_ref, row_id_ref, proj_ref, counts_ref, pick_grad_ref, tokens_ref, fetched_ref,
    query_ref, *refs
):
    out_ref, grad_ref, query, held, mixed_values, query_grad, query_sem, sem = refs[-8:]
    pltpu.make_async_copy(query_ref, query, query_sem).start()
    copy_pieces(keys, refs[:-8], held, sem)
    token_rows, features = tokens_ref.shape
    slots, value_width = fetched_ref.shape
    nkey = query.shape[0]
    key_at = lax.broadcasted_iota(jnp.int32, (slots, nkey), 1)
    row_id = row_id_ref[:, :1]
    row_hot = jnp.where(row_id // nkey == key_at, 1.0, 0.0).astype(BF16)
    col_hot = jnp.where(row_id % nkey == key_at, 1.0, 0.0).astype(BF16)
    pltpu.make_async_copy(query_ref, query, query_sem).wait()
    slot_row = dot(row_hot, query[:, features:features + width], PLAIN).astype(BF16)
    slot_col = dot(col_hot, query[:, features + width:], PLAIN).astype(BF16)
    queries = dot(tokens_ref[...], query[:, :features], LAST).astype(BF16)
    block = [queries[:, r * width:(r + 1) * width] for r in range(2 * rank)]
    row_scores = [dot(block[r], slot_row, LAST) for r in range(rank)]
    col_scores = [dot(block[rank + r], slot_col, LAST) for r in range(rank)]
    col_mixed = [sum(core_ref[r, s] * col_scores[s] for s in range(rank)) for r in range(rank)]
    row_mixed = [sum(row_scores[r] * core_ref[r, s] for r in range(rank)) for s in range(rank)]
    score = sum(row_scores[r] * col_mixed[r] for r in range(rank))
    gate = 1.0 / (1.0 + jnp.exp(-score))
    counts = counts_ref[...]
    weights = (counts * gate.astype(BF16).astype(F32)).astype(BF16)
    score_grad = pick_grad_ref[...] * gate * (1.0 - gate)

    proj = proj_ref[:1]
    fetched = fetched_ref[...]
    for e in range(proj_count):
        mixed = dot(jnp.where(proj == e, weights, jnp.zeros((), BF16)), fetched, PLAIN)
        mixed_values[:, e * value_width:(e + 1) * value_width] = mixed.astype(BF16)
    for i, factor in enumerate(col_mixed + row_mixed):
        slot_key = slot_row if i < rank else slot_col
        grad = ((score_grad * factor).astype(BF16).astype(F32) * counts).astype(BF16)
        query_grad[:, i * width:(i + 1) * width] = dot(grad, slot_key, PLAIN).astype(BF16)
    wait_for(held, sem)
    members = held.shape[0] // 4
    step = features // 4
    for c in range(4):
        cols = slice(c * step, (c + 1) * step)
        grad_ref[:, cols] = dot(query_grad[...], query[:, cols], PLAIN).astype(BF16)
        block = lanes(held, c * members, (c + 1) * members, slice(None))
        out_ref[:, cols] = dot(mixed_values[...], block, PLAIN).astype(BF16)


def vmem():
    return pl.BlockSpec(memory_space=pltpu.VMEM)


def smem():
    return pl.BlockSpec(memory_space=pltpu.SMEM)


def anywhere():
    return pl.BlockSpec(memory_space=pl.ANY)


def pieces_path(tokens, cotangent, w_query, key_row, key_col, tucker_core, proj_part, requests, table, row_id,
                slot_proj, pick_slot, nkey, proj_count):
    rank = tucker_core.shape[0]
    width = key_row.shape[1]
    token_rows, features = tokens.shape
    slots = row_id.shape[0]
    value_width = table.shape[1]
    columns = w_query.shape[1]
    query_part = jnp.concatenate([w_query.T, key_row, key_col], axis=1)
    query = lax.all_gather(query_part, "mem", axis=0, tiled=True)
    prepared = pl.pallas_call(
        functools.partial(prepare_kernel, nkey, proj_count),
        out_shape=(
            jax.ShapeDtypeStruct((token_rows, slots), F32),
            jax.ShapeDtypeStruct((slots, LANES), jnp.int32),
            jax.ShapeDtypeStruct((8, slots), jnp.int32),
        ),
        in_specs=[vmem(), vmem()],
        out_specs=(vmem(),) * 3,
        compiler_params=pltpu.CompilerParams(vmem_limit_bytes=SMALL_LIMIT),
        cost_estimate=pl.CostEstimate(flops=3 * 10**9, bytes_accessed=10**6, transcendentals=0),
        name="prepare",
    )(pick_slot, row_id[:, None])
    pieces, pair, fetched, (counts, wide_id, slot_proj) = gather_pieces(proj_part, requests, table, prepared)
    fetched = fetched.reshape(slots, value_width)
    keys = tuple(pieces)
    pieces = list(pair) + [pieces[k] for k in keys]
    members = nkey // w_query.shape[1]
    held = pltpu.VMEM((members,) + proj_part.shape, BF16)
    params = pltpu.CompilerParams(vmem_limit_bytes=VMEM_LIMIT)
    pick_grad = pl.pallas_call(
        functools.partial(values_kernel, proj_count, keys),
        out_shape=jax.ShapeDtypeStruct((token_rows, slots), F32),
        in_specs=[vmem()] * 3 + [anywhere()] * len(pieces),
        out_specs=vmem(),
        scratch_shapes=[held, pltpu.SemaphoreType.DMA],
        compiler_params=params,
        cost_estimate=pl.CostEstimate(flops=5 * 10**9, bytes_accessed=10**7, transcendentals=0),
        name="values",
    )(slot_proj, cotangent, fetched, *pieces)
    return pl.pallas_call(
        functools.partial(dense_kernel, rank, width, proj_count, keys),
        out_shape=(jax.ShapeDtypeStruct((token_rows, features), BF16),) * 2,
        in_specs=[smem()] + [vmem()] * 6 + [anywhere()] * (1 + len(pieces)),
        out_specs=(vmem(), vmem()),
        scratch_shapes=[
            pltpu.VMEM(query.shape, BF16),
            held,
            pltpu.VMEM((token_rows, proj_count * value_width), BF16),
            pltpu.VMEM((token_rows, 2 * rank * width), BF16),
            pltpu.SemaphoreType.DMA,
            pltpu.SemaphoreType.DMA,
        ],
        compiler_params=params,
        cost_estimate=pl.CostEstimate(flops=10**10, bytes_accessed=2 * 10**7, transcendentals=10**5),
        name="dense",
    )(tucker_core, wide_id, slot_proj, counts, pick_grad, tokens, fetched, query, *pieces)


def whole_path(tokens, cotangent, w_query, key_row, key_col, tucker_core, proj_part, requests, table, row_id,
               slot_proj, pick_slot, nkey, proj_count):
    rank = tucker_core.shape[0]
    width = key_row.shape[1]
    slots = row_id.shape[0]
    fetched = returned_rows(found_rows(wanted_rows(requests), table)).reshape(slots, -1)
    query_full = lax.all_gather(w_query.T, "mem", axis=0, tiled=True)
    keys = lax.all_gather(jnp.concatenate([key_row, key_col], axis=1), "mem", axis=0, tiled=True)
    proj_full = lax.all_gather(proj_part, "mem", axis=1, tiled=True)
    key_at = jnp.arange(nkey, dtype=jnp.int32)[None, :]
    row_hot = ((row_id // nkey)[:, None] == key_at).astype(BF16)
    col_hot = ((row_id % nkey)[:, None] == key_at).astype(BF16)
    slot_row = dot(row_hot, keys[:, :width], PLAIN).astype(BF16)
    slot_col = dot(col_hot, keys[:, width:], PLAIN).astype(BF16)
    spread = jnp.where(
        slot_proj[:, None, None] == jnp.arange(proj_count, dtype=jnp.int32)[None, :, None],
        fetched[:, None, :], jnp.zeros((), BF16)
    ).reshape(slots, -1)
    counts = jnp.sum(
        (pick_slot[:, :, None] == jnp.arange(slots, dtype=jnp.int32)[None, None, :]).astype(F32), axis=1
    )
    queries = dot(tokens, query_full, LAST).astype(BF16)
    row_scores = [dot(queries[:, r * width:(r + 1) * width], slot_row, LAST) for r in range(rank)]
    col_scores = [
        dot(queries[:, (rank + r) * width:(rank + r + 1) * width], slot_col, LAST) for r in range(rank)
    ]
    col_mixed = [sum(tucker_core[r, s] * col_scores[s] for s in range(rank)) for r in range(rank)]
    row_mixed = [sum(row_scores[r] * tucker_core[r, s] for r in range(rank)) for s in range(rank)]
    score = sum(row_scores[r] * col_mixed[r] for r in range(rank))
    gate = jax.nn.sigmoid(score)
    weights = counts * gate.astype(BF16).astype(F32)
    mixed = counted_dot(weights, spread, PLAIN).astype(BF16)
    memory_out = dot(mixed, proj_full, PLAIN)
    value_grad = dot(cotangent, proj_full, LAST).astype(BF16)
    pick_grad = dot(value_grad, spread, LAST)
    score_grad = pick_grad * gate * (1.0 - gate)
    blocks = []
    for mixed_scores, slot_key in ((col_mixed, slot_row), (row_mixed, slot_col)):
        for r in range(rank):
            grad = (score_grad * mixed_scores[r]).astype(BF16).astype(F32) * counts
            blocks.append(counted_dot(grad, slot_key, PLAIN).astype(BF16))
    query_grad = jnp.concatenate(blocks, axis=1)
    token_grad = dot(query_grad, query_full, PLAIN)
    return memory_out.astype(BF16), token_grad.astype(BF16)


def shards(
    mem, tokens, cotangent, w_query, key_row, key_col, tucker_core, table, w_proj, send_ids, pick_slot
):
    proj_count, value_width, _ = w_proj.shape
    requests = send_ids[0]
    owners, capacity = requests.shape
    slots = owners * capacity
    nkey = key_row.shape[0] * mem
    row_id = jnp.maximum(requests, 0) + jnp.arange(owners, dtype=jnp.int32)[:, None] * table.shape[0]
    row_id = row_id.reshape(slots)
    slot_proj = (row_id % nkey) % proj_count
    proj_part = w_proj.reshape(proj_count * value_width, -1)
    path = pieces_path if mem == 16 and w_proj.shape[2] == LANES else whole_path
    return path(tokens, cotangent, w_query, key_row, key_col, tucker_core, proj_part, requests, table, row_id,
                slot_proj, pick_slot, nkey, proj_count)


def solution(mesh):
    in_specs = (
        P(("groups", "mem"), None),
        P(("groups", "mem"), None),
        P(None, "mem"),
        P("mem", None),
        P("mem", None),
        P(),
        P("mem", None),
        P(None, None, "mem"),
        P(("groups", "mem"), None, None),
        P(("groups", "mem"), None),
    )
    out_specs = (P(("groups", "mem"), None), P(("groups", "mem"), None))
    body = functools.partial(shards, mesh.shape["mem"])
    return jax.shard_map(body, mesh=mesh, in_specs=in_specs, out_specs=out_specs, check_vma=False)
```

```python
import functools

import jax
import jax.numpy as jnp
from jax import lax
from jax.experimental import pallas as pl
from jax.experimental.pallas import tpu as pltpu
from jax.sharding import PartitionSpec as P

F32 = jnp.float32
BF16 = jnp.bfloat16
RING = (0, 2, 3, 1)
LANES = 128
LAST = ((1,), (1,))
PLAIN = ((1,), (0,))
VMEM_LIMIT = 56 * 1024 * 1024
SMALL_LIMIT = 8 * 1024 * 1024


def dot(a, b, dims):
    return lax.dot_general(a, b, (dims, ((), ())), preferred_element_type=F32)


def two_terms(x):
    high = x.astype(BF16)
    return high, (x - high.astype(F32)).astype(BF16)


def counted_dot(x, b, dims):
    high, low = two_terms(x)
    return dot(high, b, dims) + dot(low, b, dims)


def wanted_rows(requests):
    return lax.all_to_all(requests, "mem", split_axis=0, concat_axis=0, tiled=True)


def found_rows(wanted, table):
    found = jnp.take(table, jnp.maximum(wanted, 0).reshape(-1), axis=0, mode="clip")
    return found.reshape(wanted.shape + (table.shape[1],))


def returned_rows(found):
    return lax.all_to_all(found, "mem", split_axis=0, concat_axis=0, tiled=True)


def place(z, y, core):
    return (z * 2 + y) * 2 + core


def everywhere(move):
    pairs = []
    for z in range(4):
        for y in range(2):
            for core in range(2):
                pairs.append((place(z, y, core), place(*move(z, y, core))))
    return pairs


def next_z(x):
    step = {RING[i]: RING[(i + 1) % 4] for i in range(4)}
    return lax.ppermute(x, "mem", everywhere(lambda z, y, c: (step[z], y, c)))


def other_y(x):
    return lax.ppermute(x, "mem", everywhere(lambda z, y, c: (z, 1 - y, c)))


def other_core(x):
    return lax.ppermute(x, "mem", everywhere(lambda z, y, c: (z, y, 1 - c)))


def other_x(x):
    return lax.ppermute(x, "groups", [(0, 1), (1, 0)])


def ring_source(z, steps):
    index = jnp.where(z == 0, 0, jnp.where(z == 2, 1, jnp.where(z == 3, 2, 3)))
    index = (index + 4 - steps) % 4
    return jnp.where(index == 0, 0, jnp.where(index == 1, 2, jnp.where(index == 2, 3, 1)))


def tie(*values):
    return lax.optimization_barrier(values)


def own_halves(w_query, key_row, key_col, proj_part):
    features, columns = w_query.shape
    proj = proj_part.reshape(2, -1, columns, LANES)
    tall = w_query.T
    query = jnp.concatenate([tall[:, :features // 2], key_row, tall[:, features // 2:], key_col], axis=1)
    query = query.reshape(columns, 2, -1, LANES).transpose(1, 2, 0, 3)
    return jnp.concatenate([proj, query], axis=1)


def other_cores(first, second):
    first = other_core(first)
    second, first = tie(second, first)
    return first, other_core(second)


def gather_pieces(own, requests, table, prepared, near_work):
    x = lax.axis_index("groups")
    own_near = lax.dynamic_index_in_dim(own, x, axis=0, keepdims=False)
    own_far = lax.dynamic_index_in_dim(own, 1 - x, axis=0, keepdims=False)
    pieces = {}
    z1, y0, wanted, own_other = tie(next_z(own_near), other_y(own_near), wanted_rows(requests), other_core(own))
    pieces[1, 0, 0, 0], pieces[0, 1, 0, 0] = z1, y0
    z2, y1, y0f, found, pieces[1, 0, 1, 0], pieces[0, 1, 1, 0] = tie(
        next_z(z1), other_y(z1), other_x(y0), found_rows(wanted, table), *other_cores(z1, y0)
    )
    pieces[2, 0, 0, 0], pieces[1, 1, 0, 0], pieces[0, 1, 0, 1] = z2, y1, y0f
    z3, y2, y1f, prepared, pieces[2, 0, 1, 0], pieces[1, 1, 1, 0] = tie(
        next_z(z2), other_y(z2), other_x(y1), tuple(prepared), *other_cores(z2, y1)
    )
    pieces[3, 0, 0, 0], pieces[2, 1, 0, 0], pieces[1, 1, 0, 1] = z3, y2, y1f
    z1f, y3, z3f, fetched, pieces[3, 0, 1, 0], pieces[0, 1, 1, 1] = tie(
        next_z(own_far), other_y(z3), other_x(z3), returned_rows(found), *other_cores(z3, y0f)
    )
    pieces[1, 0, 0, 1], pieces[3, 1, 0, 0], pieces[3, 0, 0, 1] = z1f, y3, z3f
    y2_other, y1f_other = other_cores(y2, y1f)
    pieces[2, 1, 1, 0], pieces[3, 1, 1, 0] = y2_other, other_core(y3)
    near = {key: piece for key, piece in pieces.items() if key[3] == 0}
    z2f, y3f, y2f, near_done, pieces[1, 1, 1, 1] = tie(
        next_z(z1f), other_y(z3f), other_x(y2), near_work(near, (own, own_other), prepared, fetched), y1f_other
    )
    pieces[2, 0, 0, 1], pieces[3, 1, 0, 1], pieces[2, 1, 0, 1] = z2f, y3f, y2f
    for steps, side, far in ((1, 0, 1), (3, 0, 1), (2, 0, 1), (3, 1, 1), (2, 1, 1)):
        pieces[steps, side, 1, far] = other_core(pieces[steps, side, 0, far])
    return pieces, (own, own_other), fetched, prepared, near_done


def prepare_kernel(nkey, proj_count, pick_ref, row_id_ref, counts_ref, wide_id_ref, proj_ref):
    wide_id = jnp.broadcast_to(row_id_ref[...], wide_id_ref.shape)
    wide_id_ref[...] = wide_id
    proj_ref[...] = (wide_id % nkey % proj_count).T[:proj_ref.shape[0]]
    token_rows, slots = counts_ref.shape
    lane = lax.broadcasted_iota(jnp.int32, (token_rows, slots), 1)
    pick = pick_ref[...]
    counts = jnp.zeros((token_rows, slots), F32)
    for k in range(pick.shape[1]):
        counts += jnp.where(pick[:, k:k + 1] == lane, 1.0, 0.0)
    counts_ref[...] = counts


def placed(keys, pieces):
    me, x = lax.axis_index("mem"), lax.axis_index("groups")
    z, y, core = me // 4, (me // 2) % 2, me % 2
    for (steps, side, other, far), piece in zip(keys, pieces):
        at = place(ring_source(z, steps), 1 - y if side else y, 1 - core if other else core)
        if len(piece.shape) == 4:
            piece = piece.at[1 - x if far else x]
        yield at, piece


def wait_for(held, sem):
    pltpu.make_async_copy(held, held, sem).wait()


def lanes(held, blocks):
    return jnp.concatenate([held[:, j].reshape(-1, LANES) for j in blocks], axis=1)


def value_products(first, count, held, base, proj, cot, fetched, pick_grad):
    value_width = fetched.shape[1]
    parts = value_width // held.shape[-2]
    for e in range(count):
        block = jnp.concatenate(
            [held[m, base + e * parts:base + (e + 1) * parts].reshape(value_width, LANES) for m in range(held.shape[0])],
            axis=1,
        )
        grad = dot(cot, block, LAST).astype(BF16)
        pick_grad = jnp.where(proj == first + e, dot(grad, fetched, LAST), pick_grad)
    return pick_grad


def key_rows(use_row, row_id, keys):
    nkey = keys.shape[0]
    key_at = lax.broadcasted_iota(jnp.int32, (row_id.shape[0], nkey), 1)
    picked = jnp.where(use_row, row_id // nkey, row_id % nkey)
    return dot(jnp.where(picked == key_at, 1.0, 0.0).astype(BF16), keys, PLAIN).astype(BF16)


def near_kernel(
    proj_count, keys, row_id_ref, proj_ref, tokens_ref, cot_ref, fetched_ref, *refs
):
    pick_grad_ref, queries_ref, slot_key_ref, held, sem = refs[-5:]
    for at, piece in placed(keys, refs[:-5]):
        pltpu.make_async_copy(piece, held.at[at], sem).start()
    x = lax.axis_index("groups")
    features = tokens_ref.shape[1]
    half = features // 2
    half_count = proj_count // 2
    parts = half_count * fetched_ref.shape[1] // held.shape[2]
    key = parts + half // LANES
    wait_for(held, sem)
    slot_key_ref[...] = key_rows(x == 0, row_id_ref[:, :1], lanes(held, range(key, held.shape[1])))
    tokens = tokens_ref[:, pl.ds(pl.multiple_of(x * half, half), half)]
    queries_ref[...] = dot(tokens, lanes(held, range(parts, key)), LAST)
    pick_grad_ref[...] = value_products(
        x * half_count, half_count, held, 0, proj_ref[:1], cot_ref[...], fetched_ref[...],
        jnp.zeros(pick_grad_ref.shape, F32),
    )


def dense_kernel(
    rank, width, proj_count, keys, core_ref, row_id_ref, proj_ref, near_key_ref, tokens_ref, *refs
):
    inputs, refs = refs[:5], refs[5:]
    pieces = refs[:len(keys)]
    (out_ref, grad_ref, near_held, far_held, queries_held, pick_held, counts_held, cot_held, fetched_held,
     mixed_values, query_grad, out_held, grad_held, piece_sem, in_sem, out_sem) = refs[len(keys):]
    held_inputs = (queries_held, pick_held, counts_held, fetched_held, cot_held)
    x = lax.axis_index("groups")
    token_rows, features = tokens_ref.shape
    slots, value_width = fetched_held.shape
    columns = far_held.shape[2]
    half = features // 2
    half_count = proj_count // 2
    parts = half_count * value_width // columns
    key = parts + half // LANES
    spots = list(placed(keys, pieces))
    far = [spot for spot, k in zip(spots, keys) if k[3]]
    near = [spot for spot, k in zip(spots, keys) if not k[3]]
    query_blocks = pl.ds(parts, far_held.shape[1] - parts)
    for at, piece in far:
        pltpu.make_async_copy(piece.at[query_blocks], far_held.at[at, query_blocks], piece_sem.at[0]).start()
    copies = [pltpu.make_async_copy(a, b, in_sem.at[i]) for i, (a, b) in enumerate(zip(inputs, held_inputs))]
    for copy in copies:
        copy.start()
    for at, piece in far:
        pltpu.make_async_copy(piece.at[pl.ds(0, parts)], far_held.at[at, pl.ds(0, parts)], piece_sem.at[1]).start()
    for at, piece in near:
        pltpu.make_async_copy(piece, near_held.at[at], piece_sem.at[2]).start()

    wait_for(far_held.at[:, query_blocks], piece_sem.at[0])
    far_key = key_rows(x != 0, row_id_ref[:, :1], lanes(far_held, range(key, far_held.shape[1])))
    near_key = near_key_ref[...]
    slot_row = jnp.where(x == 0, near_key, far_key)
    slot_col = jnp.where(x == 0, far_key, near_key)
    tokens = tokens_ref[:, pl.ds(pl.multiple_of((1 - x) * half, half), half)]
    queries = dot(tokens, lanes(far_held, range(parts, key)), LAST)
    for copy in copies:
        copy.wait()
    queries = (queries + queries_held[...]).astype(BF16)
    block = [queries[:, r * width:(r + 1) * width] for r in range(2 * rank)]
    row_scores = [dot(block[r], slot_row, LAST) for r in range(rank)]
    col_scores = [dot(block[rank + r], slot_col, LAST) for r in range(rank)]
    col_mixed = [sum(core_ref[r, s] * col_scores[s] for s in range(rank)) for r in range(rank)]
    row_mixed = [sum(row_scores[r] * core_ref[r, s] for r in range(rank)) for s in range(rank)]
    score = sum(row_scores[r] * col_mixed[r] for r in range(rank))
    gate = 1.0 / (1.0 + jnp.exp(-score))
    counts = counts_held[...]
    weights = (counts * gate.astype(BF16).astype(F32)).astype(BF16)
    slope = gate * (1.0 - gate)

    proj = proj_ref[:1]
    fetched = fetched_held[...]
    for i in range(proj_count):
        e = (x if i < half_count else 1 - x) * half_count + i % half_count
        mixed = dot(jnp.where(proj == e, weights, jnp.zeros((), BF16)), fetched, PLAIN)
        mixed_values[:, i * value_width:(i + 1) * value_width] = mixed.astype(BF16)
    wait_for(far_held.at[:, pl.ds(0, parts)], piece_sem.at[1])
    pick_grad = value_products(
        (1 - x) * half_count, half_count, far_held, 0, proj, cot_held[...], fetched, pick_held[...]
    )
    score_grad = pick_grad * slope
    for i, factor in enumerate(col_mixed + row_mixed):
        slot_key = slot_row if i < rank else slot_col
        grad = ((score_grad * factor).astype(BF16).astype(F32) * counts).astype(BF16)
        query_grad[:, i * width:(i + 1) * width] = dot(grad, slot_key, PLAIN).astype(BF16)
    wait_for(near_held, piece_sem.at[2])

    members = far_held.shape[0] // 4
    step = features // 4
    sides = ((near_held, x), (far_held, 1 - x))
    for c in range(4):
        cols = pl.ds(c * step, step)
        block = jnp.concatenate([
            jnp.concatenate([held[m, :parts].reshape(-1, LANES) for m in range(c * members, (c + 1) * members)], axis=1)
            for held, _ in sides
        ], axis=0)
        out_held[:, cols] = dot(mixed_values[...], block, PLAIN).astype(BF16)
        pltpu.make_async_copy(out_held.at[:, cols], out_ref.at[:, cols], out_sem.at[0]).start()
        held, side = sides[c // 2]
        blocks = step // LANES
        first = parts + (c % 2) * blocks
        cols = pl.ds(pl.multiple_of(side * half + (c % 2) * step, step), step)
        grad_held[:, cols] = dot(query_grad[...], lanes(held, range(first, first + blocks)), PLAIN).astype(BF16)
        pltpu.make_async_copy(grad_held.at[:, cols], grad_ref.at[:, cols], out_sem.at[1]).start()
    pltpu.make_async_copy(out_held, out_ref, out_sem.at[0]).wait()
    pltpu.make_async_copy(grad_held, grad_ref, out_sem.at[1]).wait()


def vmem():
    return pl.BlockSpec(memory_space=pltpu.VMEM)


def smem():
    return pl.BlockSpec(memory_space=pltpu.SMEM)


def anywhere():
    return pl.BlockSpec(memory_space=pl.ANY)


def pieces_path(tokens, cotangent, w_query, key_row, key_col, tucker_core, proj_part, requests, table, row_id,
                slot_proj, pick_slot, nkey, proj_count):
    rank = tucker_core.shape[0]
    width = key_row.shape[1]
    token_rows, features = tokens.shape
    slots = row_id.shape[0]
    value_width = table.shape[1]
    columns = w_query.shape[1]
    own = own_halves(w_query, key_row, key_col, proj_part)
    params = pltpu.CompilerParams(vmem_limit_bytes=VMEM_LIMIT)
    prepared = pl.pallas_call(
        functools.partial(prepare_kernel, nkey, proj_count),
        out_shape=(
            jax.ShapeDtypeStruct((token_rows, slots), F32),
            jax.ShapeDtypeStruct((slots, LANES), jnp.int32),
            jax.ShapeDtypeStruct((8, slots), jnp.int32),
        ),
        in_specs=[vmem(), vmem()],
        out_specs=(vmem(),) * 3,
        compiler_params=pltpu.CompilerParams(vmem_limit_bytes=SMALL_LIMIT),
        cost_estimate=pl.CostEstimate(flops=3 * 10**9, bytes_accessed=10**6, transcendentals=0),
        name="prepare",
    )(pick_slot, row_id[:, None])
    members = nkey // columns
    plane = jax.ShapeDtypeStruct((token_rows, slots), F32)
    partial = jax.ShapeDtypeStruct((token_rows, 2 * rank * width), F32)
    held = pltpu.VMEM((members,) + own.shape[1:], BF16)

    def near_work(near, pair, prepared, fetched):
        _, wide_id, slot_proj = prepared
        keys = ((0, 0, 0, 0), (0, 0, 1, 0)) + tuple(near)
        return pl.pallas_call(
            functools.partial(near_kernel, proj_count, keys),
            out_shape=(plane, partial, jax.ShapeDtypeStruct((slots, width), BF16)),
            in_specs=[vmem()] * 5 + [anywhere()] * len(keys),
            out_specs=(vmem(),) * 3,
            scratch_shapes=[held, pltpu.SemaphoreType.DMA],
            compiler_params=params,
            cost_estimate=pl.CostEstimate(flops=5 * 10**9, bytes_accessed=10**7, transcendentals=0),
            name="near",
        )(wide_id, slot_proj, tokens, cotangent, fetched.reshape(slots, value_width), *pair, *near.values())

    pieces, pair, fetched, prepared, near_done = gather_pieces(own, requests, table, prepared, near_work)
    counts, wide_id, slot_proj = prepared
    pick_grad, queries, near_key = near_done
    keys = ((0, 0, 0, 0), (0, 0, 1, 0), (0, 0, 0, 1), (0, 0, 1, 1)) + tuple(pieces)
    tall = (token_rows, features)
    return pl.pallas_call(
        functools.partial(dense_kernel, rank, width, proj_count, keys),
        out_shape=(jax.ShapeDtypeStruct(tall, BF16),) * 2,
        in_specs=[smem()] + [vmem()] * 4 + [anywhere()] * (5 + len(keys)),
        out_specs=(anywhere(), anywhere()),
        scratch_shapes=[
            held,
            held,
            pltpu.VMEM(partial.shape, F32),
            pltpu.VMEM(plane.shape, F32),
            pltpu.VMEM(plane.shape, F32),
            pltpu.VMEM(tall, BF16),
            pltpu.VMEM((slots, value_width), BF16),
            pltpu.VMEM((token_rows, proj_count * value_width), BF16),
            pltpu.VMEM(partial.shape, BF16),
            pltpu.VMEM(tall, BF16),
            pltpu.VMEM(tall, BF16),
            pltpu.SemaphoreType.DMA((3,)),
            pltpu.SemaphoreType.DMA((5,)),
            pltpu.SemaphoreType.DMA((2,)),
        ],
        compiler_params=params,
        cost_estimate=pl.CostEstimate(flops=10**10, bytes_accessed=2 * 10**7, transcendentals=10**5),
        name="dense",
    )(
        tucker_core, wide_id, slot_proj, near_key, tokens, queries, pick_grad, counts,
        fetched.reshape(slots, value_width), cotangent, *pair, *pair, *pieces.values(),
    )


def whole_path(tokens, cotangent, w_query, key_row, key_col, tucker_core, proj_part, requests, table, row_id,
               slot_proj, pick_slot, nkey, proj_count):
    rank = tucker_core.shape[0]
    width = key_row.shape[1]
    slots = row_id.shape[0]
    fetched = returned_rows(found_rows(wanted_rows(requests), table)).reshape(slots, -1)
    query_full = lax.all_gather(w_query.T, "mem", axis=0, tiled=True)
    keys = lax.all_gather(jnp.concatenate([key_row, key_col], axis=1), "mem", axis=0, tiled=True)
    proj_full = lax.all_gather(proj_part, "mem", axis=1, tiled=True)
    key_at = jnp.arange(nkey, dtype=jnp.int32)[None, :]
    row_hot = ((row_id // nkey)[:, None] == key_at).astype(BF16)
    col_hot = ((row_id % nkey)[:, None] == key_at).astype(BF16)
    slot_row = dot(row_hot, keys[:, :width], PLAIN).astype(BF16)
    slot_col = dot(col_hot, keys[:, width:], PLAIN).astype(BF16)
    spread = jnp.where(
        slot_proj[:, None, None] == jnp.arange(proj_count, dtype=jnp.int32)[None, :, None],
        fetched[:, None, :], jnp.zeros((), BF16)
    ).reshape(slots, -1)
    counts = jnp.sum(
        (pick_slot[:, :, None] == jnp.arange(slots, dtype=jnp.int32)[None, None, :]).astype(F32), axis=1
    )
    queries = dot(tokens, query_full, LAST).astype(BF16)
    row_scores = [dot(queries[:, r * width:(r + 1) * width], slot_row, LAST) for r in range(rank)]
    col_scores = [
        dot(queries[:, (rank + r) * width:(rank + r + 1) * width], slot_col, LAST) for r in range(rank)
    ]
    col_mixed = [sum(tucker_core[r, s] * col_scores[s] for s in range(rank)) for r in range(rank)]
    row_mixed = [sum(row_scores[r] * tucker_core[r, s] for r in range(rank)) for s in range(rank)]
    score = sum(row_scores[r] * col_mixed[r] for r in range(rank))
    gate = jax.nn.sigmoid(score)
    weights = counts * gate.astype(BF16).astype(F32)
    mixed = counted_dot(weights, spread, PLAIN).astype(BF16)
    memory_out = dot(mixed, proj_full, PLAIN)
    value_grad = dot(cotangent, proj_full, LAST).astype(BF16)
    pick_grad = dot(value_grad, spread, LAST)
    score_grad = pick_grad * gate * (1.0 - gate)
    blocks = []
    for mixed_scores, slot_key in ((col_mixed, slot_row), (row_mixed, slot_col)):
        for r in range(rank):
            grad = (score_grad * mixed_scores[r]).astype(BF16).astype(F32) * counts
            blocks.append(counted_dot(grad, slot_key, PLAIN).astype(BF16))
    query_grad = jnp.concatenate(blocks, axis=1)
    token_grad = dot(query_grad, query_full, PLAIN)
    return memory_out.astype(BF16), token_grad.astype(BF16)


def shards(
    mem, tokens, cotangent, w_query, key_row, key_col, tucker_core, table, w_proj, send_ids, pick_slot
):
    proj_count, value_width, _ = w_proj.shape
    requests = send_ids[0]
    owners, capacity = requests.shape
    slots = owners * capacity
    nkey = key_row.shape[0] * mem
    row_id = jnp.maximum(requests, 0) + jnp.arange(owners, dtype=jnp.int32)[:, None] * table.shape[0]
    row_id = row_id.reshape(slots)
    slot_proj = (row_id % nkey) % proj_count
    proj_part = w_proj.reshape(proj_count * value_width, -1)
    path = pieces_path if mem == 16 and w_proj.shape[2] == LANES else whole_path
    return path(tokens, cotangent, w_query, key_row, key_col, tucker_core, proj_part, requests, table, row_id,
                slot_proj, pick_slot, nkey, proj_count)


def solution(mesh):
    in_specs = (
        P(("groups", "mem"), None),
        P(("groups", "mem"), None),
        P(None, "mem"),
        P("mem", None),
        P("mem", None),
        P(),
        P("mem", None),
        P(None, None, "mem"),
        P(("groups", "mem"), None, None),
        P(("groups", "mem"), None),
    )
    out_specs = (P(("groups", "mem"), None), P(("groups", "mem"), None))
    body = functools.partial(shards, mesh.shape["mem"])
    return jax.shard_map(body, mesh=mesh, in_specs=in_specs, out_specs=out_specs, check_vma=False)
```

```python
import functools

import jax
import jax.numpy as jnp
from jax import lax
from jax.experimental import pallas as pl
from jax.experimental.pallas import tpu as pltpu
from jax.sharding import PartitionSpec as P

F32 = jnp.float32
BF16 = jnp.bfloat16
RING = (0, 2, 3, 1)
LANES = 128
LAST = ((1,), (1,))
PLAIN = ((1,), (0,))
VMEM_LIMIT = 56 * 1024 * 1024


def dot(a, b, dims):
    return lax.dot_general(a, b, (dims, ((), ())), preferred_element_type=F32)


def two_terms(x):
    high = x.astype(BF16)
    return high, (x - high.astype(F32)).astype(BF16)


def counted_dot(x, b, dims):
    high, low = two_terms(x)
    return dot(high, b, dims) + dot(low, b, dims)


def wanted_rows(requests):
    return lax.all_to_all(requests, "mem", split_axis=0, concat_axis=0, tiled=True)


def found_rows(wanted, table):
    found = jnp.take(table, jnp.maximum(wanted, 0).reshape(-1), axis=0, mode="clip")
    return found.reshape(wanted.shape + (table.shape[1],))


def returned_rows(found):
    return lax.all_to_all(found, "mem", split_axis=0, concat_axis=0, tiled=True)


def place(z, y, core):
    return (z * 2 + y) * 2 + core


def everywhere(move):
    pairs = []
    for z in range(4):
        for y in range(2):
            for core in range(2):
                pairs.append((place(z, y, core), place(*move(z, y, core))))
    return pairs


def next_z(x):
    step = {RING[i]: RING[(i + 1) % 4] for i in range(4)}
    return lax.ppermute(x, "mem", everywhere(lambda z, y, c: (step[z], y, c)))


def other_y(x):
    return lax.ppermute(x, "mem", everywhere(lambda z, y, c: (z, 1 - y, c)))


def other_core(x):
    return lax.ppermute(x, "mem", everywhere(lambda z, y, c: (z, y, 1 - c)))


def other_x(x):
    return lax.ppermute(x, "groups", [(0, 1), (1, 0)])


def ring_source(z, steps):
    index = jnp.where(z == 0, 0, jnp.where(z == 2, 1, jnp.where(z == 3, 2, 3)))
    index = (index + 4 - steps) % 4
    return jnp.where(index == 0, 0, jnp.where(index == 1, 2, jnp.where(index == 2, 3, 1)))


def tie(*values):
    return lax.optimization_barrier(values)


def halves_kernel(query_ref, key_row_ref, key_col_ref, proj_ref, near_ref, far_ref, sems):
    x = lax.axis_index("groups")
    parts = proj_ref.shape[1]
    blocks = query_ref.shape[1] // LANES // 2
    for target, half, sem in ((near_ref, x, sems.at[0]), (far_ref, 1 - x, sems.at[1])):
        for j in range(blocks):
            cols = pl.ds(pl.multiple_of((half * blocks + j) * LANES, LANES), LANES)
            pltpu.make_async_copy(query_ref.at[:, cols], target.at[parts + j], sem).start()
        for key_ref, wanted in ((key_row_ref, 0), (key_col_ref, 1)):
            @pl.when(half == wanted)
            def _():
                for j in range(key_ref.shape[1] // LANES):
                    cols = pl.ds(j * LANES, LANES)
                    pltpu.make_async_copy(key_ref.at[:, cols], target.at[parts + blocks + j], sem).start()
        pltpu.make_async_copy(proj_ref.at[half], target.at[pl.ds(0, parts)], sem).start()
    wait_for(near_ref, sems.at[0])
    wait_for(far_ref, sems.at[1])


def own_halves(w_query, key_row, key_col, proj_part):
    features, columns = w_query.shape
    proj = proj_part.reshape(2, -1, columns, LANES)
    blocks = proj.shape[1] + (features // 2 + key_row.shape[1]) // LANES
    half = jax.ShapeDtypeStruct((blocks, columns, LANES), BF16)
    return pl.pallas_call(
        halves_kernel,
        out_shape=(half, half),
        in_specs=[anywhere()] * 4,
        out_specs=(anywhere(), anywhere()),
        scratch_shapes=[pltpu.SemaphoreType.DMA((2,))],
        compiler_params=pltpu.CompilerParams(vmem_limit_bytes=VMEM_LIMIT),
        cost_estimate=pl.CostEstimate(flops=0, bytes_accessed=4 * 10**6, transcendentals=0),
        name="halves",
    )(w_query.T, key_row, key_col, proj)


def other_cores(first, second):
    first = other_core(first)
    second, first = tie(second, first)
    return first, other_core(second)


def gather_pieces(own_near, own_far, requests, table, near_work):
    pieces = {(0, 0, 0, 0): own_near, (0, 0, 0, 1): own_far}
    z1, y0, wanted, pieces[0, 0, 1, 0], pieces[0, 0, 1, 1] = tie(
        next_z(own_near), other_y(own_near), wanted_rows(requests), other_core(own_near), other_core(own_far)
    )
    pieces[1, 0, 0, 0], pieces[0, 1, 0, 0] = z1, y0
    z2, y1, y0f, found, pieces[1, 0, 1, 0], pieces[0, 1, 1, 0] = tie(
        next_z(z1), other_y(z1), other_x(y0), found_rows(wanted, table), *other_cores(z1, y0)
    )
    pieces[2, 0, 0, 0], pieces[1, 1, 0, 0], pieces[0, 1, 0, 1] = z2, y1, y0f
    z3, y2, y1f, pieces[2, 0, 1, 0], pieces[1, 1, 1, 0] = tie(
        next_z(z2), other_y(z2), other_x(y1), *other_cores(z2, y1)
    )
    pieces[3, 0, 0, 0], pieces[2, 1, 0, 0], pieces[1, 1, 0, 1] = z3, y2, y1f
    z1f, y3, z3f, fetched, pieces[3, 0, 1, 0], pieces[0, 1, 1, 1] = tie(
        next_z(own_far), other_y(z3), other_x(z3), returned_rows(found), *other_cores(z3, y0f)
    )
    pieces[1, 0, 0, 1], pieces[3, 1, 0, 0], pieces[3, 0, 0, 1] = z1f, y3, z3f
    y2_other, y1f_other = other_cores(y2, y1f)
    pieces[2, 1, 1, 0], pieces[3, 1, 1, 0] = y2_other, other_core(y3)
    near = {key: piece for key, piece in pieces.items() if key[3] == 0}
    z2f, y3f, y2f, near_done, pieces[1, 1, 1, 1] = tie(
        next_z(z1f), other_y(z3f), other_x(y2), near_work(near, fetched), y1f_other
    )
    pieces[2, 0, 0, 1], pieces[3, 1, 0, 1], pieces[2, 1, 0, 1] = z2f, y3f, y2f
    for steps, side, far in ((1, 0, 1), (3, 0, 1), (2, 0, 1), (3, 1, 1), (2, 1, 1)):
        pieces[steps, side, 1, far] = other_core(pieces[steps, side, 0, far])
    return pieces, fetched, near_done


def placed(keys, pieces):
    me = lax.axis_index("mem")
    z, y, core = me // 4, (me // 2) % 2, me % 2
    for (steps, side, other, far), piece in zip(keys, pieces):
        at = place(ring_source(z, steps), 1 - y if side else y, 1 - core if other else core)
        yield at, piece


def wait_for(held, sem):
    pltpu.make_async_copy(held, held, sem).wait()


def lanes(held, blocks):
    return jnp.concatenate([held[:, j].reshape(-1, LANES) for j in blocks], axis=1)


def value_products(first, count, held, base, proj, cot, fetched, pick_grad):
    value_width = fetched.shape[1]
    parts = value_width // held.shape[-2]
    for e in range(count):
        block = jnp.concatenate(
            [held[m, base + e * parts:base + (e + 1) * parts].reshape(value_width, LANES) for m in range(held.shape[0])],
            axis=1,
        )
        grad = dot(cot, block, LAST).astype(BF16)
        pick_grad = jnp.where(proj == first + e, dot(grad, fetched, LAST), pick_grad)
    return pick_grad


def key_rows(use_row, row_id, keys):
    nkey = keys.shape[0]
    key_at = lax.broadcasted_iota(jnp.int32, (row_id.shape[0], nkey), 1)
    picked = jnp.where(use_row, row_id // nkey, row_id % nkey)
    return dot(jnp.where(picked == key_at, 1.0, 0.0).astype(BF16), keys, PLAIN).astype(BF16)


def slot_ids(requests, rows_each):
    owners, capacity = requests.shape
    slots = owners * capacity
    rows = jnp.broadcast_to(requests[:, None, :], (owners, capacity, capacity)).reshape(slots, capacity)
    slot = lax.broadcasted_iota(jnp.int32, (slots, capacity), 0)
    lane = lax.broadcasted_iota(jnp.int32, (slots, capacity), 1)
    local = jnp.sum(jnp.where(slot % capacity == lane, jnp.maximum(rows, 0), 0), axis=1, keepdims=True)
    return local + slot[:, :1] // capacity * rows_each


def near_kernel(
    proj_count, rows_each, keys, requests_ref, pick_ref, tokens_ref, cot_ref, fetched_ref, *refs
):
    pick_grad_ref, queries_ref, slot_key_ref, counts_ref, wide_id_ref, proj_ref, held, sem = refs[-8:]
    for at, piece in placed(keys, refs[:-8]):
        pltpu.make_async_copy(piece, held.at[at], sem).start()
    x = lax.axis_index("groups")
    features = tokens_ref.shape[1]
    half = features // 2
    half_count = proj_count // 2
    parts = half_count * fetched_ref.shape[1] // held.shape[2]
    key = parts + half // LANES
    nkey = held.shape[0] * held.shape[2]
    wide_id = jnp.broadcast_to(slot_ids(requests_ref[...], rows_each), wide_id_ref.shape)
    wide_id_ref[...] = wide_id
    proj = (wide_id % nkey % proj_count).T[:proj_ref.shape[0]]
    proj_ref[...] = proj
    token_rows, slots = counts_ref.shape
    lane = lax.broadcasted_iota(jnp.int32, (token_rows, slots), 1)
    pick = pick_ref[...].T
    counts = jnp.zeros((token_rows, slots), F32)
    for k in range(pick.shape[1]):
        counts += jnp.where(pick[:, k:k + 1] == lane, 1.0, 0.0)
    counts_ref[...] = counts
    wait_for(held, sem)
    slot_key_ref[...] = key_rows(x == 0, wide_id[:, :1], lanes(held, range(key, held.shape[1])))
    tokens = tokens_ref[:, pl.ds(pl.multiple_of(x * half, half), half)]
    queries_ref[...] = dot(tokens, lanes(held, range(parts, key)), LAST)
    pick_grad_ref[...] = value_products(
        x * half_count, half_count, held, 0, proj[:1], cot_ref[...], fetched_ref[...],
        jnp.zeros(pick_grad_ref.shape, F32),
    )


def dense_kernel(
    rank, width, proj_count, keys, core_ref, row_id_ref, proj_ref, near_key_ref, tokens_ref, *refs
):
    inputs, refs = refs[:5], refs[5:]
    pieces = refs[:len(keys)]
    (out_ref, grad_ref, near_held, far_held, queries_held, pick_held, counts_held, cot_held, fetched_held,
     mixed_values, query_grad, out_held, grad_held, piece_sem, in_sem, out_sem) = refs[len(keys):]
    held_inputs = (queries_held, pick_held, counts_held, fetched_held, cot_held)
    x = lax.axis_index("groups")
    token_rows, features = tokens_ref.shape
    slots, value_width = fetched_held.shape
    columns = far_held.shape[2]
    half = features // 2
    half_count = proj_count // 2
    parts = half_count * value_width // columns
    key = parts + half // LANES
    spots = list(placed(keys, pieces))
    far = [spot for spot, k in zip(spots, keys) if k[3]]
    near = [spot for spot, k in zip(spots, keys) if not k[3]]
    query_blocks = pl.ds(parts, far_held.shape[1] - parts)
    for at, piece in far:
        pltpu.make_async_copy(piece.at[query_blocks], far_held.at[at, query_blocks], piece_sem.at[0]).start()
    copies = [pltpu.make_async_copy(a, b, in_sem.at[i]) for i, (a, b) in enumerate(zip(inputs, held_inputs))]
    for copy in copies:
        copy.start()
    for at, piece in far:
        pltpu.make_async_copy(piece.at[pl.ds(0, parts)], far_held.at[at, pl.ds(0, parts)], piece_sem.at[1]).start()
    for at, piece in near:
        pltpu.make_async_copy(piece, near_held.at[at], piece_sem.at[2]).start()

    wait_for(far_held.at[:, query_blocks], piece_sem.at[0])
    far_key = key_rows(x != 0, row_id_ref[:, :1], lanes(far_held, range(key, far_held.shape[1])))
    near_key = near_key_ref[...]
    slot_row = jnp.where(x == 0, near_key, far_key)
    slot_col = jnp.where(x == 0, far_key, near_key)
    tokens = tokens_ref[:, pl.ds(pl.multiple_of((1 - x) * half, half), half)]
    queries = dot(tokens, lanes(far_held, range(parts, key)), LAST)
    for copy in copies:
        copy.wait()
    queries = (queries + queries_held[...]).astype(BF16)
    block = [queries[:, r * width:(r + 1) * width] for r in range(2 * rank)]
    row_scores = [dot(block[r], slot_row, LAST) for r in range(rank)]
    col_scores = [dot(block[rank + r], slot_col, LAST) for r in range(rank)]
    col_mixed = [sum(core_ref[r, s] * col_scores[s] for s in range(rank)) for r in range(rank)]
    row_mixed = [sum(row_scores[r] * core_ref[r, s] for r in range(rank)) for s in range(rank)]
    score = sum(row_scores[r] * col_mixed[r] for r in range(rank))
    gate = 1.0 / (1.0 + jnp.exp(-score))
    counts = counts_held[...]
    weights = (counts * gate.astype(BF16).astype(F32)).astype(BF16)
    slope = gate * (1.0 - gate)

    proj = proj_ref[:1]
    fetched = fetched_held[...]
    for i in range(proj_count):
        e = (x if i < half_count else 1 - x) * half_count + i % half_count
        mixed = dot(jnp.where(proj == e, weights, jnp.zeros((), BF16)), fetched, PLAIN)
        mixed_values[:, i * value_width:(i + 1) * value_width] = mixed.astype(BF16)
    wait_for(far_held.at[:, pl.ds(0, parts)], piece_sem.at[1])
    pick_grad = value_products(
        (1 - x) * half_count, half_count, far_held, 0, proj, cot_held[...], fetched, pick_held[...]
    )
    score_grad = pick_grad * slope
    for i, factor in enumerate(col_mixed + row_mixed):
        slot_key = slot_row if i < rank else slot_col
        grad = ((score_grad * factor).astype(BF16).astype(F32) * counts).astype(BF16)
        query_grad[:, i * width:(i + 1) * width] = dot(grad, slot_key, PLAIN).astype(BF16)
    wait_for(near_held, piece_sem.at[2])

    members = far_held.shape[0] // 4
    step = features // 4
    sides = ((near_held, x), (far_held, 1 - x))
    for c in range(4):
        cols = pl.ds(c * step, step)
        block = jnp.concatenate([
            jnp.concatenate([held[m, :parts].reshape(-1, LANES) for m in range(c * members, (c + 1) * members)], axis=1)
            for held, _ in sides
        ], axis=0)
        out_held[:, cols] = dot(mixed_values[...], block, PLAIN).astype(BF16)
        pltpu.make_async_copy(out_held.at[:, cols], out_ref.at[:, cols], out_sem.at[0]).start()
        held, side = sides[c // 2]
        blocks = step // LANES
        first = parts + (c % 2) * blocks
        cols = pl.ds(pl.multiple_of(side * half + (c % 2) * step, step), step)
        grad_held[:, cols] = dot(query_grad[...], lanes(held, range(first, first + blocks)), PLAIN).astype(BF16)
        pltpu.make_async_copy(grad_held.at[:, cols], grad_ref.at[:, cols], out_sem.at[1]).start()
    pltpu.make_async_copy(out_held, out_ref, out_sem.at[0]).wait()
    pltpu.make_async_copy(grad_held, grad_ref, out_sem.at[1]).wait()


def vmem():
    return pl.BlockSpec(memory_space=pltpu.VMEM)


def smem():
    return pl.BlockSpec(memory_space=pltpu.SMEM)


def anywhere():
    return pl.BlockSpec(memory_space=pl.ANY)


def pieces_path(tokens, cotangent, w_query, key_row, key_col, tucker_core, proj_part, requests, table, row_id,
                slot_proj, pick_slot, nkey, proj_count):
    rank = tucker_core.shape[0]
    width = key_row.shape[1]
    token_rows, features = tokens.shape
    slots = row_id.shape[0]
    value_width = table.shape[1]
    columns = w_query.shape[1]
    own_near, own_far = own_halves(w_query, key_row, key_col, proj_part)
    params = pltpu.CompilerParams(vmem_limit_bytes=VMEM_LIMIT)
    members = nkey // columns
    plane = jax.ShapeDtypeStruct((token_rows, slots), F32)
    partial = jax.ShapeDtypeStruct((token_rows, 2 * rank * width), F32)
    held = pltpu.VMEM((members,) + own_near.shape, BF16)

    def near_work(near, fetched):
        return pl.pallas_call(
            functools.partial(near_kernel, proj_count, table.shape[0], tuple(near)),
            out_shape=(
                plane, partial, jax.ShapeDtypeStruct((slots, width), BF16), plane,
                jax.ShapeDtypeStruct((slots, LANES), jnp.int32), jax.ShapeDtypeStruct((8, slots), jnp.int32),
            ),
            in_specs=[vmem()] * 5 + [anywhere()] * len(near),
            out_specs=(vmem(),) * 6,
            scratch_shapes=[held, pltpu.SemaphoreType.DMA],
            compiler_params=params,
            cost_estimate=pl.CostEstimate(flops=5 * 10**9, bytes_accessed=10**7, transcendentals=0),
            name="near",
        )(requests, pick_slot.T, tokens, cotangent, fetched.reshape(slots, value_width), *near.values())

    pieces, fetched, near_done = gather_pieces(own_near, own_far, requests, table, near_work)
    pick_grad, queries, near_key, counts, wide_id, slot_proj = near_done
    keys = tuple(pieces)
    tall = (token_rows, features)
    return pl.pallas_call(
        functools.partial(dense_kernel, rank, width, proj_count, keys),
        out_shape=(jax.ShapeDtypeStruct(tall, BF16),) * 2,
        in_specs=[smem()] + [vmem()] * 4 + [anywhere()] * (5 + len(keys)),
        out_specs=(anywhere(), anywhere()),
        scratch_shapes=[
            held,
            held,
            pltpu.VMEM(partial.shape, F32),
            pltpu.VMEM(plane.shape, F32),
            pltpu.VMEM(plane.shape, F32),
            pltpu.VMEM(tall, BF16),
            pltpu.VMEM((slots, value_width), BF16),
            pltpu.VMEM((token_rows, proj_count * value_width), BF16),
            pltpu.VMEM(partial.shape, BF16),
            pltpu.VMEM(tall, BF16),
            pltpu.VMEM(tall, BF16),
            pltpu.SemaphoreType.DMA((3,)),
            pltpu.SemaphoreType.DMA((5,)),
            pltpu.SemaphoreType.DMA((2,)),
        ],
        compiler_params=params,
        cost_estimate=pl.CostEstimate(flops=10**10, bytes_accessed=2 * 10**7, transcendentals=10**5),
        name="dense",
    )(
        tucker_core, wide_id, slot_proj, near_key, tokens, queries, pick_grad, counts,
        fetched.reshape(slots, value_width), cotangent, *pieces.values(),
    )


def whole_path(tokens, cotangent, w_query, key_row, key_col, tucker_core, proj_part, requests, table, row_id,
               slot_proj, pick_slot, nkey, proj_count):
    rank = tucker_core.shape[0]
    width = key_row.shape[1]
    slots = row_id.shape[0]
    fetched = returned_rows(found_rows(wanted_rows(requests), table)).reshape(slots, -1)
    query_full = lax.all_gather(w_query.T, "mem", axis=0, tiled=True)
    keys = lax.all_gather(jnp.concatenate([key_row, key_col], axis=1), "mem", axis=0, tiled=True)
    proj_full = lax.all_gather(proj_part, "mem", axis=1, tiled=True)
    key_at = jnp.arange(nkey, dtype=jnp.int32)[None, :]
    row_hot = ((row_id // nkey)[:, None] == key_at).astype(BF16)
    col_hot = ((row_id % nkey)[:, None] == key_at).astype(BF16)
    slot_row = dot(row_hot, keys[:, :width], PLAIN).astype(BF16)
    slot_col = dot(col_hot, keys[:, width:], PLAIN).astype(BF16)
    spread = jnp.where(
        slot_proj[:, None, None] == jnp.arange(proj_count, dtype=jnp.int32)[None, :, None],
        fetched[:, None, :], jnp.zeros((), BF16)
    ).reshape(slots, -1)
    counts = jnp.sum(
        (pick_slot[:, :, None] == jnp.arange(slots, dtype=jnp.int32)[None, None, :]).astype(F32), axis=1
    )
    queries = dot(tokens, query_full, LAST).astype(BF16)
    row_scores = [dot(queries[:, r * width:(r + 1) * width], slot_row, LAST) for r in range(rank)]
    col_scores = [
        dot(queries[:, (rank + r) * width:(rank + r + 1) * width], slot_col, LAST) for r in range(rank)
    ]
    col_mixed = [sum(tucker_core[r, s] * col_scores[s] for s in range(rank)) for r in range(rank)]
    row_mixed = [sum(row_scores[r] * tucker_core[r, s] for r in range(rank)) for s in range(rank)]
    score = sum(row_scores[r] * col_mixed[r] for r in range(rank))
    gate = jax.nn.sigmoid(score)
    weights = counts * gate.astype(BF16).astype(F32)
    mixed = counted_dot(weights, spread, PLAIN).astype(BF16)
    memory_out = dot(mixed, proj_full, PLAIN)
    value_grad = dot(cotangent, proj_full, LAST).astype(BF16)
    pick_grad = dot(value_grad, spread, LAST)
    score_grad = pick_grad * gate * (1.0 - gate)
    blocks = []
    for mixed_scores, slot_key in ((col_mixed, slot_row), (row_mixed, slot_col)):
        for r in range(rank):
            grad = (score_grad * mixed_scores[r]).astype(BF16).astype(F32) * counts
            blocks.append(counted_dot(grad, slot_key, PLAIN).astype(BF16))
    query_grad = jnp.concatenate(blocks, axis=1)
    token_grad = dot(query_grad, query_full, PLAIN)
    return memory_out.astype(BF16), token_grad.astype(BF16)


def shards(
    mem, tokens, cotangent, w_query, key_row, key_col, tucker_core, table, w_proj, send_ids, pick_slot
):
    proj_count, value_width, _ = w_proj.shape
    requests = send_ids[0]
    owners, capacity = requests.shape
    slots = owners * capacity
    nkey = key_row.shape[0] * mem
    row_id = jnp.maximum(requests, 0) + jnp.arange(owners, dtype=jnp.int32)[:, None] * table.shape[0]
    row_id = row_id.reshape(slots)
    slot_proj = (row_id % nkey) % proj_count
    proj_part = w_proj.reshape(proj_count * value_width, -1)
    path = pieces_path if mem == 16 and w_proj.shape[2] == LANES else whole_path
    return path(tokens, cotangent, w_query, key_row, key_col, tucker_core, proj_part, requests, table, row_id,
                slot_proj, pick_slot, nkey, proj_count)


def solution(mesh):
    in_specs = (
        P(("groups", "mem"), None),
        P(("groups", "mem"), None),
        P(None, "mem"),
        P("mem", None),
        P("mem", None),
        P(),
        P("mem", None),
        P(None, None, "mem"),
        P(("groups", "mem"), None, None),
        P(("groups", "mem"), None),
    )
    out_specs = (P(("groups", "mem"), None), P(("groups", "mem"), None))
    body = functools.partial(shards, mesh.shape["mem"])
    return jax.shard_map(body, mesh=mesh, in_specs=in_specs, out_specs=out_specs, check_vma=False)
```

```python
import functools

import jax
import jax.numpy as jnp
from jax import lax
from jax.experimental import pallas as pl
from jax.experimental.pallas import tpu as pltpu
from jax.sharding import PartitionSpec as P

F32 = jnp.float32
BF16 = jnp.bfloat16
RING = (0, 2, 3, 1)
LANES = 128
LAST = ((1,), (1,))
PLAIN = ((1,), (0,))
VMEM_LIMIT = 56 * 1024 * 1024


def dot(a, b, dims):
    return lax.dot_general(a, b, (dims, ((), ())), preferred_element_type=F32)


def two_terms(x):
    high = x.astype(BF16)
    return high, (x - high.astype(F32)).astype(BF16)


def counted_dot(x, b, dims):
    high, low = two_terms(x)
    return dot(high, b, dims) + dot(low, b, dims)


def wanted_rows(requests):
    return lax.all_to_all(requests, "mem", split_axis=0, concat_axis=0, tiled=True)


def found_rows(wanted, table):
    found = jnp.take(table, jnp.maximum(wanted, 0).reshape(-1), axis=0, mode="clip")
    return found.reshape(wanted.shape + (table.shape[1],))


def returned_rows(found):
    return lax.all_to_all(found, "mem", split_axis=0, concat_axis=0, tiled=True)


def place(z, y, core):
    return (z * 2 + y) * 2 + core


def everywhere(move):
    pairs = []
    for z in range(4):
        for y in range(2):
            for core in range(2):
                pairs.append((place(z, y, core), place(*move(z, y, core))))
    return pairs


def next_z(x):
    step = {RING[i]: RING[(i + 1) % 4] for i in range(4)}
    return lax.ppermute(x, "mem", everywhere(lambda z, y, c: (step[z], y, c)))


def other_y(x):
    return lax.ppermute(x, "mem", everywhere(lambda z, y, c: (z, 1 - y, c)))


def other_core(x):
    return lax.ppermute(x, "mem", everywhere(lambda z, y, c: (z, y, 1 - c)))


def other_x(x):
    return lax.ppermute(x, "groups", [(0, 1), (1, 0)])


def ring_source(z, steps):
    index = jnp.where(z == 0, 0, jnp.where(z == 2, 1, jnp.where(z == 3, 2, 3)))
    index = (index + 4 - steps) % 4
    return jnp.where(index == 0, 0, jnp.where(index == 1, 2, jnp.where(index == 2, 3, 1)))


def tie(*values):
    return lax.optimization_barrier(values)


def halves_kernel(query_ref, key_row_ref, key_col_ref, proj_ref, near_ref, far_ref):
    x = lax.axis_index("groups")
    parts = proj_ref.shape[1]
    blocks = query_ref.shape[1] // LANES // 2
    for target, half in ((near_ref, x), (far_ref, 1 - x)):
        target[:parts] = proj_ref[half]
        for j in range(blocks):
            target[parts + j] = query_ref[:, pl.ds(pl.multiple_of((half * blocks + j) * LANES, LANES), LANES)]
        for j in range(key_row_ref.shape[1] // LANES):
            cols = slice(j * LANES, (j + 1) * LANES)
            target[parts + blocks + j] = jnp.where(half == 0, key_row_ref[:, cols], key_col_ref[:, cols])


def own_halves(w_query, key_row, key_col, proj_part):
    features, columns = w_query.shape
    proj = proj_part.reshape(2, -1, columns, LANES)
    blocks = proj.shape[1] + (features // 2 + key_row.shape[1]) // LANES
    half = jax.ShapeDtypeStruct((blocks, columns, LANES), BF16)
    return pl.pallas_call(
        halves_kernel,
        out_shape=(half, half),
        in_specs=[vmem()] * 4,
        out_specs=(vmem(), vmem()),
        compiler_params=pltpu.CompilerParams(vmem_limit_bytes=VMEM_LIMIT),
        cost_estimate=pl.CostEstimate(flops=0, bytes_accessed=4 * 10**6, transcendentals=0),
        name="halves",
    )(w_query.T, key_row, key_col, proj)


def other_cores(first, second):
    first = other_core(first)
    second, first = tie(second, first)
    return first, other_core(second)


def gather_pieces(own_near, own_far, requests, table, near_work):
    pieces = {(0, 0, 0, 0): own_near, (0, 0, 0, 1): own_far}
    z1, y0, wanted, pieces[0, 0, 1, 0], pieces[0, 0, 1, 1] = tie(
        next_z(own_near), other_y(own_near), wanted_rows(requests), other_core(own_near), other_core(own_far)
    )
    pieces[1, 0, 0, 0], pieces[0, 1, 0, 0] = z1, y0
    z2, y1, y0f, found, pieces[1, 0, 1, 0], pieces[0, 1, 1, 0] = tie(
        next_z(z1), other_y(z1), other_x(y0), found_rows(wanted, table), *other_cores(z1, y0)
    )
    pieces[2, 0, 0, 0], pieces[1, 1, 0, 0], pieces[0, 1, 0, 1] = z2, y1, y0f
    z3, y2, y1f, pieces[2, 0, 1, 0], pieces[1, 1, 1, 0] = tie(
        next_z(z2), other_y(z2), other_x(y1), *other_cores(z2, y1)
    )
    pieces[3, 0, 0, 0], pieces[2, 1, 0, 0], pieces[1, 1, 0, 1] = z3, y2, y1f
    z1f, y3, z3f, fetched, pieces[3, 0, 1, 0], pieces[0, 1, 1, 1] = tie(
        next_z(own_far), other_y(z3), other_x(z3), returned_rows(found), *other_cores(z3, y0f)
    )
    pieces[1, 0, 0, 1], pieces[3, 1, 0, 0], pieces[3, 0, 0, 1] = z1f, y3, z3f
    y2_other, y1f_other = other_cores(y2, y1f)
    pieces[2, 1, 1, 0], pieces[3, 1, 1, 0] = y2_other, other_core(y3)
    near = {key: piece for key, piece in pieces.items() if key[3] == 0}
    z2f, y3f, y2f, near_done, pieces[1, 1, 1, 1] = tie(
        next_z(z1f), other_y(z3f), other_x(y2), near_work(near, fetched), y1f_other
    )
    pieces[2, 0, 0, 1], pieces[3, 1, 0, 1], pieces[2, 1, 0, 1] = z2f, y3f, y2f
    for steps, side, far in ((1, 0, 1), (3, 0, 1), (2, 0, 1), (3, 1, 1), (2, 1, 1)):
        pieces[steps, side, 1, far] = other_core(pieces[steps, side, 0, far])
    return pieces, fetched, near_done


def placed(keys, pieces):
    me = lax.axis_index("mem")
    z, y, core = me // 4, (me // 2) % 2, me % 2
    for (steps, side, other, far), piece in zip(keys, pieces):
        at = place(ring_source(z, steps), 1 - y if side else y, 1 - core if other else core)
        yield at, piece


def wait_for(held, sem):
    pltpu.make_async_copy(held, held, sem).wait()


def lanes(held, blocks):
    return jnp.concatenate([held[:, j].reshape(-1, LANES) for j in blocks], axis=1)


def value_products(first, count, held, base, proj, cot, fetched, pick_grad):
    value_width = fetched.shape[1]
    parts = value_width // held.shape[-2]
    for e in range(count):
        block = jnp.concatenate(
            [held[m, base + e * parts:base + (e + 1) * parts].reshape(value_width, LANES) for m in range(held.shape[0])],
            axis=1,
        )
        grad = dot(cot, block, LAST).astype(BF16)
        pick_grad = jnp.where(proj == first + e, dot(grad, fetched, LAST), pick_grad)
    return pick_grad


def one_hot_keys(use_row, row_id, nkey):
    key_at = lax.broadcasted_iota(jnp.int32, (row_id.shape[0], nkey), 1)
    picked = jnp.where(use_row, row_id // nkey, row_id % nkey)
    return jnp.where(picked == key_at, 1.0, 0.0).astype(BF16)


def slot_ids(requests, rows_each):
    owners, capacity = requests.shape
    slots = owners * capacity
    rows = jnp.broadcast_to(requests[:, None, :], (owners, capacity, capacity)).reshape(slots, capacity)
    slot = lax.broadcasted_iota(jnp.int32, (slots, capacity), 0)
    lane = lax.broadcasted_iota(jnp.int32, (slots, capacity), 1)
    local = jnp.sum(jnp.where(slot % capacity == lane, jnp.maximum(rows, 0), 0), axis=1, keepdims=True)
    return local + slot[:, :1] // capacity * rows_each


def near_kernel(
    proj_count, rows_each, keys, requests_ref, pick_ref, tokens_ref, cot_ref, fetched_ref, *refs
):
    pick_grad_ref, queries_ref, slot_key_ref, counts_ref, wide_id_ref, proj_ref, held, sem = refs[-8:]
    for at, piece in placed(keys, refs[:-8]):
        pltpu.make_async_copy(piece, held.at[at], sem).start()
    x = lax.axis_index("groups")
    features = tokens_ref.shape[1]
    half = features // 2
    half_count = proj_count // 2
    parts = half_count * fetched_ref.shape[1] // held.shape[2]
    key = parts + half // LANES
    nkey = held.shape[0] * held.shape[2]
    wide_id = jnp.broadcast_to(slot_ids(requests_ref[...], rows_each), wide_id_ref.shape)
    wide_id_ref[...] = wide_id
    proj = (wide_id % nkey % proj_count).T[:proj_ref.shape[0]]
    proj_ref[...] = proj
    token_rows, slots = counts_ref.shape
    lane = lax.broadcasted_iota(jnp.int32, (token_rows, slots), 1)
    pick = pick_ref[...].T
    counts = jnp.zeros((token_rows, slots), F32)
    for k in range(pick.shape[1]):
        counts += jnp.where(pick[:, k:k + 1] == lane, 1.0, 0.0)
    counts_ref[...] = counts
    hot = one_hot_keys(x == 0, wide_id[:, :1], nkey)
    wait_for(held, sem)
    slot_key_ref[...] = dot(hot, lanes(held, range(key, held.shape[1])), PLAIN).astype(BF16)
    tokens = tokens_ref[:, pl.ds(pl.multiple_of(x * half, half), half)]
    queries_ref[...] = dot(tokens, lanes(held, range(parts, key)), LAST)
    pick_grad_ref[...] = value_products(
        x * half_count, half_count, held, 0, proj[:1], cot_ref[...], fetched_ref[...],
        jnp.zeros(pick_grad_ref.shape, F32),
    )


def dense_kernel(
    rank, width, proj_count, keys, core_ref, row_id_ref, proj_ref, near_key_ref, tokens_ref, *refs
):
    inputs, refs = refs[:5], refs[5:]
    pieces = refs[:len(keys)]
    (out_ref, grad_ref, near_held, far_held, queries_held, pick_held, counts_held, cot_held, fetched_held,
     mixed_values, query_grad, out_held, grad_held, piece_sem, in_sem, out_sem) = refs[len(keys):]
    held_inputs = (queries_held, pick_held, counts_held, fetched_held, cot_held)
    x = lax.axis_index("groups")
    token_rows, features = tokens_ref.shape
    slots, value_width = fetched_held.shape
    columns = far_held.shape[2]
    half = features // 2
    half_count = proj_count // 2
    parts = half_count * value_width // columns
    key = parts + half // LANES
    spots = list(placed(keys, pieces))
    far = [spot for spot, k in zip(spots, keys) if k[3]]
    near = [spot for spot, k in zip(spots, keys) if not k[3]]
    query_blocks = pl.ds(parts, far_held.shape[1] - parts)
    for at, piece in far:
        pltpu.make_async_copy(piece.at[query_blocks], far_held.at[at, query_blocks], piece_sem.at[0]).start()
    copies = [pltpu.make_async_copy(a, b, in_sem.at[i]) for i, (a, b) in enumerate(zip(inputs, held_inputs))]
    for copy in copies:
        copy.start()
    for at, piece in far:
        pltpu.make_async_copy(piece.at[pl.ds(0, parts)], far_held.at[at, pl.ds(0, parts)], piece_sem.at[1]).start()
    for at, piece in near:
        pltpu.make_async_copy(piece, near_held.at[at], piece_sem.at[2]).start()

    hot = one_hot_keys(x != 0, row_id_ref[:, :1], far_held.shape[0] * columns)
    wait_for(far_held.at[:, query_blocks], piece_sem.at[0])
    far_key = dot(hot, lanes(far_held, range(key, far_held.shape[1])), PLAIN).astype(BF16)
    near_key = near_key_ref[...]
    slot_row = jnp.where(x == 0, near_key, far_key)
    slot_col = jnp.where(x == 0, far_key, near_key)
    tokens = tokens_ref[:, pl.ds(pl.multiple_of((1 - x) * half, half), half)]
    queries = dot(tokens, lanes(far_held, range(parts, key)), LAST)
    for copy in copies:
        copy.wait()
    queries = (queries + queries_held[...]).astype(BF16)
    block = [queries[:, r * width:(r + 1) * width] for r in range(2 * rank)]
    row_scores = [dot(block[r], slot_row, LAST) for r in range(rank)]
    col_scores = [dot(block[rank + r], slot_col, LAST) for r in range(rank)]
    col_mixed = [sum(core_ref[r, s] * col_scores[s] for s in range(rank)) for r in range(rank)]
    row_mixed = [sum(row_scores[r] * core_ref[r, s] for r in range(rank)) for s in range(rank)]
    score = sum(row_scores[r] * col_mixed[r] for r in range(rank))
    gate = 1.0 / (1.0 + jnp.exp(-score))
    counts = counts_held[...]
    weights = (counts * gate.astype(BF16).astype(F32)).astype(BF16)
    slope = gate * (1.0 - gate)

    proj = proj_ref[:1]
    fetched = fetched_held[...]
    for i in range(proj_count):
        e = (x if i < half_count else 1 - x) * half_count + i % half_count
        mixed = dot(jnp.where(proj == e, weights, jnp.zeros((), BF16)), fetched, PLAIN)
        mixed_values[:, i * value_width:(i + 1) * value_width] = mixed.astype(BF16)
    wait_for(far_held.at[:, pl.ds(0, parts)], piece_sem.at[1])
    pick_grad = value_products(
        (1 - x) * half_count, half_count, far_held, 0, proj, cot_held[...], fetched, pick_held[...]
    )
    score_grad = pick_grad * slope
    for i, factor in enumerate(col_mixed + row_mixed):
        slot_key = slot_row if i < rank else slot_col
        grad = ((score_grad * factor).astype(BF16).astype(F32) * counts).astype(BF16)
        query_grad[:, i * width:(i + 1) * width] = dot(grad, slot_key, PLAIN).astype(BF16)
    wait_for(near_held, piece_sem.at[2])

    members = far_held.shape[0] // 4
    step = features // 4
    sides = ((near_held, x), (far_held, 1 - x))
    for c in range(4):
        cols = pl.ds(c * step, step)
        block = jnp.concatenate([
            jnp.concatenate([held[m, :parts].reshape(-1, LANES) for m in range(c * members, (c + 1) * members)], axis=1)
            for held, _ in sides
        ], axis=0)
        out_held[:, cols] = dot(mixed_values[...], block, PLAIN).astype(BF16)
        pltpu.make_async_copy(out_held.at[:, cols], out_ref.at[:, cols], out_sem.at[0]).start()
        held, side = sides[c // 2]
        blocks = step // LANES
        first = parts + (c % 2) * blocks
        cols = pl.ds(pl.multiple_of(side * half + (c % 2) * step, step), step)
        grad_held[:, cols] = dot(query_grad[...], lanes(held, range(first, first + blocks)), PLAIN).astype(BF16)
        pltpu.make_async_copy(grad_held.at[:, cols], grad_ref.at[:, cols], out_sem.at[1]).start()
    pltpu.make_async_copy(out_held, out_ref, out_sem.at[0]).wait()
    pltpu.make_async_copy(grad_held, grad_ref, out_sem.at[1]).wait()


def vmem():
    return pl.BlockSpec(memory_space=pltpu.VMEM)


def smem():
    return pl.BlockSpec(memory_space=pltpu.SMEM)


def anywhere():
    return pl.BlockSpec(memory_space=pl.ANY)


def pieces_path(tokens, cotangent, w_query, key_row, key_col, tucker_core, proj_part, requests, table, row_id,
                slot_proj, pick_slot, nkey, proj_count):
    rank = tucker_core.shape[0]
    width = key_row.shape[1]
    token_rows, features = tokens.shape
    slots = row_id.shape[0]
    value_width = table.shape[1]
    columns = w_query.shape[1]
    own_near, own_far = own_halves(w_query, key_row, key_col, proj_part)
    params = pltpu.CompilerParams(vmem_limit_bytes=VMEM_LIMIT)
    members = nkey // columns
    plane = jax.ShapeDtypeStruct((token_rows, slots), F32)
    partial = jax.ShapeDtypeStruct((token_rows, 2 * rank * width), F32)
    held = pltpu.VMEM((members,) + own_near.shape, BF16)

    def near_work(near, fetched):
        return pl.pallas_call(
            functools.partial(near_kernel, proj_count, table.shape[0], tuple(near)),
            out_shape=(
                plane, partial, jax.ShapeDtypeStruct((slots, width), BF16), plane,
                jax.ShapeDtypeStruct((slots, LANES), jnp.int32), jax.ShapeDtypeStruct((8, slots), jnp.int32),
            ),
            in_specs=[vmem()] * 5 + [anywhere()] * len(near),
            out_specs=(vmem(),) * 6,
            scratch_shapes=[held, pltpu.SemaphoreType.DMA],
            compiler_params=params,
            cost_estimate=pl.CostEstimate(flops=5 * 10**9, bytes_accessed=10**7, transcendentals=0),
            name="near",
        )(requests, pick_slot.T, tokens, cotangent, fetched.reshape(slots, value_width), *near.values())

    pieces, fetched, near_done = gather_pieces(own_near, own_far, requests, table, near_work)
    pick_grad, queries, near_key, counts, wide_id, slot_proj = near_done
    keys = tuple(pieces)
    tall = (token_rows, features)
    return pl.pallas_call(
        functools.partial(dense_kernel, rank, width, proj_count, keys),
        out_shape=(jax.ShapeDtypeStruct(tall, BF16),) * 2,
        in_specs=[smem()] + [vmem()] * 4 + [anywhere()] * (5 + len(keys)),
        out_specs=(anywhere(), anywhere()),
        scratch_shapes=[
            held,
            held,
            pltpu.VMEM(partial.shape, F32),
            pltpu.VMEM(plane.shape, F32),
            pltpu.VMEM(plane.shape, F32),
            pltpu.VMEM(tall, BF16),
            pltpu.VMEM((slots, value_width), BF16),
            pltpu.VMEM((token_rows, proj_count * value_width), BF16),
            pltpu.VMEM(partial.shape, BF16),
            pltpu.VMEM(tall, BF16),
            pltpu.VMEM(tall, BF16),
            pltpu.SemaphoreType.DMA((3,)),
            pltpu.SemaphoreType.DMA((5,)),
            pltpu.SemaphoreType.DMA((2,)),
        ],
        compiler_params=params,
        cost_estimate=pl.CostEstimate(flops=10**10, bytes_accessed=2 * 10**7, transcendentals=10**5),
        name="dense",
    )(
        tucker_core, wide_id, slot_proj, near_key, tokens, queries, pick_grad, counts,
        fetched.reshape(slots, value_width), cotangent, *pieces.values(),
    )


def whole_path(tokens, cotangent, w_query, key_row, key_col, tucker_core, proj_part, requests, table, row_id,
               slot_proj, pick_slot, nkey, proj_count):
    rank = tucker_core.shape[0]
    width = key_row.shape[1]
    slots = row_id.shape[0]
    fetched = returned_rows(found_rows(wanted_rows(requests), table)).reshape(slots, -1)
    query_full = lax.all_gather(w_query.T, "mem", axis=0, tiled=True)
    keys = lax.all_gather(jnp.concatenate([key_row, key_col], axis=1), "mem", axis=0, tiled=True)
    proj_full = lax.all_gather(proj_part, "mem", axis=1, tiled=True)
    key_at = jnp.arange(nkey, dtype=jnp.int32)[None, :]
    row_hot = ((row_id // nkey)[:, None] == key_at).astype(BF16)
    col_hot = ((row_id % nkey)[:, None] == key_at).astype(BF16)
    slot_row = dot(row_hot, keys[:, :width], PLAIN).astype(BF16)
    slot_col = dot(col_hot, keys[:, width:], PLAIN).astype(BF16)
    spread = jnp.where(
        slot_proj[:, None, None] == jnp.arange(proj_count, dtype=jnp.int32)[None, :, None],
        fetched[:, None, :], jnp.zeros((), BF16)
    ).reshape(slots, -1)
    counts = jnp.sum(
        (pick_slot[:, :, None] == jnp.arange(slots, dtype=jnp.int32)[None, None, :]).astype(F32), axis=1
    )
    queries = dot(tokens, query_full, LAST).astype(BF16)
    row_scores = [dot(queries[:, r * width:(r + 1) * width], slot_row, LAST) for r in range(rank)]
    col_scores = [
        dot(queries[:, (rank + r) * width:(rank + r + 1) * width], slot_col, LAST) for r in range(rank)
    ]
    col_mixed = [sum(tucker_core[r, s] * col_scores[s] for s in range(rank)) for r in range(rank)]
    row_mixed = [sum(row_scores[r] * tucker_core[r, s] for r in range(rank)) for s in range(rank)]
    score = sum(row_scores[r] * col_mixed[r] for r in range(rank))
    gate = jax.nn.sigmoid(score)
    weights = counts * gate.astype(BF16).astype(F32)
    mixed = counted_dot(weights, spread, PLAIN).astype(BF16)
    memory_out = dot(mixed, proj_full, PLAIN)
    value_grad = dot(cotangent, proj_full, LAST).astype(BF16)
    pick_grad = dot(value_grad, spread, LAST)
    score_grad = pick_grad * gate * (1.0 - gate)
    blocks = []
    for mixed_scores, slot_key in ((col_mixed, slot_row), (row_mixed, slot_col)):
        for r in range(rank):
            grad = (score_grad * mixed_scores[r]).astype(BF16).astype(F32) * counts
            blocks.append(counted_dot(grad, slot_key, PLAIN).astype(BF16))
    query_grad = jnp.concatenate(blocks, axis=1)
    token_grad = dot(query_grad, query_full, PLAIN)
    return memory_out.astype(BF16), token_grad.astype(BF16)


def shards(
    mem, tokens, cotangent, w_query, key_row, key_col, tucker_core, table, w_proj, send_ids, pick_slot
):
    proj_count, value_width, _ = w_proj.shape
    requests = send_ids[0]
    owners, capacity = requests.shape
    slots = owners * capacity
    nkey = key_row.shape[0] * mem
    row_id = jnp.maximum(requests, 0) + jnp.arange(owners, dtype=jnp.int32)[:, None] * table.shape[0]
    row_id = row_id.reshape(slots)
    slot_proj = (row_id % nkey) % proj_count
    proj_part = w_proj.reshape(proj_count * value_width, -1)
    path = pieces_path if mem == 16 and w_proj.shape[2] == LANES else whole_path
    return path(tokens, cotangent, w_query, key_row, key_col, tucker_core, proj_part, requests, table, row_id,
                slot_proj, pick_slot, nkey, proj_count)


def solution(mesh):
    in_specs = (
        P(("groups", "mem"), None),
        P(("groups", "mem"), None),
        P(None, "mem"),
        P("mem", None),
        P("mem", None),
        P(),
        P("mem", None),
        P(None, None, "mem"),
        P(("groups", "mem"), None, None),
        P(("groups", "mem"), None),
    )
    out_specs = (P(("groups", "mem"), None), P(("groups", "mem"), None))
    body = functools.partial(shards, mesh.shape["mem"])
    return jax.shard_map(body, mesh=mesh, in_specs=in_specs, out_specs=out_specs, check_vma=False)
```

```python
import functools

import jax
import jax.numpy as jnp
from jax import lax
from jax.experimental import pallas as pl
from jax.experimental.pallas import tpu as pltpu
from jax.sharding import PartitionSpec as P

F32 = jnp.float32
BF16 = jnp.bfloat16
RING = (0, 2, 3, 1)
LANES = 128
LAST = ((1,), (1,))
PLAIN = ((1,), (0,))
VMEM_LIMIT = 56 * 1024 * 1024


def dot(a, b, dims):
    return lax.dot_general(a, b, (dims, ((), ())), preferred_element_type=F32)


def two_terms(x):
    high = x.astype(BF16)
    return high, (x - high.astype(F32)).astype(BF16)


def counted_dot(x, b, dims):
    high, low = two_terms(x)
    return dot(high, b, dims) + dot(low, b, dims)


def wanted_rows(requests):
    return lax.all_to_all(requests, "mem", split_axis=0, concat_axis=0, tiled=True)


def found_rows(wanted, table):
    found = jnp.take(table, jnp.maximum(wanted, 0).reshape(-1), axis=0, mode="clip")
    return found.reshape(wanted.shape + (table.shape[1],))


def returned_rows(found):
    return lax.all_to_all(found, "mem", split_axis=0, concat_axis=0, tiled=True)


def place(z, y, core):
    return (z * 2 + y) * 2 + core


def everywhere(move):
    pairs = []
    for z in range(4):
        for y in range(2):
            for core in range(2):
                pairs.append((place(z, y, core), place(*move(z, y, core))))
    return pairs


def next_z(x):
    step = {RING[i]: RING[(i + 1) % 4] for i in range(4)}
    return lax.ppermute(x, "mem", everywhere(lambda z, y, c: (step[z], y, c)))


def other_y(x):
    return lax.ppermute(x, "mem", everywhere(lambda z, y, c: (z, 1 - y, c)))


def other_core(x):
    return lax.ppermute(x, "mem", everywhere(lambda z, y, c: (z, y, 1 - c)))


def other_x(x):
    return lax.ppermute(x, "groups", [(0, 1), (1, 0)])


def ring_source(z, steps):
    index = jnp.where(z == 0, 0, jnp.where(z == 2, 1, jnp.where(z == 3, 2, 3)))
    index = (index + 4 - steps) % 4
    return jnp.where(index == 0, 0, jnp.where(index == 1, 2, jnp.where(index == 2, 3, 1)))


def tie(*values):
    return lax.optimization_barrier(values)


def halves_kernel(query_ref, key_row_ref, key_col_ref, proj_ref, near_ref, far_ref):
    x = lax.axis_index("groups")
    parts = proj_ref.shape[1]
    blocks = query_ref.shape[1] // LANES // 2
    for target, half in ((near_ref, x), (far_ref, 1 - x)):
        target[:parts] = proj_ref[half]
        for j in range(blocks):
            target[parts + j] = query_ref[:, pl.ds(pl.multiple_of((half * blocks + j) * LANES, LANES), LANES)]
        for j in range(key_row_ref.shape[1] // LANES):
            cols = slice(j * LANES, (j + 1) * LANES)
            target[parts + blocks + j] = jnp.where(half == 0, key_row_ref[:, cols], key_col_ref[:, cols])


def own_halves(w_query, key_row, key_col, proj_part):
    features, columns = w_query.shape
    proj = proj_part.reshape(2, -1, columns, LANES)
    blocks = proj.shape[1] + (features // 2 + key_row.shape[1]) // LANES
    half = jax.ShapeDtypeStruct((blocks, columns, LANES), BF16)
    return pl.pallas_call(
        halves_kernel,
        out_shape=(half, half),
        in_specs=[vmem()] * 4,
        out_specs=(vmem(), vmem()),
        compiler_params=pltpu.CompilerParams(vmem_limit_bytes=VMEM_LIMIT),
        cost_estimate=pl.CostEstimate(flops=0, bytes_accessed=4 * 10**6, transcendentals=0),
        name="halves",
    )(w_query.T, key_row, key_col, proj)


def other_cores(first, second):
    first = other_core(first)
    second, first = tie(second, first)
    return first, other_core(second)


def gather_pieces(own_near, own_far, requests, table, near_work):
    pieces = {(0, 0, 0, 0): own_near, (0, 0, 0, 1): own_far}
    z1, y0, wanted, pieces[0, 0, 1, 0], pieces[0, 0, 1, 1] = tie(
        next_z(own_near), other_y(own_near), wanted_rows(requests), other_core(own_near), other_core(own_far)
    )
    pieces[1, 0, 0, 0], pieces[0, 1, 0, 0] = z1, y0
    z2, y1, y0f, found, pieces[1, 0, 1, 0], pieces[0, 1, 1, 0] = tie(
        next_z(z1), other_y(z1), other_x(y0), found_rows(wanted, table), *other_cores(z1, y0)
    )
    pieces[2, 0, 0, 0], pieces[1, 1, 0, 0], pieces[0, 1, 0, 1] = z2, y1, y0f
    z3, y2, y1f, pieces[2, 0, 1, 0], pieces[1, 1, 1, 0] = tie(
        next_z(z2), other_y(z2), other_x(y1), *other_cores(z2, y1)
    )
    pieces[3, 0, 0, 0], pieces[2, 1, 0, 0], pieces[1, 1, 0, 1] = z3, y2, y1f
    z1f, y3, z3f, fetched, pieces[3, 0, 1, 0], pieces[0, 1, 1, 1] = tie(
        next_z(own_far), other_y(z3), other_x(z3), returned_rows(found), *other_cores(z3, y0f)
    )
    pieces[1, 0, 0, 1], pieces[3, 1, 0, 0], pieces[3, 0, 0, 1] = z1f, y3, z3f
    y2_other, y1f_other = other_cores(y2, y1f)
    pieces[2, 1, 1, 0], pieces[3, 1, 1, 0] = y2_other, other_core(y3)
    near = {key: piece for key, piece in pieces.items() if key[3] == 0}
    z2f, y3f, y2f, near_done, pieces[1, 1, 1, 1] = tie(
        next_z(z1f), other_y(z3f), other_x(y2), near_work(near, fetched), y1f_other
    )
    pieces[2, 0, 0, 1], pieces[3, 1, 0, 1], pieces[2, 1, 0, 1] = z2f, y3f, y2f
    for steps, side, far in ((1, 0, 1), (3, 0, 1), (2, 0, 1), (3, 1, 1), (2, 1, 1)):
        pieces[steps, side, 1, far] = other_core(pieces[steps, side, 0, far])
    return pieces, fetched, near_done


def placed(keys, pieces):
    me = lax.axis_index("mem")
    z, y, core = me // 4, (me // 2) % 2, me % 2
    for (steps, side, other, far), piece in zip(keys, pieces):
        at = place(ring_source(z, steps), 1 - y if side else y, 1 - core if other else core)
        yield at, piece


def wait_for(held, sem):
    pltpu.make_async_copy(held, held, sem).wait()


def lanes(held, blocks):
    return jnp.concatenate([held[:, j].reshape(-1, LANES) for j in blocks], axis=1)


def value_products(first, count, held, base, proj, cot, fetched, pick_grad):
    value_width = fetched.shape[1]
    parts = value_width // held.shape[-2]
    for e in range(count):
        block = jnp.concatenate(
            [held[m, base + e * parts:base + (e + 1) * parts].reshape(value_width, LANES) for m in range(held.shape[0])],
            axis=1,
        )
        grad = dot(cot, block, LAST).astype(BF16)
        pick_grad = jnp.where(proj == first + e, dot(grad, fetched, LAST), pick_grad)
    return pick_grad


def one_hot_keys(use_row, row_id, nkey):
    key_at = lax.broadcasted_iota(jnp.int32, (row_id.shape[0], nkey), 1)
    picked = jnp.where(use_row, row_id // nkey, row_id % nkey)
    return jnp.where(picked == key_at, 1.0, 0.0).astype(BF16)


def slot_ids(requests, rows_each):
    owners, capacity = requests.shape
    slots = owners * capacity
    rows = jnp.broadcast_to(requests[:, None, :], (owners, capacity, capacity)).reshape(slots, capacity)
    slot = lax.broadcasted_iota(jnp.int32, (slots, capacity), 0)
    lane = lax.broadcasted_iota(jnp.int32, (slots, capacity), 1)
    local = jnp.sum(jnp.where(slot % capacity == lane, jnp.maximum(rows, 0), 0), axis=1, keepdims=True)
    return local + slot[:, :1] // capacity * rows_each


def near_kernel(
    proj_count, rows_each, keys, requests_ref, pick_ref, tokens_ref, cot_ref, fetched_ref, *refs
):
    pick_grad_ref, queries_ref, slot_key_ref, counts_ref, wide_id_ref, proj_ref, held, sem = refs[-8:]
    for at, piece in placed(keys, refs[:-8]):
        pltpu.make_async_copy(piece, held.at[at], sem).start()
    x = lax.axis_index("groups")
    features = tokens_ref.shape[1]
    half = features // 2
    half_count = proj_count // 2
    parts = half_count * fetched_ref.shape[1] // held.shape[2]
    key = parts + half // LANES
    nkey = held.shape[0] * held.shape[2]
    wide_id = jnp.broadcast_to(slot_ids(requests_ref[...], rows_each), wide_id_ref.shape)
    wide_id_ref[...] = wide_id
    proj = (wide_id % nkey % proj_count).T[:proj_ref.shape[0]]
    proj_ref[...] = proj
    token_rows, slots = counts_ref.shape
    lane = lax.broadcasted_iota(jnp.int32, (token_rows, slots), 1)
    pick = pick_ref[...].T
    counts = jnp.zeros((token_rows, slots), F32)
    for k in range(pick.shape[1]):
        counts += jnp.where(pick[:, k:k + 1] == lane, 1.0, 0.0)
    counts_ref[...] = counts
    hot = one_hot_keys(x == 0, wide_id[:, :1], nkey)
    wait_for(held, sem)
    slot_key_ref[...] = dot(hot, lanes(held, range(key, held.shape[1])), PLAIN).astype(BF16)
    tokens = tokens_ref[:, pl.ds(pl.multiple_of(x * half, half), half)]
    queries_ref[...] = dot(tokens, lanes(held, range(parts, key)), LAST)
    pick_grad_ref[...] = value_products(
        x * half_count, half_count, held, 0, proj[:1], cot_ref[...], fetched_ref[...],
        jnp.zeros(pick_grad_ref.shape, F32),
    )


def dense_kernel(
    rank, width, proj_count, keys, core_ref, *refs
):
    inputs, refs = refs[:9], refs[9:]
    pieces = refs[:len(keys)]
    (out_ref, grad_ref, near_held, far_held, queries_held, pick_held, counts_held, cot_held, fetched_held,
     row_id_held, proj_held, near_key_held, tokens_held, mixed_values, query_grad, out_held, grad_held, piece_sem, in_sem, out_sem) = refs[len(keys):]
    held_inputs = (
        row_id_held, tokens_held, near_key_held, proj_held, queries_held, counts_held, cot_held, fetched_held, pick_held
    )
    x = lax.axis_index("groups")
    token_rows, features = tokens_held.shape
    slots, value_width = fetched_held.shape
    columns = far_held.shape[2]
    half = features // 2
    half_count = proj_count // 2
    parts = half_count * value_width // columns
    key = parts + half // LANES
    spots = list(placed(keys, pieces))
    far = [spot for spot, k in zip(spots, keys) if k[3]]
    near = [spot for spot, k in zip(spots, keys) if not k[3]]
    query_blocks = pl.ds(parts, far_held.shape[1] - parts)
    copies = [pltpu.make_async_copy(a, b, in_sem.at[i]) for i, (a, b) in enumerate(zip(inputs, held_inputs))]
    copies[0].start()
    for at, piece in far:
        pltpu.make_async_copy(piece.at[query_blocks], far_held.at[at, query_blocks], piece_sem.at[0]).start()
    for copy in copies[1:6]:
        copy.start()
    for at, piece in far:
        pltpu.make_async_copy(piece.at[pl.ds(0, parts)], far_held.at[at, pl.ds(0, parts)], piece_sem.at[1]).start()
    for copy in copies[6:]:
        copy.start()
    for at, piece in near:
        pltpu.make_async_copy(piece, near_held.at[at], piece_sem.at[2]).start()

    copies[0].wait()
    hot = one_hot_keys(x != 0, row_id_held[:, :1], far_held.shape[0] * columns)
    wait_for(far_held.at[:, query_blocks], piece_sem.at[0])
    for copy in copies[1:6]:
        copy.wait()
    far_key = dot(hot, lanes(far_held, range(key, far_held.shape[1])), PLAIN).astype(BF16)
    near_key = near_key_held[...]
    slot_row = jnp.where(x == 0, near_key, far_key)
    slot_col = jnp.where(x == 0, far_key, near_key)
    tokens = tokens_held[:, pl.ds(pl.multiple_of((1 - x) * half, half), half)]
    queries = (dot(tokens, lanes(far_held, range(parts, key)), LAST) + queries_held[...]).astype(BF16)
    block = [queries[:, r * width:(r + 1) * width] for r in range(2 * rank)]
    row_scores = [dot(block[r], slot_row, LAST) for r in range(rank)]
    col_scores = [dot(block[rank + r], slot_col, LAST) for r in range(rank)]
    wait_for(far_held.at[:, pl.ds(0, parts)], piece_sem.at[1])
    for copy in copies[6:]:
        copy.wait()
    wait_for(near_held, piece_sem.at[2])
    proj = proj_held[:1]
    fetched = fetched_held[...]
    pick_grad = value_products(
        (1 - x) * half_count, half_count, far_held, 0, proj, cot_held[...], fetched, pick_held[...]
    )
    col_mixed = [sum(core_ref[r, s] * col_scores[s] for s in range(rank)) for r in range(rank)]
    row_mixed = [sum(row_scores[r] * core_ref[r, s] for r in range(rank)) for s in range(rank)]
    score = sum(row_scores[r] * col_mixed[r] for r in range(rank))
    gate = 1.0 / (1.0 + jnp.exp(-score))
    counts = counts_held[...]
    weights = (counts * gate.astype(BF16).astype(F32)).astype(BF16)
    slope = gate * (1.0 - gate)
    for i in range(proj_count):
        e = (x if i < half_count else 1 - x) * half_count + i % half_count
        mixed = dot(jnp.where(proj == e, weights, jnp.zeros((), BF16)), fetched, PLAIN)
        mixed_values[:, i * value_width:(i + 1) * value_width] = mixed.astype(BF16)

    members = far_held.shape[0] // 4
    step = features // 4
    sides = ((near_held, x), (far_held, 1 - x))
    for c in range(4):
        cols = pl.ds(c * step, step)
        block = jnp.concatenate([
            jnp.concatenate([held[m, :parts].reshape(-1, LANES) for m in range(c * members, (c + 1) * members)], axis=1)
            for held, _ in sides
        ], axis=0)
        out_held[:, cols] = dot(mixed_values[...], block, PLAIN).astype(BF16)
        pltpu.make_async_copy(out_held.at[:, cols], out_ref.at[:, cols], out_sem.at[0]).start()
    score_grad = pick_grad * slope
    for i, factor in enumerate(col_mixed + row_mixed):
        slot_key = slot_row if i < rank else slot_col
        grad = ((score_grad * factor).astype(BF16).astype(F32) * counts).astype(BF16)
        query_grad[:, i * width:(i + 1) * width] = dot(grad, slot_key, PLAIN).astype(BF16)
    for c in range(4):
        held, side = sides[c // 2]
        blocks = step // LANES
        first = parts + (c % 2) * blocks
        cols = pl.ds(pl.multiple_of(side * half + (c % 2) * step, step), step)
        grad_held[:, cols] = dot(query_grad[...], lanes(held, range(first, first + blocks)), PLAIN).astype(BF16)
        pltpu.make_async_copy(grad_held.at[:, cols], grad_ref.at[:, cols], out_sem.at[1]).start()
    pltpu.make_async_copy(out_held, out_ref, out_sem.at[0]).wait()
    pltpu.make_async_copy(grad_held, grad_ref, out_sem.at[1]).wait()


def vmem():
    return pl.BlockSpec(memory_space=pltpu.VMEM)


def smem():
    return pl.BlockSpec(memory_space=pltpu.SMEM)


def anywhere():
    return pl.BlockSpec(memory_space=pl.ANY)


def pieces_path(tokens, cotangent, w_query, key_row, key_col, tucker_core, proj_part, requests, table, row_id,
                slot_proj, pick_slot, nkey, proj_count):
    rank = tucker_core.shape[0]
    width = key_row.shape[1]
    token_rows, features = tokens.shape
    slots = row_id.shape[0]
    value_width = table.shape[1]
    columns = w_query.shape[1]
    own_near, own_far = own_halves(w_query, key_row, key_col, proj_part)
    params = pltpu.CompilerParams(vmem_limit_bytes=VMEM_LIMIT)
    members = nkey // columns
    plane = jax.ShapeDtypeStruct((token_rows, slots), F32)
    partial = jax.ShapeDtypeStruct((token_rows, 2 * rank * width), F32)
    held = pltpu.VMEM((members,) + own_near.shape, BF16)

    def near_work(near, fetched):
        return pl.pallas_call(
            functools.partial(near_kernel, proj_count, table.shape[0], tuple(near)),
            out_shape=(
                plane, partial, jax.ShapeDtypeStruct((slots, width), BF16), plane,
                jax.ShapeDtypeStruct((slots, LANES), jnp.int32), jax.ShapeDtypeStruct((8, slots), jnp.int32),
            ),
            in_specs=[vmem()] * 5 + [anywhere()] * len(near),
            out_specs=(vmem(),) * 6,
            scratch_shapes=[held, pltpu.SemaphoreType.DMA],
            compiler_params=params,
            cost_estimate=pl.CostEstimate(flops=5 * 10**9, bytes_accessed=10**7, transcendentals=0),
            name="near",
        )(requests, pick_slot.T, tokens, cotangent, fetched.reshape(slots, value_width), *near.values())

    pieces, fetched, near_done = gather_pieces(own_near, own_far, requests, table, near_work)
    pick_grad, queries, near_key, counts, wide_id, slot_proj = near_done
    keys = tuple(pieces)
    tall = (token_rows, features)
    return pl.pallas_call(
        functools.partial(dense_kernel, rank, width, proj_count, keys),
        out_shape=(jax.ShapeDtypeStruct(tall, BF16),) * 2,
        in_specs=[smem()] + [anywhere()] * (9 + len(keys)),
        out_specs=(anywhere(), anywhere()),
        scratch_shapes=[
            held,
            held,
            pltpu.VMEM(partial.shape, F32),
            pltpu.VMEM(plane.shape, F32),
            pltpu.VMEM(plane.shape, F32),
            pltpu.VMEM(tall, BF16),
            pltpu.VMEM((slots, value_width), BF16),
            pltpu.VMEM(wide_id.shape, jnp.int32),
            pltpu.VMEM(slot_proj.shape, jnp.int32),
            pltpu.VMEM(near_key.shape, BF16),
            pltpu.VMEM(tall, BF16),
            pltpu.VMEM((token_rows, proj_count * value_width), BF16),
            pltpu.VMEM(partial.shape, BF16),
            pltpu.VMEM(tall, BF16),
            pltpu.VMEM(tall, BF16),
            pltpu.SemaphoreType.DMA((3,)),
            pltpu.SemaphoreType.DMA((9,)),
            pltpu.SemaphoreType.DMA((2,)),
        ],
        compiler_params=params,
        cost_estimate=pl.CostEstimate(flops=10**10, bytes_accessed=2 * 10**7, transcendentals=10**5),
        name="dense",
    )(
        tucker_core, wide_id, tokens, near_key, slot_proj, queries, counts, cotangent,
        fetched.reshape(slots, value_width), pick_grad, *pieces.values(),
    )


def whole_path(tokens, cotangent, w_query, key_row, key_col, tucker_core, proj_part, requests, table, row_id,
               slot_proj, pick_slot, nkey, proj_count):
    rank = tucker_core.shape[0]
    width = key_row.shape[1]
    slots = row_id.shape[0]
    fetched = returned_rows(found_rows(wanted_rows(requests), table)).reshape(slots, -1)
    query_full = lax.all_gather(w_query.T, "mem", axis=0, tiled=True)
    keys = lax.all_gather(jnp.concatenate([key_row, key_col], axis=1), "mem", axis=0, tiled=True)
    proj_full = lax.all_gather(proj_part, "mem", axis=1, tiled=True)
    key_at = jnp.arange(nkey, dtype=jnp.int32)[None, :]
    row_hot = ((row_id // nkey)[:, None] == key_at).astype(BF16)
    col_hot = ((row_id % nkey)[:, None] == key_at).astype(BF16)
    slot_row = dot(row_hot, keys[:, :width], PLAIN).astype(BF16)
    slot_col = dot(col_hot, keys[:, width:], PLAIN).astype(BF16)
    spread = jnp.where(
        slot_proj[:, None, None] == jnp.arange(proj_count, dtype=jnp.int32)[None, :, None],
        fetched[:, None, :], jnp.zeros((), BF16)
    ).reshape(slots, -1)
    counts = jnp.sum(
        (pick_slot[:, :, None] == jnp.arange(slots, dtype=jnp.int32)[None, None, :]).astype(F32), axis=1
    )
    queries = dot(tokens, query_full, LAST).astype(BF16)
    row_scores = [dot(queries[:, r * width:(r + 1) * width], slot_row, LAST) for r in range(rank)]
    col_scores = [
        dot(queries[:, (rank + r) * width:(rank + r + 1) * width], slot_col, LAST) for r in range(rank)
    ]
    col_mixed = [sum(tucker_core[r, s] * col_scores[s] for s in range(rank)) for r in range(rank)]
    row_mixed = [sum(row_scores[r] * tucker_core[r, s] for r in range(rank)) for s in range(rank)]
    score = sum(row_scores[r] * col_mixed[r] for r in range(rank))
    gate = jax.nn.sigmoid(score)
    weights = counts * gate.astype(BF16).astype(F32)
    mixed = counted_dot(weights, spread, PLAIN).astype(BF16)
    memory_out = dot(mixed, proj_full, PLAIN)
    value_grad = dot(cotangent, proj_full, LAST).astype(BF16)
    pick_grad = dot(value_grad, spread, LAST)
    score_grad = pick_grad * gate * (1.0 - gate)
    blocks = []
    for mixed_scores, slot_key in ((col_mixed, slot_row), (row_mixed, slot_col)):
        for r in range(rank):
            grad = (score_grad * mixed_scores[r]).astype(BF16).astype(F32) * counts
            blocks.append(counted_dot(grad, slot_key, PLAIN).astype(BF16))
    query_grad = jnp.concatenate(blocks, axis=1)
    token_grad = dot(query_grad, query_full, PLAIN)
    return memory_out.astype(BF16), token_grad.astype(BF16)


def shards(
    mem, tokens, cotangent, w_query, key_row, key_col, tucker_core, table, w_proj, send_ids, pick_slot
):
    proj_count, value_width, _ = w_proj.shape
    requests = send_ids[0]
    owners, capacity = requests.shape
    slots = owners * capacity
    nkey = key_row.shape[0] * mem
    row_id = jnp.maximum(requests, 0) + jnp.arange(owners, dtype=jnp.int32)[:, None] * table.shape[0]
    row_id = row_id.reshape(slots)
    slot_proj = (row_id % nkey) % proj_count
    proj_part = w_proj.reshape(proj_count * value_width, -1)
    path = pieces_path if mem == 16 and w_proj.shape[2] == LANES else whole_path
    return path(tokens, cotangent, w_query, key_row, key_col, tucker_core, proj_part, requests, table, row_id,
                slot_proj, pick_slot, nkey, proj_count)


def solution(mesh):
    in_specs = (
        P(("groups", "mem"), None),
        P(("groups", "mem"), None),
        P(None, "mem"),
        P("mem", None),
        P("mem", None),
        P(),
        P("mem", None),
        P(None, None, "mem"),
        P(("groups", "mem"), None, None),
        P(("groups", "mem"), None),
    )
    out_specs = (P(("groups", "mem"), None), P(("groups", "mem"), None))
    body = functools.partial(shards, mesh.shape["mem"])
    return jax.shard_map(body, mesh=mesh, in_specs=in_specs, out_specs=out_specs, check_vma=False)
```

```python
import functools

import jax
import jax.numpy as jnp
from jax import lax
from jax.experimental import pallas as pl
from jax.experimental.pallas import tpu as pltpu
from jax.sharding import PartitionSpec as P

F32 = jnp.float32
BF16 = jnp.bfloat16
RING = (0, 2, 3, 1)
LANES = 128
LAST = ((1,), (1,))
PLAIN = ((1,), (0,))
VMEM_LIMIT = 56 * 1024 * 1024


def dot(a, b, dims):
    return lax.dot_general(a, b, (dims, ((), ())), preferred_element_type=F32)


def two_terms(x):
    high = x.astype(BF16)
    return high, (x - high.astype(F32)).astype(BF16)


def counted_dot(x, b, dims):
    high, low = two_terms(x)
    return dot(high, b, dims) + dot(low, b, dims)


def wanted_rows(requests):
    return lax.all_to_all(requests, "mem", split_axis=0, concat_axis=0, tiled=True)


def found_rows(wanted, table):
    found = jnp.take(table, jnp.maximum(wanted, 0).reshape(-1), axis=0, mode="clip")
    return found.reshape(wanted.shape + (table.shape[1],))


def returned_rows(found):
    return lax.all_to_all(found, "mem", split_axis=0, concat_axis=0, tiled=True)


def place(z, y, core):
    return (z * 2 + y) * 2 + core


def everywhere(move):
    pairs = []
    for z in range(4):
        for y in range(2):
            for core in range(2):
                pairs.append((place(z, y, core), place(*move(z, y, core))))
    return pairs


def next_z(x):
    step = {RING[i]: RING[(i + 1) % 4] for i in range(4)}
    return lax.ppermute(x, "mem", everywhere(lambda z, y, c: (step[z], y, c)))


def other_y(x):
    return lax.ppermute(x, "mem", everywhere(lambda z, y, c: (z, 1 - y, c)))


def other_core(x):
    return lax.ppermute(x, "mem", everywhere(lambda z, y, c: (z, y, 1 - c)))


def other_x(x):
    return lax.ppermute(x, "groups", [(0, 1), (1, 0)])


def ring_source(z, steps):
    index = jnp.where(z == 0, 0, jnp.where(z == 2, 1, jnp.where(z == 3, 2, 3)))
    index = (index + 4 - steps) % 4
    return jnp.where(index == 0, 0, jnp.where(index == 1, 2, jnp.where(index == 2, 3, 1)))


def tie(*values):
    return lax.optimization_barrier(values)


def halves_kernel(query_ref, key_row_ref, key_col_ref, proj_ref, near_ref, far_ref):
    x = lax.axis_index("groups")
    parts = proj_ref.shape[1]
    blocks = query_ref.shape[1] // LANES // 2
    for target, half in ((near_ref, x), (far_ref, 1 - x)):
        target[:parts] = proj_ref[half]
        for j in range(blocks):
            target[parts + j] = query_ref[:, pl.ds(pl.multiple_of((half * blocks + j) * LANES, LANES), LANES)]
        for j in range(key_row_ref.shape[1] // LANES):
            cols = slice(j * LANES, (j + 1) * LANES)
            target[parts + blocks + j] = jnp.where(half == 0, key_row_ref[:, cols], key_col_ref[:, cols])


def own_halves(w_query, key_row, key_col, proj_part):
    features, columns = w_query.shape
    proj = proj_part.reshape(2, -1, columns, LANES)
    blocks = proj.shape[1] + (features // 2 + key_row.shape[1]) // LANES
    half = jax.ShapeDtypeStruct((blocks, columns, LANES), BF16)
    return pl.pallas_call(
        halves_kernel,
        out_shape=(half, half),
        in_specs=[vmem()] * 4,
        out_specs=(vmem(), vmem()),
        compiler_params=pltpu.CompilerParams(vmem_limit_bytes=VMEM_LIMIT),
        cost_estimate=pl.CostEstimate(flops=0, bytes_accessed=4 * 10**6, transcendentals=0),
        name="halves",
    )(w_query.T, key_row, key_col, proj)


def other_cores(first, second, *awaited):
    first = other_core(first)
    second, first, *awaited = tie(second, first, *awaited)
    return first, other_core(second), *awaited


def gather_pieces(own_near, own_far, requests, table, near_work):
    pieces = {(0, 0, 0, 0): own_near, (0, 0, 0, 1): own_far}
    z1, y0, wanted, pieces[0, 0, 1, 0], pieces[0, 0, 1, 1] = tie(
        next_z(own_near), other_y(own_near), wanted_rows(requests), other_core(own_near), other_core(own_far)
    )
    pieces[1, 0, 0, 0], pieces[0, 1, 0, 0] = z1, y0
    y0f, z1f = other_x(y0), other_x(z1)
    z2, y1, found, pieces[1, 0, 1, 0], pieces[0, 1, 1, 0] = tie(
        next_z(z1), other_y(z1), found_rows(wanted, table), *other_cores(z1, y0)
    )
    pieces[2, 0, 0, 0], pieces[1, 1, 0, 0] = z2, y1
    z3, y2, y1f, pieces[2, 0, 1, 0], pieces[1, 1, 1, 0], y0f, z1f = tie(
        next_z(z2), other_y(z2), other_x(y1), *other_cores(z2, y1, y0f, z1f)
    )
    pieces[3, 0, 0, 0], pieces[2, 1, 0, 0], pieces[1, 1, 0, 1] = z3, y2, y1f
    pieces[0, 1, 0, 1], pieces[1, 0, 0, 1] = y0f, z1f
    y3, z3f, fetched, pieces[3, 0, 1, 0], pieces[0, 1, 1, 1] = tie(
        other_y(z3), other_x(z3), returned_rows(found), *other_cores(z3, y0f)
    )
    pieces[3, 1, 0, 0], pieces[3, 0, 0, 1] = y3, z3f
    y2_other, y1f_other = other_cores(y2, y1f)
    pieces[2, 1, 1, 0], pieces[3, 1, 1, 0] = y2_other, other_core(y3)
    near = {key: piece for key, piece in pieces.items() if key[3] == 0}
    z2f, y3f, y2f, near_done, pieces[1, 1, 1, 1] = tie(
        next_z(z1f), other_y(z3f), other_x(y2), near_work(near, fetched), y1f_other
    )
    pieces[2, 0, 0, 1], pieces[3, 1, 0, 1], pieces[2, 1, 0, 1] = z2f, y3f, y2f
    for steps, side, far in ((1, 0, 1), (3, 0, 1), (2, 0, 1), (3, 1, 1), (2, 1, 1)):
        pieces[steps, side, 1, far] = other_core(pieces[steps, side, 0, far])
    return pieces, fetched, near_done


def placed(keys, pieces):
    me = lax.axis_index("mem")
    z, y, core = me // 4, (me // 2) % 2, me % 2
    for (steps, side, other, far), piece in zip(keys, pieces):
        at = place(ring_source(z, steps), 1 - y if side else y, 1 - core if other else core)
        yield at, piece


def wait_for(held, sem):
    pltpu.make_async_copy(held, held, sem).wait()


def lanes(held, blocks):
    return jnp.concatenate([held[:, j].reshape(-1, LANES) for j in blocks], axis=1)


def value_products(first, count, held, base, proj, cot, fetched, pick_grad):
    value_width = fetched.shape[1]
    parts = value_width // held.shape[-2]
    for e in range(count):
        block = jnp.concatenate(
            [held[m, base + e * parts:base + (e + 1) * parts].reshape(value_width, LANES) for m in range(held.shape[0])],
            axis=1,
        )
        grad = dot(cot, block, LAST).astype(BF16)
        pick_grad = jnp.where(proj == first + e, dot(grad, fetched, LAST), pick_grad)
    return pick_grad


def one_hot_keys(use_row, row_id, nkey):
    key_at = lax.broadcasted_iota(jnp.int32, (row_id.shape[0], nkey), 1)
    picked = jnp.where(use_row, row_id // nkey, row_id % nkey)
    return jnp.where(picked == key_at, 1.0, 0.0).astype(BF16)


def slot_ids(requests, rows_each):
    owners, capacity = requests.shape
    slots = owners * capacity
    rows = jnp.broadcast_to(requests[:, None, :], (owners, capacity, capacity)).reshape(slots, capacity)
    slot = lax.broadcasted_iota(jnp.int32, (slots, capacity), 0)
    lane = lax.broadcasted_iota(jnp.int32, (slots, capacity), 1)
    local = jnp.sum(jnp.where(slot % capacity == lane, jnp.maximum(rows, 0), 0), axis=1, keepdims=True)
    return local + slot[:, :1] // capacity * rows_each


def near_kernel(
    proj_count, rows_each, keys, requests_ref, pick_ref, tokens_ref, cot_ref, fetched_ref, *refs
):
    pick_grad_ref, queries_ref, slot_key_ref, counts_ref, wide_id_ref, proj_ref, held, sem = refs[-8:]
    for at, piece in placed(keys, refs[:-8]):
        pltpu.make_async_copy(piece, held.at[at], sem).start()
    x = lax.axis_index("groups")
    features = tokens_ref.shape[1]
    half = features // 2
    half_count = proj_count // 2
    parts = half_count * fetched_ref.shape[1] // held.shape[2]
    key = parts + half // LANES
    nkey = held.shape[0] * held.shape[2]
    wide_id = jnp.broadcast_to(slot_ids(requests_ref[...], rows_each), wide_id_ref.shape)
    wide_id_ref[...] = wide_id
    proj = (wide_id % nkey % proj_count).T[:proj_ref.shape[0]]
    proj_ref[...] = proj
    token_rows, slots = counts_ref.shape
    lane = lax.broadcasted_iota(jnp.int32, (token_rows, slots), 1)
    pick = pick_ref[...].T
    counts = jnp.zeros((token_rows, slots), F32)
    for k in range(pick.shape[1]):
        counts += jnp.where(pick[:, k:k + 1] == lane, 1.0, 0.0)
    counts_ref[...] = counts
    hot = one_hot_keys(x == 0, wide_id[:, :1], nkey)
    wait_for(held, sem)
    slot_key_ref[...] = dot(hot, lanes(held, range(key, held.shape[1])), PLAIN).astype(BF16)
    tokens = tokens_ref[:, pl.ds(pl.multiple_of(x * half, half), half)]
    queries_ref[...] = dot(tokens, lanes(held, range(parts, key)), LAST)
    pick_grad_ref[...] = value_products(
        x * half_count, half_count, held, 0, proj[:1], cot_ref[...], fetched_ref[...],
        jnp.zeros(pick_grad_ref.shape, F32),
    )


def dense_kernel(
    rank, width, proj_count, keys, core_ref, *refs
):
    inputs, refs = refs[:9], refs[9:]
    pieces = refs[:len(keys)]
    (out_ref, grad_ref, near_held, far_held, queries_held, pick_held, counts_held, cot_held, fetched_held,
     row_id_held, proj_held, near_key_held, tokens_held, mixed_values, query_grad, out_held, grad_held, piece_sem, in_sem, out_sem) = refs[len(keys):]
    held_inputs = (
        row_id_held, tokens_held, near_key_held, proj_held, queries_held, counts_held, cot_held, fetched_held, pick_held
    )
    x = lax.axis_index("groups")
    token_rows, features = tokens_held.shape
    slots, value_width = fetched_held.shape
    columns = far_held.shape[2]
    half = features // 2
    half_count = proj_count // 2
    parts = half_count * value_width // columns
    key = parts + half // LANES
    spots = list(placed(keys, pieces))
    far = [spot for spot, k in zip(spots, keys) if k[3]]
    near = [spot for spot, k in zip(spots, keys) if not k[3]]
    query_blocks = pl.ds(parts, far_held.shape[1] - parts)
    copies = [pltpu.make_async_copy(a, b, in_sem.at[i]) for i, (a, b) in enumerate(zip(inputs, held_inputs))]
    copies[0].start()
    for at, piece in far:
        pltpu.make_async_copy(piece.at[query_blocks], far_held.at[at, query_blocks], piece_sem.at[0]).start()
    for copy in copies[1:6]:
        copy.start()
    for at, piece in far:
        pltpu.make_async_copy(piece.at[pl.ds(0, parts)], far_held.at[at, pl.ds(0, parts)], piece_sem.at[1]).start()
    for copy in copies[6:]:
        copy.start()
    for at, piece in near:
        pltpu.make_async_copy(piece, near_held.at[at], piece_sem.at[2]).start()

    copies[0].wait()
    hot = one_hot_keys(x != 0, row_id_held[:, :1], far_held.shape[0] * columns)
    wait_for(far_held.at[:, query_blocks], piece_sem.at[0])
    for copy in copies[1:6]:
        copy.wait()
    far_key = dot(hot, lanes(far_held, range(key, far_held.shape[1])), PLAIN).astype(BF16)
    near_key = near_key_held[...]
    slot_row = jnp.where(x == 0, near_key, far_key)
    slot_col = jnp.where(x == 0, far_key, near_key)
    tokens = tokens_held[:, pl.ds(pl.multiple_of((1 - x) * half, half), half)]
    queries = (dot(tokens, lanes(far_held, range(parts, key)), LAST) + queries_held[...]).astype(BF16)
    block = [queries[:, r * width:(r + 1) * width] for r in range(2 * rank)]
    row_scores = [dot(block[r], slot_row, LAST) for r in range(rank)]
    col_scores = [dot(block[rank + r], slot_col, LAST) for r in range(rank)]
    wait_for(far_held.at[:, pl.ds(0, parts)], piece_sem.at[1])
    for copy in copies[6:]:
        copy.wait()
    wait_for(near_held, piece_sem.at[2])
    proj = proj_held[:1]
    fetched = fetched_held[...]
    pick_grad = value_products(
        (1 - x) * half_count, half_count, far_held, 0, proj, cot_held[...], fetched, pick_held[...]
    )
    col_mixed = [sum(core_ref[r, s] * col_scores[s] for s in range(rank)) for r in range(rank)]
    row_mixed = [sum(row_scores[r] * core_ref[r, s] for r in range(rank)) for s in range(rank)]
    score = sum(row_scores[r] * col_mixed[r] for r in range(rank))
    gate = 1.0 / (1.0 + jnp.exp(-score))
    counts = counts_held[...]
    weights = (counts * gate.astype(BF16).astype(F32)).astype(BF16)
    slope = gate * (1.0 - gate)
    for i in range(proj_count):
        e = (x if i < half_count else 1 - x) * half_count + i % half_count
        mixed = dot(jnp.where(proj == e, weights, jnp.zeros((), BF16)), fetched, PLAIN)
        mixed_values[:, i * value_width:(i + 1) * value_width] = mixed.astype(BF16)

    members = far_held.shape[0] // 4
    step = features // 4
    sides = ((near_held, x), (far_held, 1 - x))
    for c in range(4):
        cols = pl.ds(c * step, step)
        block = jnp.concatenate([
            jnp.concatenate([held[m, :parts].reshape(-1, LANES) for m in range(c * members, (c + 1) * members)], axis=1)
            for held, _ in sides
        ], axis=0)
        out_held[:, cols] = dot(mixed_values[...], block, PLAIN).astype(BF16)
        pltpu.make_async_copy(out_held.at[:, cols], out_ref.at[:, cols], out_sem.at[0]).start()
    score_grad = pick_grad * slope
    for i, factor in enumerate(col_mixed + row_mixed):
        slot_key = slot_row if i < rank else slot_col
        grad = ((score_grad * factor).astype(BF16).astype(F32) * counts).astype(BF16)
        query_grad[:, i * width:(i + 1) * width] = dot(grad, slot_key, PLAIN).astype(BF16)
    for c in range(4):
        held, side = sides[c // 2]
        blocks = step // LANES
        first = parts + (c % 2) * blocks
        cols = pl.ds(pl.multiple_of(side * half + (c % 2) * step, step), step)
        grad_held[:, cols] = dot(query_grad[...], lanes(held, range(first, first + blocks)), PLAIN).astype(BF16)
        pltpu.make_async_copy(grad_held.at[:, cols], grad_ref.at[:, cols], out_sem.at[1]).start()
    pltpu.make_async_copy(out_held, out_ref, out_sem.at[0]).wait()
    pltpu.make_async_copy(grad_held, grad_ref, out_sem.at[1]).wait()


def vmem():
    return pl.BlockSpec(memory_space=pltpu.VMEM)


def smem():
    return pl.BlockSpec(memory_space=pltpu.SMEM)


def anywhere():
    return pl.BlockSpec(memory_space=pl.ANY)


def pieces_path(tokens, cotangent, w_query, key_row, key_col, tucker_core, proj_part, requests, table, row_id,
                slot_proj, pick_slot, nkey, proj_count):
    rank = tucker_core.shape[0]
    width = key_row.shape[1]
    token_rows, features = tokens.shape
    slots = row_id.shape[0]
    value_width = table.shape[1]
    columns = w_query.shape[1]
    own_near, own_far = own_halves(w_query, key_row, key_col, proj_part)
    params = pltpu.CompilerParams(vmem_limit_bytes=VMEM_LIMIT)
    members = nkey // columns
    plane = jax.ShapeDtypeStruct((token_rows, slots), F32)
    partial = jax.ShapeDtypeStruct((token_rows, 2 * rank * width), F32)
    held = pltpu.VMEM((members,) + own_near.shape, BF16)

    def near_work(near, fetched):
        return pl.pallas_call(
            functools.partial(near_kernel, proj_count, table.shape[0], tuple(near)),
            out_shape=(
                plane, partial, jax.ShapeDtypeStruct((slots, width), BF16), plane,
                jax.ShapeDtypeStruct((slots, LANES), jnp.int32), jax.ShapeDtypeStruct((8, slots), jnp.int32),
            ),
            in_specs=[vmem()] * 5 + [anywhere()] * len(near),
            out_specs=(vmem(),) * 6,
            scratch_shapes=[held, pltpu.SemaphoreType.DMA],
            compiler_params=params,
            cost_estimate=pl.CostEstimate(flops=5 * 10**9, bytes_accessed=10**7, transcendentals=0),
            name="near",
        )(requests, pick_slot.T, tokens, cotangent, fetched.reshape(slots, value_width), *near.values())

    pieces, fetched, near_done = gather_pieces(own_near, own_far, requests, table, near_work)
    pick_grad, queries, near_key, counts, wide_id, slot_proj = near_done
    keys = tuple(pieces)
    tall = (token_rows, features)
    return pl.pallas_call(
        functools.partial(dense_kernel, rank, width, proj_count, keys),
        out_shape=(jax.ShapeDtypeStruct(tall, BF16),) * 2,
        in_specs=[smem()] + [anywhere()] * (9 + len(keys)),
        out_specs=(anywhere(), anywhere()),
        scratch_shapes=[
            held,
            held,
            pltpu.VMEM(partial.shape, F32),
            pltpu.VMEM(plane.shape, F32),
            pltpu.VMEM(plane.shape, F32),
            pltpu.VMEM(tall, BF16),
            pltpu.VMEM((slots, value_width), BF16),
            pltpu.VMEM(wide_id.shape, jnp.int32),
            pltpu.VMEM(slot_proj.shape, jnp.int32),
            pltpu.VMEM(near_key.shape, BF16),
            pltpu.VMEM(tall, BF16),
            pltpu.VMEM((token_rows, proj_count * value_width), BF16),
            pltpu.VMEM(partial.shape, BF16),
            pltpu.VMEM(tall, BF16),
            pltpu.VMEM(tall, BF16),
            pltpu.SemaphoreType.DMA((3,)),
            pltpu.SemaphoreType.DMA((9,)),
            pltpu.SemaphoreType.DMA((2,)),
        ],
        compiler_params=params,
        cost_estimate=pl.CostEstimate(flops=10**10, bytes_accessed=2 * 10**7, transcendentals=10**5),
        name="dense",
    )(
        tucker_core, wide_id, tokens, near_key, slot_proj, queries, counts, cotangent,
        fetched.reshape(slots, value_width), pick_grad, *pieces.values(),
    )


def whole_path(tokens, cotangent, w_query, key_row, key_col, tucker_core, proj_part, requests, table, row_id,
               slot_proj, pick_slot, nkey, proj_count):
    rank = tucker_core.shape[0]
    width = key_row.shape[1]
    slots = row_id.shape[0]
    fetched = returned_rows(found_rows(wanted_rows(requests), table)).reshape(slots, -1)
    query_full = lax.all_gather(w_query.T, "mem", axis=0, tiled=True)
    keys = lax.all_gather(jnp.concatenate([key_row, key_col], axis=1), "mem", axis=0, tiled=True)
    proj_full = lax.all_gather(proj_part, "mem", axis=1, tiled=True)
    key_at = jnp.arange(nkey, dtype=jnp.int32)[None, :]
    row_hot = ((row_id // nkey)[:, None] == key_at).astype(BF16)
    col_hot = ((row_id % nkey)[:, None] == key_at).astype(BF16)
    slot_row = dot(row_hot, keys[:, :width], PLAIN).astype(BF16)
    slot_col = dot(col_hot, keys[:, width:], PLAIN).astype(BF16)
    spread = jnp.where(
        slot_proj[:, None, None] == jnp.arange(proj_count, dtype=jnp.int32)[None, :, None],
        fetched[:, None, :], jnp.zeros((), BF16)
    ).reshape(slots, -1)
    counts = jnp.sum(
        (pick_slot[:, :, None] == jnp.arange(slots, dtype=jnp.int32)[None, None, :]).astype(F32), axis=1
    )
    queries = dot(tokens, query_full, LAST).astype(BF16)
    row_scores = [dot(queries[:, r * width:(r + 1) * width], slot_row, LAST) for r in range(rank)]
    col_scores = [
        dot(queries[:, (rank + r) * width:(rank + r + 1) * width], slot_col, LAST) for r in range(rank)
    ]
    col_mixed = [sum(tucker_core[r, s] * col_scores[s] for s in range(rank)) for r in range(rank)]
    row_mixed = [sum(row_scores[r] * tucker_core[r, s] for r in range(rank)) for s in range(rank)]
    score = sum(row_scores[r] * col_mixed[r] for r in range(rank))
    gate = jax.nn.sigmoid(score)
    weights = counts * gate.astype(BF16).astype(F32)
    mixed = counted_dot(weights, spread, PLAIN).astype(BF16)
    memory_out = dot(mixed, proj_full, PLAIN)
    value_grad = dot(cotangent, proj_full, LAST).astype(BF16)
    pick_grad = dot(value_grad, spread, LAST)
    score_grad = pick_grad * gate * (1.0 - gate)
    blocks = []
    for mixed_scores, slot_key in ((col_mixed, slot_row), (row_mixed, slot_col)):
        for r in range(rank):
            grad = (score_grad * mixed_scores[r]).astype(BF16).astype(F32) * counts
            blocks.append(counted_dot(grad, slot_key, PLAIN).astype(BF16))
    query_grad = jnp.concatenate(blocks, axis=1)
    token_grad = dot(query_grad, query_full, PLAIN)
    return memory_out.astype(BF16), token_grad.astype(BF16)


def shards(
    mem, tokens, cotangent, w_query, key_row, key_col, tucker_core, table, w_proj, send_ids, pick_slot
):
    proj_count, value_width, _ = w_proj.shape
    requests = send_ids[0]
    owners, capacity = requests.shape
    slots = owners * capacity
    nkey = key_row.shape[0] * mem
    row_id = jnp.maximum(requests, 0) + jnp.arange(owners, dtype=jnp.int32)[:, None] * table.shape[0]
    row_id = row_id.reshape(slots)
    slot_proj = (row_id % nkey) % proj_count
    proj_part = w_proj.reshape(proj_count * value_width, -1)
    path = pieces_path if mem == 16 and w_proj.shape[2] == LANES else whole_path
    return path(tokens, cotangent, w_query, key_row, key_col, tucker_core, proj_part, requests, table, row_id,
                slot_proj, pick_slot, nkey, proj_count)


def solution(mesh):
    in_specs = (
        P(("groups", "mem"), None),
        P(("groups", "mem"), None),
        P(None, "mem"),
        P("mem", None),
        P("mem", None),
        P(),
        P("mem", None),
        P(None, None, "mem"),
        P(("groups", "mem"), None, None),
        P(("groups", "mem"), None),
    )
    out_specs = (P(("groups", "mem"), None), P(("groups", "mem"), None))
    body = functools.partial(shards, mesh.shape["mem"])
    return jax.shard_map(body, mesh=mesh, in_specs=in_specs, out_specs=out_specs, check_vma=False)
```

```python
import functools

import jax
import jax.numpy as jnp
from jax import lax
from jax.experimental import pallas as pl
from jax.experimental.pallas import tpu as pltpu
from jax.sharding import PartitionSpec as P

F32 = jnp.float32
BF16 = jnp.bfloat16
RING = (0, 2, 3, 1)
LANES = 128
LAST = ((1,), (1,))
PLAIN = ((1,), (0,))
VMEM_LIMIT = 56 * 1024 * 1024


def dot(a, b, dims):
    return lax.dot_general(a, b, (dims, ((), ())), preferred_element_type=F32)


def two_terms(x):
    high = x.astype(BF16)
    return high, (x - high.astype(F32)).astype(BF16)


def counted_dot(x, b, dims):
    high, low = two_terms(x)
    return dot(high, b, dims) + dot(low, b, dims)


def wanted_rows(requests):
    return lax.all_to_all(requests, "mem", split_axis=0, concat_axis=0, tiled=True)


def found_rows(wanted, table):
    found = jnp.take(table, jnp.maximum(wanted, 0).reshape(-1), axis=0, mode="clip")
    return found.reshape(wanted.shape + (table.shape[1],))


def returned_rows(found):
    return lax.all_to_all(found, "mem", split_axis=0, concat_axis=0, tiled=True)


def place(z, y, core):
    return (z * 2 + y) * 2 + core


def everywhere(move):
    pairs = []
    for z in range(4):
        for y in range(2):
            for core in range(2):
                pairs.append((place(z, y, core), place(*move(z, y, core))))
    return pairs


def next_z(x):
    step = {RING[i]: RING[(i + 1) % 4] for i in range(4)}
    return lax.ppermute(x, "mem", everywhere(lambda z, y, c: (step[z], y, c)))


def other_y(x):
    return lax.ppermute(x, "mem", everywhere(lambda z, y, c: (z, 1 - y, c)))


def other_core(x):
    return lax.ppermute(x, "mem", everywhere(lambda z, y, c: (z, y, 1 - c)))


def other_x(x):
    return lax.ppermute(x, "groups", [(0, 1), (1, 0)])


def ring_source(z, steps):
    index = jnp.where(z == 0, 0, jnp.where(z == 2, 1, jnp.where(z == 3, 2, 3)))
    index = (index + 4 - steps) % 4
    return jnp.where(index == 0, 0, jnp.where(index == 1, 2, jnp.where(index == 2, 3, 1)))


def tie(*values):
    return lax.optimization_barrier(values)


def halves_kernel(query_ref, key_row_ref, key_col_ref, proj_ref, near_ref, far_ref):
    x = lax.axis_index("groups")
    parts = proj_ref.shape[1]
    blocks = query_ref.shape[1] // LANES // 2
    for target, half in ((near_ref, x), (far_ref, 1 - x)):
        target[:parts] = proj_ref[half]
        for j in range(blocks):
            target[parts + j] = query_ref[:, pl.ds(pl.multiple_of((half * blocks + j) * LANES, LANES), LANES)]
        for j in range(key_row_ref.shape[1] // LANES):
            cols = slice(j * LANES, (j + 1) * LANES)
            target[parts + blocks + j] = jnp.where(half == 0, key_row_ref[:, cols], key_col_ref[:, cols])


def own_halves(w_query, key_row, key_col, proj_part):
    features, columns = w_query.shape
    proj = proj_part.reshape(2, -1, columns, LANES)
    blocks = proj.shape[1] + (features // 2 + key_row.shape[1]) // LANES
    half = jax.ShapeDtypeStruct((blocks, columns, LANES), BF16)
    return pl.pallas_call(
        halves_kernel,
        out_shape=(half, half),
        in_specs=[vmem()] * 4,
        out_specs=(vmem(), vmem()),
        compiler_params=pltpu.CompilerParams(vmem_limit_bytes=VMEM_LIMIT),
        cost_estimate=pl.CostEstimate(flops=0, bytes_accessed=4 * 10**6, transcendentals=0),
        name="halves",
    )(w_query.T, key_row, key_col, proj)


def other_cores(first, second):
    first = other_core(first)
    second, first = tie(second, first)
    return first, other_core(second)


def gather_pieces(own_near, own_far, requests, table, near_work):
    pieces = {(0, 0, 0, 0): own_near, (0, 0, 0, 1): own_far}
    z1, y0, wanted, pieces[0, 0, 1, 0], pieces[0, 0, 1, 1] = tie(
        next_z(own_near), other_y(own_near), wanted_rows(requests), other_core(own_near), other_core(own_far)
    )
    pieces[1, 0, 0, 0], pieces[0, 1, 0, 0] = z1, y0
    z2, y1, y0f, found, pieces[1, 0, 1, 0], pieces[0, 1, 1, 0] = tie(
        next_z(z1), other_y(z1), other_x(y0), found_rows(wanted, table), *other_cores(z1, y0)
    )
    pieces[2, 0, 0, 0], pieces[1, 1, 0, 0], pieces[0, 1, 0, 1] = z2, y1, y0f
    z3, y2, y1f, pieces[2, 0, 1, 0], pieces[1, 1, 1, 0] = tie(
        next_z(z2), other_y(z2), other_x(y1), *other_cores(z2, y1)
    )
    pieces[3, 0, 0, 0], pieces[2, 1, 0, 0], pieces[1, 1, 0, 1] = z3, y2, y1f
    z1f, y3, z3f, fetched, pieces[3, 0, 1, 0], pieces[0, 1, 1, 1], pieces[2, 1, 1, 0] = tie(
        next_z(own_far), other_y(z3), other_x(z3), returned_rows(found), *other_cores(z3, y0f), other_core(y2)
    )
    pieces[1, 0, 0, 1], pieces[3, 1, 0, 0], pieces[3, 0, 0, 1] = z1f, y3, z3f
    pieces[3, 1, 1, 0] = other_core(y3)
    near = {key: piece for key, piece in pieces.items() if key[3] == 0}
    z2f, y3f, y2f = next_z(z1f), other_y(z3f), other_x(y2)
    near_done, y1f, z1f, z3f = tie(near_work(near, fetched), y1f, z1f, z3f)
    z2f, y3f, y2f, pieces[1, 1, 1, 1], pieces[1, 0, 1, 1], pieces[3, 0, 1, 1] = tie(
        z2f, y3f, y2f, other_core(y1f), other_core(z1f), other_core(z3f)
    )
    pieces[2, 0, 0, 1], pieces[3, 1, 0, 1], pieces[2, 1, 0, 1] = z2f, y3f, y2f
    pieces[2, 0, 1, 1], pieces[3, 1, 1, 1], pieces[2, 1, 1, 1] = other_core(z2f), other_core(y3f), other_core(y2f)
    return pieces, fetched, near_done


def placed(keys, pieces):
    me = lax.axis_index("mem")
    z, y, core = me // 4, (me // 2) % 2, me % 2
    for (steps, side, other, far), piece in zip(keys, pieces):
        at = place(ring_source(z, steps), 1 - y if side else y, 1 - core if other else core)
        yield at, piece


def wait_for(held, sem):
    pltpu.make_async_copy(held, held, sem).wait()


def lanes(held, blocks):
    return jnp.concatenate([held[:, j].reshape(-1, LANES) for j in blocks], axis=1)


def value_products(first, count, held, base, proj, cot, fetched, pick_grad):
    value_width = fetched.shape[1]
    parts = value_width // held.shape[-2]
    for e in range(count):
        block = jnp.concatenate(
            [held[m, base + e * parts:base + (e + 1) * parts].reshape(value_width, LANES) for m in range(held.shape[0])],
            axis=1,
        )
        grad = dot(cot, block, LAST).astype(BF16)
        pick_grad = jnp.where(proj == first + e, dot(grad, fetched, LAST), pick_grad)
    return pick_grad


def one_hot_keys(use_row, row_id, nkey):
    key_at = lax.broadcasted_iota(jnp.int32, (row_id.shape[0], nkey), 1)
    picked = jnp.where(use_row, row_id // nkey, row_id % nkey)
    return jnp.where(picked == key_at, 1.0, 0.0).astype(BF16)


def slot_ids(requests, rows_each):
    owners, capacity = requests.shape
    slots = owners * capacity
    rows = jnp.broadcast_to(requests[:, None, :], (owners, capacity, capacity)).reshape(slots, capacity)
    slot = lax.broadcasted_iota(jnp.int32, (slots, capacity), 0)
    lane = lax.broadcasted_iota(jnp.int32, (slots, capacity), 1)
    local = jnp.sum(jnp.where(slot % capacity == lane, jnp.maximum(rows, 0), 0), axis=1, keepdims=True)
    return local + slot[:, :1] // capacity * rows_each


def near_kernel(
    proj_count, rows_each, keys, requests_ref, pick_ref, tokens_ref, cot_ref, fetched_ref, *refs
):
    pick_grad_ref, queries_ref, slot_key_ref, counts_ref, wide_id_ref, proj_ref, held, sem = refs[-8:]
    for at, piece in placed(keys, refs[:-8]):
        pltpu.make_async_copy(piece, held.at[at], sem).start()
    x = lax.axis_index("groups")
    features = tokens_ref.shape[1]
    half = features // 2
    half_count = proj_count // 2
    parts = half_count * fetched_ref.shape[1] // held.shape[2]
    key = parts + half // LANES
    nkey = held.shape[0] * held.shape[2]
    wide_id = jnp.broadcast_to(slot_ids(requests_ref[...], rows_each), wide_id_ref.shape)
    wide_id_ref[...] = wide_id
    proj = (wide_id % nkey % proj_count).T[:proj_ref.shape[0]]
    proj_ref[...] = proj
    token_rows, slots = counts_ref.shape
    lane = lax.broadcasted_iota(jnp.int32, (token_rows, slots), 1)
    pick = pick_ref[...].T
    counts = jnp.zeros((token_rows, slots), F32)
    for k in range(pick.shape[1]):
        counts += jnp.where(pick[:, k:k + 1] == lane, 1.0, 0.0)
    counts_ref[...] = counts
    hot = one_hot_keys(x == 0, wide_id[:, :1], nkey)
    wait_for(held, sem)
    slot_key_ref[...] = dot(hot, lanes(held, range(key, held.shape[1])), PLAIN).astype(BF16)
    tokens = tokens_ref[:, pl.ds(pl.multiple_of(x * half, half), half)]
    queries_ref[...] = dot(tokens, lanes(held, range(parts, key)), LAST)
    pick_grad_ref[...] = value_products(
        x * half_count, half_count, held, 0, proj[:1], cot_ref[...], fetched_ref[...],
        jnp.zeros(pick_grad_ref.shape, F32),
    )


def dense_kernel(
    rank, width, proj_count, keys, core_ref, *refs
):
    inputs, refs = refs[:9], refs[9:]
    pieces = refs[:len(keys)]
    (out_ref, grad_ref, near_held, far_held, queries_held, pick_held, counts_held, cot_held, fetched_held,
     row_id_held, proj_held, near_key_held, tokens_held, mixed_values, query_grad, out_held, grad_held, piece_sem, in_sem, out_sem) = refs[len(keys):]
    held_inputs = (
        row_id_held, tokens_held, near_key_held, proj_held, queries_held, counts_held, cot_held, fetched_held, pick_held
    )
    x = lax.axis_index("groups")
    token_rows, features = tokens_held.shape
    slots, value_width = fetched_held.shape
    columns = far_held.shape[2]
    half = features // 2
    half_count = proj_count // 2
    parts = half_count * value_width // columns
    key = parts + half // LANES
    spots = list(placed(keys, pieces))
    far = [spot for spot, k in zip(spots, keys) if k[3]]
    near = [spot for spot, k in zip(spots, keys) if not k[3]]
    query_blocks = pl.ds(parts, far_held.shape[1] - parts)
    copies = [pltpu.make_async_copy(a, b, in_sem.at[i]) for i, (a, b) in enumerate(zip(inputs, held_inputs))]
    copies[0].start()
    for at, piece in far:
        pltpu.make_async_copy(piece.at[query_blocks], far_held.at[at, query_blocks], piece_sem.at[0]).start()
    for copy in copies[1:6]:
        copy.start()
    for at, piece in far:
        pltpu.make_async_copy(piece.at[pl.ds(0, parts)], far_held.at[at, pl.ds(0, parts)], piece_sem.at[1]).start()
    for copy in copies[6:]:
        copy.start()
    for at, piece in near:
        pltpu.make_async_copy(piece, near_held.at[at], piece_sem.at[2]).start()

    copies[0].wait()
    hot = one_hot_keys(x != 0, row_id_held[:, :1], far_held.shape[0] * columns)
    wait_for(far_held.at[:, query_blocks], piece_sem.at[0])
    for copy in copies[1:6]:
        copy.wait()
    far_key = dot(hot, lanes(far_held, range(key, far_held.shape[1])), PLAIN).astype(BF16)
    near_key = near_key_held[...]
    slot_row = jnp.where(x == 0, near_key, far_key)
    slot_col = jnp.where(x == 0, far_key, near_key)
    tokens = tokens_held[:, pl.ds(pl.multiple_of((1 - x) * half, half), half)]
    queries = (dot(tokens, lanes(far_held, range(parts, key)), LAST) + queries_held[...]).astype(BF16)
    block = [queries[:, r * width:(r + 1) * width] for r in range(2 * rank)]
    row_scores = [dot(block[r], slot_row, LAST) for r in range(rank)]
    col_scores = [dot(block[rank + r], slot_col, LAST) for r in range(rank)]
    wait_for(far_held.at[:, pl.ds(0, parts)], piece_sem.at[1])
    for copy in copies[6:]:
        copy.wait()
    wait_for(near_held, piece_sem.at[2])
    proj = proj_held[:1]
    fetched = fetched_held[...]
    pick_grad = value_products(
        (1 - x) * half_count, half_count, far_held, 0, proj, cot_held[...], fetched, pick_held[...]
    )
    col_mixed = [sum(core_ref[r, s] * col_scores[s] for s in range(rank)) for r in range(rank)]
    row_mixed = [sum(row_scores[r] * core_ref[r, s] for r in range(rank)) for s in range(rank)]
    score = sum(row_scores[r] * col_mixed[r] for r in range(rank))
    gate = 1.0 / (1.0 + jnp.exp(-score))
    counts = counts_held[...]
    weights = (counts * gate.astype(BF16).astype(F32)).astype(BF16)
    slope = gate * (1.0 - gate)
    for i in range(proj_count):
        e = (x if i < half_count else 1 - x) * half_count + i % half_count
        mixed = dot(jnp.where(proj == e, weights, jnp.zeros((), BF16)), fetched, PLAIN)
        mixed_values[:, i * value_width:(i + 1) * value_width] = mixed.astype(BF16)

    members = far_held.shape[0] // 4
    step = features // 4
    sides = ((near_held, x), (far_held, 1 - x))
    for c in range(4):
        cols = pl.ds(c * step, step)
        block = jnp.concatenate([
            jnp.concatenate([held[m, :parts].reshape(-1, LANES) for m in range(c * members, (c + 1) * members)], axis=1)
            for held, _ in sides
        ], axis=0)
        out_held[:, cols] = dot(mixed_values[...], block, PLAIN).astype(BF16)
        pltpu.make_async_copy(out_held.at[:, cols], out_ref.at[:, cols], out_sem.at[0]).start()
    score_grad = pick_grad * slope
    for i, factor in enumerate(col_mixed + row_mixed):
        slot_key = slot_row if i < rank else slot_col
        grad = ((score_grad * factor).astype(BF16).astype(F32) * counts).astype(BF16)
        query_grad[:, i * width:(i + 1) * width] = dot(grad, slot_key, PLAIN).astype(BF16)
    for c in range(4):
        held, side = sides[c // 2]
        blocks = step // LANES
        first = parts + (c % 2) * blocks
        cols = pl.ds(pl.multiple_of(side * half + (c % 2) * step, step), step)
        grad_held[:, cols] = dot(query_grad[...], lanes(held, range(first, first + blocks)), PLAIN).astype(BF16)
        pltpu.make_async_copy(grad_held.at[:, cols], grad_ref.at[:, cols], out_sem.at[1]).start()
    pltpu.make_async_copy(out_held, out_ref, out_sem.at[0]).wait()
    pltpu.make_async_copy(grad_held, grad_ref, out_sem.at[1]).wait()


def vmem():
    return pl.BlockSpec(memory_space=pltpu.VMEM)


def smem():
    return pl.BlockSpec(memory_space=pltpu.SMEM)


def anywhere():
    return pl.BlockSpec(memory_space=pl.ANY)


def pieces_path(tokens, cotangent, w_query, key_row, key_col, tucker_core, proj_part, requests, table, row_id,
                slot_proj, pick_slot, nkey, proj_count):
    rank = tucker_core.shape[0]
    width = key_row.shape[1]
    token_rows, features = tokens.shape
    slots = row_id.shape[0]
    value_width = table.shape[1]
    columns = w_query.shape[1]
    own_near, own_far = own_halves(w_query, key_row, key_col, proj_part)
    params = pltpu.CompilerParams(vmem_limit_bytes=VMEM_LIMIT)
    members = nkey // columns
    plane = jax.ShapeDtypeStruct((token_rows, slots), F32)
    partial = jax.ShapeDtypeStruct((token_rows, 2 * rank * width), F32)
    held = pltpu.VMEM((members,) + own_near.shape, BF16)

    def near_work(near, fetched):
        return pl.pallas_call(
            functools.partial(near_kernel, proj_count, table.shape[0], tuple(near)),
            out_shape=(
                plane, partial, jax.ShapeDtypeStruct((slots, width), BF16), plane,
                jax.ShapeDtypeStruct((slots, LANES), jnp.int32), jax.ShapeDtypeStruct((8, slots), jnp.int32),
            ),
            in_specs=[vmem()] * 5 + [anywhere()] * len(near),
            out_specs=(vmem(),) * 6,
            scratch_shapes=[held, pltpu.SemaphoreType.DMA],
            compiler_params=params,
            cost_estimate=pl.CostEstimate(flops=5 * 10**9, bytes_accessed=10**7, transcendentals=0),
            name="near",
        )(requests, pick_slot.T, tokens, cotangent, fetched.reshape(slots, value_width), *near.values())

    pieces, fetched, near_done = gather_pieces(own_near, own_far, requests, table, near_work)
    pick_grad, queries, near_key, counts, wide_id, slot_proj = near_done
    keys = tuple(pieces)
    tall = (token_rows, features)
    return pl.pallas_call(
        functools.partial(dense_kernel, rank, width, proj_count, keys),
        out_shape=(jax.ShapeDtypeStruct(tall, BF16),) * 2,
        in_specs=[smem()] + [anywhere()] * (9 + len(keys)),
        out_specs=(anywhere(), anywhere()),
        scratch_shapes=[
            held,
            held,
            pltpu.VMEM(partial.shape, F32),
            pltpu.VMEM(plane.shape, F32),
            pltpu.VMEM(plane.shape, F32),
            pltpu.VMEM(tall, BF16),
            pltpu.VMEM((slots, value_width), BF16),
            pltpu.VMEM(wide_id.shape, jnp.int32),
            pltpu.VMEM(slot_proj.shape, jnp.int32),
            pltpu.VMEM(near_key.shape, BF16),
            pltpu.VMEM(tall, BF16),
            pltpu.VMEM((token_rows, proj_count * value_width), BF16),
            pltpu.VMEM(partial.shape, BF16),
            pltpu.VMEM(tall, BF16),
            pltpu.VMEM(tall, BF16),
            pltpu.SemaphoreType.DMA((3,)),
            pltpu.SemaphoreType.DMA((9,)),
            pltpu.SemaphoreType.DMA((2,)),
        ],
        compiler_params=params,
        cost_estimate=pl.CostEstimate(flops=10**10, bytes_accessed=2 * 10**7, transcendentals=10**5),
        name="dense",
    )(
        tucker_core, wide_id, tokens, near_key, slot_proj, queries, counts, cotangent,
        fetched.reshape(slots, value_width), pick_grad, *pieces.values(),
    )


def whole_path(tokens, cotangent, w_query, key_row, key_col, tucker_core, proj_part, requests, table, row_id,
               slot_proj, pick_slot, nkey, proj_count):
    rank = tucker_core.shape[0]
    width = key_row.shape[1]
    slots = row_id.shape[0]
    fetched = returned_rows(found_rows(wanted_rows(requests), table)).reshape(slots, -1)
    query_full = lax.all_gather(w_query.T, "mem", axis=0, tiled=True)
    keys = lax.all_gather(jnp.concatenate([key_row, key_col], axis=1), "mem", axis=0, tiled=True)
    proj_full = lax.all_gather(proj_part, "mem", axis=1, tiled=True)
    key_at = jnp.arange(nkey, dtype=jnp.int32)[None, :]
    row_hot = ((row_id // nkey)[:, None] == key_at).astype(BF16)
    col_hot = ((row_id % nkey)[:, None] == key_at).astype(BF16)
    slot_row = dot(row_hot, keys[:, :width], PLAIN).astype(BF16)
    slot_col = dot(col_hot, keys[:, width:], PLAIN).astype(BF16)
    spread = jnp.where(
        slot_proj[:, None, None] == jnp.arange(proj_count, dtype=jnp.int32)[None, :, None],
        fetched[:, None, :], jnp.zeros((), BF16)
    ).reshape(slots, -1)
    counts = jnp.sum(
        (pick_slot[:, :, None] == jnp.arange(slots, dtype=jnp.int32)[None, None, :]).astype(F32), axis=1
    )
    queries = dot(tokens, query_full, LAST).astype(BF16)
    row_scores = [dot(queries[:, r * width:(r + 1) * width], slot_row, LAST) for r in range(rank)]
    col_scores = [
        dot(queries[:, (rank + r) * width:(rank + r + 1) * width], slot_col, LAST) for r in range(rank)
    ]
    col_mixed = [sum(tucker_core[r, s] * col_scores[s] for s in range(rank)) for r in range(rank)]
    row_mixed = [sum(row_scores[r] * tucker_core[r, s] for r in range(rank)) for s in range(rank)]
    score = sum(row_scores[r] * col_mixed[r] for r in range(rank))
    gate = jax.nn.sigmoid(score)
    weights = counts * gate.astype(BF16).astype(F32)
    mixed = counted_dot(weights, spread, PLAIN).astype(BF16)
    memory_out = dot(mixed, proj_full, PLAIN)
    value_grad = dot(cotangent, proj_full, LAST).astype(BF16)
    pick_grad = dot(value_grad, spread, LAST)
    score_grad = pick_grad * gate * (1.0 - gate)
    blocks = []
    for mixed_scores, slot_key in ((col_mixed, slot_row), (row_mixed, slot_col)):
        for r in range(rank):
            grad = (score_grad * mixed_scores[r]).astype(BF16).astype(F32) * counts
            blocks.append(counted_dot(grad, slot_key, PLAIN).astype(BF16))
    query_grad = jnp.concatenate(blocks, axis=1)
    token_grad = dot(query_grad, query_full, PLAIN)
    return memory_out.astype(BF16), token_grad.astype(BF16)


def shards(
    mem, tokens, cotangent, w_query, key_row, key_col, tucker_core, table, w_proj, send_ids, pick_slot
):
    proj_count, value_width, _ = w_proj.shape
    requests = send_ids[0]
    owners, capacity = requests.shape
    slots = owners * capacity
    nkey = key_row.shape[0] * mem
    row_id = jnp.maximum(requests, 0) + jnp.arange(owners, dtype=jnp.int32)[:, None] * table.shape[0]
    row_id = row_id.reshape(slots)
    slot_proj = (row_id % nkey) % proj_count
    proj_part = w_proj.reshape(proj_count * value_width, -1)
    path = pieces_path if mem == 16 and w_proj.shape[2] == LANES else whole_path
    return path(tokens, cotangent, w_query, key_row, key_col, tucker_core, proj_part, requests, table, row_id,
                slot_proj, pick_slot, nkey, proj_count)


def solution(mesh):
    in_specs = (
        P(("groups", "mem"), None),
        P(("groups", "mem"), None),
        P(None, "mem"),
        P("mem", None),
        P("mem", None),
        P(),
        P("mem", None),
        P(None, None, "mem"),
        P(("groups", "mem"), None, None),
        P(("groups", "mem"), None),
    )
    out_specs = (P(("groups", "mem"), None), P(("groups", "mem"), None))
    body = functools.partial(shards, mesh.shape["mem"])
    return jax.shard_map(body, mesh=mesh, in_specs=in_specs, out_specs=out_specs, check_vma=False)
```

```python
import functools

import jax
import jax.numpy as jnp
from jax import lax
from jax.experimental import pallas as pl
from jax.experimental.pallas import tpu as pltpu
from jax.sharding import PartitionSpec as P

F32 = jnp.float32
BF16 = jnp.bfloat16
RING = (0, 2, 3, 1)
LANES = 128
LAST = ((1,), (1,))
PLAIN = ((1,), (0,))
VMEM_LIMIT = 56 * 1024 * 1024


def dot(a, b, dims):
    return lax.dot_general(a, b, (dims, ((), ())), preferred_element_type=F32)


def two_terms(x):
    high = x.astype(BF16)
    return high, (x - high.astype(F32)).astype(BF16)


def counted_dot(x, b, dims):
    high, low = two_terms(x)
    return dot(high, b, dims) + dot(low, b, dims)


def wanted_rows(requests):
    return lax.all_to_all(requests, "mem", split_axis=0, concat_axis=0, tiled=True)


def found_rows(wanted, table):
    found = jnp.take(table, jnp.maximum(wanted, 0).reshape(-1), axis=0, mode="clip")
    return found.reshape(wanted.shape + (table.shape[1],))


def returned_rows(found):
    return lax.all_to_all(found, "mem", split_axis=0, concat_axis=0, tiled=True)


def place(z, y, core):
    return (z * 2 + y) * 2 + core


def everywhere(move):
    pairs = []
    for z in range(4):
        for y in range(2):
            for core in range(2):
                pairs.append((place(z, y, core), place(*move(z, y, core))))
    return pairs


def next_z(x):
    step = {RING[i]: RING[(i + 1) % 4] for i in range(4)}
    return lax.ppermute(x, "mem", everywhere(lambda z, y, c: (step[z], y, c)))


def other_y(x):
    return lax.ppermute(x, "mem", everywhere(lambda z, y, c: (z, 1 - y, c)))


def other_core(x):
    return lax.ppermute(x, "mem", everywhere(lambda z, y, c: (z, y, 1 - c)))


def other_x(x):
    return lax.ppermute(x, "groups", [(0, 1), (1, 0)])


def ring_source(z, steps):
    index = jnp.where(z == 0, 0, jnp.where(z == 2, 1, jnp.where(z == 3, 2, 3)))
    index = (index + 4 - steps) % 4
    return jnp.where(index == 0, 0, jnp.where(index == 1, 2, jnp.where(index == 2, 3, 1)))


def tie(*values):
    return lax.optimization_barrier(values)


def halves_kernel(query_ref, key_row_ref, key_col_ref, proj_ref, near_ref, far_ref):
    x = lax.axis_index("groups")
    parts = proj_ref.shape[1]
    blocks = query_ref.shape[1] // LANES // 2
    for target, half in ((near_ref, x), (far_ref, 1 - x)):
        target[:parts] = proj_ref[half]
        for j in range(blocks):
            target[parts + j] = query_ref[:, pl.ds(pl.multiple_of((half * blocks + j) * LANES, LANES), LANES)]
        for j in range(key_row_ref.shape[1] // LANES):
            cols = slice(j * LANES, (j + 1) * LANES)
            target[parts + blocks + j] = jnp.where(half == 0, key_row_ref[:, cols], key_col_ref[:, cols])


def own_halves(w_query, key_row, key_col, proj_part):
    features, columns = w_query.shape
    proj = proj_part.reshape(2, -1, columns, LANES)
    blocks = proj.shape[1] + (features // 2 + key_row.shape[1]) // LANES
    half = jax.ShapeDtypeStruct((blocks, columns, LANES), BF16)
    return pl.pallas_call(
        halves_kernel,
        out_shape=(half, half),
        in_specs=[vmem()] * 4,
        out_specs=(vmem(), vmem()),
        compiler_params=pltpu.CompilerParams(vmem_limit_bytes=VMEM_LIMIT),
        cost_estimate=pl.CostEstimate(flops=0, bytes_accessed=4 * 10**6, transcendentals=0),
        name="halves",
    )(w_query.T, key_row, key_col, proj)


def other_cores(first, second, *awaited):
    first = other_core(first)
    second, first, *awaited = tie(second, first, *awaited)
    return first, other_core(second), *awaited


def gather_pieces(own_near, own_far, requests, table, near_work):
    pieces = {(0, 0, 0, 0): own_near, (0, 0, 0, 1): own_far}
    z1, y0, wanted, pieces[0, 0, 1, 0], pieces[0, 0, 1, 1] = tie(
        next_z(own_near), other_y(own_near), wanted_rows(requests), other_core(own_near), other_core(own_far)
    )
    pieces[1, 0, 0, 0], pieces[0, 1, 0, 0] = z1, y0
    z1f = next_z(own_far)
    z2, y1, y0f, found, pieces[1, 0, 1, 0], pieces[0, 1, 1, 0], z1f = tie(
        next_z(z1), other_y(z1), other_x(y0), found_rows(wanted, table), *other_cores(z1, y0, z1f)
    )
    pieces[2, 0, 0, 0], pieces[1, 1, 0, 0], pieces[0, 1, 0, 1] = z2, y1, y0f
    z3, y2, y1f, pieces[2, 0, 1, 0], pieces[1, 1, 1, 0] = tie(
        next_z(z2), other_y(z2), other_x(y1), *other_cores(z2, y1)
    )
    pieces[3, 0, 0, 0], pieces[2, 1, 0, 0], pieces[1, 1, 0, 1] = z3, y2, y1f
    y3, z3f, fetched, pieces[3, 0, 1, 0], pieces[0, 1, 1, 1], pieces[2, 1, 1, 0] = tie(
        other_y(z3), other_x(z3), returned_rows(found), *other_cores(z3, y0f), other_core(y2)
    )
    pieces[1, 0, 0, 1], pieces[3, 1, 0, 0], pieces[3, 0, 0, 1] = z1f, y3, z3f
    pieces[3, 1, 1, 0] = other_core(y3)
    near = {key: piece for key, piece in pieces.items() if key[3] == 0}
    z2f, y3f, y2f = next_z(z1f), other_y(z3f), other_x(y2)
    near_done, y1f, z1f, z3f = tie(near_work(near, fetched), y1f, z1f, z3f)
    z2f, y3f, y2f, pieces[1, 1, 1, 1], pieces[1, 0, 1, 1], pieces[3, 0, 1, 1] = tie(
        z2f, y3f, y2f, other_core(y1f), other_core(z1f), other_core(z3f)
    )
    pieces[2, 0, 0, 1], pieces[3, 1, 0, 1], pieces[2, 1, 0, 1] = z2f, y3f, y2f
    pieces[2, 0, 1, 1], pieces[3, 1, 1, 1], pieces[2, 1, 1, 1] = other_core(z2f), other_core(y3f), other_core(y2f)
    return pieces, fetched, near_done


def placed(keys, pieces):
    me = lax.axis_index("mem")
    z, y, core = me // 4, (me // 2) % 2, me % 2
    for (steps, side, other, far), piece in zip(keys, pieces):
        at = place(ring_source(z, steps), 1 - y if side else y, 1 - core if other else core)
        yield at, piece


def wait_for(held, sem):
    pltpu.make_async_copy(held, held, sem).wait()


def lanes(held, blocks):
    return jnp.concatenate([held[:, j].reshape(-1, LANES) for j in blocks], axis=1)


def value_products(first, count, held, base, proj, cot, fetched, pick_grad):
    value_width = fetched.shape[1]
    parts = value_width // held.shape[-2]
    for e in range(count):
        block = jnp.concatenate(
            [held[m, base + e * parts:base + (e + 1) * parts].reshape(value_width, LANES) for m in range(held.shape[0])],
            axis=1,
        )
        grad = dot(cot, block, LAST).astype(BF16)
        pick_grad = jnp.where(proj == first + e, dot(grad, fetched, LAST), pick_grad)
    return pick_grad


def one_hot_keys(use_row, row_id, nkey):
    key_at = lax.broadcasted_iota(jnp.int32, (row_id.shape[0], nkey), 1)
    picked = jnp.where(use_row, row_id // nkey, row_id % nkey)
    return jnp.where(picked == key_at, 1.0, 0.0).astype(BF16)


def slot_ids(requests, rows_each):
    owners, capacity = requests.shape
    slots = owners * capacity
    rows = jnp.broadcast_to(requests[:, None, :], (owners, capacity, capacity)).reshape(slots, capacity)
    slot = lax.broadcasted_iota(jnp.int32, (slots, capacity), 0)
    lane = lax.broadcasted_iota(jnp.int32, (slots, capacity), 1)
    local = jnp.sum(jnp.where(slot % capacity == lane, jnp.maximum(rows, 0), 0), axis=1, keepdims=True)
    return local + slot[:, :1] // capacity * rows_each


def near_kernel(
    proj_count, rows_each, keys, requests_ref, pick_ref, tokens_ref, cot_ref, fetched_ref, *refs
):
    pick_grad_ref, queries_ref, slot_key_ref, counts_ref, wide_id_ref, proj_ref, held, sem = refs[-8:]
    for at, piece in placed(keys, refs[:-8]):
        pltpu.make_async_copy(piece, held.at[at], sem).start()
    x = lax.axis_index("groups")
    features = tokens_ref.shape[1]
    half = features // 2
    half_count = proj_count // 2
    parts = half_count * fetched_ref.shape[1] // held.shape[2]
    key = parts + half // LANES
    nkey = held.shape[0] * held.shape[2]
    wide_id = jnp.broadcast_to(slot_ids(requests_ref[...], rows_each), wide_id_ref.shape)
    wide_id_ref[...] = wide_id
    proj = (wide_id % nkey % proj_count).T[:proj_ref.shape[0]]
    proj_ref[...] = proj
    token_rows, slots = counts_ref.shape
    lane = lax.broadcasted_iota(jnp.int32, (token_rows, slots), 1)
    pick = pick_ref[...].T
    counts = jnp.zeros((token_rows, slots), F32)
    for k in range(pick.shape[1]):
        counts += jnp.where(pick[:, k:k + 1] == lane, 1.0, 0.0)
    counts_ref[...] = counts
    hot = one_hot_keys(x == 0, wide_id[:, :1], nkey)
    wait_for(held, sem)
    slot_key_ref[...] = dot(hot, lanes(held, range(key, held.shape[1])), PLAIN).astype(BF16)
    tokens = tokens_ref[:, pl.ds(pl.multiple_of(x * half, half), half)]
    queries_ref[...] = dot(tokens, lanes(held, range(parts, key)), LAST)
    pick_grad_ref[...] = value_products(
        x * half_count, half_count, held, 0, proj[:1], cot_ref[...], fetched_ref[...],
        jnp.zeros(pick_grad_ref.shape, F32),
    )


def dense_kernel(
    rank, width, proj_count, keys, core_ref, *refs
):
    inputs, refs = refs[:9], refs[9:]
    pieces = refs[:len(keys)]
    (out_ref, grad_ref, near_held, far_held, queries_held, pick_held, counts_held, cot_held, fetched_held,
     row_id_held, proj_held, near_key_held, tokens_held, mixed_values, query_grad, out_held, grad_held, piece_sem, in_sem, out_sem) = refs[len(keys):]
    held_inputs = (
        row_id_held, tokens_held, near_key_held, proj_held, queries_held, counts_held, cot_held, fetched_held, pick_held
    )
    x = lax.axis_index("groups")
    token_rows, features = tokens_held.shape
    slots, value_width = fetched_held.shape
    columns = far_held.shape[2]
    half = features // 2
    half_count = proj_count // 2
    parts = half_count * value_width // columns
    key = parts + half // LANES
    spots = list(placed(keys, pieces))
    far = [spot for spot, k in zip(spots, keys) if k[3]]
    near = [spot for spot, k in zip(spots, keys) if not k[3]]
    query_blocks = pl.ds(parts, far_held.shape[1] - parts)
    copies = [pltpu.make_async_copy(a, b, in_sem.at[i]) for i, (a, b) in enumerate(zip(inputs, held_inputs))]
    copies[0].start()
    for at, piece in far:
        pltpu.make_async_copy(piece.at[query_blocks], far_held.at[at, query_blocks], piece_sem.at[0]).start()
    for copy in copies[1:6]:
        copy.start()
    for at, piece in far:
        pltpu.make_async_copy(piece.at[pl.ds(0, parts)], far_held.at[at, pl.ds(0, parts)], piece_sem.at[1]).start()
    for copy in copies[6:]:
        copy.start()
    for at, piece in near:
        pltpu.make_async_copy(piece, near_held.at[at], piece_sem.at[2]).start()

    copies[0].wait()
    hot = one_hot_keys(x != 0, row_id_held[:, :1], far_held.shape[0] * columns)
    wait_for(far_held.at[:, query_blocks], piece_sem.at[0])
    for copy in copies[1:6]:
        copy.wait()
    far_key = dot(hot, lanes(far_held, range(key, far_held.shape[1])), PLAIN).astype(BF16)
    near_key = near_key_held[...]
    slot_row = jnp.where(x == 0, near_key, far_key)
    slot_col = jnp.where(x == 0, far_key, near_key)
    tokens = tokens_held[:, pl.ds(pl.multiple_of((1 - x) * half, half), half)]
    queries = (dot(tokens, lanes(far_held, range(parts, key)), LAST) + queries_held[...]).astype(BF16)
    block = [queries[:, r * width:(r + 1) * width] for r in range(2 * rank)]
    row_scores = [dot(block[r], slot_row, LAST) for r in range(rank)]
    col_scores = [dot(block[rank + r], slot_col, LAST) for r in range(rank)]
    wait_for(far_held.at[:, pl.ds(0, parts)], piece_sem.at[1])
    for copy in copies[6:]:
        copy.wait()
    wait_for(near_held, piece_sem.at[2])
    proj = proj_held[:1]
    fetched = fetched_held[...]
    pick_grad = value_products(
        (1 - x) * half_count, half_count, far_held, 0, proj, cot_held[...], fetched, pick_held[...]
    )
    col_mixed = [sum(core_ref[r, s] * col_scores[s] for s in range(rank)) for r in range(rank)]
    row_mixed = [sum(row_scores[r] * core_ref[r, s] for r in range(rank)) for s in range(rank)]
    score = sum(row_scores[r] * col_mixed[r] for r in range(rank))
    gate = 1.0 / (1.0 + jnp.exp(-score))
    counts = counts_held[...]
    weights = (counts * gate.astype(BF16).astype(F32)).astype(BF16)
    slope = gate * (1.0 - gate)
    for i in range(proj_count):
        e = (x if i < half_count else 1 - x) * half_count + i % half_count
        mixed = dot(jnp.where(proj == e, weights, jnp.zeros((), BF16)), fetched, PLAIN)
        mixed_values[:, i * value_width:(i + 1) * value_width] = mixed.astype(BF16)

    members = far_held.shape[0] // 4
    step = features // 4
    sides = ((near_held, x), (far_held, 1 - x))
    for c in range(4):
        cols = pl.ds(c * step, step)
        block = jnp.concatenate([
            jnp.concatenate([held[m, :parts].reshape(-1, LANES) for m in range(c * members, (c + 1) * members)], axis=1)
            for held, _ in sides
        ], axis=0)
        out_held[:, cols] = dot(mixed_values[...], block, PLAIN).astype(BF16)
        pltpu.make_async_copy(out_held.at[:, cols], out_ref.at[:, cols], out_sem.at[0]).start()
    score_grad = pick_grad * slope
    for i, factor in enumerate(col_mixed + row_mixed):
        slot_key = slot_row if i < rank else slot_col
        grad = ((score_grad * factor).astype(BF16).astype(F32) * counts).astype(BF16)
        query_grad[:, i * width:(i + 1) * width] = dot(grad, slot_key, PLAIN).astype(BF16)
    for c in range(4):
        held, side = sides[c // 2]
        blocks = step // LANES
        first = parts + (c % 2) * blocks
        cols = pl.ds(pl.multiple_of(side * half + (c % 2) * step, step), step)
        grad_held[:, cols] = dot(query_grad[...], lanes(held, range(first, first + blocks)), PLAIN).astype(BF16)
        pltpu.make_async_copy(grad_held.at[:, cols], grad_ref.at[:, cols], out_sem.at[1]).start()
    pltpu.make_async_copy(out_held, out_ref, out_sem.at[0]).wait()
    pltpu.make_async_copy(grad_held, grad_ref, out_sem.at[1]).wait()


def vmem():
    return pl.BlockSpec(memory_space=pltpu.VMEM)


def smem():
    return pl.BlockSpec(memory_space=pltpu.SMEM)


def anywhere():
    return pl.BlockSpec(memory_space=pl.ANY)


def pieces_path(tokens, cotangent, w_query, key_row, key_col, tucker_core, proj_part, requests, table, row_id,
                slot_proj, pick_slot, nkey, proj_count):
    rank = tucker_core.shape[0]
    width = key_row.shape[1]
    token_rows, features = tokens.shape
    slots = row_id.shape[0]
    value_width = table.shape[1]
    columns = w_query.shape[1]
    own_near, own_far = own_halves(w_query, key_row, key_col, proj_part)
    params = pltpu.CompilerParams(vmem_limit_bytes=VMEM_LIMIT)
    members = nkey // columns
    plane = jax.ShapeDtypeStruct((token_rows, slots), F32)
    partial = jax.ShapeDtypeStruct((token_rows, 2 * rank * width), F32)
    held = pltpu.VMEM((members,) + own_near.shape, BF16)

    def near_work(near, fetched):
        return pl.pallas_call(
            functools.partial(near_kernel, proj_count, table.shape[0], tuple(near)),
            out_shape=(
                plane, partial, jax.ShapeDtypeStruct((slots, width), BF16), plane,
                jax.ShapeDtypeStruct((slots, LANES), jnp.int32), jax.ShapeDtypeStruct((8, slots), jnp.int32),
            ),
            in_specs=[vmem()] * 5 + [anywhere()] * len(near),
            out_specs=(vmem(),) * 6,
            scratch_shapes=[held, pltpu.SemaphoreType.DMA],
            compiler_params=params,
            cost_estimate=pl.CostEstimate(flops=5 * 10**9, bytes_accessed=10**7, transcendentals=0),
            name="near",
        )(requests, pick_slot.T, tokens, cotangent, fetched.reshape(slots, value_width), *near.values())

    pieces, fetched, near_done = gather_pieces(own_near, own_far, requests, table, near_work)
    pick_grad, queries, near_key, counts, wide_id, slot_proj = near_done
    keys = tuple(pieces)
    tall = (token_rows, features)
    return pl.pallas_call(
        functools.partial(dense_kernel, rank, width, proj_count, keys),
        out_shape=(jax.ShapeDtypeStruct(tall, BF16),) * 2,
        in_specs=[smem()] + [anywhere()] * (9 + len(keys)),
        out_specs=(anywhere(), anywhere()),
        scratch_shapes=[
            held,
            held,
            pltpu.VMEM(partial.shape, F32),
            pltpu.VMEM(plane.shape, F32),
            pltpu.VMEM(plane.shape, F32),
            pltpu.VMEM(tall, BF16),
            pltpu.VMEM((slots, value_width), BF16),
            pltpu.VMEM(wide_id.shape, jnp.int32),
            pltpu.VMEM(slot_proj.shape, jnp.int32),
            pltpu.VMEM(near_key.shape, BF16),
            pltpu.VMEM(tall, BF16),
            pltpu.VMEM((token_rows, proj_count * value_width), BF16),
            pltpu.VMEM(partial.shape, BF16),
            pltpu.VMEM(tall, BF16),
            pltpu.VMEM(tall, BF16),
            pltpu.SemaphoreType.DMA((3,)),
            pltpu.SemaphoreType.DMA((9,)),
            pltpu.SemaphoreType.DMA((2,)),
        ],
        compiler_params=params,
        cost_estimate=pl.CostEstimate(flops=10**10, bytes_accessed=2 * 10**7, transcendentals=10**5),
        name="dense",
    )(
        tucker_core, wide_id, tokens, near_key, slot_proj, queries, counts, cotangent,
        fetched.reshape(slots, value_width), pick_grad, *pieces.values(),
    )


def whole_path(tokens, cotangent, w_query, key_row, key_col, tucker_core, proj_part, requests, table, row_id,
               slot_proj, pick_slot, nkey, proj_count):
    rank = tucker_core.shape[0]
    width = key_row.shape[1]
    slots = row_id.shape[0]
    fetched = returned_rows(found_rows(wanted_rows(requests), table)).reshape(slots, -1)
    query_full = lax.all_gather(w_query.T, "mem", axis=0, tiled=True)
    keys = lax.all_gather(jnp.concatenate([key_row, key_col], axis=1), "mem", axis=0, tiled=True)
    proj_full = lax.all_gather(proj_part, "mem", axis=1, tiled=True)
    key_at = jnp.arange(nkey, dtype=jnp.int32)[None, :]
    row_hot = ((row_id // nkey)[:, None] == key_at).astype(BF16)
    col_hot = ((row_id % nkey)[:, None] == key_at).astype(BF16)
    slot_row = dot(row_hot, keys[:, :width], PLAIN).astype(BF16)
    slot_col = dot(col_hot, keys[:, width:], PLAIN).astype(BF16)
    spread = jnp.where(
        slot_proj[:, None, None] == jnp.arange(proj_count, dtype=jnp.int32)[None, :, None],
        fetched[:, None, :], jnp.zeros((), BF16)
    ).reshape(slots, -1)
    counts = jnp.sum(
        (pick_slot[:, :, None] == jnp.arange(slots, dtype=jnp.int32)[None, None, :]).astype(F32), axis=1
    )
    queries = dot(tokens, query_full, LAST).astype(BF16)
    row_scores = [dot(queries[:, r * width:(r + 1) * width], slot_row, LAST) for r in range(rank)]
    col_scores = [
        dot(queries[:, (rank + r) * width:(rank + r + 1) * width], slot_col, LAST) for r in range(rank)
    ]
    col_mixed = [sum(tucker_core[r, s] * col_scores[s] for s in range(rank)) for r in range(rank)]
    row_mixed = [sum(row_scores[r] * tucker_core[r, s] for r in range(rank)) for s in range(rank)]
    score = sum(row_scores[r] * col_mixed[r] for r in range(rank))
    gate = jax.nn.sigmoid(score)
    weights = counts * gate.astype(BF16).astype(F32)
    mixed = counted_dot(weights, spread, PLAIN).astype(BF16)
    memory_out = dot(mixed, proj_full, PLAIN)
    value_grad = dot(cotangent, proj_full, LAST).astype(BF16)
    pick_grad = dot(value_grad, spread, LAST)
    score_grad = pick_grad * gate * (1.0 - gate)
    blocks = []
    for mixed_scores, slot_key in ((col_mixed, slot_row), (row_mixed, slot_col)):
        for r in range(rank):
            grad = (score_grad * mixed_scores[r]).astype(BF16).astype(F32) * counts
            blocks.append(counted_dot(grad, slot_key, PLAIN).astype(BF16))
    query_grad = jnp.concatenate(blocks, axis=1)
    token_grad = dot(query_grad, query_full, PLAIN)
    return memory_out.astype(BF16), token_grad.astype(BF16)


def shards(
    mem, tokens, cotangent, w_query, key_row, key_col, tucker_core, table, w_proj, send_ids, pick_slot
):
    proj_count, value_width, _ = w_proj.shape
    requests = send_ids[0]
    owners, capacity = requests.shape
    slots = owners * capacity
    nkey = key_row.shape[0] * mem
    row_id = jnp.maximum(requests, 0) + jnp.arange(owners, dtype=jnp.int32)[:, None] * table.shape[0]
    row_id = row_id.reshape(slots)
    slot_proj = (row_id % nkey) % proj_count
    proj_part = w_proj.reshape(proj_count * value_width, -1)
    path = pieces_path if mem == 16 and w_proj.shape[2] == LANES else whole_path
    return path(tokens, cotangent, w_query, key_row, key_col, tucker_core, proj_part, requests, table, row_id,
                slot_proj, pick_slot, nkey, proj_count)


def solution(mesh):
    in_specs = (
        P(("groups", "mem"), None),
        P(("groups", "mem"), None),
        P(None, "mem"),
        P("mem", None),
        P("mem", None),
        P(),
        P("mem", None),
        P(None, None, "mem"),
        P(("groups", "mem"), None, None),
        P(("groups", "mem"), None),
    )
    out_specs = (P(("groups", "mem"), None), P(("groups", "mem"), None))
    body = functools.partial(shards, mesh.shape["mem"])
    return jax.shard_map(body, mesh=mesh, in_specs=in_specs, out_specs=out_specs, check_vma=False)
```

```python
import functools

import jax
import jax.numpy as jnp
from jax import lax
from jax.experimental import pallas as pl
from jax.experimental.pallas import tpu as pltpu
from jax.sharding import PartitionSpec as P

F32 = jnp.float32
BF16 = jnp.bfloat16
RING = (0, 2, 3, 1)
LANES = 128
LAST = ((1,), (1,))
PLAIN = ((1,), (0,))
VMEM_LIMIT = 56 * 1024 * 1024


def dot(a, b, dims):
    return lax.dot_general(a, b, (dims, ((), ())), preferred_element_type=F32)


def two_terms(x):
    high = x.astype(BF16)
    return high, (x - high.astype(F32)).astype(BF16)


def counted_dot(x, b, dims):
    high, low = two_terms(x)
    return dot(high, b, dims) + dot(low, b, dims)


def wanted_rows(requests):
    return lax.all_to_all(requests, "mem", split_axis=0, concat_axis=0, tiled=True)


def found_rows(wanted, table):
    found = jnp.take(table, jnp.maximum(wanted, 0).reshape(-1), axis=0, mode="clip")
    return found.reshape(wanted.shape + (table.shape[1],))


def returned_rows(found):
    return lax.all_to_all(found, "mem", split_axis=0, concat_axis=0, tiled=True)


def place(z, y, core):
    return (z * 2 + y) * 2 + core


def everywhere(move):
    pairs = []
    for z in range(4):
        for y in range(2):
            for core in range(2):
                pairs.append((place(z, y, core), place(*move(z, y, core))))
    return pairs


def next_z(x):
    step = {RING[i]: RING[(i + 1) % 4] for i in range(4)}
    return lax.ppermute(x, "mem", everywhere(lambda z, y, c: (step[z], y, c)))


def other_y(x):
    return lax.ppermute(x, "mem", everywhere(lambda z, y, c: (z, 1 - y, c)))


def other_core(x):
    return lax.ppermute(x, "mem", everywhere(lambda z, y, c: (z, y, 1 - c)))


def other_x(x):
    return lax.ppermute(x, "groups", [(0, 1), (1, 0)])


def ring_source(z, steps):
    index = jnp.where(z == 0, 0, jnp.where(z == 2, 1, jnp.where(z == 3, 2, 3)))
    index = (index + 4 - steps) % 4
    return jnp.where(index == 0, 0, jnp.where(index == 1, 2, jnp.where(index == 2, 3, 1)))


def tie(*values):
    return lax.optimization_barrier(values)


def halves_kernel(query_ref, key_row_ref, key_col_ref, proj_ref, near_ref, far_ref):
    x = lax.axis_index("groups")
    parts = proj_ref.shape[1]
    blocks = query_ref.shape[1] // LANES // 2
    for target, half in ((near_ref, x), (far_ref, 1 - x)):
        target[:parts] = proj_ref[half]
        for j in range(blocks):
            target[parts + j] = query_ref[:, pl.ds(pl.multiple_of((half * blocks + j) * LANES, LANES), LANES)]
        for j in range(key_row_ref.shape[1] // LANES):
            cols = slice(j * LANES, (j + 1) * LANES)
            target[parts + blocks + j] = jnp.where(half == 0, key_row_ref[:, cols], key_col_ref[:, cols])


def own_halves(w_query, key_row, key_col, proj_part):
    features, columns = w_query.shape
    proj = proj_part.reshape(2, -1, columns, LANES)
    blocks = proj.shape[1] + (features // 2 + key_row.shape[1]) // LANES
    half = jax.ShapeDtypeStruct((blocks, columns, LANES), BF16)
    return pl.pallas_call(
        halves_kernel,
        out_shape=(half, half),
        in_specs=[vmem()] * 4,
        out_specs=(vmem(), vmem()),
        compiler_params=pltpu.CompilerParams(vmem_limit_bytes=VMEM_LIMIT),
        cost_estimate=pl.CostEstimate(flops=0, bytes_accessed=4 * 10**6, transcendentals=0),
        name="halves",
    )(w_query.T, key_row, key_col, proj)


def other_cores(first, second):
    first = other_core(first)
    second, first = tie(second, first)
    return first, other_core(second)


def gather_pieces(own_near, own_far, requests, table, near_work):
    pieces = {(0, 0, 0, 0): own_near, (0, 0, 0, 1): own_far}
    z1, y0, wanted, pieces[0, 0, 1, 0], pieces[0, 0, 1, 1] = tie(
        next_z(own_near), other_y(own_near), wanted_rows(requests), other_core(own_near), other_core(own_far)
    )
    pieces[1, 0, 0, 0], pieces[0, 1, 0, 0] = z1, y0
    z2, y1, y0f, found, pieces[1, 0, 1, 0], pieces[0, 1, 1, 0] = tie(
        next_z(z1), other_y(z1), other_x(y0), found_rows(wanted, table), *other_cores(z1, y0)
    )
    pieces[2, 0, 0, 0], pieces[1, 1, 0, 0], pieces[0, 1, 0, 1] = z2, y1, y0f
    z3, y2, y1f, pieces[2, 0, 1, 0], pieces[1, 1, 1, 0] = tie(
        next_z(z2), other_y(z2), other_x(y1), *other_cores(z2, y1)
    )
    pieces[3, 0, 0, 0], pieces[2, 1, 0, 0], pieces[1, 1, 0, 1] = z3, y2, y1f
    z1f, y3, z3f, fetched, pieces[3, 0, 1, 0], pieces[0, 1, 1, 1], pieces[2, 1, 1, 0] = tie(
        next_z(own_far), other_y(z3), other_x(z3), returned_rows(found), *other_cores(z3, y0f), other_core(y2)
    )
    pieces[1, 0, 0, 1], pieces[3, 1, 0, 0], pieces[3, 0, 0, 1] = z1f, y3, z3f
    pieces[3, 1, 1, 0] = other_core(y3)
    near = {key: piece for key, piece in pieces.items() if key[3] == 0}
    z2f, y3f, y2f = next_z(z1f), other_y(z3f), other_x(y2)
    near_done, y1f, z1f, z3f = tie(near_work(near, fetched), y1f, z1f, z3f)
    z2f, y3f, y2f, pieces[1, 1, 1, 1], pieces[1, 0, 1, 1], pieces[3, 0, 1, 1] = tie(
        z2f, y3f, y2f, other_core(y1f), other_core(z1f), other_core(z3f)
    )
    pieces[2, 0, 0, 1], pieces[3, 1, 0, 1], pieces[2, 1, 0, 1] = z2f, y3f, y2f
    pieces[2, 0, 1, 1], pieces[3, 1, 1, 1], pieces[2, 1, 1, 1] = other_core(z2f), other_core(y3f), other_core(y2f)
    return pieces, fetched, near_done


def placed(keys, pieces):
    me = lax.axis_index("mem")
    z, y, core = me // 4, (me // 2) % 2, me % 2
    for (steps, side, other, far), piece in zip(keys, pieces):
        at = place(ring_source(z, steps), 1 - y if side else y, 1 - core if other else core)
        yield at, piece


def wait_for(held, sem):
    pltpu.make_async_copy(held, held, sem).wait()


def lanes(held, blocks):
    return jnp.concatenate([held[:, j].reshape(-1, LANES) for j in blocks], axis=1)


def value_products(first, count, held, base, proj, cot, fetched, pick_grad):
    value_width = fetched.shape[1]
    parts = value_width // held.shape[-2]
    for e in range(count):
        block = jnp.concatenate(
            [held[m, base + e * parts:base + (e + 1) * parts].reshape(value_width, LANES) for m in range(held.shape[0])],
            axis=1,
        )
        grad = dot(cot, block, LAST).astype(BF16)
        pick_grad = jnp.where(proj == first + e, dot(grad, fetched, LAST), pick_grad)
    return pick_grad


def one_hot_keys(use_row, row_id, nkey):
    key_at = lax.broadcasted_iota(jnp.int32, (row_id.shape[0], nkey), 1)
    picked = jnp.where(use_row, row_id // nkey, row_id % nkey)
    return jnp.where(picked == key_at, 1.0, 0.0).astype(BF16)


def slot_ids(requests, rows_each):
    owners, capacity = requests.shape
    slots = owners * capacity
    rows = jnp.broadcast_to(requests[:, None, :], (owners, capacity, capacity)).reshape(slots, capacity)
    slot = lax.broadcasted_iota(jnp.int32, (slots, capacity), 0)
    lane = lax.broadcasted_iota(jnp.int32, (slots, capacity), 1)
    local = jnp.sum(jnp.where(slot % capacity == lane, jnp.maximum(rows, 0), 0), axis=1, keepdims=True)
    return local + slot[:, :1] // capacity * rows_each


def near_kernel(
    proj_count, rows_each, keys, requests_ref, pick_ref, tokens_ref, cot_ref, fetched_ref, *refs
):
    pick_grad_ref, queries_ref, slot_key_ref, counts_ref, wide_id_ref, proj_ref, held, sem = refs[-8:]
    for at, piece in placed(keys, refs[:-8]):
        pltpu.make_async_copy(piece, held.at[at], sem).start()
    x = lax.axis_index("groups")
    features = tokens_ref.shape[1]
    half = features // 2
    half_count = proj_count // 2
    parts = half_count * fetched_ref.shape[1] // held.shape[2]
    key = parts + half // LANES
    nkey = held.shape[0] * held.shape[2]
    wide_id = jnp.broadcast_to(slot_ids(requests_ref[...], rows_each), wide_id_ref.shape)
    wide_id_ref[...] = wide_id
    proj = (wide_id % nkey % proj_count).T[:proj_ref.shape[0]]
    proj_ref[...] = proj
    token_rows, slots = counts_ref.shape
    lane = lax.broadcasted_iota(jnp.int32, (token_rows, slots), 1)
    pick = pick_ref[...].T
    counts = jnp.zeros((token_rows, slots), F32)
    for k in range(pick.shape[1]):
        counts += jnp.where(pick[:, k:k + 1] == lane, 1.0, 0.0)
    counts_ref[...] = counts
    hot = one_hot_keys(x == 0, wide_id[:, :1], nkey)
    wait_for(held, sem)
    slot_key_ref[...] = dot(hot, lanes(held, range(key, held.shape[1])), PLAIN).astype(BF16)
    tokens = tokens_ref[:, pl.ds(pl.multiple_of(x * half, half), half)]
    queries_ref[...] = dot(tokens, lanes(held, range(parts, key)), LAST)
    pick_grad_ref[...] = value_products(
        x * half_count, half_count, held, 0, proj[:1], cot_ref[...], fetched_ref[...],
        jnp.zeros(pick_grad_ref.shape, F32),
    )


def dense_kernel(
    rank, width, proj_count, keys, core_ref, *refs
):
    inputs, refs = refs[:9], refs[9:]
    pieces = refs[:len(keys)]
    (out_ref, grad_ref, near_held, far_held, queries_held, pick_held, counts_held, cot_held, fetched_held,
     row_id_held, proj_held, near_key_held, tokens_held, mixed_values, query_grad, out_held, grad_held, piece_sem, in_sem, out_sem) = refs[len(keys):]
    held_inputs = (
        row_id_held, tokens_held, near_key_held, proj_held, queries_held, counts_held, cot_held, fetched_held, pick_held
    )
    x = lax.axis_index("groups")
    token_rows, features = tokens_held.shape
    slots, value_width = fetched_held.shape
    columns = far_held.shape[2]
    half = features // 2
    half_count = proj_count // 2
    parts = half_count * value_width // columns
    key = parts + half // LANES
    spots = list(placed(keys, pieces))
    far = [spot for spot, k in zip(spots, keys) if k[3]]
    near = [spot for spot, k in zip(spots, keys) if not k[3]]
    query_blocks = pl.ds(parts, far_held.shape[1] - parts)
    copies = [pltpu.make_async_copy(a, b, in_sem.at[i]) for i, (a, b) in enumerate(zip(inputs, held_inputs))]
    copies[0].start()
    for at, piece in far:
        pltpu.make_async_copy(piece.at[query_blocks], far_held.at[at, query_blocks], piece_sem.at[0]).start()
    for i in (1, 2, 4):
        copies[i].start()
    for at, piece in far:
        pltpu.make_async_copy(piece.at[pl.ds(0, parts)], far_held.at[at, pl.ds(0, parts)], piece_sem.at[1]).start()
    for i in (6, 7, 3, 8, 5):
        copies[i].start()
    for at, piece in near:
        pltpu.make_async_copy(piece, near_held.at[at], piece_sem.at[2]).start()

    copies[0].wait()
    hot = one_hot_keys(x != 0, row_id_held[:, :1], far_held.shape[0] * columns)
    wait_for(far_held.at[:, query_blocks], piece_sem.at[0])
    far_key = dot(hot, lanes(far_held, range(key, far_held.shape[1])), PLAIN).astype(BF16)
    copies[1].wait()
    copies[2].wait()
    near_key = near_key_held[...]
    slot_row = jnp.where(x == 0, near_key, far_key)
    slot_col = jnp.where(x == 0, far_key, near_key)
    tokens = tokens_held[:, pl.ds(pl.multiple_of((1 - x) * half, half), half)]
    queries = dot(tokens, lanes(far_held, range(parts, key)), LAST)
    copies[4].wait()
    queries = (queries + queries_held[...]).astype(BF16)
    block = [queries[:, r * width:(r + 1) * width] for r in range(2 * rank)]
    row_scores = [dot(block[r], slot_row, LAST) for r in range(rank)]
    col_scores = [dot(block[rank + r], slot_col, LAST) for r in range(rank)]
    wait_for(far_held.at[:, pl.ds(0, parts)], piece_sem.at[1])
    for i in (6, 7, 3, 8, 5):
        copies[i].wait()
    proj = proj_held[:1]
    fetched = fetched_held[...]
    pick_grad = value_products(
        (1 - x) * half_count, half_count, far_held, 0, proj, cot_held[...], fetched, pick_held[...]
    )
    col_mixed = [sum(core_ref[r, s] * col_scores[s] for s in range(rank)) for r in range(rank)]
    row_mixed = [sum(row_scores[r] * core_ref[r, s] for r in range(rank)) for s in range(rank)]
    score = sum(row_scores[r] * col_mixed[r] for r in range(rank))
    gate = 1.0 / (1.0 + jnp.exp(-score))
    counts = counts_held[...]
    weights = (counts * gate.astype(BF16).astype(F32)).astype(BF16)
    slope = gate * (1.0 - gate)
    for i in range(proj_count):
        e = (x if i < half_count else 1 - x) * half_count + i % half_count
        mixed = dot(jnp.where(proj == e, weights, jnp.zeros((), BF16)), fetched, PLAIN)
        mixed_values[:, i * value_width:(i + 1) * value_width] = mixed.astype(BF16)

    wait_for(near_held, piece_sem.at[2])
    members = far_held.shape[0] // 4
    step = features // 4
    sides = ((near_held, x), (far_held, 1 - x))
    for c in range(4):
        cols = pl.ds(c * step, step)
        block = jnp.concatenate([
            jnp.concatenate([held[m, :parts].reshape(-1, LANES) for m in range(c * members, (c + 1) * members)], axis=1)
            for held, _ in sides
        ], axis=0)
        out_held[:, cols] = dot(mixed_values[...], block, PLAIN).astype(BF16)
        pltpu.make_async_copy(out_held.at[:, cols], out_ref.at[:, cols], out_sem.at[0]).start()
    score_grad = pick_grad * slope
    for i, factor in enumerate(col_mixed + row_mixed):
        slot_key = slot_row if i < rank else slot_col
        grad = ((score_grad * factor).astype(BF16).astype(F32) * counts).astype(BF16)
        query_grad[:, i * width:(i + 1) * width] = dot(grad, slot_key, PLAIN).astype(BF16)
    for c in range(4):
        held, side = sides[c // 2]
        blocks = step // LANES
        first = parts + (c % 2) * blocks
        cols = pl.ds(pl.multiple_of(side * half + (c % 2) * step, step), step)
        grad_held[:, cols] = dot(query_grad[...], lanes(held, range(first, first + blocks)), PLAIN).astype(BF16)
        pltpu.make_async_copy(grad_held.at[:, cols], grad_ref.at[:, cols], out_sem.at[1]).start()
    pltpu.make_async_copy(out_held, out_ref, out_sem.at[0]).wait()
    pltpu.make_async_copy(grad_held, grad_ref, out_sem.at[1]).wait()


def vmem():
    return pl.BlockSpec(memory_space=pltpu.VMEM)


def smem():
    return pl.BlockSpec(memory_space=pltpu.SMEM)


def anywhere():
    return pl.BlockSpec(memory_space=pl.ANY)


def pieces_path(tokens, cotangent, w_query, key_row, key_col, tucker_core, proj_part, requests, table, row_id,
                slot_proj, pick_slot, nkey, proj_count):
    rank = tucker_core.shape[0]
    width = key_row.shape[1]
    token_rows, features = tokens.shape
    slots = row_id.shape[0]
    value_width = table.shape[1]
    columns = w_query.shape[1]
    own_near, own_far = own_halves(w_query, key_row, key_col, proj_part)
    params = pltpu.CompilerParams(vmem_limit_bytes=VMEM_LIMIT)
    members = nkey // columns
    plane = jax.ShapeDtypeStruct((token_rows, slots), F32)
    partial = jax.ShapeDtypeStruct((token_rows, 2 * rank * width), F32)
    held = pltpu.VMEM((members,) + own_near.shape, BF16)

    def near_work(near, fetched):
        return pl.pallas_call(
            functools.partial(near_kernel, proj_count, table.shape[0], tuple(near)),
            out_shape=(
                plane, partial, jax.ShapeDtypeStruct((slots, width), BF16), plane,
                jax.ShapeDtypeStruct((slots, LANES), jnp.int32), jax.ShapeDtypeStruct((8, slots), jnp.int32),
            ),
            in_specs=[vmem()] * 5 + [anywhere()] * len(near),
            out_specs=(vmem(),) * 6,
            scratch_shapes=[held, pltpu.SemaphoreType.DMA],
            compiler_params=params,
            cost_estimate=pl.CostEstimate(flops=5 * 10**9, bytes_accessed=10**7, transcendentals=0),
            name="near",
        )(requests, pick_slot.T, tokens, cotangent, fetched.reshape(slots, value_width), *near.values())

    pieces, fetched, near_done = gather_pieces(own_near, own_far, requests, table, near_work)
    pick_grad, queries, near_key, counts, wide_id, slot_proj = near_done
    keys = tuple(pieces)
    tall = (token_rows, features)
    return pl.pallas_call(
        functools.partial(dense_kernel, rank, width, proj_count, keys),
        out_shape=(jax.ShapeDtypeStruct(tall, BF16),) * 2,
        in_specs=[smem()] + [anywhere()] * (9 + len(keys)),
        out_specs=(anywhere(), anywhere()),
        scratch_shapes=[
            held,
            held,
            pltpu.VMEM(partial.shape, F32),
            pltpu.VMEM(plane.shape, F32),
            pltpu.VMEM(plane.shape, F32),
            pltpu.VMEM(tall, BF16),
            pltpu.VMEM((slots, value_width), BF16),
            pltpu.VMEM(wide_id.shape, jnp.int32),
            pltpu.VMEM(slot_proj.shape, jnp.int32),
            pltpu.VMEM(near_key.shape, BF16),
            pltpu.VMEM(tall, BF16),
            pltpu.VMEM((token_rows, proj_count * value_width), BF16),
            pltpu.VMEM(partial.shape, BF16),
            pltpu.VMEM(tall, BF16),
            pltpu.VMEM(tall, BF16),
            pltpu.SemaphoreType.DMA((3,)),
            pltpu.SemaphoreType.DMA((9,)),
            pltpu.SemaphoreType.DMA((2,)),
        ],
        compiler_params=params,
        cost_estimate=pl.CostEstimate(flops=10**10, bytes_accessed=2 * 10**7, transcendentals=10**5),
        name="dense",
    )(
        tucker_core, wide_id, tokens, near_key, slot_proj, queries, counts, cotangent,
        fetched.reshape(slots, value_width), pick_grad, *pieces.values(),
    )


def whole_path(tokens, cotangent, w_query, key_row, key_col, tucker_core, proj_part, requests, table, row_id,
               slot_proj, pick_slot, nkey, proj_count):
    rank = tucker_core.shape[0]
    width = key_row.shape[1]
    slots = row_id.shape[0]
    fetched = returned_rows(found_rows(wanted_rows(requests), table)).reshape(slots, -1)
    query_full = lax.all_gather(w_query.T, "mem", axis=0, tiled=True)
    keys = lax.all_gather(jnp.concatenate([key_row, key_col], axis=1), "mem", axis=0, tiled=True)
    proj_full = lax.all_gather(proj_part, "mem", axis=1, tiled=True)
    key_at = jnp.arange(nkey, dtype=jnp.int32)[None, :]
    row_hot = ((row_id // nkey)[:, None] == key_at).astype(BF16)
    col_hot = ((row_id % nkey)[:, None] == key_at).astype(BF16)
    slot_row = dot(row_hot, keys[:, :width], PLAIN).astype(BF16)
    slot_col = dot(col_hot, keys[:, width:], PLAIN).astype(BF16)
    spread = jnp.where(
        slot_proj[:, None, None] == jnp.arange(proj_count, dtype=jnp.int32)[None, :, None],
        fetched[:, None, :], jnp.zeros((), BF16)
    ).reshape(slots, -1)
    counts = jnp.sum(
        (pick_slot[:, :, None] == jnp.arange(slots, dtype=jnp.int32)[None, None, :]).astype(F32), axis=1
    )
    queries = dot(tokens, query_full, LAST).astype(BF16)
    row_scores = [dot(queries[:, r * width:(r + 1) * width], slot_row, LAST) for r in range(rank)]
    col_scores = [
        dot(queries[:, (rank + r) * width:(rank + r + 1) * width], slot_col, LAST) for r in range(rank)
    ]
    col_mixed = [sum(tucker_core[r, s] * col_scores[s] for s in range(rank)) for r in range(rank)]
    row_mixed = [sum(row_scores[r] * tucker_core[r, s] for r in range(rank)) for s in range(rank)]
    score = sum(row_scores[r] * col_mixed[r] for r in range(rank))
    gate = jax.nn.sigmoid(score)
    weights = counts * gate.astype(BF16).astype(F32)
    mixed = counted_dot(weights, spread, PLAIN).astype(BF16)
    memory_out = dot(mixed, proj_full, PLAIN)
    value_grad = dot(cotangent, proj_full, LAST).astype(BF16)
    pick_grad = dot(value_grad, spread, LAST)
    score_grad = pick_grad * gate * (1.0 - gate)
    blocks = []
    for mixed_scores, slot_key in ((col_mixed, slot_row), (row_mixed, slot_col)):
        for r in range(rank):
            grad = (score_grad * mixed_scores[r]).astype(BF16).astype(F32) * counts
            blocks.append(counted_dot(grad, slot_key, PLAIN).astype(BF16))
    query_grad = jnp.concatenate(blocks, axis=1)
    token_grad = dot(query_grad, query_full, PLAIN)
    return memory_out.astype(BF16), token_grad.astype(BF16)


def shards(
    mem, tokens, cotangent, w_query, key_row, key_col, tucker_core, table, w_proj, send_ids, pick_slot
):
    proj_count, value_width, _ = w_proj.shape
    requests = send_ids[0]
    owners, capacity = requests.shape
    slots = owners * capacity
    nkey = key_row.shape[0] * mem
    row_id = jnp.maximum(requests, 0) + jnp.arange(owners, dtype=jnp.int32)[:, None] * table.shape[0]
    row_id = row_id.reshape(slots)
    slot_proj = (row_id % nkey) % proj_count
    proj_part = w_proj.reshape(proj_count * value_width, -1)
    path = pieces_path if mem == 16 and w_proj.shape[2] == LANES else whole_path
    return path(tokens, cotangent, w_query, key_row, key_col, tucker_core, proj_part, requests, table, row_id,
                slot_proj, pick_slot, nkey, proj_count)


def solution(mesh):
    in_specs = (
        P(("groups", "mem"), None),
        P(("groups", "mem"), None),
        P(None, "mem"),
        P("mem", None),
        P("mem", None),
        P(),
        P("mem", None),
        P(None, None, "mem"),
        P(("groups", "mem"), None, None),
        P(("groups", "mem"), None),
    )
    out_specs = (P(("groups", "mem"), None), P(("groups", "mem"), None))
    body = functools.partial(shards, mesh.shape["mem"])
    return jax.shard_map(body, mesh=mesh, in_specs=in_specs, out_specs=out_specs, check_vma=False)
```

```python
import functools

import jax
import jax.numpy as jnp
from jax import lax
from jax.experimental import pallas as pl
from jax.experimental.pallas import tpu as pltpu
from jax.sharding import PartitionSpec as P

F32 = jnp.float32
BF16 = jnp.bfloat16
RING = (0, 2, 3, 1)
LANES = 128
LAST = ((1,), (1,))
PLAIN = ((1,), (0,))
VMEM_LIMIT = 56 * 1024 * 1024


def dot(a, b, dims):
    return lax.dot_general(a, b, (dims, ((), ())), preferred_element_type=F32)


def two_terms(x):
    high = x.astype(BF16)
    return high, (x - high.astype(F32)).astype(BF16)


def counted_dot(x, b, dims):
    high, low = two_terms(x)
    return dot(high, b, dims) + dot(low, b, dims)


def wanted_rows(requests):
    return lax.all_to_all(requests, "mem", split_axis=0, concat_axis=0, tiled=True)


def found_rows(wanted, table):
    found = jnp.take(table, jnp.maximum(wanted, 0).reshape(-1), axis=0, mode="clip")
    return found.reshape(wanted.shape + (table.shape[1],))


def returned_rows(found):
    return lax.all_to_all(found, "mem", split_axis=0, concat_axis=0, tiled=True)


def place(z, y, core):
    return (z * 2 + y) * 2 + core


def everywhere(move):
    pairs = []
    for z in range(4):
        for y in range(2):
            for core in range(2):
                pairs.append((place(z, y, core), place(*move(z, y, core))))
    return pairs


def next_z(x):
    step = {RING[i]: RING[(i + 1) % 4] for i in range(4)}
    return lax.ppermute(x, "mem", everywhere(lambda z, y, c: (step[z], y, c)))


def other_y(x):
    return lax.ppermute(x, "mem", everywhere(lambda z, y, c: (z, 1 - y, c)))


def other_core(x):
    return lax.ppermute(x, "mem", everywhere(lambda z, y, c: (z, y, 1 - c)))


def other_x(x):
    return lax.ppermute(x, "groups", [(0, 1), (1, 0)])


def ring_source(z, steps):
    index = jnp.where(z == 0, 0, jnp.where(z == 2, 1, jnp.where(z == 3, 2, 3)))
    index = (index + 4 - steps) % 4
    return jnp.where(index == 0, 0, jnp.where(index == 1, 2, jnp.where(index == 2, 3, 1)))


def tie(*values):
    return lax.optimization_barrier(values)


def halves_kernel(query_ref, key_row_ref, key_col_ref, proj_ref, near_ref, far_ref):
    x = lax.axis_index("groups")
    parts = proj_ref.shape[1]
    blocks = query_ref.shape[1] // LANES // 2
    for target, half in ((near_ref, x), (far_ref, 1 - x)):
        target[:parts] = proj_ref[half]
        for j in range(blocks):
            target[parts + j] = query_ref[:, pl.ds(pl.multiple_of((half * blocks + j) * LANES, LANES), LANES)]
        for j in range(key_row_ref.shape[1] // LANES):
            cols = slice(j * LANES, (j + 1) * LANES)
            target[parts + blocks + j] = jnp.where(half == 0, key_row_ref[:, cols], key_col_ref[:, cols])


def own_halves(w_query, key_row, key_col, proj_part):
    features, columns = w_query.shape
    proj = proj_part.reshape(2, -1, columns, LANES)
    blocks = proj.shape[1] + (features // 2 + key_row.shape[1]) // LANES
    half = jax.ShapeDtypeStruct((blocks, columns, LANES), BF16)
    return pl.pallas_call(
        halves_kernel,
        out_shape=(half, half),
        in_specs=[vmem()] * 4,
        out_specs=(vmem(), vmem()),
        compiler_params=pltpu.CompilerParams(vmem_limit_bytes=VMEM_LIMIT),
        cost_estimate=pl.CostEstimate(flops=0, bytes_accessed=4 * 10**6, transcendentals=0),
        name="halves",
    )(w_query.T, key_row, key_col, proj)


def other_cores(first, second):
    first = other_core(first)
    second, first = tie(second, first)
    return first, other_core(second)


def gather_pieces(own_near, own_far, requests, table, near_work):
    pieces = {(0, 0, 0, 0): own_near, (0, 0, 0, 1): own_far}
    z1, y0, wanted, pieces[0, 0, 1, 0], pieces[0, 0, 1, 1] = tie(
        next_z(own_near), other_y(own_near), wanted_rows(requests), other_core(own_near), other_core(own_far)
    )
    pieces[1, 0, 0, 0], pieces[0, 1, 0, 0] = z1, y0
    z2, y1, y0f, found, pieces[1, 0, 1, 0], pieces[0, 1, 1, 0] = tie(
        next_z(z1), other_y(z1), other_x(y0), found_rows(wanted, table), *other_cores(z1, y0)
    )
    pieces[2, 0, 0, 0], pieces[1, 1, 0, 0], pieces[0, 1, 0, 1] = z2, y1, y0f
    z3, y2, y1f, pieces[2, 0, 1, 0], pieces[1, 1, 1, 0] = tie(
        next_z(z2), other_y(z2), other_x(y1), *other_cores(z2, y1)
    )
    pieces[3, 0, 0, 0], pieces[2, 1, 0, 0], pieces[1, 1, 0, 1] = z3, y2, y1f
    z1f, y3, z3f, fetched, pieces[3, 0, 1, 0], pieces[0, 1, 1, 1], pieces[2, 1, 1, 0], pieces[1, 1, 1, 1] = tie(
        next_z(own_far), other_y(z3), other_x(z3), returned_rows(found), *other_cores(z3, y0f), *other_cores(y2, y1f)
    )
    pieces[1, 0, 0, 1], pieces[3, 1, 0, 0], pieces[3, 0, 0, 1] = z1f, y3, z3f
    pieces[3, 1, 1, 0] = other_core(y3)
    near = {key: piece for key, piece in pieces.items() if key[3] == 0}
    z2f, y3f, y2f = next_z(z1f), other_y(z3f), other_x(y2)
    near_done, y1f, z1f, z3f = tie(near_work(near, fetched), y1f, z1f, z3f)
    z2f, y3f, y2f, pieces[1, 0, 1, 1], pieces[3, 0, 1, 1] = tie(z2f, y3f, y2f, other_core(z1f), other_core(z3f))
    pieces[2, 0, 0, 1], pieces[3, 1, 0, 1], pieces[2, 1, 0, 1] = z2f, y3f, y2f
    pieces[2, 0, 1, 1], pieces[3, 1, 1, 1], pieces[2, 1, 1, 1] = other_core(z2f), other_core(y3f), other_core(y2f)
    return pieces, fetched, near_done


def placed(keys, pieces):
    me = lax.axis_index("mem")
    z, y, core = me // 4, (me // 2) % 2, me % 2
    for (steps, side, other, far), piece in zip(keys, pieces):
        at = place(ring_source(z, steps), 1 - y if side else y, 1 - core if other else core)
        yield at, piece


def wait_for(held, sem):
    pltpu.make_async_copy(held, held, sem).wait()


def lanes(held, blocks):
    return jnp.concatenate([held[:, j].reshape(-1, LANES) for j in blocks], axis=1)


def value_products(first, count, held, base, proj, cot, fetched, pick_grad):
    value_width = fetched.shape[1]
    parts = value_width // held.shape[-2]
    for e in range(count):
        block = jnp.concatenate(
            [held[m, base + e * parts:base + (e + 1) * parts].reshape(value_width, LANES) for m in range(held.shape[0])],
            axis=1,
        )
        grad = dot(cot, block, LAST).astype(BF16)
        pick_grad = jnp.where(proj == first + e, dot(grad, fetched, LAST), pick_grad)
    return pick_grad


def one_hot_keys(use_row, row_id, nkey):
    key_at = lax.broadcasted_iota(jnp.int32, (row_id.shape[0], nkey), 1)
    picked = jnp.where(use_row, row_id // nkey, row_id % nkey)
    return jnp.where(picked == key_at, 1.0, 0.0).astype(BF16)


def slot_ids(requests, rows_each):
    owners, capacity = requests.shape
    slots = owners * capacity
    rows = jnp.broadcast_to(requests[:, None, :], (owners, capacity, capacity)).reshape(slots, capacity)
    slot = lax.broadcasted_iota(jnp.int32, (slots, capacity), 0)
    lane = lax.broadcasted_iota(jnp.int32, (slots, capacity), 1)
    local = jnp.sum(jnp.where(slot % capacity == lane, jnp.maximum(rows, 0), 0), axis=1, keepdims=True)
    return local + slot[:, :1] // capacity * rows_each


def near_kernel(
    proj_count, rows_each, keys, requests_ref, pick_ref, tokens_ref, cot_ref, fetched_ref, *refs
):
    pick_grad_ref, queries_ref, slot_key_ref, counts_ref, wide_id_ref, proj_ref, held, sem = refs[-8:]
    for at, piece in placed(keys, refs[:-8]):
        pltpu.make_async_copy(piece, held.at[at], sem).start()
    x = lax.axis_index("groups")
    features = tokens_ref.shape[1]
    half = features // 2
    half_count = proj_count // 2
    parts = half_count * fetched_ref.shape[1] // held.shape[2]
    key = parts + half // LANES
    nkey = held.shape[0] * held.shape[2]
    wide_id = jnp.broadcast_to(slot_ids(requests_ref[...], rows_each), wide_id_ref.shape)
    wide_id_ref[...] = wide_id
    proj = (wide_id % nkey % proj_count).T[:proj_ref.shape[0]]
    proj_ref[...] = proj
    token_rows, slots = counts_ref.shape
    lane = lax.broadcasted_iota(jnp.int32, (token_rows, slots), 1)
    pick = pick_ref[...].T
    counts = jnp.zeros((token_rows, slots), F32)
    for k in range(pick.shape[1]):
        counts += jnp.where(pick[:, k:k + 1] == lane, 1.0, 0.0)
    counts_ref[...] = counts
    hot = one_hot_keys(x == 0, wide_id[:, :1], nkey)
    wait_for(held, sem)
    slot_key_ref[...] = dot(hot, lanes(held, range(key, held.shape[1])), PLAIN).astype(BF16)
    tokens = tokens_ref[:, pl.ds(pl.multiple_of(x * half, half), half)]
    queries_ref[...] = dot(tokens, lanes(held, range(parts, key)), LAST)
    pick_grad_ref[...] = value_products(
        x * half_count, half_count, held, 0, proj[:1], cot_ref[...], fetched_ref[...],
        jnp.zeros(pick_grad_ref.shape, F32),
    )


def dense_kernel(
    rank, width, proj_count, keys, core_ref, *refs
):
    inputs, refs = refs[:9], refs[9:]
    pieces = refs[:len(keys)]
    (out_ref, grad_ref, near_held, far_held, queries_held, pick_held, counts_held, cot_held, fetched_held,
     row_id_held, proj_held, near_key_held, tokens_held, mixed_values, query_grad, out_held, grad_held, piece_sem, in_sem, out_sem) = refs[len(keys):]
    held_inputs = (
        row_id_held, tokens_held, near_key_held, proj_held, queries_held, counts_held, cot_held, fetched_held, pick_held
    )
    x = lax.axis_index("groups")
    token_rows, features = tokens_held.shape
    slots, value_width = fetched_held.shape
    columns = far_held.shape[2]
    half = features // 2
    half_count = proj_count // 2
    parts = half_count * value_width // columns
    key = parts + half // LANES
    spots = list(placed(keys, pieces))
    far = [spot for spot, k in zip(spots, keys) if k[3]]
    near = [spot for spot, k in zip(spots, keys) if not k[3]]
    query_blocks = pl.ds(parts, far_held.shape[1] - parts)
    copies = [pltpu.make_async_copy(a, b, in_sem.at[i]) for i, (a, b) in enumerate(zip(inputs, held_inputs))]
    copies[0].start()
    for at, piece in far:
        pltpu.make_async_copy(piece.at[query_blocks], far_held.at[at, query_blocks], piece_sem.at[0]).start()
    for copy in copies[1:6]:
        copy.start()
    for at, piece in far:
        pltpu.make_async_copy(piece.at[pl.ds(0, parts)], far_held.at[at, pl.ds(0, parts)], piece_sem.at[1]).start()
    for copy in copies[6:]:
        copy.start()
    for at, piece in near:
        pltpu.make_async_copy(piece, near_held.at[at], piece_sem.at[2]).start()

    copies[0].wait()
    hot = one_hot_keys(x != 0, row_id_held[:, :1], far_held.shape[0] * columns)
    wait_for(far_held.at[:, query_blocks], piece_sem.at[0])
    for copy in copies[1:6]:
        copy.wait()
    far_key = dot(hot, lanes(far_held, range(key, far_held.shape[1])), PLAIN).astype(BF16)
    near_key = near_key_held[...]
    slot_row = jnp.where(x == 0, near_key, far_key)
    slot_col = jnp.where(x == 0, far_key, near_key)
    tokens = tokens_held[:, pl.ds(pl.multiple_of((1 - x) * half, half), half)]
    queries = (dot(tokens, lanes(far_held, range(parts, key)), LAST) + queries_held[...]).astype(BF16)
    block = [queries[:, r * width:(r + 1) * width] for r in range(2 * rank)]
    row_scores = [dot(block[r], slot_row, LAST) for r in range(rank)]
    col_scores = [dot(block[rank + r], slot_col, LAST) for r in range(rank)]
    wait_for(far_held.at[:, pl.ds(0, parts)], piece_sem.at[1])
    for copy in copies[6:]:
        copy.wait()
    wait_for(near_held, piece_sem.at[2])
    proj = proj_held[:1]
    fetched = fetched_held[...]
    pick_grad = value_products(
        (1 - x) * half_count, half_count, far_held, 0, proj, cot_held[...], fetched, pick_held[...]
    )
    col_mixed = [sum(core_ref[r, s] * col_scores[s] for s in range(rank)) for r in range(rank)]
    row_mixed = [sum(row_scores[r] * core_ref[r, s] for r in range(rank)) for s in range(rank)]
    score = sum(row_scores[r] * col_mixed[r] for r in range(rank))
    gate = 1.0 / (1.0 + jnp.exp(-score))
    counts = counts_held[...]
    weights = (counts * gate.astype(BF16).astype(F32)).astype(BF16)
    slope = gate * (1.0 - gate)
    for i in range(proj_count):
        e = (x if i < half_count else 1 - x) * half_count + i % half_count
        mixed = dot(jnp.where(proj == e, weights, jnp.zeros((), BF16)), fetched, PLAIN)
        mixed_values[:, i * value_width:(i + 1) * value_width] = mixed.astype(BF16)

    members = far_held.shape[0] // 4
    step = features // 4
    sides = ((near_held, x), (far_held, 1 - x))
    for c in range(4):
        cols = pl.ds(c * step, step)
        block = jnp.concatenate([
            jnp.concatenate([held[m, :parts].reshape(-1, LANES) for m in range(c * members, (c + 1) * members)], axis=1)
            for held, _ in sides
        ], axis=0)
        out_held[:, cols] = dot(mixed_values[...], block, PLAIN).astype(BF16)
        pltpu.make_async_copy(out_held.at[:, cols], out_ref.at[:, cols], out_sem.at[0]).start()
    score_grad = pick_grad * slope
    for i, factor in enumerate(col_mixed + row_mixed):
        slot_key = slot_row if i < rank else slot_col
        grad = ((score_grad * factor).astype(BF16).astype(F32) * counts).astype(BF16)
        query_grad[:, i * width:(i + 1) * width] = dot(grad, slot_key, PLAIN).astype(BF16)
    for c in range(4):
        held, side = sides[c // 2]
        blocks = step // LANES
        first = parts + (c % 2) * blocks
        cols = pl.ds(pl.multiple_of(side * half + (c % 2) * step, step), step)
        grad_held[:, cols] = dot(query_grad[...], lanes(held, range(first, first + blocks)), PLAIN).astype(BF16)
        pltpu.make_async_copy(grad_held.at[:, cols], grad_ref.at[:, cols], out_sem.at[1]).start()
    pltpu.make_async_copy(out_held, out_ref, out_sem.at[0]).wait()
    pltpu.make_async_copy(grad_held, grad_ref, out_sem.at[1]).wait()


def vmem():
    return pl.BlockSpec(memory_space=pltpu.VMEM)


def smem():
    return pl.BlockSpec(memory_space=pltpu.SMEM)


def anywhere():
    return pl.BlockSpec(memory_space=pl.ANY)


def pieces_path(tokens, cotangent, w_query, key_row, key_col, tucker_core, proj_part, requests, table, row_id,
                slot_proj, pick_slot, nkey, proj_count):
    rank = tucker_core.shape[0]
    width = key_row.shape[1]
    token_rows, features = tokens.shape
    slots = row_id.shape[0]
    value_width = table.shape[1]
    columns = w_query.shape[1]
    own_near, own_far = own_halves(w_query, key_row, key_col, proj_part)
    params = pltpu.CompilerParams(vmem_limit_bytes=VMEM_LIMIT)
    members = nkey // columns
    plane = jax.ShapeDtypeStruct((token_rows, slots), F32)
    partial = jax.ShapeDtypeStruct((token_rows, 2 * rank * width), F32)
    held = pltpu.VMEM((members,) + own_near.shape, BF16)

    def near_work(near, fetched):
        return pl.pallas_call(
            functools.partial(near_kernel, proj_count, table.shape[0], tuple(near)),
            out_shape=(
                plane, partial, jax.ShapeDtypeStruct((slots, width), BF16), plane,
                jax.ShapeDtypeStruct((slots, LANES), jnp.int32), jax.ShapeDtypeStruct((8, slots), jnp.int32),
            ),
            in_specs=[vmem()] * 5 + [anywhere()] * len(near),
            out_specs=(vmem(),) * 6,
            scratch_shapes=[held, pltpu.SemaphoreType.DMA],
            compiler_params=params,
            cost_estimate=pl.CostEstimate(flops=5 * 10**9, bytes_accessed=10**7, transcendentals=0),
            name="near",
        )(requests, pick_slot.T, tokens, cotangent, fetched.reshape(slots, value_width), *near.values())

    pieces, fetched, near_done = gather_pieces(own_near, own_far, requests, table, near_work)
    pick_grad, queries, near_key, counts, wide_id, slot_proj = near_done
    keys = tuple(pieces)
    tall = (token_rows, features)
    return pl.pallas_call(
        functools.partial(dense_kernel, rank, width, proj_count, keys),
        out_shape=(jax.ShapeDtypeStruct(tall, BF16),) * 2,
        in_specs=[smem()] + [anywhere()] * (9 + len(keys)),
        out_specs=(anywhere(), anywhere()),
        scratch_shapes=[
            held,
            held,
            pltpu.VMEM(partial.shape, F32),
            pltpu.VMEM(plane.shape, F32),
            pltpu.VMEM(plane.shape, F32),
            pltpu.VMEM(tall, BF16),
            pltpu.VMEM((slots, value_width), BF16),
            pltpu.VMEM(wide_id.shape, jnp.int32),
            pltpu.VMEM(slot_proj.shape, jnp.int32),
            pltpu.VMEM(near_key.shape, BF16),
            pltpu.VMEM(tall, BF16),
            pltpu.VMEM((token_rows, proj_count * value_width), BF16),
            pltpu.VMEM(partial.shape, BF16),
            pltpu.VMEM(tall, BF16),
            pltpu.VMEM(tall, BF16),
            pltpu.SemaphoreType.DMA((3,)),
            pltpu.SemaphoreType.DMA((9,)),
            pltpu.SemaphoreType.DMA((2,)),
        ],
        compiler_params=params,
        cost_estimate=pl.CostEstimate(flops=10**10, bytes_accessed=2 * 10**7, transcendentals=10**5),
        name="dense",
    )(
        tucker_core, wide_id, tokens, near_key, slot_proj, queries, counts, cotangent,
        fetched.reshape(slots, value_width), pick_grad, *pieces.values(),
    )


def whole_path(tokens, cotangent, w_query, key_row, key_col, tucker_core, proj_part, requests, table, row_id,
               slot_proj, pick_slot, nkey, proj_count):
    rank = tucker_core.shape[0]
    width = key_row.shape[1]
    slots = row_id.shape[0]
    fetched = returned_rows(found_rows(wanted_rows(requests), table)).reshape(slots, -1)
    query_full = lax.all_gather(w_query.T, "mem", axis=0, tiled=True)
    keys = lax.all_gather(jnp.concatenate([key_row, key_col], axis=1), "mem", axis=0, tiled=True)
    proj_full = lax.all_gather(proj_part, "mem", axis=1, tiled=True)
    key_at = jnp.arange(nkey, dtype=jnp.int32)[None, :]
    row_hot = ((row_id // nkey)[:, None] == key_at).astype(BF16)
    col_hot = ((row_id % nkey)[:, None] == key_at).astype(BF16)
    slot_row = dot(row_hot, keys[:, :width], PLAIN).astype(BF16)
    slot_col = dot(col_hot, keys[:, width:], PLAIN).astype(BF16)
    spread = jnp.where(
        slot_proj[:, None, None] == jnp.arange(proj_count, dtype=jnp.int32)[None, :, None],
        fetched[:, None, :], jnp.zeros((), BF16)
    ).reshape(slots, -1)
    counts = jnp.sum(
        (pick_slot[:, :, None] == jnp.arange(slots, dtype=jnp.int32)[None, None, :]).astype(F32), axis=1
    )
    queries = dot(tokens, query_full, LAST).astype(BF16)
    row_scores = [dot(queries[:, r * width:(r + 1) * width], slot_row, LAST) for r in range(rank)]
    col_scores = [
        dot(queries[:, (rank + r) * width:(rank + r + 1) * width], slot_col, LAST) for r in range(rank)
    ]
    col_mixed = [sum(tucker_core[r, s] * col_scores[s] for s in range(rank)) for r in range(rank)]
    row_mixed = [sum(row_scores[r] * tucker_core[r, s] for r in range(rank)) for s in range(rank)]
    score = sum(row_scores[r] * col_mixed[r] for r in range(rank))
    gate = jax.nn.sigmoid(score)
    weights = counts * gate.astype(BF16).astype(F32)
    mixed = counted_dot(weights, spread, PLAIN).astype(BF16)
    memory_out = dot(mixed, proj_full, PLAIN)
    value_grad = dot(cotangent, proj_full, LAST).astype(BF16)
    pick_grad = dot(value_grad, spread, LAST)
    score_grad = pick_grad * gate * (1.0 - gate)
    blocks = []
    for mixed_scores, slot_key in ((col_mixed, slot_row), (row_mixed, slot_col)):
        for r in range(rank):
            grad = (score_grad * mixed_scores[r]).astype(BF16).astype(F32) * counts
            blocks.append(counted_dot(grad, slot_key, PLAIN).astype(BF16))
    query_grad = jnp.concatenate(blocks, axis=1)
    token_grad = dot(query_grad, query_full, PLAIN)
    return memory_out.astype(BF16), token_grad.astype(BF16)


def shards(
    mem, tokens, cotangent, w_query, key_row, key_col, tucker_core, table, w_proj, send_ids, pick_slot
):
    proj_count, value_width, _ = w_proj.shape
    requests = send_ids[0]
    owners, capacity = requests.shape
    slots = owners * capacity
    nkey = key_row.shape[0] * mem
    row_id = jnp.maximum(requests, 0) + jnp.arange(owners, dtype=jnp.int32)[:, None] * table.shape[0]
    row_id = row_id.reshape(slots)
    slot_proj = (row_id % nkey) % proj_count
    proj_part = w_proj.reshape(proj_count * value_width, -1)
    path = pieces_path if mem == 16 and w_proj.shape[2] == LANES else whole_path
    return path(tokens, cotangent, w_query, key_row, key_col, tucker_core, proj_part, requests, table, row_id,
                slot_proj, pick_slot, nkey, proj_count)


def solution(mesh):
    in_specs = (
        P(("groups", "mem"), None),
        P(("groups", "mem"), None),
        P(None, "mem"),
        P("mem", None),
        P("mem", None),
        P(),
        P("mem", None),
        P(None, None, "mem"),
        P(("groups", "mem"), None, None),
        P(("groups", "mem"), None),
    )
    out_specs = (P(("groups", "mem"), None), P(("groups", "mem"), None))
    body = functools.partial(shards, mesh.shape["mem"])
    return jax.shard_map(body, mesh=mesh, in_specs=in_specs, out_specs=out_specs, check_vma=False)
```

```python
import functools

import jax
import jax.numpy as jnp
from jax import lax
from jax.experimental import pallas as pl
from jax.experimental.pallas import tpu as pltpu
from jax.sharding import PartitionSpec as P

F32 = jnp.float32
BF16 = jnp.bfloat16
RING = (0, 2, 3, 1)
LANES = 128
LAST = ((1,), (1,))
PLAIN = ((1,), (0,))
VMEM_LIMIT = 56 * 1024 * 1024


def dot(a, b, dims):
    return lax.dot_general(a, b, (dims, ((), ())), preferred_element_type=F32)


def two_terms(x):
    high = x.astype(BF16)
    return high, (x - high.astype(F32)).astype(BF16)


def counted_dot(x, b, dims):
    high, low = two_terms(x)
    return dot(high, b, dims) + dot(low, b, dims)


def wanted_rows(requests):
    return lax.all_to_all(requests, "mem", split_axis=0, concat_axis=0, tiled=True)


def found_rows(wanted, table):
    found = jnp.take(table, jnp.maximum(wanted, 0).reshape(-1), axis=0, mode="clip")
    return found.reshape(wanted.shape + (table.shape[1],))


def returned_rows(found):
    return lax.all_to_all(found, "mem", split_axis=0, concat_axis=0, tiled=True)


def place(z, y, core):
    return (z * 2 + y) * 2 + core


def everywhere(move):
    pairs = []
    for z in range(4):
        for y in range(2):
            for core in range(2):
                pairs.append((place(z, y, core), place(*move(z, y, core))))
    return pairs


def next_z(x):
    step = {RING[i]: RING[(i + 1) % 4] for i in range(4)}
    return lax.ppermute(x, "mem", everywhere(lambda z, y, c: (step[z], y, c)))


def other_y(x):
    return lax.ppermute(x, "mem", everywhere(lambda z, y, c: (z, 1 - y, c)))


def other_core(x):
    return lax.ppermute(x, "mem", everywhere(lambda z, y, c: (z, y, 1 - c)))


def other_x(x):
    return lax.ppermute(x, "groups", [(0, 1), (1, 0)])


def ring_source(z, steps):
    index = jnp.where(z == 0, 0, jnp.where(z == 2, 1, jnp.where(z == 3, 2, 3)))
    index = (index + 4 - steps) % 4
    return jnp.where(index == 0, 0, jnp.where(index == 1, 2, jnp.where(index == 2, 3, 1)))


def tie(*values):
    return lax.optimization_barrier(values)


def halves_kernel(query_ref, key_row_ref, key_col_ref, proj_ref, near_ref, far_ref):
    x = lax.axis_index("groups")
    parts = proj_ref.shape[1]
    blocks = query_ref.shape[1] // LANES // 2
    for target, half in ((near_ref, x), (far_ref, 1 - x)):
        target[:parts] = proj_ref[half]
        for j in range(blocks):
            target[parts + j] = query_ref[:, pl.ds(pl.multiple_of((half * blocks + j) * LANES, LANES), LANES)]
        for j in range(key_row_ref.shape[1] // LANES):
            cols = slice(j * LANES, (j + 1) * LANES)
            target[parts + blocks + j] = jnp.where(half == 0, key_row_ref[:, cols], key_col_ref[:, cols])


def own_halves(w_query, key_row, key_col, proj_part):
    features, columns = w_query.shape
    proj = proj_part.reshape(2, -1, columns, LANES)
    blocks = proj.shape[1] + (features // 2 + key_row.shape[1]) // LANES
    half = jax.ShapeDtypeStruct((blocks, columns, LANES), BF16)
    return pl.pallas_call(
        halves_kernel,
        out_shape=(half, half),
        in_specs=[vmem()] * 4,
        out_specs=(vmem(), vmem()),
        compiler_params=pltpu.CompilerParams(vmem_limit_bytes=VMEM_LIMIT),
        cost_estimate=pl.CostEstimate(flops=0, bytes_accessed=4 * 10**6, transcendentals=0),
        name="halves",
    )(w_query.T, key_row, key_col, proj)


def other_cores(first, second):
    first = other_core(first)
    second, first = tie(second, first)
    return first, other_core(second)


def gather_pieces(own_near, own_far, requests, table, near_work):
    pieces = {(0, 0, 0, 0): own_near, (0, 0, 0, 1): own_far}
    z1, y0, wanted, pieces[0, 0, 1, 0], pieces[0, 0, 1, 1] = tie(
        next_z(own_near), other_y(own_near), wanted_rows(requests), other_core(own_near), other_core(own_far)
    )
    pieces[1, 0, 0, 0], pieces[0, 1, 0, 0] = z1, y0
    z2, y1, y0f, found, pieces[1, 0, 1, 0], pieces[0, 1, 1, 0] = tie(
        next_z(z1), other_y(z1), other_x(y0), found_rows(wanted, table), *other_cores(z1, y0)
    )
    pieces[2, 0, 0, 0], pieces[1, 1, 0, 0], pieces[0, 1, 0, 1] = z2, y1, y0f
    z3, y2, y1f, pieces[2, 0, 1, 0], pieces[1, 1, 1, 0] = tie(
        next_z(z2), other_y(z2), other_x(y1), *other_cores(z2, y1)
    )
    pieces[3, 0, 0, 0], pieces[2, 1, 0, 0], pieces[1, 1, 0, 1] = z3, y2, y1f
    fetched = returned_rows(found)
    z1f, y3, z3f, pieces[3, 0, 1, 0], pieces[0, 1, 1, 1], pieces[2, 1, 1, 0], pieces[1, 1, 1, 1] = tie(
        next_z(own_far), other_y(z3), other_x(z3), *other_cores(z3, y0f), *other_cores(y2, y1f)
    )
    pieces[1, 0, 0, 1], pieces[3, 1, 0, 0], pieces[3, 0, 0, 1] = z1f, y3, z3f
    pieces[3, 1, 1, 0] = other_core(y3)
    near = {key: piece for key, piece in pieces.items() if key[3] == 0}
    z2f, y3f, y2f = next_z(z1f), other_y(z3f), other_x(y2)
    near_done, y1f, z1f, z3f = tie(near_work(near, fetched), y1f, z1f, z3f)
    z2f, y3f, y2f, pieces[1, 0, 1, 1], pieces[3, 0, 1, 1] = tie(z2f, y3f, y2f, other_core(z1f), other_core(z3f))
    pieces[2, 0, 0, 1], pieces[3, 1, 0, 1], pieces[2, 1, 0, 1] = z2f, y3f, y2f
    pieces[2, 0, 1, 1], pieces[3, 1, 1, 1], pieces[2, 1, 1, 1] = other_core(z2f), other_core(y3f), other_core(y2f)
    return pieces, fetched, near_done


def placed(keys, pieces):
    me = lax.axis_index("mem")
    z, y, core = me // 4, (me // 2) % 2, me % 2
    for (steps, side, other, far), piece in zip(keys, pieces):
        at = place(ring_source(z, steps), 1 - y if side else y, 1 - core if other else core)
        yield at, piece


def wait_for(held, sem):
    pltpu.make_async_copy(held, held, sem).wait()


def lanes(held, blocks):
    return jnp.concatenate([held[:, j].reshape(-1, LANES) for j in blocks], axis=1)


def value_products(first, count, held, base, proj, cot, fetched, pick_grad):
    value_width = fetched.shape[1]
    parts = value_width // held.shape[-2]
    for e in range(count):
        block = jnp.concatenate(
            [held[m, base + e * parts:base + (e + 1) * parts].reshape(value_width, LANES) for m in range(held.shape[0])],
            axis=1,
        )
        grad = dot(cot, block, LAST).astype(BF16)
        pick_grad = jnp.where(proj == first + e, dot(grad, fetched, LAST), pick_grad)
    return pick_grad


def one_hot_keys(use_row, row_id, nkey):
    key_at = lax.broadcasted_iota(jnp.int32, (row_id.shape[0], nkey), 1)
    picked = jnp.where(use_row, row_id // nkey, row_id % nkey)
    return jnp.where(picked == key_at, 1.0, 0.0).astype(BF16)


def slot_ids(requests, rows_each):
    owners, capacity = requests.shape
    slots = owners * capacity
    rows = jnp.broadcast_to(requests[:, None, :], (owners, capacity, capacity)).reshape(slots, capacity)
    slot = lax.broadcasted_iota(jnp.int32, (slots, capacity), 0)
    lane = lax.broadcasted_iota(jnp.int32, (slots, capacity), 1)
    local = jnp.sum(jnp.where(slot % capacity == lane, jnp.maximum(rows, 0), 0), axis=1, keepdims=True)
    return local + slot[:, :1] // capacity * rows_each


def near_kernel(
    proj_count, rows_each, keys, requests_ref, pick_ref, tokens_ref, cot_ref, fetched_ref, *refs
):
    pick_grad_ref, queries_ref, slot_key_ref, counts_ref, wide_id_ref, proj_ref, held, sem = refs[-8:]
    for at, piece in placed(keys, refs[:-8]):
        pltpu.make_async_copy(piece, held.at[at], sem).start()
    x = lax.axis_index("groups")
    features = tokens_ref.shape[1]
    half = features // 2
    half_count = proj_count // 2
    parts = half_count * fetched_ref.shape[1] // held.shape[2]
    key = parts + half // LANES
    nkey = held.shape[0] * held.shape[2]
    wide_id = jnp.broadcast_to(slot_ids(requests_ref[...], rows_each), wide_id_ref.shape)
    wide_id_ref[...] = wide_id
    proj = (wide_id % nkey % proj_count).T[:proj_ref.shape[0]]
    proj_ref[...] = proj
    token_rows, slots = counts_ref.shape
    lane = lax.broadcasted_iota(jnp.int32, (token_rows, slots), 1)
    pick = pick_ref[...].T
    counts = jnp.zeros((token_rows, slots), F32)
    for k in range(pick.shape[1]):
        counts += jnp.where(pick[:, k:k + 1] == lane, 1.0, 0.0)
    counts_ref[...] = counts
    hot = one_hot_keys(x == 0, wide_id[:, :1], nkey)
    wait_for(held, sem)
    slot_key_ref[...] = dot(hot, lanes(held, range(key, held.shape[1])), PLAIN).astype(BF16)
    tokens = tokens_ref[:, pl.ds(pl.multiple_of(x * half, half), half)]
    queries_ref[...] = dot(tokens, lanes(held, range(parts, key)), LAST)
    pick_grad_ref[...] = value_products(
        x * half_count, half_count, held, 0, proj[:1], cot_ref[...], fetched_ref[...],
        jnp.zeros(pick_grad_ref.shape, F32),
    )


def dense_kernel(
    rank, width, proj_count, keys, core_ref, *refs
):
    inputs, refs = refs[:9], refs[9:]
    pieces = refs[:len(keys)]
    (out_ref, grad_ref, near_held, far_held, queries_held, pick_held, counts_held, cot_held, fetched_held,
     row_id_held, proj_held, near_key_held, tokens_held, mixed_values, query_grad, out_held, grad_held, piece_sem, in_sem, out_sem) = refs[len(keys):]
    held_inputs = (
        row_id_held, tokens_held, near_key_held, proj_held, queries_held, counts_held, cot_held, fetched_held, pick_held
    )
    x = lax.axis_index("groups")
    token_rows, features = tokens_held.shape
    slots, value_width = fetched_held.shape
    columns = far_held.shape[2]
    half = features // 2
    half_count = proj_count // 2
    parts = half_count * value_width // columns
    key = parts + half // LANES
    spots = list(placed(keys, pieces))
    far = [spot for spot, k in zip(spots, keys) if k[3]]
    near = [spot for spot, k in zip(spots, keys) if not k[3]]
    query_blocks = pl.ds(parts, far_held.shape[1] - parts)
    copies = [pltpu.make_async_copy(a, b, in_sem.at[i]) for i, (a, b) in enumerate(zip(inputs, held_inputs))]
    copies[0].start()
    for at, piece in far:
        pltpu.make_async_copy(piece.at[query_blocks], far_held.at[at, query_blocks], piece_sem.at[0]).start()
    for copy in copies[1:6]:
        copy.start()
    for at, piece in far:
        pltpu.make_async_copy(piece.at[pl.ds(0, parts)], far_held.at[at, pl.ds(0, parts)], piece_sem.at[1]).start()
    for copy in copies[6:]:
        copy.start()
    for at, piece in near:
        pltpu.make_async_copy(piece, near_held.at[at], piece_sem.at[2]).start()

    copies[0].wait()
    hot = one_hot_keys(x != 0, row_id_held[:, :1], far_held.shape[0] * columns)
    wait_for(far_held.at[:, query_blocks], piece_sem.at[0])
    for copy in copies[1:6]:
        copy.wait()
    far_key = dot(hot, lanes(far_held, range(key, far_held.shape[1])), PLAIN).astype(BF16)
    near_key = near_key_held[...]
    slot_row = jnp.where(x == 0, near_key, far_key)
    slot_col = jnp.where(x == 0, far_key, near_key)
    tokens = tokens_held[:, pl.ds(pl.multiple_of((1 - x) * half, half), half)]
    queries = (dot(tokens, lanes(far_held, range(parts, key)), LAST) + queries_held[...]).astype(BF16)
    block = [queries[:, r * width:(r + 1) * width] for r in range(2 * rank)]
    row_scores = [dot(block[r], slot_row, LAST) for r in range(rank)]
    col_scores = [dot(block[rank + r], slot_col, LAST) for r in range(rank)]
    wait_for(far_held.at[:, pl.ds(0, parts)], piece_sem.at[1])
    for copy in copies[6:]:
        copy.wait()
    wait_for(near_held, piece_sem.at[2])
    proj = proj_held[:1]
    fetched = fetched_held[...]
    pick_grad = value_products(
        (1 - x) * half_count, half_count, far_held, 0, proj, cot_held[...], fetched, pick_held[...]
    )
    col_mixed = [sum(core_ref[r, s] * col_scores[s] for s in range(rank)) for r in range(rank)]
    row_mixed = [sum(row_scores[r] * core_ref[r, s] for r in range(rank)) for s in range(rank)]
    score = sum(row_scores[r] * col_mixed[r] for r in range(rank))
    gate = 1.0 / (1.0 + jnp.exp(-score))
    counts = counts_held[...]
    weights = (counts * gate.astype(BF16).astype(F32)).astype(BF16)
    slope = gate * (1.0 - gate)
    for i in range(proj_count):
        e = (x if i < half_count else 1 - x) * half_count + i % half_count
        mixed = dot(jnp.where(proj == e, weights, jnp.zeros((), BF16)), fetched, PLAIN)
        mixed_values[:, i * value_width:(i + 1) * value_width] = mixed.astype(BF16)

    members = far_held.shape[0] // 4
    step = features // 4
    sides = ((near_held, x), (far_held, 1 - x))
    for c in range(4):
        cols = pl.ds(c * step, step)
        block = jnp.concatenate([
            jnp.concatenate([held[m, :parts].reshape(-1, LANES) for m in range(c * members, (c + 1) * members)], axis=1)
            for held, _ in sides
        ], axis=0)
        out_held[:, cols] = dot(mixed_values[...], block, PLAIN).astype(BF16)
        pltpu.make_async_copy(out_held.at[:, cols], out_ref.at[:, cols], out_sem.at[0]).start()
    score_grad = pick_grad * slope
    for i, factor in enumerate(col_mixed + row_mixed):
        slot_key = slot_row if i < rank else slot_col
        grad = ((score_grad * factor).astype(BF16).astype(F32) * counts).astype(BF16)
        query_grad[:, i * width:(i + 1) * width] = dot(grad, slot_key, PLAIN).astype(BF16)
    for c in range(4):
        held, side = sides[c // 2]
        blocks = step // LANES
        first = parts + (c % 2) * blocks
        cols = pl.ds(pl.multiple_of(side * half + (c % 2) * step, step), step)
        grad_held[:, cols] = dot(query_grad[...], lanes(held, range(first, first + blocks)), PLAIN).astype(BF16)
        pltpu.make_async_copy(grad_held.at[:, cols], grad_ref.at[:, cols], out_sem.at[1]).start()
    pltpu.make_async_copy(out_held, out_ref, out_sem.at[0]).wait()
    pltpu.make_async_copy(grad_held, grad_ref, out_sem.at[1]).wait()


def vmem():
    return pl.BlockSpec(memory_space=pltpu.VMEM)


def smem():
    return pl.BlockSpec(memory_space=pltpu.SMEM)


def anywhere():
    return pl.BlockSpec(memory_space=pl.ANY)


def pieces_path(tokens, cotangent, w_query, key_row, key_col, tucker_core, proj_part, requests, table, row_id,
                slot_proj, pick_slot, nkey, proj_count):
    rank = tucker_core.shape[0]
    width = key_row.shape[1]
    token_rows, features = tokens.shape
    slots = row_id.shape[0]
    value_width = table.shape[1]
    columns = w_query.shape[1]
    own_near, own_far = own_halves(w_query, key_row, key_col, proj_part)
    params = pltpu.CompilerParams(vmem_limit_bytes=VMEM_LIMIT)
    members = nkey // columns
    plane = jax.ShapeDtypeStruct((token_rows, slots), F32)
    partial = jax.ShapeDtypeStruct((token_rows, 2 * rank * width), F32)
    held = pltpu.VMEM((members,) + own_near.shape, BF16)

    def near_work(near, fetched):
        return pl.pallas_call(
            functools.partial(near_kernel, proj_count, table.shape[0], tuple(near)),
            out_shape=(
                plane, partial, jax.ShapeDtypeStruct((slots, width), BF16), plane,
                jax.ShapeDtypeStruct((slots, LANES), jnp.int32), jax.ShapeDtypeStruct((8, slots), jnp.int32),
            ),
            in_specs=[vmem()] * 5 + [anywhere()] * len(near),
            out_specs=(vmem(),) * 6,
            scratch_shapes=[held, pltpu.SemaphoreType.DMA],
            compiler_params=params,
            cost_estimate=pl.CostEstimate(flops=5 * 10**9, bytes_accessed=10**7, transcendentals=0),
            name="near",
        )(requests, pick_slot.T, tokens, cotangent, fetched.reshape(slots, value_width), *near.values())

    pieces, fetched, near_done = gather_pieces(own_near, own_far, requests, table, near_work)
    pick_grad, queries, near_key, counts, wide_id, slot_proj = near_done
    keys = tuple(pieces)
    tall = (token_rows, features)
    return pl.pallas_call(
        functools.partial(dense_kernel, rank, width, proj_count, keys),
        out_shape=(jax.ShapeDtypeStruct(tall, BF16),) * 2,
        in_specs=[smem()] + [anywhere()] * (9 + len(keys)),
        out_specs=(anywhere(), anywhere()),
        scratch_shapes=[
            held,
            held,
            pltpu.VMEM(partial.shape, F32),
            pltpu.VMEM(plane.shape, F32),
            pltpu.VMEM(plane.shape, F32),
            pltpu.VMEM(tall, BF16),
            pltpu.VMEM((slots, value_width), BF16),
            pltpu.VMEM(wide_id.shape, jnp.int32),
            pltpu.VMEM(slot_proj.shape, jnp.int32),
            pltpu.VMEM(near_key.shape, BF16),
            pltpu.VMEM(tall, BF16),
            pltpu.VMEM((token_rows, proj_count * value_width), BF16),
            pltpu.VMEM(partial.shape, BF16),
            pltpu.VMEM(tall, BF16),
            pltpu.VMEM(tall, BF16),
            pltpu.SemaphoreType.DMA((3,)),
            pltpu.SemaphoreType.DMA((9,)),
            pltpu.SemaphoreType.DMA((2,)),
        ],
        compiler_params=params,
        cost_estimate=pl.CostEstimate(flops=10**10, bytes_accessed=2 * 10**7, transcendentals=10**5),
        name="dense",
    )(
        tucker_core, wide_id, tokens, near_key, slot_proj, queries, counts, cotangent,
        fetched.reshape(slots, value_width), pick_grad, *pieces.values(),
    )


def whole_path(tokens, cotangent, w_query, key_row, key_col, tucker_core, proj_part, requests, table, row_id,
               slot_proj, pick_slot, nkey, proj_count):
    rank = tucker_core.shape[0]
    width = key_row.shape[1]
    slots = row_id.shape[0]
    fetched = returned_rows(found_rows(wanted_rows(requests), table)).reshape(slots, -1)
    query_full = lax.all_gather(w_query.T, "mem", axis=0, tiled=True)
    keys = lax.all_gather(jnp.concatenate([key_row, key_col], axis=1), "mem", axis=0, tiled=True)
    proj_full = lax.all_gather(proj_part, "mem", axis=1, tiled=True)
    key_at = jnp.arange(nkey, dtype=jnp.int32)[None, :]
    row_hot = ((row_id // nkey)[:, None] == key_at).astype(BF16)
    col_hot = ((row_id % nkey)[:, None] == key_at).astype(BF16)
    slot_row = dot(row_hot, keys[:, :width], PLAIN).astype(BF16)
    slot_col = dot(col_hot, keys[:, width:], PLAIN).astype(BF16)
    spread = jnp.where(
        slot_proj[:, None, None] == jnp.arange(proj_count, dtype=jnp.int32)[None, :, None],
        fetched[:, None, :], jnp.zeros((), BF16)
    ).reshape(slots, -1)
    counts = jnp.sum(
        (pick_slot[:, :, None] == jnp.arange(slots, dtype=jnp.int32)[None, None, :]).astype(F32), axis=1
    )
    queries = dot(tokens, query_full, LAST).astype(BF16)
    row_scores = [dot(queries[:, r * width:(r + 1) * width], slot_row, LAST) for r in range(rank)]
    col_scores = [
        dot(queries[:, (rank + r) * width:(rank + r + 1) * width], slot_col, LAST) for r in range(rank)
    ]
    col_mixed = [sum(tucker_core[r, s] * col_scores[s] for s in range(rank)) for r in range(rank)]
    row_mixed = [sum(row_scores[r] * tucker_core[r, s] for r in range(rank)) for s in range(rank)]
    score = sum(row_scores[r] * col_mixed[r] for r in range(rank))
    gate = jax.nn.sigmoid(score)
    weights = counts * gate.astype(BF16).astype(F32)
    mixed = counted_dot(weights, spread, PLAIN).astype(BF16)
    memory_out = dot(mixed, proj_full, PLAIN)
    value_grad = dot(cotangent, proj_full, LAST).astype(BF16)
    pick_grad = dot(value_grad, spread, LAST)
    score_grad = pick_grad * gate * (1.0 - gate)
    blocks = []
    for mixed_scores, slot_key in ((col_mixed, slot_row), (row_mixed, slot_col)):
        for r in range(rank):
            grad = (score_grad * mixed_scores[r]).astype(BF16).astype(F32) * counts
            blocks.append(counted_dot(grad, slot_key, PLAIN).astype(BF16))
    query_grad = jnp.concatenate(blocks, axis=1)
    token_grad = dot(query_grad, query_full, PLAIN)
    return memory_out.astype(BF16), token_grad.astype(BF16)


def shards(
    mem, tokens, cotangent, w_query, key_row, key_col, tucker_core, table, w_proj, send_ids, pick_slot
):
    proj_count, value_width, _ = w_proj.shape
    requests = send_ids[0]
    owners, capacity = requests.shape
    slots = owners * capacity
    nkey = key_row.shape[0] * mem
    row_id = jnp.maximum(requests, 0) + jnp.arange(owners, dtype=jnp.int32)[:, None] * table.shape[0]
    row_id = row_id.reshape(slots)
    slot_proj = (row_id % nkey) % proj_count
    proj_part = w_proj.reshape(proj_count * value_width, -1)
    path = pieces_path if mem == 16 and w_proj.shape[2] == LANES else whole_path
    return path(tokens, cotangent, w_query, key_row, key_col, tucker_core, proj_part, requests, table, row_id,
                slot_proj, pick_slot, nkey, proj_count)


def solution(mesh):
    in_specs = (
        P(("groups", "mem"), None),
        P(("groups", "mem"), None),
        P(None, "mem"),
        P("mem", None),
        P("mem", None),
        P(),
        P("mem", None),
        P(None, None, "mem"),
        P(("groups", "mem"), None, None),
        P(("groups", "mem"), None),
    )
    out_specs = (P(("groups", "mem"), None), P(("groups", "mem"), None))
    body = functools.partial(shards, mesh.shape["mem"])
    return jax.shard_map(body, mesh=mesh, in_specs=in_specs, out_specs=out_specs, check_vma=False)
```
